32 devices in a mesh: rep: 2 (over y), shard: 16 (over z, x, core).
Axes of the slice: x: 2, y: 2, z: 4, core: 2. Of those that a mesh axis runs over, the one named last changes fastest.
Arguments:
- inputs: bfloat16 [32, 256, 768], P(('rep', 'shard')), may hold values from -6 to 6
- segment_ids: int32 [32, 256], P(('rep', 'shard')), may hold values from 0 to 3, never falling along the last dimension, each value on 1 to 170 neighbouring positions
- qkv_weight: bfloat16 [2, 768, 2304], P(None, 'shard'), may hold values from -0.21875 to 0.21875
- out_weight: bfloat16 [2, 768, 768], P(None, 'shard'), may hold values from -1.75 to 1.75
- gate_weight: bfloat16 [2, 768, 3072], P(None, 'shard'), may hold values from -0.21875 to 0.21875
- up_weight: bfloat16 [2, 768, 3072], P(None, 'shard'), may hold values from -0.21875 to 0.21875
- down_weight: bfloat16 [2, 3072, 768], P(None, 'shard'), may hold values from -0.109375 to 0.109375
- first_gain: bfloat16 [2, 768], P(None, 'shard'), may hold values from 0.5 to 1.5
- first_bias: bfloat16 [2, 768], P(None, 'shard'), may hold values from -1.796875 to 1.796875
- second_gain: bfloat16 [2, 768], P(None, 'shard'), may hold values from 0.5 to 1.5
- second_bias: bfloat16 [2, 768], P(None, 'shard'), may hold values from -1.796875 to 1.796875
- cotangent: bfloat16 [32, 256, 768], P(('rep', 'shard')), may hold values from -6 to 6
Outputs:
- output: bfloat16 [32, 256, 768], P(('rep', 'shard'))
- input_gradient: float32 [32, 256, 768], P(('rep', 'shard'))
- qkv_gradient: float32 [2, 768, 2304], P(None, 'shard')
- out_gradient: float32 [2, 768, 768], P(None, 'shard')
- gate_gradient: float32 [2, 768, 3072], P(None, 'shard')
- up_gradient: float32 [2, 768, 3072], P(None, 'shard')
- down_gradient: float32 [2, 3072, 768], P(None, 'shard')
- first_gain_gradient: float32 [2, 768], P(None, 'shard')
- first_bias_gradient: float32 [2, 768], P(None, 'shard')
- second_gain_gradient: float32 [2, 768], P(None, 'shard')
- second_bias_gradient: float32 [2, 768], P(None, 'shard')
The draws below stay inside these ranges and needn't reach their ends.
Inputs may be any that keep to these rules, and one draw needn't show every extreme that they name: `segment_ids`: segment numbers never fall along a sequence; each document has 1 to 170 tokens.
All inputs are finite; a program needn't handle non-finite values.
Results may differ from the reference program's by a relative error of at most 0.029.
Values may be sent and summed in bfloat16 or wider, within the bound.
A program may use at most 192 MiB of HBM per device.

```python
import math
import jax
import jax.numpy as jnp
import numpy as np
from jax import lax

D = 768
HEADS = 12
HEAD = 64
FF = 3072
LAYERS = 2
SEQ = 256
SEGS = 4
DOC_MOST = 170
NSEQ = 32


def level_of(stream_key, extent, split, low, largest):
    factor_of, own = 1.0, jax.random.fold_in(stream_key, 6)
    for dim, shards_of in split:
        draws = jnp.exp(jax.random.uniform(jax.random.fold_in(own, dim), (shards_of,), jnp.float32, low / len(split), largest / len(split)))
        factor_of = factor_of * jnp.repeat(draws, extent[dim] // shards_of).reshape([-1 if axis == dim else 1 for axis in range(len(extent))])
    return factor_of


def length_profile(number_of, total, most, skew):
    portions = [(1 << 20) // math.isqrt(standing ** skew) + 1 for standing in range(2, number_of + 1)]
    surplus, counts = total - most - (number_of - 1), [1] * (number_of - 1)
    while surplus > 0:
        movable = [i for i in range(number_of - 1) if counts[i] < most]
        mass, left = sum([portions[i] for i in movable]), surplus
        for i in movable:
            addition = min(most - counts[i], max(1, left * portions[i] // mass), surplus)
            counts[i] = counts[i] + addition
            surplus = surplus - addition
    return np.array([most] + counts)


def ragged_sizes(key, number_of, total, most, lean):
    if number_of == 2:
        one = jax.random.randint(key, (), max(1, total - most), min(most, total - 1) + 1)
        return jnp.stack([one, total - one])
    lengths = jnp.asarray(length_profile(number_of, total, most, lean), jnp.int32)
    twos = (number_of - 1) // 2
    source_of, taker = lengths[1:1 + 2 * twos:2], lengths[2:2 + 2 * twos:2]
    slack = jnp.minimum(source_of - 1, most - taker)
    passed = jax.random.randint(jax.random.fold_in(key, 1), (twos,), 0, 1 << 20) % (slack + 1)
    lengths = lengths.at[1:1 + 2 * twos:2].set(source_of - passed).at[2:2 + 2 * twos:2].set(taker + passed)
    return lengths[jax.random.permutation(jax.random.fold_in(key, 2), number_of)]


def bell_draw(rng, extent, spread, bound, pieces=(), kind=jnp.bfloat16):
    level = level_of(rng, extent, pieces, -0.22, 0.18) if pieces else 1.0
    values = jax.random.normal(rng, extent, jnp.float32) * spread * level
    return jnp.minimum(jnp.maximum(values, -bound), bound).astype(kind)


def setup_inputs(seed: int = 0) -> dict:
    splits = jax.random.split(jax.random.key(seed), 13)
    inputs = bell_draw(splits[0], (NSEQ, SEQ, D), 1.0, 6.0, ((0, 32),))
    segment_ids = jax.vmap(lambda own: jnp.searchsorted(jnp.cumsum(ragged_sizes(own, SEGS, SEQ, DOC_MOST, 1)), jnp.arange(SEQ), side="right"))(jax.random.split(splits[1], NSEQ)).reshape((NSEQ, SEQ)).astype(jnp.int32)
    qkv_weight = bell_draw(splits[2], (LAYERS, D, 3 * D), D ** -0.5, 0.21875, ((1, 16),))
    out_weight = bell_draw(splits[3], (LAYERS, D, D), (D // 64) ** -0.5, 1.75, ((1, 16),))
    gate_weight = bell_draw(splits[4], (LAYERS, D, FF), D ** -0.5, 0.21875, ((1, 16),))
    up_weight = bell_draw(splits[5], (LAYERS, D, FF), D ** -0.5, 0.21875, ((1, 16),))
    down_weight = bell_draw(splits[6], (LAYERS, FF, D), FF ** -0.5, 0.109375, ((1, 16),))
    first_gain = jnp.clip(1.0 + 0.1 * jax.random.normal(splits[7], (LAYERS, D), jnp.float32), 0.5, 1.5).astype(jnp.bfloat16)
    first_bias = bell_draw(splits[8], (LAYERS, D), 0.3, 1.796875, ((1, 16),))
    second_gain = jnp.clip(1.0 + 0.1 * jax.random.normal(splits[9], (LAYERS, D), jnp.float32), 0.5, 1.5).astype(jnp.bfloat16)
    second_bias = bell_draw(splits[10], (LAYERS, D), 0.3, 1.796875, ((1, 16),))
    cotangent = bell_draw(splits[11], (NSEQ, SEQ, D), 1.0, 6.0, ((0, 32),))
    return {"inputs": inputs, "segment_ids": segment_ids, "qkv_weight": qkv_weight, "out_weight": out_weight, "gate_weight": gate_weight, "up_weight": up_weight, "down_weight": down_weight, "first_gain": first_gain, "first_bias": first_bias, "second_gain": second_gain, "second_bias": second_bias, "cotangent": cotangent}


@jax.custom_vjp
def low(v):
    return lax.optimization_barrier(v.astype(jnp.bfloat16)).astype(jnp.float32)

@jax.custom_vjp
def low_back(v):
    return v

def low_keep(v):
    return (low(v), None)

def low_pass(kept, grad):
    return (grad,)

def back_keep(v):
    return (v, None)

def back_low(kept, grad):
    return (low(grad),)
low.defvjp(low_keep, low_pass)
low_back.defvjp(back_keep, back_low)
highest = lax.Precision.HIGHEST
eps_norm = 1e-12
rope_base = 1000.0
masked_score = -1e+30

def positions_of(segment_row):
    token_index = jnp.arange(segment_row.shape[0], dtype=jnp.int32)
    before = jnp.concatenate([segment_row[:1] - 1, segment_row[:-1]])
    starts = jnp.where(segment_row != before, token_index, jnp.zeros_like(token_index))
    return token_index - lax.cummax(starts, axis=0)

def rotary_tables(position):
    half_width = HEAD // 2
    frequency = rope_base ** (-2.0 * jnp.arange(half_width, dtype=jnp.float32) / HEAD)
    angles = position.astype(jnp.float32)[:, None] * frequency[None, :]
    return (jnp.cos(angles), jnp.sin(angles))

def rotate(values, cosine_table, sine_table):
    half_width = values.shape[-1] // 2
    lead_half = values[..., :half_width]
    tail_half = values[..., half_width:]
    cos_wide = cosine_table[:, None, :]
    sin_wide = sine_table[:, None, :]
    return jnp.concatenate([lead_half * cos_wide - tail_half * sin_wide, tail_half * cos_wide + lead_half * sin_wide], axis=-1)

def layer_norm(values, gain_row, bias_row):
    mean_row = lax.optimization_barrier(jnp.mean(values, axis=-1, keepdims=True))
    centred = values - mean_row
    variance = lax.optimization_barrier(jnp.mean(centred * centred, axis=-1, keepdims=True))
    return centred * lax.rsqrt(variance + eps_norm) * gain_row + bias_row

def forward_sequence(hidden_state, segment_row, params):
    qkv_all, out_all, gate_all, up_all, down_all, gain_one, bias_one, gain_two, bias_two = params
    token_count, model_width = hidden_state.shape
    cosine_table, sine_table = rotary_tables(positions_of(segment_row))
    allowed = segment_row[:, None] == segment_row[None, :]
    score_scale = 1.0 / math.sqrt(HEAD)
    for layer_index in range(LAYERS):
        state_low = low(hidden_state)
        projected = low_back(jnp.dot(state_low, qkv_all[layer_index], precision=highest))
        queries = projected[:, :model_width].reshape(token_count, HEADS, HEAD)
        key_rows = projected[:, model_width:2 * model_width].reshape(token_count, HEADS, HEAD)
        value_rows = projected[:, 2 * model_width:].reshape(token_count, HEADS, HEAD)
        queries = low(rotate(queries, cosine_table, sine_table))
        key_rows = low(rotate(key_rows, cosine_table, sine_table))
        value_rows = low(value_rows)
        scores = low_back(jnp.einsum('qhd,khd->hqk', queries, key_rows, precision=highest) * score_scale)
        scores = jnp.where(allowed[None], scores, masked_score)
        probabilities = jax.nn.softmax(scores, axis=-1)
        attended = jnp.einsum('hqk,khd->qhd', low(probabilities), value_rows, precision=highest)
        attended = low_back(attended.reshape(token_count, model_width))
        branch = low_back(jnp.dot(low(attended), out_all[layer_index], precision=highest))
        middle = layer_norm(hidden_state + branch, gain_one[layer_index], bias_one[layer_index])
        middle_low = low(middle)
        gate_pre = low_back(jnp.dot(middle_low, gate_all[layer_index], precision=highest))
        up_pre = low_back(jnp.dot(middle_low, up_all[layer_index], precision=highest))
        activated = low(jax.nn.silu(gate_pre) * up_pre)
        feed = low_back(jnp.dot(activated, down_all[layer_index], precision=highest))
        hidden_state = layer_norm(middle + feed, gain_two[layer_index], bias_two[layer_index])
    return hidden_state

def reference(inputs, segment_ids, qkv_weight, out_weight, gate_weight, up_weight, down_weight, first_gain, first_bias, second_gain, second_bias, cotangent):
    params = tuple((weight_item.astype(jnp.float32) for weight_item in (qkv_weight, out_weight, gate_weight, up_weight, down_weight, first_gain, first_bias, second_gain, second_bias)))

    def one_sequence(totals, block_item):
        row_input, row_segment, row_cotangent = block_item

        def run_forward(values, weights):
            return forward_sequence(values, row_segment, weights)
        result, pullback = jax.vjp(run_forward, row_input.astype(jnp.float32), params)
        grad_input, grad_params = pullback(row_cotangent.astype(jnp.float32))
        totals = jax.tree.map(lambda total_item, extra_item: total_item + extra_item, totals, grad_params)
        return (totals, (result.astype(jnp.bfloat16), grad_input))
    zero_totals = jax.tree.map(jnp.zeros_like, params)
    totals, (output, input_gradient) = lax.scan(one_sequence, zero_totals, (inputs, segment_ids, cotangent))
    qkv_gradient, out_gradient, gate_gradient, up_gradient, down_gradient, first_gain_gradient, first_bias_gradient, second_gain_gradient, second_bias_gradient = totals
    return (output, input_gradient, qkv_gradient, out_gradient, gate_gradient, up_gradient, down_gradient, first_gain_gradient, first_bias_gradient, second_gain_gradient, second_bias_gradient)
```

```python
import functools
import math

import jax
import jax.numpy as jnp
from jax import lax
from jax.experimental import pallas as pl
from jax.experimental.pallas import tpu as pltpu
from jax.sharding import PartitionSpec as P

HEADS = 12
HEAD = 64
eps_norm = 1e-12
rope_base = 1000.0
masked_score = -1e30
MESH = pl.DeviceIdType.MESH
BF = jnp.bfloat16
F32 = jnp.float32
T = 256
D = 768
G = 8
QW = 1152
OW = 384
AW = QW + OW + 128
FS = 768
PAIRS = HEADS // 2


def dot(a, b):
    return jnp.dot(a, b, preferred_element_type=F32)


def dot_t(a, b):
    return lax.dot_general(a, b, (((1,), (1,)), ((), ())), preferred_element_type=F32)


def tile(j, width):
    return pl.ds(pl.multiple_of(j * width, width), width)


def chip_rows(g):
    return pl.ds(pl.multiple_of(g * 96, 96), 96)


def shard_rows(g, c):
    return pl.ds(pl.multiple_of(g * 96 + c * 48, 48), 48)


class Place:
    def __init__(self):
        self.y = lax.axis_index("rep")
        s = lax.axis_index("shard")
        self.c, self.x, self.z = s % 2, (s // 2) % 2, s // 4
        self.g = s // 2
        self.slot = 2 * self.y + self.c

    def at(self, y, z, x, c):
        return (y, z * 4 + x * 2 + c)

    def core(self):
        return self.at(self.y, self.z, self.x, 1 - self.c)

    def xside(self):
        return self.at(self.y, self.z, 1 - self.x, self.c)

    def yside(self):
        return self.at(1 - self.y, self.z, self.x, self.c)

    def zside(self, k):
        return self.at(self.y, (self.z + k) % 4, self.x, self.c)

    def chip(self, k, x):
        return 2 * ((self.z + 4 - k) % 4) + x

    def everyone(self):
        return [self.core(), self.xside(), self.yside()] + [self.zside(k) for k in (1, 2, 3)]


def greet(place):
    barrier = pltpu.get_barrier_semaphore()
    for who in place.everyone():
        pl.semaphore_signal(barrier, inc=1, device_id=who, device_id_type=MESH)
    pl.semaphore_wait(barrier, 6)


class Mail:
    def __init__(self):
        self.sent = []

    def send(self, src, dst, send_sem, recv_sem, who, tag=None):
        copy = pltpu.make_async_remote_copy(src, dst, send_sem, recv_sem, device_id=who, device_id_type=MESH)
        copy.start()
        self.sent.append((tag, copy))

    def local(self, src, dst, sem):
        copy = pltpu.make_async_copy(src, dst, sem)
        copy.start()
        return copy

    def arrive(self, dst, send_sem, recv_sem, who):
        pltpu.make_async_remote_copy(dst, dst, send_sem, recv_sem, device_id=who, device_id_type=MESH).wait_recv()

    def gone(self, tag):
        for t, copy in self.sent:
            if t == tag:
                copy.wait_send()
        self.sent = [(t, copy) for t, copy in self.sent if t != tag]

    def finish(self):
        for _, copy in self.sent:
            copy.wait_send()
        self.sent = []


def swap_halves(v, low_half):
    return jnp.where(low_half, pltpu.roll(v, 96, 1), pltpu.roll(v, 32, 1))


def head_mask(rows, width):
    return lax.broadcasted_iota(jnp.int32, (rows, width), 1) % 128 < HEAD


def forward_kernel(
    x_ref, cos_ref, sin_ref, segc_ref, segr_ref, qkv_ref, outw_ref, par_ref, gu_ref, dn_ref,
    y_ref, A_o, F_o, Q_o, ST_o, P_o, TG_o, TT_o, N_o, I_o, PV_o,
    A, F, Q, ST, Pb, TG, TT, N, I, PV, S, AT, MF, AC, H, bias, FD, RC, RY,
    ls, s_gu, r_gu, s_az, r_az, s_ax, r_ax, s_ay, r_ay, s_ac, r_ac, s_fz, r_fz, s_fx, r_fx,
    s_m, r_m, s_rc, r_rc, s_ry, r_ry, os,
):
    pc = Place()
    y, z, x, c, g, slot = pc.y, pc.z, pc.x, pc.c, pc.g, pc.slot
    ml = Mail()
    LAY = (0, 1)
    ks = (1, 3, 2)

    own_a, own_f = [], []
    for l in LAY:
        own_a.append([])
        for h in range(2):
            dst = A.at[l, h, g, c]
            own_a[l].append(ml.local(qkv_ref.at[l, :, pl.ds(QW * h, QW)], dst.at[:, pl.ds(0, QW)], ls.at[l, h]))
            own_a[l].append(ml.local(outw_ref.at[l, :, pl.ds(OW * h, OW)], dst.at[:, pl.ds(QW, OW)], ls.at[l, 2 + h]))
            own_a[l].append(ml.local(par_ref.at[l, h], dst.at[:, pl.ds(QW + OW, 128)], ls.at[l, 4 + h]))
        own_f.append([
            ml.local(gu_ref.at[l, c, y], F.at[l, shard_rows(g, c), pl.ds(0, 2 * FS)], ls.at[l, 6]),
            ml.local(dn_ref.at[l, y], F.at[l, chip_rows(g), pl.ds(2 * FS, D)], ls.at[l, 7]),
        ])
    greet(pc)

    def gu_send(l):
        ml.send(gu_ref.at[l, 1 - c, y], F.at[l, shard_rows(g, c), pl.ds(0, 2 * FS)], s_gu.at[l], r_gu.at[l], pc.core())

    def gu_arrive(l):
        ml.arrive(F.at[l, shard_rows(g, 1 - c), pl.ds(0, 2 * FS)], s_gu.at[l], r_gu.at[l], pc.core())

    def a_own(l):
        for copy in own_a[l]:
            copy.wait()
        block = A.at[l, y, g, c]
        for i in ks:
            ml.send(block, block, s_az.at[l, i], r_az.at[l, i], pc.zside(i))
        ml.send(block, block, s_ax.at[l, 0], r_ax.at[l, 0], pc.xside())

    def a_z(l, k):
        block = A.at[l, y, pc.chip(k, x), c]
        ml.arrive(block, s_az.at[l, k], r_az.at[l, k], pc.zside(k))
        ml.send(block, block, s_ax.at[l, k], r_ax.at[l, k], pc.xside())
        ml.send(block, block, s_ay.at[l, k], r_ay.at[l, k], pc.yside())

    def a_x(l, k):
        block = A.at[l, y, pc.chip(k, 1 - x), c]
        ml.arrive(block, s_ax.at[l, k], r_ax.at[l, k], pc.xside())
        ml.send(block, block, s_ay.at[l, 4 + k], r_ay.at[l, 4 + k], pc.yside())

    def a_c(l, h):
        block = A.at[l, h, :, c]
        ml.send(block, block, s_ac.at[l, h], r_ac.at[l, h], pc.core())

    def a_y(l, k, xx, j):
        ml.arrive(A.at[l, 1 - y, pc.chip(k, xx), c], s_ay.at[l, j], r_ay.at[l, j], pc.yside())

    def a_c_arrive(l, h):
        ml.arrive(A.at[l, h, :, 1 - c], s_ac.at[l, h], r_ac.at[l, h], pc.core())

    def f_own(l):
        for copy in own_f[l]:
            copy.wait()
        gu_arrive(l)
        block = F.at[l, chip_rows(g)]
        for i in ks:
            ml.send(block, block, s_fz.at[l, i], r_fz.at[l, i], pc.zside(i))
        ml.send(block, block, s_fx.at[l, 0], r_fx.at[l, 0], pc.xside())

    def f_z(l, k):
        block = F.at[l, chip_rows(pc.chip(k, x))]
        ml.arrive(block, s_fz.at[l, k], r_fz.at[l, k], pc.zside(k))
        ml.send(block, block, s_fx.at[l, k], r_fx.at[l, k], pc.xside())

    def f_x(l, k):
        ml.arrive(F.at[l, chip_rows(pc.chip(k, 1 - x))], s_fx.at[l, k], r_fx.at[l, k], pc.xside())

    def attn_gather(l):
        for k in ks:
            a_z(l, k)
        for k in (0,) + ks:
            a_x(l, k)
        a_c(l, y)

    def attn_ready(l):
        for k in ks:
            a_y(l, k, x, k)
        for k in (0,) + ks:
            a_y(l, k, 1 - x, 4 + k)
        a_c(l, 1 - y)
        a_c_arrive(l, y)
        a_c_arrive(l, 1 - y)

    out_copies = []

    def save(src, dst, i):
        out_copies.append(ml.local(src, dst, os.at[i]))

    pair_mask = head_mask(T, 128)
    low_half = lax.broadcasted_iota(jnp.int32, (T, 128), 1) % HEAD < HEAD // 2
    onehot = (lax.broadcasted_iota(jnp.int32, (8, 128), 0) == lax.broadcasted_iota(jnp.int32, (8, 128), 1)).astype(F32).astype(BF)

    def project(l):
        st = S[...]
        cos, sin = cos_ref[...], sin_ref[...]
        for j in range(6):
            h, off = j // 3, (j % 3) * 384
            w = A[l, h, :, :, :, off:off + 384].reshape(D, 384)
            r = dot(st, w)
            kind = j // 2
            for t in range(3):
                v = r[:, 128 * t:128 * t + 128]
                if kind < 2:
                    v = v * cos + swap_halves(v, low_half) * sin
                col = (j % 2) * 384 + 128 * t
                Q[l, kind, :, col:col + 128] = v.astype(BF)

    def attention(l):
        def pair(p, carry):
            cols = tile(p, 128)
            q, kk, v = Q[l, 0, :, cols], Q[l, 1, :, cols], Q[l, 2, :, cols]
            outs = []
            for h in range(2):
                qh = jnp.where(pair_mask == (h == 0), q, jnp.zeros_like(q))
                s = dot_t(qh, kk) * 0.125 + bias[...]
                e = jnp.exp(s - jnp.max(s, axis=1, keepdims=True))
                pr = (e * (1.0 / jnp.sum(e, axis=1, keepdims=True))).astype(BF)
                Pb[l, 2 * p + h] = pr
                outs.append(dot(pr, v))
            AT[:, cols] = jnp.where(pair_mask, outs[0], outs[1]).astype(BF)
            return carry
        lax.fori_loop(0, PAIRS, pair, 0)

    def params(l):
        for h in range(2):
            w = A[l, h, :, :, :, QW + OW:].reshape(D, 128)
            PV[l, h] = dot_t(onehot, w)

    def out_project(l):
        for h in range(2):
            w = A[l, h, :, :, :, QW:QW + OW].reshape(D, OW)
            H[:, h * OW:h * OW + OW] = H[:, h * OW:h * OW + OW] + dot(AT[...], w)

    def norm(l, i, dst, extra):
        gain, shift = PV[l, i, 0:1, :], PV[l, i, 1:2, :]
        def rows_of(j, carry):
            rows = tile(j, 32)
            v = H[rows, :]
            if extra is not None:
                v = v + extra(rows)
            cen = v - jnp.mean(v, axis=1, keepdims=True)
            inv = lax.rsqrt(jnp.mean(cen * cen, axis=1, keepdims=True) + eps_norm)
            n = cen * inv
            N[l, i, rows, :] = n
            I[l, i, rows, :] = jnp.broadcast_to(inv, (32, 128))
            m = n * gain + shift
            H[rows, :] = m
            dst[rows, :] = m.astype(BF)
            return carry
        lax.fori_loop(0, T // 32, rows_of, 0)

    def ffn_up(l, yy):
        two = pl.ds(2 * yy, 2)
        def cols_of(j, carry):
            cols = tile(j, 256)
            xx = MF[l, two].reshape(2 * T, D)
            gate = dot(xx, F[l, :, cols])
            up = dot(xx, F[l, :, pl.ds(pl.multiple_of(FS + j * 256, 256), 256)])
            act = gate * jax.nn.sigmoid(gate) * up
            TG[l, 0, two, :, cols] = gate.astype(BF).reshape(2, T, 256)
            TG[l, 1, two, :, cols] = up.astype(BF).reshape(2, T, 256)
            AC[two, :, cols] = act.astype(BF).reshape(2, T, 256)
            return carry
        lax.fori_loop(0, FS // 256, cols_of, 0)

    def ffn_down(l, yy, cc, add):
        s_ = 2 * yy + cc
        def cols_of(j, carry):
            cols = tile(j, 256)
            w = F[l, :, pl.ds(pl.multiple_of(2 * FS + j * 256, 256), 256)]
            r = dot(AC[s_], w)
            if add:
                r = r + RC[l, yy, :, cols].astype(F32)
            FD[l, s_, :, cols] = r.astype(BF)
            return carry
        lax.fori_loop(0, D // 256, cols_of, 0)

    def turn(src, dst, col):
        def tile_of(j, carry):
            cols = tile(j, 128)
            dst[cols, pl.ds(pl.multiple_of(col, T), T)] = src[:, cols].T
            return carry
        lax.fori_loop(0, D // 128, tile_of, 0)

    def turn_slots(src, dst):
        def slot_of(i, carry):
            turn(src.at[i], dst, i * T)
            return carry
        lax.fori_loop(0, 4, slot_of, 0)

    def mid_exchange(l):
        mine = MF.at[l, slot]
        ml.send(mine, mine, s_m.at[l, 0], r_m.at[l, 0], pc.yside())
        ml.send(mine, mine, s_m.at[l, 1], r_m.at[l, 1], pc.core())

    def feed_forward(l):
        other_y = MF.at[l, 2 * (1 - y) + c]
        ml.arrive(MF.at[l, 2 * y + 1 - c], s_m.at[l, 1], r_m.at[l, 1], pc.core())
        ffn_up(l, y)
        ml.arrive(other_y, s_m.at[l, 0], r_m.at[l, 0], pc.yside())
        ml.send(other_y, other_y, s_m.at[l, 2], r_m.at[l, 2], pc.core())
        ml.arrive(MF.at[l, 2 * (1 - y) + 1 - c], s_m.at[l, 2], r_m.at[l, 2], pc.core())
        ffn_up(l, 1 - y)
        def to_core(i, yy):
            ffn_down(l, yy, 1 - c, False)
            ml.send(FD.at[l, 2 * yy + 1 - c], RC.at[l, yy], s_rc.at[l, i], r_rc.at[l, i], pc.core())
        to_core(0, 1 - y)
        ml.arrive(RC.at[l, 1 - y], s_rc.at[l, 0], r_rc.at[l, 0], pc.core())
        ffn_down(l, 1 - y, c, True)
        ml.send(FD.at[l, 2 * (1 - y) + c], RY.at[l], s_ry.at[l], r_ry.at[l], pc.yside())
        to_core(1, y)
        ml.arrive(RC.at[l, y], s_rc.at[l, 1], r_rc.at[l, 1], pc.core())
        ffn_down(l, y, c, True)
        turn_slots(MF.at[l], TT.at[l, 0])
        turn_slots(AC, TT.at[l, 1])
        ml.arrive(RY.at[l], s_ry.at[l], r_ry.at[l], pc.yside())

    gu_send(0)
    gu_send(1)
    a_own(0)
    a_own(1)
    bias[...] = jnp.where(segc_ref[:, 0:1] == segr_ref[0:1, :], 0.0, masked_score)
    H[...] = x_ref[...].astype(F32)
    S[...] = x_ref[...]
    attn_gather(0)
    f_own(0)
    attn_gather(1)
    f_own(1)
    attn_ready(0)
    for l in LAY:
        if l == 1:
            attn_ready(1)
        params(l)
        project(l)
        turn(S, ST.at[l, 0], 0)
        attention(l)
        if l == 0:
            for k in ks:
                f_z(0, k)
        out_project(l)
        norm(l, 0, MF.at[l, slot], None)
        mid_exchange(l)
        turn(AT, ST.at[l, 1], 0)
        if l == 0:
            for k in (0,) + ks:
                f_x(0, k)
        else:
            for k in ks:
                f_z(1, k)
            for k in (0,) + ks:
                f_x(1, k)
        feed_forward(l)
        extra = lambda rows, l=l: FD[l, slot, rows, :].astype(F32) + RY[l, rows, :].astype(F32)
        norm(l, 1, y_ref if l == 1 else S, extra)
    for i, (src, dst) in enumerate([(A, A_o), (F, F_o), (Q, Q_o), (ST, ST_o), (Pb, P_o), (TG, TG_o), (TT, TT_o), (N, N_o), (I, I_o), (PV, PV_o)]):
        save(src, dst, i)
    for copy in out_copies:
        copy.wait()
    ml.finish()


FWD_SHAPES = [
    ((2, 2, G, 2, 48, AW), BF),
    ((2, D, 2 * FS + D), BF),
    ((2, 3, T, D), BF),
    ((2, 2, D, T), BF),
    ((2, HEADS, T, T), BF),
    ((2, 2, 4, T, FS), BF),
    ((2, 2, D, 4 * T), BF),
    ((2, 2, T, D), F32),
    ((2, 2, T, 128), F32),
    ((2, 2, 8, D), F32),
]


def sems(*shape):
    return pltpu.SemaphoreType.DMA(shape)


def forward_call(args):
    any_spec = pl.BlockSpec(memory_space=pl.ANY)
    vm = pl.BlockSpec(memory_space=pltpu.VMEM)
    return pl.pallas_call(
        forward_kernel,
        out_shape=[jax.ShapeDtypeStruct((T, D), BF)] + [jax.ShapeDtypeStruct(s, d) for s, d in FWD_SHAPES],
        in_specs=[vm] * 5 + [any_spec] * 5,
        out_specs=[vm] + [any_spec] * len(FWD_SHAPES),
        scratch_shapes=[pltpu.VMEM(s, d) for s, d in FWD_SHAPES]
        + [
            pltpu.VMEM((T, D), BF),
            pltpu.VMEM((T, D), BF),
            pltpu.VMEM((2, 4, T, D), BF),
            pltpu.VMEM((4, T, FS), BF),
            pltpu.VMEM((T, D), F32),
            pltpu.VMEM((T, T), F32),
            pltpu.VMEM((2, 4, T, D), BF),
            pltpu.VMEM((2, 2, T, D), BF),
            pltpu.VMEM((2, T, D), BF),
            sems(2, 8),
            sems(2), sems(2),
            sems(2, 4), sems(2, 4),
            sems(2, 4), sems(2, 4),
            sems(2, 8), sems(2, 8),
            sems(2, 2), sems(2, 2),
            sems(2, 4), sems(2, 4),
            sems(2, 4), sems(2, 4),
            sems(2, 3), sems(2, 3),
            sems(2, 2), sems(2, 2),
            sems(2), sems(2),
            sems(len(FWD_SHAPES)),
        ],
        compiler_params=pltpu.CompilerParams(collective_id=0, has_side_effects=True, vmem_limit_bytes=60 * 2**20),
        cost_estimate=pl.CostEstimate(flops=10**10, bytes_accessed=10**8, transcendentals=0),
        name="forward",
    )(*args)


def backward_kernel(
    cot_ref, cos_ref, sin_ref, A_i, F_i, Q_i, ST_i, P_i, TG_i, TT_i, N_i, I_i, PV_i,
    gin_ref, GUG, DNG, AF,
    A, F, Q, ST, Pb, TG, TT, N, I, PV,
    U, GF, GB, GA, GP, FD, RC, RY, FG, RFX, RFZ, FR, AG, RAC, RAY, RAX, RAZ, V,
    ls, s_m, r_m, s_rc, r_rc, s_ry, r_ry,
    s_fx, r_fx, s_fz, r_fz, s_fc, r_fc, s_fy, r_fy,
    s_ac, r_ac, s_ay, r_ay, s_ax, r_ax, s_az, r_az, s_af, r_af,
):
    pc = Place()
    y, z, x, c, slot = pc.y, pc.z, pc.x, pc.c, pc.slot
    ml = Mail()
    ks = (1, 3, 2)
    places = {
        "PV": (PV_i, PV, 0), "N": (N_i, N, 1), "I": (I_i, I, 2), "TT": (TT_i, TT, 3), "F": (F_i, F, 4), "TG": (TG_i, TG, 5),
        "ST": (ST_i, ST, 6), "A": (A_i, A, 7), "P": (P_i, Pb, 8), "Q": (Q_i, Q, 9),
    }
    loading = {}

    def load(l, *names):
        for name in names:
            src, dst, i = places[name]
            loading[name] = ml.local(src.at[l], dst, ls.at[i])

    def need(*names):
        for name in names:
            if name in loading:
                loading.pop(name).wait()

    load(1, "PV", "N", "I", "TT", "F", "TG", "ST", "A", "P", "Q")
    U[...] = cot_ref[...].astype(F32)
    greet(pc)

    fcols = (pl.ds(2 * FS, D), pl.ds(0, FS), pl.ds(FS, FS))

    def fx_send(l, j):
        ml.send(FG.at[:, 1 - x, :, fcols[j]], RFX.at[l, j], s_fx.at[l, j], r_fx.at[l, j], pc.xside(), ("fx", l, j))

    def fx_task(l, j):
        ml.arrive(RFX.at[l, j], s_fx.at[l, j], r_fx.at[l, j], pc.xside())
        def add(zz, carry):
            for half in range(2):
                rows = pl.ds(48 * half, 48)
                RFX[l, j, zz, rows, :] = (RFX[l, j, zz, rows, :].astype(F32) + FG[zz, x, rows, fcols[j]].astype(F32)).astype(BF)
            return carry
        lax.fori_loop(0, 4, add, 0)
        for k in ks:
            ml.send(RFX.at[l, j, (z + k) % 4], RFZ.at[l, j, k - 1], s_fz.at[l, j, k], r_fz.at[l, j, k], pc.zside(k))

    def fz_task(l, j):
        for k in ks:
            ml.arrive(RFZ.at[l, j, k - 1], s_fz.at[l, j, k], r_fz.at[l, j, k], pc.zside(k))
        def total(start):
            rows = pl.ds(start, 48)
            t = RFX[l, j, z, rows, :].astype(F32)
            for k in range(3):
                t = t + RFZ[l, j, k, rows, :].astype(F32)
            return t.astype(BF)
        if j == 0:
            for half in range(2):
                DNG[l, y, pl.ds(48 * half, 48), :] = total(48 * half)
            ml.send(DNG.at[l, y], DNG.at[l, y], s_fy.at[l, 0], r_fy.at[l, 0], pc.yside())
        else:
            FR[l, j - 1] = total(pl.multiple_of((1 - c) * 48, 48))
            ml.send(FR.at[l, j - 1], GUG.at[l, j - 1, c, y], s_fc.at[l, j], r_fc.at[l, j], pc.core())
            GUG[l, j - 1, c, y] = total(pl.multiple_of(c * 48, 48))

    def fc_task(l, j):
        ml.arrive(GUG.at[l, j - 1, 1 - c, y], s_fc.at[l, j], r_fc.at[l, j], pc.core())
        block = GUG.at[l, j - 1, :, y]
        ml.send(block, block, s_fy.at[l, j], r_fy.at[l, j], pc.yside())

    def fy_task(l, j):
        block = DNG.at[l, 1 - y] if j == 0 else GUG.at[l, j - 1, :, 1 - y]
        ml.arrive(block, s_fy.at[l, j], r_fy.at[l, j], pc.yside())

    def ac_send(l, i):
        h = (1 - y, y)[i]
        ml.send(AG.at[h, :, :, 1 - c], RAC.at[l, i], s_ac.at[l, i], r_ac.at[l, i], pc.core(), ("ac", l))

    def ac_task(l, i):
        h = (1 - y, y)[i]
        ml.arrive(RAC.at[l, i], s_ac.at[l, i], r_ac.at[l, i], pc.core())
        def add(n, carry):
            zz, xx = n // 2, n % 2
            for cols in (pl.ds(0, 768), pl.ds(768, 896)):
                RAC[l, i, zz, xx, :, cols] = (RAC[l, i, zz, xx, :, cols].astype(F32) + AG[h, zz, xx, c, :, cols].astype(F32)).astype(BF)
            return carry
        lax.fori_loop(0, 8, add, 0)
        if i == 0:
            ml.send(RAC.at[l, 0], RAY.at[l], s_ay.at[l], r_ay.at[l], pc.yside())

    def ay_task(l):
        ml.arrive(RAY.at[l], s_ay.at[l], r_ay.at[l], pc.yside())
        def add(n, carry):
            zz, xx = n // 2, n % 2
            for cols in (pl.ds(0, 768), pl.ds(768, 896)):
                RAC[l, 1, zz, xx, :, cols] = (RAC[l, 1, zz, xx, :, cols].astype(F32) + RAY[l, zz, xx, :, cols].astype(F32)).astype(BF)
            return carry
        lax.fori_loop(0, 8, add, 0)
        ml.send(RAC.at[l, 1, :, 1 - x], RAX.at[l], s_ax.at[l], r_ax.at[l], pc.xside())

    def ax_task(l):
        ml.arrive(RAX.at[l], s_ax.at[l], r_ax.at[l], pc.xside())
        def add(zz, carry):
            for cols in (pl.ds(0, 768), pl.ds(768, 896)):
                RAX[l, zz, :, cols] = (RAX[l, zz, :, cols].astype(F32) + RAC[l, 1, zz, x, :, cols].astype(F32)).astype(BF)
            return carry
        lax.fori_loop(0, 4, add, 0)
        for k in ks:
            ml.send(RAX.at[l, (z + k) % 4], RAZ.at[l, k - 1], s_az.at[l, k], r_az.at[l, k], pc.zside(k))

    def az_task(l):
        for k in ks:
            ml.arrive(RAZ.at[l, k - 1], s_az.at[l, k], r_az.at[l, k], pc.zside(k))
        for cols in (pl.ds(0, 768), pl.ds(768, 896)):
            t = RAX[l, z, :, cols].astype(F32)
            for k in range(3):
                t = t + RAZ[l, k, :, cols].astype(F32)
            AF[l, y, :, cols] = t.astype(BF)
        ml.send(AF.at[l, y], AF.at[l, y], s_af.at[l], r_af.at[l], pc.yside())

    def af_task(l):
        ml.arrive(AF.at[l, 1 - y], s_af.at[l], r_af.at[l], pc.yside())

    pair_mask = head_mask(T, 128)
    low_half = lax.broadcasted_iota(jnp.int32, (T, 128), 1) % HEAD < HEAD // 2
    onehot = (lax.broadcasted_iota(jnp.int32, (8, 128), 0) == lax.broadcasted_iota(jnp.int32, (8, 128), 1)).astype(F32).astype(BF)

    def norm_back(i, extra, dst):
        gain = PV[i, 0:1, :]
        def rows_of(j, carry):
            gs, bs = carry
            rows = tile(j, 32)
            u = U[rows, :]
            if extra is not None:
                u = u + extra(rows)
            n = N[i, rows, :]
            un = u * n
            gs = gs + un.reshape(4, 8, D).sum(0)
            bs = bs + u.reshape(4, 8, D).sum(0)
            m1 = jnp.mean(u * gain, axis=1, keepdims=True)
            m2 = jnp.mean(un * gain, axis=1, keepdims=True)
            r = I[i, rows, 0:1] * (u * gain - m1 - n * m2)
            U[rows, :] = r
            dst[rows, :] = r.astype(BF)
            return gs, bs
        zero = jnp.zeros((8, D), F32)
        gs, bs = lax.fori_loop(0, T // 32, rows_of, (zero, zero))
        row = lax.broadcasted_iota(jnp.int32, (8, D), 0)
        V[i] = jnp.where(row == 0, gs.sum(0, keepdims=True), jnp.where(row == 1, bs.sum(0, keepdims=True), 0.0))

    def act_back(l, yy):
        two = pl.ds(2 * yy, 2)
        def cols_of(j, carry):
            cols = tile(j, 256)
            ga = dot_t(GF[l, two].reshape(2 * T, D), F[cols, 2 * FS:])
            gate = TG[0, two, :, cols].reshape(2 * T, 256).astype(F32)
            up = TG[1, two, :, cols].reshape(2 * T, 256).astype(F32)
            sg = jax.nn.sigmoid(gate)
            gg = ga * up * sg * (1.0 + gate * (1.0 - sg))
            gu = ga * gate * sg
            TG[0, two, :, cols] = gg.astype(BF).reshape(2, T, 256)
            TG[1, two, :, cols] = gu.astype(BF).reshape(2, T, 256)
            return carry
        lax.fori_loop(0, FS // 256, cols_of, 0)

    def mid_back(yy, cc, add, l):
        s_ = 2 * yy + cc
        def cols_of(j, carry):
            cols = tile(j, 256)
            r = dot_t(TG[0, s_], F[cols, 0:FS]) + dot_t(TG[1, s_], F[cols, FS:2 * FS])
            if add:
                r = r + RC[l, yy, :, cols].astype(F32)
            FD[s_, :, cols] = r.astype(BF)
            return carry
        lax.fori_loop(0, D // 256, cols_of, 0)

    def weight_grad(l, j):
        def cols_of(n, carry):
            cols = tile(n, 256)
            if j == 0:
                right = GF[l, :, :, cols].reshape(4 * T, 256)
            else:
                right = TG[j - 1, :, :, cols].reshape(4 * T, 256)
            r = dot(TT[0 if j else 1], right)
            off = (2 * FS, 0, FS)[j]
            FG[:, :, :, pl.ds(pl.multiple_of(off + n * 256, 256), 256)] = r.astype(BF).reshape(4, 2, 96, 256)
            return carry
        lax.fori_loop(0, 3, cols_of, 0)

    def mid_sums(l):
        def to_core(i, yy):
            mid_back(yy, 1 - c, False, l)
            ml.send(FD.at[2 * yy + 1 - c], RC.at[l, yy], s_rc.at[l, i], r_rc.at[l, i], pc.core(), ("fd", l))
        to_core(0, 1 - y)
        ml.arrive(RC.at[l, 1 - y], s_rc.at[l, 0], r_rc.at[l, 0], pc.core())
        mid_back(1 - y, c, True, l)
        ml.send(FD.at[2 * (1 - y) + c], RY.at[l], s_ry.at[l], r_ry.at[l], pc.yside(), ("fd", l))
        to_core(1, y)
        ml.arrive(RC.at[l, y], s_rc.at[l, 1], r_rc.at[l, 1], pc.core())
        mid_back(y, c, True, l)

    def out_back():
        acc = None
        for h in range(2):
            r = dot(ST[1], GB[:, h * OW:h * OW + OW])
            AG[h, :, :, :, :, QW:QW + OW] = r.astype(BF).reshape(4, 2, 2, 48, OW)
        for h in range(2):
            t = dot_t(GB[:, h * OW:h * OW + OW], A[h, :, :, :, QW:QW + OW].reshape(D, OW))
            acc = t if acc is None else acc + t
        GA[...] = acc.astype(BF)

    def attention_back():
        def pair(p, carry):
            cols = tile(p, 128)
            q, kk, v, ga = Q[0, :, cols], Q[1, :, cols], Q[2, :, cols], GA[:, cols]
            dq, dk, dv = [], [], []
            for h in range(2):
                pl_ = Pb[2 * p + h]
                pr = pl_.astype(F32)
                gh = jnp.where(pair_mask == (h == 0), ga, jnp.zeros_like(ga))
                dp = dot_t(gh, v)
                ds = (pr * (dp - jnp.sum(dp * pr, axis=1, keepdims=True))).astype(BF)
                dq.append(dot(ds, kk))
                dk.append(dot(ds.T, q))
                dv.append(dot(pl_.T, ga))
            cos, sin = cos_ref[...], sin_ref[...]
            def back(pair_of):
                m = jnp.where(pair_mask, pair_of[0], pair_of[1]) * 0.125
                return (m * cos - swap_halves(m, low_half) * sin).astype(BF)
            GP[0, :, cols] = back(dq)
            GP[1, :, cols] = back(dk)
            GP[2, :, cols] = jnp.where(pair_mask, dv[0], dv[1]).astype(BF)
            return carry
        lax.fori_loop(0, PAIRS, pair, 0)

    def gp_chunk(j):
        return GP[j // 2, :, (j % 2) * 384:(j % 2) * 384 + 384]

    def qkv_grad(h):
        for j in range(3 * h, 3 * h + 3):
            off = (j % 3) * 384
            r = dot(ST[0], gp_chunk(j))
            AG[h, :, :, :, :, off:off + 384] = r.astype(BF).reshape(4, 2, 2, 48, 384)

    def param_grad():
        for h in range(2):
            r = lax.dot_general(V[h].astype(BF), onehot, (((0,), (0,)), ((), ())), preferred_element_type=F32)
            AG[h, :, :, :, :, QW + OW:] = r.astype(BF).reshape(4, 2, 2, 48, 128)

    def input_back():
        acc = U[...]
        for j in range(6):
            off = (j % 3) * 384
            acc = acc + dot_t(gp_chunk(j), A[j // 3, :, :, :, off:off + 384].reshape(D, 384))
        U[...] = acc

    for l in (1, 0):
        need("PV", "N", "I")
        norm_back(1, None, GF.at[l, slot])
        mine = GF.at[l, slot]
        ml.send(mine, mine, s_m.at[l, 0], r_m.at[l, 0], pc.yside())
        ml.send(mine, mine, s_m.at[l, 1], r_m.at[l, 1], pc.core())
        if l == 0:
            ml.gone(("fd", 1))
            ay_task(1)
            fz_task(1, 0)
        need("TT", "F", "TG")
        ml.arrive(GF.at[l, 2 * y + 1 - c], s_m.at[l, 1], r_m.at[l, 1], pc.core())
        act_back(l, y)
        other = GF.at[l, 2 * (1 - y) + c]
        ml.arrive(other, s_m.at[l, 0], r_m.at[l, 0], pc.yside())
        ml.send(other, other, s_m.at[l, 2], r_m.at[l, 2], pc.core())
        ml.arrive(GF.at[l, 2 * (1 - y) + 1 - c], s_m.at[l, 2], r_m.at[l, 2], pc.core())
        ml.gone(("fx", 1, 0)) if l == 0 else None
        weight_grad(l, 0)
        fx_send(l, 0)
        act_back(l, 1 - y)
        mid_sums(l)
        if l == 1:
            load(0, "F")
        ml.gone(("fx", 1, 1)) if l == 0 else None
        weight_grad(l, 1)
        fx_send(l, 1)
        ml.gone(("fx", 1, 2)) if l == 0 else None
        weight_grad(l, 2)
        fx_send(l, 2)
        if l == 1:
            load(0, "TT", "TG")
        ml.arrive(RY.at[l], s_ry.at[l], r_ry.at[l], pc.yside())
        norm_back(0, lambda rows: FD[slot, rows, :].astype(F32) + RY[l, rows, :].astype(F32), GB)
        if l == 1:
            load(0, "N", "I")
        if l == 0:
            ax_task(1)
            fz_task(1, 1)
            fz_task(1, 2)
            fc_task(1, 1)
            fc_task(1, 2)
        need("ST", "A")
        param_grad()
        out_back()
        if l == 1:
            load(0, "PV")
        fx_task(l, 0)
        need("P", "Q")
        attention_back()
        if l == 1:
            load(0, "P", "Q")
        for i in range(2):
            for h in range(2):
                pass
        qkv_grad(0)
        qkv_grad(1)
        ac_send(l, 0)
        ac_send(l, 1)
        if l == 1:
            load(0, "ST")
        fx_task(l, 1)
        input_back()
        if l == 1:
            load(0, "A")
        fx_task(l, 2)
        ac_task(l, 0)
        ac_task(l, 1)
        if l == 1:
            ml.gone(("ac", 1))
    gin_ref[...] = U[...]
    ay_task(0)
    az_task(1)
    fz_task(0, 0)
    fz_task(0, 1)
    fz_task(0, 2)
    fc_task(0, 1)
    fc_task(0, 2)
    ax_task(0)
    az_task(0)
    for l in (1, 0):
        for j in range(3):
            fy_task(l, j)
        af_task(l)
    ml.finish()


def backward_call(cot, cos, sin, kept):
    any_spec = pl.BlockSpec(memory_space=pl.ANY)
    vm = pl.BlockSpec(memory_space=pltpu.VMEM)
    return pl.pallas_call(
        backward_kernel,
        out_shape=[
            jax.ShapeDtypeStruct((T, D), F32),
            jax.ShapeDtypeStruct((2, 2, 2, 2, 48, FS), BF),
            jax.ShapeDtypeStruct((2, 2, 96, D), BF),
            jax.ShapeDtypeStruct((2, 2, 48, AW), BF),
        ],
        in_specs=[vm] * 3 + [any_spec] * len(kept),
        out_specs=[vm] * 4,
        scratch_shapes=[pltpu.VMEM(s[1:], d) for s, d in FWD_SHAPES]
        + [
            pltpu.VMEM((T, D), F32),
            pltpu.VMEM((2, 4, T, D), BF),
            pltpu.VMEM((T, D), BF),
            pltpu.VMEM((T, D), BF),
            pltpu.VMEM((3, T, D), BF),
            pltpu.VMEM((4, T, D), BF),
            pltpu.VMEM((2, 2, T, D), BF),
            pltpu.VMEM((2, T, D), BF),
            pltpu.VMEM((4, 2, 96, 2 * FS + D), BF),
            pltpu.VMEM((2, 3, 4, 96, D), BF),
            pltpu.VMEM((2, 3, 3, 96, D), BF),
            pltpu.VMEM((2, 2, 48, D), BF),
            pltpu.VMEM((2, 4, 2, 2, 48, AW), BF),
            pltpu.VMEM((2, 2, 4, 2, 48, AW), BF),
            pltpu.VMEM((2, 4, 2, 48, AW), BF),
            pltpu.VMEM((2, 4, 48, AW), BF),
            pltpu.VMEM((2, 3, 48, AW), BF),
            pltpu.VMEM((2, 8, D), F32),
            sems(10),
            sems(2, 3), sems(2, 3),
            sems(2, 2), sems(2, 2),
            sems(2), sems(2),
            sems(2, 3), sems(2, 3),
            sems(2, 3, 4), sems(2, 3, 4),
            sems(2, 3), sems(2, 3),
            sems(2, 3), sems(2, 3),
            sems(2, 2), sems(2, 2),
            sems(2), sems(2),
            sems(2), sems(2),
            sems(2, 4), sems(2, 4),
            sems(2), sems(2),
        ],
        compiler_params=pltpu.CompilerParams(collective_id=1, has_side_effects=True, vmem_limit_bytes=60 * 2**20),
        cost_estimate=pl.CostEstimate(flops=2 * 10**10, bytes_accessed=10**8, transcendentals=0),
        name="backward",
    )(cot, cos, sin, *kept)


def epilogue(gug, dng, af):
    def uncut(v):
        return v.astype(F32).reshape(2, 2, 2, 48, G, 96).transpose(0, 3, 4, 1, 2, 5).reshape(2, 48, G * 4 * 96)
    af = af.astype(F32)
    both = lambda a, b: jnp.concatenate([af[:, 0, :, a:b], af[:, 1, :, a:b]], axis=-1)
    return (
        both(0, QW), both(QW, QW + OW), uncut(gug[:, 0]), uncut(gug[:, 1]), dng.astype(F32).reshape(2, 192, D),
        af[:, 0, :, QW + OW], af[:, 0, :, QW + OW + 1], af[:, 1, :, QW + OW], af[:, 1, :, QW + OW + 1],
    )


def positions_of(segment_row):
    token_index = jnp.arange(segment_row.shape[0], dtype=jnp.int32)
    before = jnp.concatenate([segment_row[:1] - 1, segment_row[:-1]])
    starts = jnp.where(segment_row != before, token_index, jnp.zeros_like(token_index))
    return token_index - lax.cummax(starts, axis=0)


def rotary_tables(position):
    half_width = HEAD // 2
    frequency = rope_base ** (-2.0 * jnp.arange(half_width, dtype=F32) / HEAD)
    angles = position.astype(F32)[:, None] * frequency[None, :]
    return jnp.cos(angles), jnp.sin(angles)


def prologue(inputs, segment_ids, qkv_weight, out_weight, gate_weight, up_weight, down_weight,
             first_gain, first_bias, second_gain, second_bias):
    seg = segment_ids[0]
    cos, sin = rotary_tables(positions_of(seg))
    cos = jnp.concatenate([cos] * 4, axis=1)
    sin = jnp.concatenate([-sin, sin] * 2, axis=1)
    segc = jnp.broadcast_to(seg[:, None], (T, 128))
    segr = jnp.broadcast_to(seg[None, :], (8, T))
    par = jnp.stack([jnp.stack([first_gain, first_bias], -1), jnp.stack([second_gain, second_bias], -1)], 1)
    par = jnp.pad(par, ((0, 0), (0, 0), (0, 0), (0, 126)))
    def cut(w):
        return w.reshape(2, 48, G, 2, 2, 96).transpose(0, 3, 4, 1, 2, 5).reshape(2, 2, 2, 48, FS)
    gu = jnp.concatenate([cut(gate_weight), cut(up_weight)], -1)
    dn = down_weight.reshape(2, 2, 96, D)
    return inputs[0], cos, sin, segc, segr, qkv_weight, out_weight, par, gu, dn


def rotate(values, cosine_table, sine_table):
    half_width = values.shape[-1] // 2
    lead_half = values[..., :half_width]
    tail_half = values[..., half_width:]
    cos_wide = cosine_table[:, None, :]
    sin_wide = sine_table[:, None, :]
    return jnp.concatenate(
        [lead_half * cos_wide - tail_half * sin_wide, tail_half * cos_wide + lead_half * sin_wide],
        axis=-1,
    )


def unrotate(values, cosine_table, sine_table):
    half_width = values.shape[-1] // 2
    lead_half = values[..., :half_width]
    tail_half = values[..., half_width:]
    cos_wide = cosine_table[:, None, :]
    sin_wide = sine_table[:, None, :]
    return jnp.concatenate(
        [lead_half * cos_wide + tail_half * sin_wide, tail_half * cos_wide - lead_half * sin_wide],
        axis=-1,
    )


def norm_forward(values, gain_row, bias_row):
    mean_row = jnp.mean(values, axis=-1, keepdims=True)
    centred = values - mean_row
    variance = jnp.mean(centred * centred, axis=-1, keepdims=True)
    inverse = lax.rsqrt(variance + eps_norm)
    normed = centred * inverse
    return (normed * gain_row + bias_row, normed, inverse)


def norm_backward(upstream, normed, inverse, gain_row):
    scaled = upstream * gain_row
    gain_sum = jnp.sum(upstream * normed, axis=0)
    bias_sum = jnp.sum(upstream, axis=0)
    grad_input = inverse * (
        scaled
        - jnp.mean(scaled, axis=-1, keepdims=True)
        - normed * jnp.mean(scaled * normed, axis=-1, keepdims=True)
    )
    return (grad_input, gain_sum, bias_sum)


def times_transposed(left_side, right_side):
    return lax.dot_general(
        left_side, right_side, (((1,), (1,)), ((), ())), preferred_element_type=jnp.float32
    )


def outer_sum(left_side, right_side):
    return lax.dot_general(
        left_side, right_side, (((0,), (0,)), ((), ())), preferred_element_type=jnp.float32
    )


def to_pairs(values):
    token_count = values.shape[0]
    return values.reshape(token_count, HEADS // 2, 2 * HEAD).transpose(1, 0, 2)


def from_pairs(values):
    return values.transpose(1, 0, 2).reshape(values.shape[1], HEADS * HEAD)


def pair_scores(query_pair, key_pair, allowed, score_scale):
    token_count = query_pair.shape[0]
    queries = query_pair.reshape(token_count, 2, HEAD)
    key_rows = key_pair.reshape(token_count, 2, HEAD)
    scores = (
        jnp.einsum("qhd,khd->hqk", queries, key_rows, preferred_element_type=jnp.float32)
        * score_scale
    )
    return (jnp.where(allowed[None], scores, masked_score), queries, key_rows)


def pair_forward(block_item, allowed, score_scale):
    query_pair, key_pair, value_pair = block_item
    token_count = query_pair.shape[0]
    scores, queries, key_rows = pair_scores(query_pair, key_pair, allowed, score_scale)
    row_top = jnp.max(scores, axis=-1, keepdims=True)
    exponent = jnp.exp(scores - row_top)
    row_total = jnp.sum(exponent, axis=-1, keepdims=True)
    probabilities = exponent / row_total
    logsum = row_top[..., 0] + jnp.log(row_total[..., 0])
    value_rows = value_pair.reshape(token_count, 2, HEAD)
    attended = jnp.einsum(
        "hqk,khd->qhd",
        probabilities.astype(jnp.bfloat16),
        value_rows,
        preferred_element_type=jnp.float32,
    )
    return (attended.reshape(token_count, 2 * HEAD), logsum)


def pair_backward(block_item, allowed, score_scale):
    query_pair, key_pair, value_pair, grad_pair, logsum = block_item
    token_count = query_pair.shape[0]
    scores, queries, key_rows = pair_scores(query_pair, key_pair, allowed, score_scale)
    probabilities = jnp.exp(scores - logsum[..., None])
    value_rows = value_pair.reshape(token_count, 2, HEAD)
    grad_rows = grad_pair.reshape(token_count, 2, HEAD)
    grad_probs = jnp.einsum(
        "qhd,khd->hqk", grad_rows, value_rows, preferred_element_type=jnp.float32
    )
    grad_values = jnp.einsum(
        "hqk,qhd->khd",
        probabilities.astype(jnp.bfloat16),
        grad_rows,
        preferred_element_type=jnp.float32,
    )
    grad_scores = probabilities * (
        grad_probs - jnp.sum(grad_probs * probabilities, axis=-1, keepdims=True)
    )
    grad_scores = grad_scores.astype(jnp.bfloat16)
    grad_queries = (
        jnp.einsum("hqk,khd->qhd", grad_scores, key_rows, preferred_element_type=jnp.float32)
        * score_scale
    )
    grad_keys = (
        jnp.einsum("hqk,qhd->khd", grad_scores, queries, preferred_element_type=jnp.float32)
        * score_scale
    )
    return (
        grad_queries.reshape(token_count, 2 * HEAD),
        grad_keys.reshape(token_count, 2 * HEAD),
        grad_values.reshape(token_count, 2 * HEAD),
    )


def layer_forward(hidden_state, weights, cosine_table, sine_table, allowed, score_scale):
    qkv_full, out_full, gate_full, up_full, down_full, gain_one, bias_one, gain_two, bias_two = (
        weights
    )
    token_count, model_width = hidden_state.shape
    state_low = hidden_state.astype(jnp.bfloat16)
    projected = jnp.dot(state_low, qkv_full, preferred_element_type=jnp.float32)
    queries = rotate(
        projected[:, :model_width].reshape(token_count, HEADS, HEAD), cosine_table, sine_table
    )
    queries = queries.astype(jnp.bfloat16).reshape(token_count, model_width)
    key_rows = rotate(
        projected[:, model_width : 2 * model_width].reshape(token_count, HEADS, HEAD),
        cosine_table,
        sine_table,
    )
    key_rows = key_rows.astype(jnp.bfloat16).reshape(token_count, model_width)
    value_rows = projected[:, 2 * model_width :].astype(jnp.bfloat16)

    def attend_pair(block_item):
        return pair_forward(block_item, allowed, score_scale)

    attended_pairs, logsum = lax.map(
        attend_pair, (to_pairs(queries), to_pairs(key_rows), to_pairs(value_rows))
    )
    attended = from_pairs(attended_pairs).astype(jnp.bfloat16)
    branch = jnp.dot(attended, out_full, preferred_element_type=jnp.float32)
    middle, normed_one, inverse_one = norm_forward(
        hidden_state + branch, gain_one.astype(jnp.float32), bias_one.astype(jnp.float32)
    )
    middle_low = middle.astype(jnp.bfloat16)
    gate_pre = jnp.dot(middle_low, gate_full, preferred_element_type=jnp.float32)
    up_pre = jnp.dot(middle_low, up_full, preferred_element_type=jnp.float32)
    activated = (jax.nn.silu(gate_pre) * up_pre).astype(jnp.bfloat16)
    feed = jnp.dot(activated, down_full, preferred_element_type=jnp.float32)
    result, normed_two, inverse_two = norm_forward(
        middle + feed, gain_two.astype(jnp.float32), bias_two.astype(jnp.float32)
    )
    stored = (
        state_low,
        queries,
        key_rows,
        value_rows,
        logsum,
        attended,
        normed_one,
        inverse_one,
        middle_low,
        gate_pre,
        up_pre,
        activated,
        normed_two,
        inverse_two,
    )
    return (result, stored)


def layer_backward(upstream, weights, stored, cosine_table, sine_table, allowed, score_scale):
    qkv_full, out_full, gate_full, up_full, down_full, gain_one, bias_one, gain_two, bias_two = (
        weights
    )
    (
        state_low,
        queries,
        key_rows,
        value_rows,
        logsum,
        attended,
        normed_one,
        inverse_one,
        middle_low,
        gate_pre,
        up_pre,
        activated,
        normed_two,
        inverse_two,
    ) = stored
    token_count, model_width = upstream.shape
    grad_mid, gain_two_sum, bias_two_sum = norm_backward(
        upstream, normed_two, inverse_two, gain_two.astype(jnp.float32)
    )
    grad_feed = grad_mid.astype(jnp.bfloat16)
    down_sum = outer_sum(activated, grad_feed)
    grad_act = times_transposed(grad_feed, down_full)
    sigmoid_gate = jax.nn.sigmoid(gate_pre)
    grad_gate = (grad_act * up_pre * sigmoid_gate * (1.0 + gate_pre * (1.0 - sigmoid_gate))).astype(
        jnp.bfloat16
    )
    grad_up = (grad_act * gate_pre * sigmoid_gate).astype(jnp.bfloat16)
    gate_sum = outer_sum(middle_low, grad_gate)
    up_sum = outer_sum(middle_low, grad_up)
    grad_middle = (
        grad_mid + times_transposed(grad_gate, gate_full) + times_transposed(grad_up, up_full)
    )
    grad_sum, gain_one_sum, bias_one_sum = norm_backward(
        grad_middle, normed_one, inverse_one, gain_one.astype(jnp.float32)
    )
    grad_branch = grad_sum.astype(jnp.bfloat16)
    out_sum = outer_sum(attended, grad_branch)
    grad_attended = times_transposed(grad_branch, out_full).astype(jnp.bfloat16)

    def attend_back(block_item):
        return pair_backward(block_item, allowed, score_scale)

    grad_query_pairs, grad_key_pairs, grad_value_pairs = lax.map(
        attend_back,
        (
            to_pairs(queries),
            to_pairs(key_rows),
            to_pairs(value_rows),
            to_pairs(grad_attended),
            logsum,
        ),
    )
    grad_queries = unrotate(
        from_pairs(grad_query_pairs).reshape(token_count, HEADS, HEAD), cosine_table, sine_table
    ).reshape(token_count, model_width)
    grad_keys = unrotate(
        from_pairs(grad_key_pairs).reshape(token_count, HEADS, HEAD), cosine_table, sine_table
    ).reshape(token_count, model_width)
    grad_projected = jnp.concatenate(
        [grad_queries, grad_keys, from_pairs(grad_value_pairs)], axis=1
    ).astype(jnp.bfloat16)
    qkv_sum = outer_sum(state_low, grad_projected)
    grad_input = grad_sum + times_transposed(grad_projected, qkv_full)
    return (
        grad_input,
        (
            qkv_sum,
            out_sum,
            gate_sum,
            up_sum,
            down_sum,
            gain_one_sum,
            bias_one_sum,
            gain_two_sum,
            bias_two_sum,
        ),
    )


def general(inputs, segment_ids, qkv_weight, out_weight, gate_weight, up_weight, down_weight,
            first_gain, first_bias, second_gain, second_bias, cotangent):
    params = (qkv_weight, out_weight, gate_weight, up_weight, down_weight, first_gain, first_bias, second_gain, second_bias)
    layers = qkv_weight.shape[0]
    segment_row = segment_ids[0]
    cosine_table, sine_table = rotary_tables(positions_of(segment_row))
    allowed = segment_row[:, None] == segment_row[None, :]
    score_scale = 1.0 / math.sqrt(HEAD)
    hidden_state = inputs[0].astype(F32)
    fetched, saved = [], []
    for layer_index in range(layers):
        weights = tuple(lax.all_gather(w[layer_index], "shard", axis=0, tiled=True) for w in params)
        fetched.append(weights)
        hidden_state, stored = layer_forward(hidden_state, weights, cosine_table, sine_table, allowed, score_scale)
        saved.append(stored)
    upstream = cotangent[0].astype(F32)
    shared = [None] * layers
    for layer_index in reversed(range(layers)):
        upstream, gradients = layer_backward(
            upstream, fetched[layer_index], saved[layer_index], cosine_table, sine_table, allowed, score_scale
        )
        owned = [lax.psum_scatter(v, "shard", scatter_dimension=0, tiled=True) for v in gradients]
        shared[layer_index] = [lax.psum(v.astype(BF), "rep").astype(F32) for v in owned]
    stacked = [jnp.stack([shared[layer_index][member] for layer_index in range(layers)]) for member in range(9)]
    return (hidden_state.astype(BF)[None], upstream[None], *stacked)


def special(inputs, segment_ids, qkv_weight, out_weight, gate_weight, up_weight, down_weight,
            first_gain, first_bias, second_gain, second_bias, cotangent):
    staged = prologue(inputs, segment_ids, qkv_weight, out_weight, gate_weight, up_weight, down_weight,
                      first_gain, first_bias, second_gain, second_bias)
    output, *kept = forward_call(staged)
    gin, gug, dng, af = backward_call(cotangent[0], staged[1], staged[2], kept)
    return (output[None], gin[None]) + epilogue(gug, dng, af)


IN_SPECS = (
    P(("rep", "shard"), None, None), P(("rep", "shard"), None),
) + (P(None, "shard", None),) * 5 + (P(None, "shard"),) * 4 + (P(("rep", "shard"), None, None),)
OUT_SPECS = (P(("rep", "shard"), None, None),) * 2 + (P(None, "shard", None),) * 5 + (P(None, "shard"),) * 4


def solution(mesh):
    fits = dict(mesh.shape) == {"rep": 2, "shard": 2 * G}
    return jax.shard_map(special if fits else general, mesh=mesh, in_specs=IN_SPECS, out_specs=OUT_SPECS, check_vma=False)
```

```python
import functools
import math

import jax
import jax.numpy as jnp
import numpy as np
from jax import lax
from jax.experimental import pallas as pl
from jax.experimental.pallas import tpu as pltpu
from jax.sharding import PartitionSpec as P

HEADS = 12
HEAD = 64
eps_norm = 1e-12
rope_base = 1000.0
masked_score = -1e30
MESH = pl.DeviceIdType.MESH
BF = jnp.bfloat16
F32 = jnp.float32
T = 256
D = 768
G = 8
QW = 1152
OW = 384
AW = QW + OW + 128
FS = 768
PAIRS = HEADS // 2


def dot(a, b):
    return jnp.dot(a, b, preferred_element_type=F32)


def dot_t(a, b):
    return lax.dot_general(a, b, (((1,), (1,)), ((), ())), preferred_element_type=F32)


def tile(j, width):
    return pl.ds(pl.multiple_of(j * width, width), width)


def chip_rows(g):
    return pl.ds(pl.multiple_of(g * 96, 96), 96)


def shard_rows(g, c):
    return pl.ds(pl.multiple_of(g * 96 + c * 48, 48), 48)


class Place:
    def __init__(self):
        self.y = lax.axis_index("rep")
        s = lax.axis_index("shard")
        self.c, self.x, self.z = s % 2, (s // 2) % 2, s // 4
        self.g = s // 2
        self.slot = 2 * self.y + self.c

    def at(self, y, z, x, c):
        return (y, z * 4 + x * 2 + c)

    def core(self):
        return self.at(self.y, self.z, self.x, 1 - self.c)

    def xside(self):
        return self.at(self.y, self.z, 1 - self.x, self.c)

    def yside(self):
        return self.at(1 - self.y, self.z, self.x, self.c)

    def zside(self, k):
        return self.at(self.y, (self.z + k) % 4, self.x, self.c)

    def zto(self, z):
        return self.at(self.y, z, self.x, self.c)

    def near(self):
        return self.z + 1 - 2 * (self.z % 2)

    def across(self):
        return 3 - self.z

    def source(self, i):
        return (self.near(), 2 - self.z // 2, 3 - 3 * (self.z // 2))[i]

    def chip_from(self, i, x):
        return 2 * (self.z if i is None else self.source(i)) + x

    def chip(self, k, x):
        return 2 * ((self.z + 4 - k) % 4) + x

    def line(self):
        return [self.core(), self.xside(), self.yside(), self.zto(self.near()), self.zto(self.across())]

    def everyone(self):
        return [self.core(), self.xside(), self.yside()] + [self.zside(k) for k in (1, 2, 3)]


def greet(partners):
    barrier = pltpu.get_barrier_semaphore()
    for who in partners:
        pl.semaphore_signal(barrier, inc=1, device_id=who, device_id_type=MESH)
    pl.semaphore_wait(barrier, len(partners))


class Mail:
    def __init__(self):
        self.sent = []
        self.some = []

    def send(self, src, dst, send_sem, recv_sem, who, tag=None):
        copy = pltpu.make_async_remote_copy(src, dst, send_sem, recv_sem, device_id=who, device_id_type=MESH)
        copy.start()
        self.sent.append((tag, copy))

    def send_if(self, cond, src, dst, send_sem, recv_sem, who):
        copy = pltpu.make_async_remote_copy(src, dst, send_sem, recv_sem, device_id=who, device_id_type=MESH)
        pl.when(cond)(copy.start)
        self.some.append((cond, copy))

    def local(self, src, dst, sem):
        copy = pltpu.make_async_copy(src, dst, sem)
        copy.start()
        return copy

    def arrive(self, dst, send_sem, recv_sem, who):
        pltpu.make_async_remote_copy(dst, dst, send_sem, recv_sem, device_id=who, device_id_type=MESH).wait_recv()

    def gone(self, tag):
        for t, copy in self.sent:
            if t == tag:
                copy.wait_send()
        self.sent = [(t, copy) for t, copy in self.sent if t != tag]

    def finish(self):
        for _, copy in self.sent:
            copy.wait_send()
        for cond, copy in self.some:
            pl.when(cond)(copy.wait_send)


def swap_halves(v, low_half):
    return jnp.where(low_half, pltpu.roll(v, 96, 1), pltpu.roll(v, 32, 1))


def head_mask(rows, width):
    return lax.broadcasted_iota(jnp.int32, (rows, width), 1) % 128 < HEAD


def forward_kernel(
    x_ref, seg_ref, freq_ref, qkv_ref, outw_ref, par_ref, gate_ref, up_ref, dn_ref,
    y_ref, A_o, F_o, Q_o, ST_o, P_o, TG_o, TT_o, N_o, I_o, PV_o, cos_ref, sin_ref,
    A, F, Q, ST, Pb, TG, TT, N, I, PV, S, AT, MF, AC, H, bias, FD, RC, RY, W, GU,
    ls, s_gu, r_gu, s_az, r_az, s_ax, r_ax, s_ay, r_ay, s_ac, r_ac, s_fz, r_fz, s_fx, r_fx,
    s_m, r_m, s_rc, r_rc, s_ry, r_ry, os,
):
    pc = Place()
    y, z, x, c, g, slot = pc.y, pc.z, pc.x, pc.c, pc.g, pc.slot
    ml = Mail()
    LAY = (0, 1)
    mid = z % 3 != 0
    near, across = pc.zto(pc.near()), pc.zto(pc.across())
    THREE = (0, 1, 2)

    own_a, own_f = [], []
    for l in LAY:
        own_a.append([])
        for h in range(2):
            dst = A.at[l, h, g, c]
            own_a[l].append(ml.local(qkv_ref.at[l, :, pl.ds(QW * h, QW)], dst.at[:, pl.ds(0, QW)], ls.at[l, h]))
            own_a[l].append(ml.local(outw_ref.at[l, :, pl.ds(OW * h, OW)], dst.at[:, pl.ds(QW, OW)], ls.at[l, 2 + h]))
            own_a[l].append(ml.local(par_ref.at[l, h], dst.at[:, pl.ds(QW + OW, 128)], ls.at[l, 4 + h]))
    wide = [ml.local(gate_ref, W.at[0], ls.at[0, 6]), ml.local(up_ref, W.at[1], ls.at[1, 6])]
    for l in LAY:
        own_f.append(ml.local(dn_ref.at[l, pl.ds(pl.multiple_of(y * 96, 96), 96)], F.at[l, chip_rows(g), pl.ds(2 * FS, D)], ls.at[l, 7]))
    greet(pc.line())

    def gu_send(l):
        ml.send(GU.at[l, 1 - c, y], F.at[l, shard_rows(g, c), pl.ds(0, 2 * FS)], s_gu.at[l], r_gu.at[l], pc.core())

    def gu_arrive(l):
        ml.arrive(F.at[l, shard_rows(g, 1 - c), pl.ds(0, 2 * FS)], s_gu.at[l], r_gu.at[l], pc.core())

    def line_own(block, ss, rs):
        ml.send(block, block, ss.at[0], rs.at[0], near)
        ml.send_if(mid, block, block, ss.at[1], rs.at[1], across)

    def line_pass(i, block, ss, rs):
        ml.arrive(block, ss.at[0], rs.at[i], near)
        to, at = ((across, 2), (near, 1), (near, 2))[i]
        ml.send_if(mid, block, block, ss.at[2 + i], rs.at[at], to)

    def a_own(l):
        for copy in own_a[l]:
            copy.wait()
        block = A.at[l, y, g, c]
        ml.send(block, block, s_ax.at[l, 0], r_ax.at[l, 0], pc.xside())
        line_own(block, s_az.at[l], r_az.at[l])

    def a_z(l, i):
        block = A.at[l, y, pc.chip_from(i, x), c]
        line_pass(i, block, s_az.at[l], r_az.at[l])
        ml.send(block, block, s_ax.at[l, 1 + i], r_ax.at[l, 1 + i], pc.xside())

    def a_yo(l, i):
        block = A.at[l, y, pc.chip_from(i, x), c]
        ml.send(block, block, s_ay.at[l, i], r_ay.at[l, i], pc.yside())

    FOUR = (None, 0, 1, 2)

    def a_x(l, j):
        ml.arrive(A.at[l, y, pc.chip_from(FOUR[j], 1 - x), c], s_ax.at[l, j], r_ax.at[l, j], pc.xside())

    def a_yx(l, j):
        block = A.at[l, y, pc.chip_from(FOUR[j], 1 - x), c]
        ml.send(block, block, s_ay.at[l, 3 + j], r_ay.at[l, 3 + j], pc.yside())

    def a_c(l, h):
        block = A.at[l, h, :, c]
        ml.send(block, block, s_ac.at[l, h], r_ac.at[l, h], pc.core())

    def a_y(l, i, xx, n):
        ml.arrive(A.at[l, 1 - y, pc.chip_from(i, xx), c], s_ay.at[l, n], r_ay.at[l, n], pc.yside())

    def a_c_arrive(l, h):
        ml.arrive(A.at[l, h, :, 1 - c], s_ac.at[l, h], r_ac.at[l, h], pc.core())

    parts = (pl.ds(0, 2 * FS), pl.ds(2 * FS, D))

    def f_ready(l):
        for w in range(2):
            F[l, shard_rows(g, c), w * FS:w * FS + FS] = GU[l, c, y, :, w * FS:w * FS + FS]
        own_f[l].wait()
        gu_arrive(l)

    def f_own_z(l, p):
        line_own(F.at[l, chip_rows(g), parts[p]], s_fz.at[l, p], r_fz.at[l, p])

    def f_own_x(l, p):
        block = F.at[l, chip_rows(g), parts[p]]
        ml.send(block, block, s_fx.at[l, p, 0], r_fx.at[l, p, 0], pc.xside())

    def f_z(l, p, i):
        block = F.at[l, chip_rows(pc.chip_from(i, x)), parts[p]]
        line_pass(i, block, s_fz.at[l, p], r_fz.at[l, p])
        ml.send(block, block, s_fx.at[l, p, 1 + i], r_fx.at[l, p, 1 + i], pc.xside())

    def f_x(l, p):
        for j in range(4):
            ml.arrive(F.at[l, chip_rows(pc.chip_from(FOUR[j], 1 - x)), parts[p]], s_fx.at[l, p, j], r_fx.at[l, p, j], pc.xside())

    def attn_ready(l):
        for i in THREE:
            a_y(l, i, x, i)
        for j in range(4):
            a_y(l, FOUR[j], 1 - x, 3 + j)
        a_c(l, 1 - y)
        a_c_arrive(l, y)
        a_c_arrive(l, 1 - y)

    out_copies = []

    def save(src, dst, i):
        out_copies.append(ml.local(src, dst, os.at[i]))

    pair_mask = head_mask(T, 128)
    low_half = lax.broadcasted_iota(jnp.int32, (T, 128), 1) % HEAD < HEAD // 2
    onehot = (lax.broadcasted_iota(jnp.int32, (8, 128), 0) == lax.broadcasted_iota(jnp.int32, (8, 128), 1)).astype(F32).astype(BF)

    def tables():
        wide_row = jnp.broadcast_to(seg_ref[...].astype(F32), (T, T))
        same = wide_row.T == wide_row
        bias[...] = jnp.where(same, 0.0, masked_score)
        at = lax.broadcasted_iota(jnp.int32, (T, T), 1).astype(F32)
        first = jnp.min(jnp.where(same, at, float(T)), axis=1, keepdims=True)
        position = lax.broadcasted_iota(jnp.int32, (T, 128), 0).astype(F32) - first
        angle = position * freq_ref[0:1, :]
        sine = jnp.sin(angle)
        cos_ref[...] = jnp.cos(angle)
        sin_ref[...] = jnp.where(low_half, -sine, sine)

    def permute():
        for copy in wide:
            copy.wait()
        def of(i, carry):
            l, w = i // 2, i % 2
            v = W[w, l]
            for cc in range(2):
                for yy in range(2):
                    pieces = [v[:, 384 * j + 192 * cc + 96 * yy:384 * j + 192 * cc + 96 * yy + 96] for j in range(G)]
                    GU[l, cc, yy, :, tile(w, FS)] = jnp.concatenate(pieces, axis=1)
            return carry
        lax.fori_loop(0, 4, of, 0)

    def project(l):
        st = S[...]
        cos, sin = cos_ref[...], sin_ref[...]
        for j in range(6):
            h, off = j // 3, (j % 3) * 384
            w = A[l, h, :, :, :, off:off + 384].reshape(D, 384)
            r = dot(st, w)
            kind = j // 2
            for t in range(3):
                v = r[:, 128 * t:128 * t + 128]
                if kind < 2:
                    v = v * cos + swap_halves(v, low_half) * sin
                col = (j % 2) * 384 + 128 * t
                Q[l, kind, :, col:col + 128] = v.astype(BF)

    def attention(l):
        def pair(p, carry):
            cols = tile(p, 128)
            q, kk, v = Q[l, 0, :, cols], Q[l, 1, :, cols], Q[l, 2, :, cols]
            outs = []
            for h in range(2):
                qh = jnp.where(pair_mask == (h == 0), q, jnp.zeros_like(q))
                s = dot_t(qh, kk) * 0.125 + bias[...]
                e = jnp.exp(s - jnp.max(s, axis=1, keepdims=True))
                pr = (e * (1.0 / jnp.sum(e, axis=1, keepdims=True))).astype(BF)
                Pb[l, 2 * p + h] = pr
                outs.append(dot(pr, v))
            AT[:, cols] = jnp.where(pair_mask, outs[0], outs[1]).astype(BF)
            return carry
        lax.fori_loop(0, PAIRS, pair, 0)

    def params(l):
        for h in range(2):
            w = A[l, h, :, :, :, QW + OW:].reshape(D, 128)
            PV[l, h] = dot_t(onehot, w)

    def out_project(l):
        for h in range(2):
            w = A[l, h, :, :, :, QW:QW + OW].reshape(D, OW)
            H[:, h * OW:h * OW + OW] = H[:, h * OW:h * OW + OW] + dot(AT[...], w)

    def norm(l, i, dst, extra):
        gain, shift = PV[l, i, 0:1, :], PV[l, i, 1:2, :]
        def rows_of(j, carry):
            rows = tile(j, 32)
            v = H[rows, :]
            if extra is not None:
                v = v + extra(rows)
            cen = v - jnp.mean(v, axis=1, keepdims=True)
            inv = lax.rsqrt(jnp.mean(cen * cen, axis=1, keepdims=True) + eps_norm)
            n = cen * inv
            N[l, i, rows, :] = n
            I[l, i, rows, :] = jnp.broadcast_to(inv, (32, 128))
            m = n * gain + shift
            H[rows, :] = m
            dst[rows, :] = m.astype(BF)
            return carry
        lax.fori_loop(0, T // 32, rows_of, 0)

    def ffn_up(l, yy):
        two = pl.ds(2 * yy, 2)
        def cols_of(j, carry):
            cols = tile(j, 256)
            xx = MF[l, two].reshape(2 * T, D)
            gate = dot(xx, F[l, :, cols])
            up = dot(xx, F[l, :, pl.ds(pl.multiple_of(FS + j * 256, 256), 256)])
            act = gate * jax.nn.sigmoid(gate) * up
            TG[l, 0, two, :, cols] = gate.astype(BF).reshape(2, T, 256)
            TG[l, 1, two, :, cols] = up.astype(BF).reshape(2, T, 256)
            AC[two, :, cols] = act.astype(BF).reshape(2, T, 256)
            return carry
        lax.fori_loop(0, FS // 256, cols_of, 0)

    def ffn_down(l, yy, cc, add):
        s_ = 2 * yy + cc
        def cols_of(j, carry):
            cols = tile(j, 256)
            w = F[l, :, pl.ds(pl.multiple_of(2 * FS + j * 256, 256), 256)]
            r = dot(AC[s_], w)
            if add:
                r = r + RC[l, yy, :, cols].astype(F32)
            FD[l, s_, :, cols] = r.astype(BF)
            return carry
        lax.fori_loop(0, D // 256, cols_of, 0)

    def turn(src, dst, col):
        def tile_of(j, carry):
            cols = tile(j, 128)
            dst[cols, pl.ds(pl.multiple_of(col, T), T)] = src[:, cols].T
            return carry
        lax.fori_loop(0, D // 128, tile_of, 0)

    def turn_slots(src, dst):
        def slot_of(i, carry):
            turn(src.at[i], dst, i * T)
            return carry
        lax.fori_loop(0, 4, slot_of, 0)

    def mid_exchange(l):
        mine = MF.at[l, slot]
        ml.send(mine, mine, s_m.at[l, 0], r_m.at[l, 0], pc.yside())
        ml.send(mine, mine, s_m.at[l, 1], r_m.at[l, 1], pc.core())

    def feed_forward(l, before_up=(), before_down=(), after_y=(), before_ry=()):
        run(before_up)
        other_y = MF.at[l, 2 * (1 - y) + c]
        ml.arrive(MF.at[l, 2 * y + 1 - c], s_m.at[l, 1], r_m.at[l, 1], pc.core())
        f_x(l, 0)
        ffn_up(l, y)
        ml.arrive(other_y, s_m.at[l, 0], r_m.at[l, 0], pc.yside())
        ml.send(other_y, other_y, s_m.at[l, 2], r_m.at[l, 2], pc.core())
        ml.arrive(MF.at[l, 2 * (1 - y) + 1 - c], s_m.at[l, 2], r_m.at[l, 2], pc.core())
        ffn_up(l, 1 - y)
        run(before_down)
        f_x(l, 1)
        def to_core(i, yy):
            ffn_down(l, yy, 1 - c, False)
            ml.send(FD.at[l, 2 * yy + 1 - c], RC.at[l, yy], s_rc.at[l, i], r_rc.at[l, i], pc.core())
        to_core(0, 1 - y)
        ml.arrive(RC.at[l, 1 - y], s_rc.at[l, 0], r_rc.at[l, 0], pc.core())
        ffn_down(l, 1 - y, c, True)
        ml.send(FD.at[l, 2 * (1 - y) + c], RY.at[l], s_ry.at[l], r_ry.at[l], pc.yside())
        run(after_y)
        to_core(1, y)
        ml.arrive(RC.at[l, y], s_rc.at[l, 1], r_rc.at[l, 1], pc.core())
        ffn_down(l, y, c, True)
        turn_slots(MF.at[l], TT.at[l, 0])
        turn_slots(AC, TT.at[l, 1])
        run(before_ry)
        ml.arrive(RY.at[l], s_ry.at[l], r_ry.at[l], pc.yside())

    def run(steps):
        for step, *what in steps:
            step(*what)

    a_own(0)
    a_own(1)
    permute()
    gu_send(0)
    gu_send(1)
    H[...] = x_ref[...].astype(F32)
    S[...] = x_ref[...]
    for i in THREE:
        a_z(0, i)
        a_yo(0, i)
    f_ready(0)
    f_own_z(0, 0)
    f_own_z(0, 1)
    f_ready(1)
    for j in range(4):
        a_x(0, j)
        a_yx(0, j)
    a_c(0, y)
    f_own_x(0, 0)
    for i in THREE:
        a_z(1, i)
    f_own_x(0, 1)
    f_own_z(1, 0)
    f_own_z(1, 1)
    tables()
    turn(S, ST.at[0, 0], 0)
    f_z(0, 0, 0)
    for j in range(4):
        a_x(1, j)
    a_c(1, y)
    a_yo(1, 0)
    a_yo(1, 1)
    f_z(0, 0, 1)
    attn_ready(0)
    save(A.at[0], A_o.at[0], 0)
    params(0)
    project(0)
    f_z(0, 0, 2)
    f_z(0, 1, 0)
    attention(0)
    f_z(0, 1, 1)
    f_z(0, 1, 2)
    f_own_x(1, 0)
    out_project(0)
    norm(0, 0, MF.at[0, slot], None)
    mid_exchange(0)
    turn(AT, ST.at[0, 1], 0)
    a_yo(1, 2)
    a_yx(1, 0)
    a_yx(1, 1)
    feed_forward(
        0,
        before_up=[(f_own_x, 1, 1), (f_z, 1, 0, 0)],
        before_down=[(f_z, 1, 0, 1)],
        after_y=[(a_yx, 1, 2), (a_yx, 1, 3)],
        before_ry=[(f_z, 1, 0, 2)],
    )
    save(F.at[0], F_o.at[0], 1)
    save(TT.at[0], TT_o.at[0], 2)
    save(TG.at[0], TG_o.at[0], 3)
    feed = lambda l: lambda rows: FD[l, slot, rows, :].astype(F32) + RY[l, rows, :].astype(F32)
    norm(0, 1, S, feed(0))
    f_z(1, 1, 0)
    attn_ready(1)
    f_z(1, 1, 1)
    save(A.at[1], A_o.at[1], 4)
    params(1)
    project(1)
    attention(1)
    f_z(1, 1, 2)
    save(Pb, P_o, 5)
    save(Q, Q_o, 6)
    out_project(1)
    norm(1, 0, MF.at[1, slot], None)
    mid_exchange(1)
    turn(S, ST.at[1, 0], 0)
    turn(AT, ST.at[1, 1], 0)
    save(ST, ST_o, 7)
    feed_forward(1)
    save(F.at[1], F_o.at[1], 8)
    norm(1, 1, y_ref, feed(1))
    save(TG.at[1], TG_o.at[1], 9)
    save(TT.at[1], TT_o.at[1], 10)
    save(N, N_o, 11)
    save(I, I_o, 12)
    save(PV, PV_o, 13)
    for copy in out_copies:
        copy.wait()
    ml.finish()


FWD_SHAPES = [
    ((2, 2, G, 2, 48, AW), BF),
    ((2, D, 2 * FS + D), BF),
    ((2, 3, T, D), BF),
    ((2, 2, D, T), BF),
    ((2, HEADS, T, T), BF),
    ((2, 2, 4, T, FS), BF),
    ((2, 2, D, 4 * T), BF),
    ((2, 2, T, D), F32),
    ((2, 2, T, 128), F32),
    ((2, 2, 8, D), F32),
]


def sems(*shape):
    return pltpu.SemaphoreType.DMA(shape)


def forward_call(args):
    any_spec = pl.BlockSpec(memory_space=pl.ANY)
    vm = pl.BlockSpec(memory_space=pltpu.VMEM)
    return pl.pallas_call(
        forward_kernel,
        out_shape=[jax.ShapeDtypeStruct((T, D), BF)]
        + [jax.ShapeDtypeStruct(s, d) for s, d in FWD_SHAPES]
        + [jax.ShapeDtypeStruct((T, 128), F32)] * 2,
        in_specs=[vm] * 3 + [any_spec] * 6,
        out_specs=[vm] + [any_spec] * len(FWD_SHAPES) + [vm] * 2,
        scratch_shapes=[pltpu.VMEM(s, d) for s, d in FWD_SHAPES]
        + [
            pltpu.VMEM((T, D), BF),
            pltpu.VMEM((T, D), BF),
            pltpu.VMEM((2, 4, T, D), BF),
            pltpu.VMEM((4, T, FS), BF),
            pltpu.VMEM((T, D), F32),
            pltpu.VMEM((T, T), F32),
            pltpu.VMEM((2, 4, T, D), BF),
            pltpu.VMEM((2, 2, T, D), BF),
            pltpu.VMEM((2, T, D), BF),
            pltpu.VMEM((2, 2, 48, 4 * FS), BF),
            pltpu.VMEM((2, 2, 2, 48, 2 * FS), BF),
            sems(2, 8),
            sems(2), sems(2),
            sems(2, 5), sems(2, 3),
            sems(2, 4), sems(2, 4),
            sems(2, 7), sems(2, 7),
            sems(2, 2), sems(2, 2),
            sems(2, 2, 5), sems(2, 2, 3),
            sems(2, 2, 4), sems(2, 2, 4),
            sems(2, 3), sems(2, 3),
            sems(2, 2), sems(2, 2),
            sems(2), sems(2),
            sems(14),
        ],
        compiler_params=pltpu.CompilerParams(collective_id=0, has_side_effects=True, vmem_limit_bytes=60 * 2**20),
        cost_estimate=pl.CostEstimate(flops=10**10, bytes_accessed=10**8, transcendentals=0),
        name="forward",
    )(*args)


def backward_kernel(
    cot_ref, cos_ref, sin_ref, A_i, F_i, Q_i, ST_i, P_i, TG_i, TT_i, N_i, I_i, PV_i,
    gin_ref, GUG, DNG, AF,
    A, F, Q, ST, Pb, TG, TT, N, I, PV,
    U, GF, GB, GA, GP, FD, RC, RY, FG, RFX, RFZ, FR, AG, RAC, RAY, RAX, RAZ, V,
    ls, s_m, r_m, s_rc, r_rc, s_ry, r_ry,
    s_fx, r_fx, s_fz, r_fz, s_fc, r_fc, s_fy, r_fy,
    s_ac, r_ac, s_ay, r_ay, s_ax, r_ax, s_az, r_az, s_af, r_af,
):
    pc = Place()
    y, z, x, c, slot = pc.y, pc.z, pc.x, pc.c, pc.slot
    ml = Mail()
    ks = (1, 3, 2)
    places = {
        "PV": (PV_i, PV, 0), "N": (N_i, N, 1), "I": (I_i, I, 2), "TT": (TT_i, TT, 3), "F": (F_i, F, 4), "TG": (TG_i, TG, 5),
        "ST": (ST_i, ST, 6), "A": (A_i, A, 7), "P": (P_i, Pb, 8), "Q": (Q_i, Q, 9),
    }
    loading = {}

    def load(l, *names):
        for name in names:
            src, dst, i = places[name]
            loading[name] = ml.local(src.at[l], dst, ls.at[i])

    def need(*names):
        for name in names:
            if name in loading:
                loading.pop(name).wait()

    load(1, "PV", "N", "I", "TT", "F", "TG", "ST", "A", "P", "Q")
    U[...] = cot_ref[...].astype(F32)
    greet(pc.everyone())

    fcols = (pl.ds(2 * FS, D), pl.ds(0, FS), pl.ds(FS, FS))

    def fx_send(l, j):
        ml.send(FG.at[:, 1 - x, :, fcols[j]], RFX.at[l, j], s_fx.at[l, j], r_fx.at[l, j], pc.xside(), ("fx", l, j))

    def fx_task(l, j):
        ml.arrive(RFX.at[l, j], s_fx.at[l, j], r_fx.at[l, j], pc.xside())
        def add(zz, carry):
            for half in range(2):
                rows = pl.ds(48 * half, 48)
                RFX[l, j, zz, rows, :] = (RFX[l, j, zz, rows, :].astype(F32) + FG[zz, x, rows, fcols[j]].astype(F32)).astype(BF)
            return carry
        lax.fori_loop(0, 4, add, 0)
        for k in ks:
            ml.send(RFX.at[l, j, (z + k) % 4], RFZ.at[l, j, k - 1], s_fz.at[l, j, k], r_fz.at[l, j, k], pc.zside(k))

    def fz_task(l, j):
        for k in ks:
            ml.arrive(RFZ.at[l, j, k - 1], s_fz.at[l, j, k], r_fz.at[l, j, k], pc.zside(k))
        def total(start):
            rows = pl.ds(start, 48)
            t = RFX[l, j, z, rows, :].astype(F32)
            for k in range(3):
                t = t + RFZ[l, j, k, rows, :].astype(F32)
            return t.astype(BF)
        if j == 0:
            for half in range(2):
                DNG[l, y, pl.ds(48 * half, 48), :] = total(48 * half)
            ml.send(DNG.at[l, y], DNG.at[l, y], s_fy.at[l, 0], r_fy.at[l, 0], pc.yside())
        else:
            FR[l, j - 1] = total(pl.multiple_of((1 - c) * 48, 48))
            ml.send(FR.at[l, j - 1], GUG.at[l, j - 1, c, y], s_fc.at[l, j], r_fc.at[l, j], pc.core())
            GUG[l, j - 1, c, y] = total(pl.multiple_of(c * 48, 48))

    def fc_task(l, j):
        ml.arrive(GUG.at[l, j - 1, 1 - c, y], s_fc.at[l, j], r_fc.at[l, j], pc.core())
        block = GUG.at[l, j - 1, :, y]
        ml.send(block, block, s_fy.at[l, j], r_fy.at[l, j], pc.yside())

    def fy_task(l, j):
        block = DNG.at[l, 1 - y] if j == 0 else GUG.at[l, j - 1, :, 1 - y]
        ml.arrive(block, s_fy.at[l, j], r_fy.at[l, j], pc.yside())

    def ac_send(l, i):
        h = (1 - y, y)[i]
        ml.send(AG.at[h, :, :, 1 - c], RAC.at[l, i], s_ac.at[l, i], r_ac.at[l, i], pc.core(), ("ac", l))

    def ac_task(l, i):
        h = (1 - y, y)[i]
        ml.arrive(RAC.at[l, i], s_ac.at[l, i], r_ac.at[l, i], pc.core())
        def add(n, carry):
            zz, xx = n // 2, n % 2
            for cols in (pl.ds(0, 768), pl.ds(768, 896)):
                RAC[l, i, zz, xx, :, cols] = (RAC[l, i, zz, xx, :, cols].astype(F32) + AG[h, zz, xx, c, :, cols].astype(F32)).astype(BF)
            return carry
        lax.fori_loop(0, 8, add, 0)
        if i == 0:
            ml.send(RAC.at[l, 0], RAY.at[l], s_ay.at[l], r_ay.at[l], pc.yside())

    def ay_task(l):
        ml.arrive(RAY.at[l], s_ay.at[l], r_ay.at[l], pc.yside())
        def add(n, carry):
            zz, xx = n // 2, n % 2
            for cols in (pl.ds(0, 768), pl.ds(768, 896)):
                RAC[l, 1, zz, xx, :, cols] = (RAC[l, 1, zz, xx, :, cols].astype(F32) + RAY[l, zz, xx, :, cols].astype(F32)).astype(BF)
            return carry
        lax.fori_loop(0, 8, add, 0)
        ml.send(RAC.at[l, 1, :, 1 - x], RAX.at[l], s_ax.at[l], r_ax.at[l], pc.xside())

    def ax_task(l):
        ml.arrive(RAX.at[l], s_ax.at[l], r_ax.at[l], pc.xside())
        def add(zz, carry):
            for cols in (pl.ds(0, 768), pl.ds(768, 896)):
                RAX[l, zz, :, cols] = (RAX[l, zz, :, cols].astype(F32) + RAC[l, 1, zz, x, :, cols].astype(F32)).astype(BF)
            return carry
        lax.fori_loop(0, 4, add, 0)
        for k in ks:
            ml.send(RAX.at[l, (z + k) % 4], RAZ.at[l, k - 1], s_az.at[l, k], r_az.at[l, k], pc.zside(k))

    def az_task(l):
        for k in ks:
            ml.arrive(RAZ.at[l, k - 1], s_az.at[l, k], r_az.at[l, k], pc.zside(k))
        for cols in (pl.ds(0, 768), pl.ds(768, 896)):
            t = RAX[l, z, :, cols].astype(F32)
            for k in range(3):
                t = t + RAZ[l, k, :, cols].astype(F32)
            AF[l, y, :, cols] = t.astype(BF)
        ml.send(AF.at[l, y], AF.at[l, y], s_af.at[l], r_af.at[l], pc.yside())

    def af_task(l):
        ml.arrive(AF.at[l, 1 - y], s_af.at[l], r_af.at[l], pc.yside())

    pair_mask = head_mask(T, 128)
    low_half = lax.broadcasted_iota(jnp.int32, (T, 128), 1) % HEAD < HEAD // 2
    onehot = (lax.broadcasted_iota(jnp.int32, (8, 128), 0) == lax.broadcasted_iota(jnp.int32, (8, 128), 1)).astype(F32).astype(BF)

    def norm_back(i, extra, dst):
        gain = PV[i, 0:1, :]
        def rows_of(j, carry):
            gs, bs = carry
            rows = tile(j, 32)
            u = U[rows, :]
            if extra is not None:
                u = u + extra(rows)
            n = N[i, rows, :]
            un = u * n
            gs = gs + un.reshape(4, 8, D).sum(0)
            bs = bs + u.reshape(4, 8, D).sum(0)
            m1 = jnp.mean(u * gain, axis=1, keepdims=True)
            m2 = jnp.mean(un * gain, axis=1, keepdims=True)
            r = I[i, rows, 0:1] * (u * gain - m1 - n * m2)
            U[rows, :] = r
            dst[rows, :] = r.astype(BF)
            return gs, bs
        zero = jnp.zeros((8, D), F32)
        gs, bs = lax.fori_loop(0, T // 32, rows_of, (zero, zero))
        row = lax.broadcasted_iota(jnp.int32, (8, D), 0)
        V[i] = jnp.where(row == 0, gs.sum(0, keepdims=True), jnp.where(row == 1, bs.sum(0, keepdims=True), 0.0))

    def act_back(l, yy):
        two = pl.ds(2 * yy, 2)
        def cols_of(j, carry):
            cols = tile(j, 256)
            ga = dot_t(GF[l, two].reshape(2 * T, D), F[cols, 2 * FS:])
            gate = TG[0, two, :, cols].reshape(2 * T, 256).astype(F32)
            up = TG[1, two, :, cols].reshape(2 * T, 256).astype(F32)
            sg = jax.nn.sigmoid(gate)
            gg = ga * up * sg * (1.0 + gate * (1.0 - sg))
            gu = ga * gate * sg
            TG[0, two, :, cols] = gg.astype(BF).reshape(2, T, 256)
            TG[1, two, :, cols] = gu.astype(BF).reshape(2, T, 256)
            return carry
        lax.fori_loop(0, FS // 256, cols_of, 0)

    def mid_back(yy, cc, add, l):
        s_ = 2 * yy + cc
        def cols_of(j, carry):
            cols = tile(j, 256)
            r = dot_t(TG[0, s_], F[cols, 0:FS]) + dot_t(TG[1, s_], F[cols, FS:2 * FS])
            if add:
                r = r + RC[l, yy, :, cols].astype(F32)
            FD[s_, :, cols] = r.astype(BF)
            return carry
        lax.fori_loop(0, D // 256, cols_of, 0)

    def weight_grad(l, j):
        def cols_of(n, carry):
            cols = tile(n, 256)
            if j == 0:
                right = GF[l, :, :, cols].reshape(4 * T, 256)
            else:
                right = TG[j - 1, :, :, cols].reshape(4 * T, 256)
            r = dot(TT[0 if j else 1], right)
            off = (2 * FS, 0, FS)[j]
            FG[:, :, :, pl.ds(pl.multiple_of(off + n * 256, 256), 256)] = r.astype(BF).reshape(4, 2, 96, 256)
            return carry
        lax.fori_loop(0, 3, cols_of, 0)

    def mid_sums(l):
        def to_core(i, yy):
            mid_back(yy, 1 - c, False, l)
            ml.send(FD.at[2 * yy + 1 - c], RC.at[l, yy], s_rc.at[l, i], r_rc.at[l, i], pc.core(), ("fd", l))
        to_core(0, 1 - y)
        ml.arrive(RC.at[l, 1 - y], s_rc.at[l, 0], r_rc.at[l, 0], pc.core())
        mid_back(1 - y, c, True, l)
        ml.send(FD.at[2 * (1 - y) + c], RY.at[l], s_ry.at[l], r_ry.at[l], pc.yside(), ("fd", l))
        to_core(1, y)
        ml.arrive(RC.at[l, y], s_rc.at[l, 1], r_rc.at[l, 1], pc.core())
        mid_back(y, c, True, l)

    def out_back():
        acc = None
        for h in range(2):
            r = dot(ST[1], GB[:, h * OW:h * OW + OW])
            AG[h, :, :, :, :, QW:QW + OW] = r.astype(BF).reshape(4, 2, 2, 48, OW)
        for h in range(2):
            t = dot_t(GB[:, h * OW:h * OW + OW], A[h, :, :, :, QW:QW + OW].reshape(D, OW))
            acc = t if acc is None else acc + t
        GA[...] = acc.astype(BF)

    def attention_back():
        def pair(p, carry):
            cols = tile(p, 128)
            q, kk, v, ga = Q[0, :, cols], Q[1, :, cols], Q[2, :, cols], GA[:, cols]
            dq, dk, dv = [], [], []
            for h in range(2):
                pl_ = Pb[2 * p + h]
                pr = pl_.astype(F32)
                gh = jnp.where(pair_mask == (h == 0), ga, jnp.zeros_like(ga))
                dp = dot_t(gh, v)
                ds = (pr * (dp - jnp.sum(dp * pr, axis=1, keepdims=True))).astype(BF)
                dq.append(dot(ds, kk))
                dk.append(dot(ds.T, q))
                dv.append(dot(pl_.T, ga))
            cos, sin = cos_ref[...], sin_ref[...]
            def back(pair_of):
                m = jnp.where(pair_mask, pair_of[0], pair_of[1]) * 0.125
                return (m * cos - swap_halves(m, low_half) * sin).astype(BF)
            GP[0, :, cols] = back(dq)
            GP[1, :, cols] = back(dk)
            GP[2, :, cols] = jnp.where(pair_mask, dv[0], dv[1]).astype(BF)
            return carry
        lax.fori_loop(0, PAIRS, pair, 0)

    def gp_chunk(j):
        return GP[j // 2, :, (j % 2) * 384:(j % 2) * 384 + 384]

    def qkv_grad(h):
        for j in range(3 * h, 3 * h + 3):
            off = (j % 3) * 384
            r = dot(ST[0], gp_chunk(j))
            AG[h, :, :, :, :, off:off + 384] = r.astype(BF).reshape(4, 2, 2, 48, 384)

    def param_grad():
        for h in range(2):
            r = lax.dot_general(V[h].astype(BF), onehot, (((0,), (0,)), ((), ())), preferred_element_type=F32)
            AG[h, :, :, :, :, QW + OW:] = r.astype(BF).reshape(4, 2, 2, 48, 128)

    def input_back():
        acc = U[...]
        for j in range(6):
            off = (j % 3) * 384
            acc = acc + dot_t(gp_chunk(j), A[j // 3, :, :, :, off:off + 384].reshape(D, 384))
        U[...] = acc

    for l in (1, 0):
        need("PV", "N", "I")
        norm_back(1, None, GF.at[l, slot])
        mine = GF.at[l, slot]
        ml.send(mine, mine, s_m.at[l, 0], r_m.at[l, 0], pc.yside())
        ml.send(mine, mine, s_m.at[l, 1], r_m.at[l, 1], pc.core())
        if l == 0:
            ml.gone(("fd", 1))
            ay_task(1)
            fz_task(1, 0)
        need("TT", "F", "TG")
        ml.arrive(GF.at[l, 2 * y + 1 - c], s_m.at[l, 1], r_m.at[l, 1], pc.core())
        act_back(l, y)
        other = GF.at[l, 2 * (1 - y) + c]
        ml.arrive(other, s_m.at[l, 0], r_m.at[l, 0], pc.yside())
        ml.send(other, other, s_m.at[l, 2], r_m.at[l, 2], pc.core())
        ml.arrive(GF.at[l, 2 * (1 - y) + 1 - c], s_m.at[l, 2], r_m.at[l, 2], pc.core())
        ml.gone(("fx", 1, 0)) if l == 0 else None
        weight_grad(l, 0)
        fx_send(l, 0)
        act_back(l, 1 - y)
        mid_sums(l)
        if l == 1:
            load(0, "F")
        ml.gone(("fx", 1, 1)) if l == 0 else None
        weight_grad(l, 1)
        fx_send(l, 1)
        ml.gone(("fx", 1, 2)) if l == 0 else None
        weight_grad(l, 2)
        fx_send(l, 2)
        if l == 1:
            load(0, "TT", "TG")
        ml.arrive(RY.at[l], s_ry.at[l], r_ry.at[l], pc.yside())
        norm_back(0, lambda rows: FD[slot, rows, :].astype(F32) + RY[l, rows, :].astype(F32), GB)
        if l == 1:
            load(0, "N", "I")
        if l == 0:
            ax_task(1)
            fz_task(1, 1)
            fz_task(1, 2)
            fc_task(1, 1)
            fc_task(1, 2)
        need("ST", "A")
        param_grad()
        out_back()
        if l == 1:
            load(0, "PV")
        fx_task(l, 0)
        need("P", "Q")
        attention_back()
        if l == 1:
            load(0, "P", "Q")
        for i in range(2):
            for h in range(2):
                pass
        qkv_grad(0)
        qkv_grad(1)
        ac_send(l, 0)
        ac_send(l, 1)
        if l == 1:
            load(0, "ST")
        fx_task(l, 1)
        input_back()
        if l == 1:
            load(0, "A")
        fx_task(l, 2)
        ac_task(l, 0)
        ac_task(l, 1)
        if l == 1:
            ml.gone(("ac", 1))
    gin_ref[...] = U[...]
    ay_task(0)
    az_task(1)
    fz_task(0, 0)
    fz_task(0, 1)
    fz_task(0, 2)
    fc_task(0, 1)
    fc_task(0, 2)
    ax_task(0)
    az_task(0)
    for l in (1, 0):
        for j in range(3):
            fy_task(l, j)
        af_task(l)
    ml.finish()


def backward_call(cot, cos, sin, kept):
    any_spec = pl.BlockSpec(memory_space=pl.ANY)
    vm = pl.BlockSpec(memory_space=pltpu.VMEM)
    return pl.pallas_call(
        backward_kernel,
        out_shape=[
            jax.ShapeDtypeStruct((T, D), F32),
            jax.ShapeDtypeStruct((2, 2, 2, 2, 48, FS), BF),
            jax.ShapeDtypeStruct((2, 2, 96, D), BF),
            jax.ShapeDtypeStruct((2, 2, 48, AW), BF),
        ],
        in_specs=[vm] * 3 + [any_spec] * len(kept),
        out_specs=[vm] * 4,
        scratch_shapes=[pltpu.VMEM(s[1:], d) for s, d in FWD_SHAPES]
        + [
            pltpu.VMEM((T, D), F32),
            pltpu.VMEM((2, 4, T, D), BF),
            pltpu.VMEM((T, D), BF),
            pltpu.VMEM((T, D), BF),
            pltpu.VMEM((3, T, D), BF),
            pltpu.VMEM((4, T, D), BF),
            pltpu.VMEM((2, 2, T, D), BF),
            pltpu.VMEM((2, T, D), BF),
            pltpu.VMEM((4, 2, 96, 2 * FS + D), BF),
            pltpu.VMEM((2, 3, 4, 96, D), BF),
            pltpu.VMEM((2, 3, 3, 96, D), BF),
            pltpu.VMEM((2, 2, 48, D), BF),
            pltpu.VMEM((2, 4, 2, 2, 48, AW), BF),
            pltpu.VMEM((2, 2, 4, 2, 48, AW), BF),
            pltpu.VMEM((2, 4, 2, 48, AW), BF),
            pltpu.VMEM((2, 4, 48, AW), BF),
            pltpu.VMEM((2, 3, 48, AW), BF),
            pltpu.VMEM((2, 8, D), F32),
            sems(10),
            sems(2, 3), sems(2, 3),
            sems(2, 2), sems(2, 2),
            sems(2), sems(2),
            sems(2, 3), sems(2, 3),
            sems(2, 3, 4), sems(2, 3, 4),
            sems(2, 3), sems(2, 3),
            sems(2, 3), sems(2, 3),
            sems(2, 2), sems(2, 2),
            sems(2), sems(2),
            sems(2), sems(2),
            sems(2, 4), sems(2, 4),
            sems(2), sems(2),
        ],
        compiler_params=pltpu.CompilerParams(collective_id=1, has_side_effects=True, vmem_limit_bytes=60 * 2**20),
        cost_estimate=pl.CostEstimate(flops=2 * 10**10, bytes_accessed=10**8, transcendentals=0),
        name="backward",
    )(cot, cos, sin, *kept)


def finish_kernel(gug, dng, af, qkv_o, out_o, gate_o, up_o, down_o, g1_o, b1_o, g2_o, b2_o):
    for l in range(2):
        for h in range(2):
            qkv_o[l, :, h * QW:h * QW + QW] = af[l, h, :, 0:QW].astype(F32)
            out_o[l, :, h * OW:h * OW + OW] = af[l, h, :, QW:QW + OW].astype(F32)
            turned = af[l, h, :, QW + OW:].astype(F32).T
            for i, ref in enumerate(((g1_o, b1_o), (g2_o, b2_o))[h]):
                ref[l:l + 1, :] = turned[i:i + 1, :]
            down_o[l, 96 * h:96 * h + 96, :] = dng[l, h].astype(F32)
    def of(n, carry):
        l, j = n // G, n % G
        for w, ref in enumerate((gate_o, up_o)):
            pairs = gug[l, w, :, :, :, tile(j // 4, 384)]
            for m in range(4):
                def put(m=m):
                    pieces = [pairs[cc, yy, :, 96 * m:96 * m + 96].astype(F32) for cc in range(2) for yy in range(2)]
                    ref[l, :, tile(j, 384)] = jnp.concatenate(pieces, axis=1)
                pl.when(j % 4 == m)(put)
        return carry
    lax.fori_loop(0, 2 * G, of, 0)


def epilogue(gug, dng, af):
    vm = pl.BlockSpec(memory_space=pltpu.VMEM)
    shapes = [(2, 48, 3 * D), (2, 48, D), (2, 48, 4 * FS), (2, 48, 4 * FS), (2, 192, D)] + [(2, 48)] * 4
    return tuple(pl.pallas_call(
        finish_kernel,
        out_shape=[jax.ShapeDtypeStruct(v, F32) for v in shapes],
        in_specs=[vm] * 3,
        out_specs=[vm] * len(shapes),
        compiler_params=pltpu.CompilerParams(vmem_limit_bytes=40 * 2**20),
        cost_estimate=pl.CostEstimate(flops=10**6, bytes_accessed=10**7, transcendentals=0),
        name="finish",
    )(gug, dng, af))


def positions_of(segment_row):
    token_index = jnp.arange(segment_row.shape[0], dtype=jnp.int32)
    before = jnp.concatenate([segment_row[:1] - 1, segment_row[:-1]])
    starts = jnp.where(segment_row != before, token_index, jnp.zeros_like(token_index))
    return token_index - lax.cummax(starts, axis=0)


def rotary_tables(position):
    half_width = HEAD // 2
    frequency = rope_base ** (-2.0 * jnp.arange(half_width, dtype=F32) / HEAD)
    angles = position.astype(F32)[:, None] * frequency[None, :]
    return jnp.cos(angles), jnp.sin(angles)


def prologue(inputs, segment_ids, qkv_weight, out_weight, gate_weight, up_weight, down_weight,
             first_gain, first_bias, second_gain, second_bias):
    frequency = rope_base ** (-2.0 * np.arange(HEAD // 2, dtype=np.float32) / HEAD)
    freq = jnp.asarray(np.tile(frequency.astype(np.float32)[None, :], (8, 4)))
    par = jnp.stack([jnp.stack([first_gain, first_bias], -1), jnp.stack([second_gain, second_bias], -1)], 1)
    par = jnp.pad(par, ((0, 0), (0, 0), (0, 0), (0, 126)))
    return inputs[0], segment_ids, freq, qkv_weight, out_weight, par, gate_weight, up_weight, down_weight


def rotate(values, cosine_table, sine_table):
    half_width = values.shape[-1] // 2
    lead_half = values[..., :half_width]
    tail_half = values[..., half_width:]
    cos_wide = cosine_table[:, None, :]
    sin_wide = sine_table[:, None, :]
    return jnp.concatenate(
        [lead_half * cos_wide - tail_half * sin_wide, tail_half * cos_wide + lead_half * sin_wide],
        axis=-1,
    )


def unrotate(values, cosine_table, sine_table):
    half_width = values.shape[-1] // 2
    lead_half = values[..., :half_width]
    tail_half = values[..., half_width:]
    cos_wide = cosine_table[:, None, :]
    sin_wide = sine_table[:, None, :]
    return jnp.concatenate(
        [lead_half * cos_wide + tail_half * sin_wide, tail_half * cos_wide - lead_half * sin_wide],
        axis=-1,
    )


def norm_forward(values, gain_row, bias_row):
    mean_row = jnp.mean(values, axis=-1, keepdims=True)
    centred = values - mean_row
    variance = jnp.mean(centred * centred, axis=-1, keepdims=True)
    inverse = lax.rsqrt(variance + eps_norm)
    normed = centred * inverse
    return (normed * gain_row + bias_row, normed, inverse)


def norm_backward(upstream, normed, inverse, gain_row):
    scaled = upstream * gain_row
    gain_sum = jnp.sum(upstream * normed, axis=0)
    bias_sum = jnp.sum(upstream, axis=0)
    grad_input = inverse * (
        scaled
        - jnp.mean(scaled, axis=-1, keepdims=True)
        - normed * jnp.mean(scaled * normed, axis=-1, keepdims=True)
    )
    return (grad_input, gain_sum, bias_sum)


def times_transposed(left_side, right_side):
    return lax.dot_general(
        left_side, right_side, (((1,), (1,)), ((), ())), preferred_element_type=jnp.float32
    )


def outer_sum(left_side, right_side):
    return lax.dot_general(
        left_side, right_side, (((0,), (0,)), ((), ())), preferred_element_type=jnp.float32
    )


def to_pairs(values):
    token_count = values.shape[0]
    return values.reshape(token_count, HEADS // 2, 2 * HEAD).transpose(1, 0, 2)


def from_pairs(values):
    return values.transpose(1, 0, 2).reshape(values.shape[1], HEADS * HEAD)


def pair_scores(query_pair, key_pair, allowed, score_scale):
    token_count = query_pair.shape[0]
    queries = query_pair.reshape(token_count, 2, HEAD)
    key_rows = key_pair.reshape(token_count, 2, HEAD)
    scores = (
        jnp.einsum("qhd,khd->hqk", queries, key_rows, preferred_element_type=jnp.float32)
        * score_scale
    )
    return (jnp.where(allowed[None], scores, masked_score), queries, key_rows)


def pair_forward(block_item, allowed, score_scale):
    query_pair, key_pair, value_pair = block_item
    token_count = query_pair.shape[0]
    scores, queries, key_rows = pair_scores(query_pair, key_pair, allowed, score_scale)
    row_top = jnp.max(scores, axis=-1, keepdims=True)
    exponent = jnp.exp(scores - row_top)
    row_total = jnp.sum(exponent, axis=-1, keepdims=True)
    probabilities = exponent / row_total
    logsum = row_top[..., 0] + jnp.log(row_total[..., 0])
    value_rows = value_pair.reshape(token_count, 2, HEAD)
    attended = jnp.einsum(
        "hqk,khd->qhd",
        probabilities.astype(jnp.bfloat16),
        value_rows,
        preferred_element_type=jnp.float32,
    )
    return (attended.reshape(token_count, 2 * HEAD), logsum)


def pair_backward(block_item, allowed, score_scale):
    query_pair, key_pair, value_pair, grad_pair, logsum = block_item
    token_count = query_pair.shape[0]
    scores, queries, key_rows = pair_scores(query_pair, key_pair, allowed, score_scale)
    probabilities = jnp.exp(scores - logsum[..., None])
    value_rows = value_pair.reshape(token_count, 2, HEAD)
    grad_rows = grad_pair.reshape(token_count, 2, HEAD)
    grad_probs = jnp.einsum(
        "qhd,khd->hqk", grad_rows, value_rows, preferred_element_type=jnp.float32
    )
    grad_values = jnp.einsum(
        "hqk,qhd->khd",
        probabilities.astype(jnp.bfloat16),
        grad_rows,
        preferred_element_type=jnp.float32,
    )
    grad_scores = probabilities * (
        grad_probs - jnp.sum(grad_probs * probabilities, axis=-1, keepdims=True)
    )
    grad_scores = grad_scores.astype(jnp.bfloat16)
    grad_queries = (
        jnp.einsum("hqk,khd->qhd", grad_scores, key_rows, preferred_element_type=jnp.float32)
        * score_scale
    )
    grad_keys = (
        jnp.einsum("hqk,qhd->khd", grad_scores, queries, preferred_element_type=jnp.float32)
        * score_scale
    )
    return (
        grad_queries.reshape(token_count, 2 * HEAD),
        grad_keys.reshape(token_count, 2 * HEAD),
        grad_values.reshape(token_count, 2 * HEAD),
    )


def layer_forward(hidden_state, weights, cosine_table, sine_table, allowed, score_scale):
    qkv_full, out_full, gate_full, up_full, down_full, gain_one, bias_one, gain_two, bias_two = (
        weights
    )
    token_count, model_width = hidden_state.shape
    state_low = hidden_state.astype(jnp.bfloat16)
    projected = jnp.dot(state_low, qkv_full, preferred_element_type=jnp.float32)
    queries = rotate(
        projected[:, :model_width].reshape(token_count, HEADS, HEAD), cosine_table, sine_table
    )
    queries = queries.astype(jnp.bfloat16).reshape(token_count, model_width)
    key_rows = rotate(
        projected[:, model_width : 2 * model_width].reshape(token_count, HEADS, HEAD),
        cosine_table,
        sine_table,
    )
    key_rows = key_rows.astype(jnp.bfloat16).reshape(token_count, model_width)
    value_rows = projected[:, 2 * model_width :].astype(jnp.bfloat16)

    def attend_pair(block_item):
        return pair_forward(block_item, allowed, score_scale)

    attended_pairs, logsum = lax.map(
        attend_pair, (to_pairs(queries), to_pairs(key_rows), to_pairs(value_rows))
    )
    attended = from_pairs(attended_pairs).astype(jnp.bfloat16)
    branch = jnp.dot(attended, out_full, preferred_element_type=jnp.float32)
    middle, normed_one, inverse_one = norm_forward(
        hidden_state + branch, gain_one.astype(jnp.float32), bias_one.astype(jnp.float32)
    )
    middle_low = middle.astype(jnp.bfloat16)
    gate_pre = jnp.dot(middle_low, gate_full, preferred_element_type=jnp.float32)
    up_pre = jnp.dot(middle_low, up_full, preferred_element_type=jnp.float32)
    activated = (jax.nn.silu(gate_pre) * up_pre).astype(jnp.bfloat16)
    feed = jnp.dot(activated, down_full, preferred_element_type=jnp.float32)
    result, normed_two, inverse_two = norm_forward(
        middle + feed, gain_two.astype(jnp.float32), bias_two.astype(jnp.float32)
    )
    stored = (
        state_low,
        queries,
        key_rows,
        value_rows,
        logsum,
        attended,
        normed_one,
        inverse_one,
        middle_low,
        gate_pre,
        up_pre,
        activated,
        normed_two,
        inverse_two,
    )
    return (result, stored)


def layer_backward(upstream, weights, stored, cosine_table, sine_table, allowed, score_scale):
    qkv_full, out_full, gate_full, up_full, down_full, gain_one, bias_one, gain_two, bias_two = (
        weights
    )
    (
        state_low,
        queries,
        key_rows,
        value_rows,
        logsum,
        attended,
        normed_one,
        inverse_one,
        middle_low,
        gate_pre,
        up_pre,
        activated,
        normed_two,
        inverse_two,
    ) = stored
    token_count, model_width = upstream.shape
    grad_mid, gain_two_sum, bias_two_sum = norm_backward(
        upstream, normed_two, inverse_two, gain_two.astype(jnp.float32)
    )
    grad_feed = grad_mid.astype(jnp.bfloat16)
    down_sum = outer_sum(activated, grad_feed)
    grad_act = times_transposed(grad_feed, down_full)
    sigmoid_gate = jax.nn.sigmoid(gate_pre)
    grad_gate = (grad_act * up_pre * sigmoid_gate * (1.0 + gate_pre * (1.0 - sigmoid_gate))).astype(
        jnp.bfloat16
    )
    grad_up = (grad_act * gate_pre * sigmoid_gate).astype(jnp.bfloat16)
    gate_sum = outer_sum(middle_low, grad_gate)
    up_sum = outer_sum(middle_low, grad_up)
    grad_middle = (
        grad_mid + times_transposed(grad_gate, gate_full) + times_transposed(grad_up, up_full)
    )
    grad_sum, gain_one_sum, bias_one_sum = norm_backward(
        grad_middle, normed_one, inverse_one, gain_one.astype(jnp.float32)
    )
    grad_branch = grad_sum.astype(jnp.bfloat16)
    out_sum = outer_sum(attended, grad_branch)
    grad_attended = times_transposed(grad_branch, out_full).astype(jnp.bfloat16)

    def attend_back(block_item):
        return pair_backward(block_item, allowed, score_scale)

    grad_query_pairs, grad_key_pairs, grad_value_pairs = lax.map(
        attend_back,
        (
            to_pairs(queries),
            to_pairs(key_rows),
            to_pairs(value_rows),
            to_pairs(grad_attended),
            logsum,
        ),
    )
    grad_queries = unrotate(
        from_pairs(grad_query_pairs).reshape(token_count, HEADS, HEAD), cosine_table, sine_table
    ).reshape(token_count, model_width)
    grad_keys = unrotate(
        from_pairs(grad_key_pairs).reshape(token_count, HEADS, HEAD), cosine_table, sine_table
    ).reshape(token_count, model_width)
    grad_projected = jnp.concatenate(
        [grad_queries, grad_keys, from_pairs(grad_value_pairs)], axis=1
    ).astype(jnp.bfloat16)
    qkv_sum = outer_sum(state_low, grad_projected)
    grad_input = grad_sum + times_transposed(grad_projected, qkv_full)
    return (
        grad_input,
        (
            qkv_sum,
            out_sum,
            gate_sum,
            up_sum,
            down_sum,
            gain_one_sum,
            bias_one_sum,
            gain_two_sum,
            bias_two_sum,
        ),
    )


def general(inputs, segment_ids, qkv_weight, out_weight, gate_weight, up_weight, down_weight,
            first_gain, first_bias, second_gain, second_bias, cotangent):
    params = (qkv_weight, out_weight, gate_weight, up_weight, down_weight, first_gain, first_bias, second_gain, second_bias)
    layers = qkv_weight.shape[0]
    segment_row = segment_ids[0]
    cosine_table, sine_table = rotary_tables(positions_of(segment_row))
    allowed = segment_row[:, None] == segment_row[None, :]
    score_scale = 1.0 / math.sqrt(HEAD)
    hidden_state = inputs[0].astype(F32)
    fetched, saved = [], []
    for layer_index in range(layers):
        weights = tuple(lax.all_gather(w[layer_index], "shard", axis=0, tiled=True) for w in params)
        fetched.append(weights)
        hidden_state, stored = layer_forward(hidden_state, weights, cosine_table, sine_table, allowed, score_scale)
        saved.append(stored)
    upstream = cotangent[0].astype(F32)
    shared = [None] * layers
    for layer_index in reversed(range(layers)):
        upstream, gradients = layer_backward(
            upstream, fetched[layer_index], saved[layer_index], cosine_table, sine_table, allowed, score_scale
        )
        owned = [lax.psum_scatter(v, "shard", scatter_dimension=0, tiled=True) for v in gradients]
        shared[layer_index] = [lax.psum(v.astype(BF), "rep").astype(F32) for v in owned]
    stacked = [jnp.stack([shared[layer_index][member] for layer_index in range(layers)]) for member in range(9)]
    return (hidden_state.astype(BF)[None], upstream[None], *stacked)


def special(inputs, segment_ids, qkv_weight, out_weight, gate_weight, up_weight, down_weight,
            first_gain, first_bias, second_gain, second_bias, cotangent):
    staged = prologue(inputs, segment_ids, qkv_weight, out_weight, gate_weight, up_weight, down_weight,
                      first_gain, first_bias, second_gain, second_bias)
    output, *kept, cos, sin = forward_call(staged)
    gin, gug, dng, af = backward_call(cotangent[0], cos, sin, kept)
    return (output[None], gin[None]) + epilogue(gug, dng, af)


IN_SPECS = (
    P(("rep", "shard"), None, None), P(("rep", "shard"), None),
) + (P(None, "shard", None),) * 5 + (P(None, "shard"),) * 4 + (P(("rep", "shard"), None, None),)
OUT_SPECS = (P(("rep", "shard"), None, None),) * 2 + (P(None, "shard", None),) * 5 + (P(None, "shard"),) * 4


def solution(mesh):
    fits = dict(mesh.shape) == {"rep": 2, "shard": 2 * G}
    return jax.shard_map(special if fits else general, mesh=mesh, in_specs=IN_SPECS, out_specs=OUT_SPECS, check_vma=False)
```

```python
import functools
import math

import jax
import jax.numpy as jnp
import numpy as np
from jax import lax
from jax.experimental import pallas as pl
from jax.experimental.pallas import tpu as pltpu
from jax.sharding import PartitionSpec as P

HEADS = 12
HEAD = 64
eps_norm = 1e-12
rope_base = 1000.0
masked_score = -1e30
MESH = pl.DeviceIdType.MESH
BF = jnp.bfloat16
F32 = jnp.float32
T = 256
D = 768
G = 8
QW = 1152
OW = 384
AW = QW + OW + 128
FS = 768
PAIRS = HEADS // 2


def dot(a, b):
    return jnp.dot(a, b, preferred_element_type=F32)


def dot_t(a, b):
    return lax.dot_general(a, b, (((1,), (1,)), ((), ())), preferred_element_type=F32)


def tile(j, width):
    return pl.ds(pl.multiple_of(j * width, width), width)


def chip_rows(g):
    return pl.ds(pl.multiple_of(g * 96, 96), 96)


def shard_rows(g, c):
    return pl.ds(pl.multiple_of(g * 96 + c * 48, 48), 48)


class Place:
    def __init__(self):
        self.y = lax.axis_index("rep")
        s = lax.axis_index("shard")
        self.c, self.x, self.z = s % 2, (s // 2) % 2, s // 4
        self.g = s // 2
        self.slot = 2 * self.y + self.c

    def at(self, y, z, x, c):
        return (y, z * 4 + x * 2 + c)

    def core(self):
        return self.at(self.y, self.z, self.x, 1 - self.c)

    def xside(self):
        return self.at(self.y, self.z, 1 - self.x, self.c)

    def yside(self):
        return self.at(1 - self.y, self.z, self.x, self.c)

    def zside(self, k):
        return self.at(self.y, (self.z + k) % 4, self.x, self.c)

    def zto(self, z):
        return self.at(self.y, z, self.x, self.c)

    def near(self):
        return self.z + 1 - 2 * (self.z % 2)

    def across(self):
        return 3 - self.z

    def source(self, i):
        return (self.near(), 2 - self.z // 2, 3 - 3 * (self.z // 2))[i]

    def chip_from(self, i, x):
        return 2 * (self.z if i is None else self.source(i)) + x

    def chip(self, k, x):
        return 2 * ((self.z + 4 - k) % 4) + x

    def line(self):
        return [self.core(), self.xside(), self.yside(), self.zto(self.near()), self.zto(self.across())]

    def everyone(self):
        return [self.core(), self.xside(), self.yside()] + [self.zside(k) for k in (1, 2, 3)]


def greet(partners):
    barrier = pltpu.get_barrier_semaphore()
    for who in partners:
        pl.semaphore_signal(barrier, inc=1, device_id=who, device_id_type=MESH)
    pl.semaphore_wait(barrier, len(partners))


class Mail:
    def __init__(self):
        self.sent = []
        self.some = []

    def send(self, src, dst, send_sem, recv_sem, who, tag=None):
        copy = pltpu.make_async_remote_copy(src, dst, send_sem, recv_sem, device_id=who, device_id_type=MESH)
        copy.start()
        self.sent.append((tag, copy))

    def later(self, src, dst, send_sem, recv_sem, who, cond):
        copy = pltpu.make_async_remote_copy(src, dst, send_sem, recv_sem, device_id=who, device_id_type=MESH)
        self.some.append((cond, copy))
        return copy

    def send_if(self, cond, src, dst, send_sem, recv_sem, who):
        copy = pltpu.make_async_remote_copy(src, dst, send_sem, recv_sem, device_id=who, device_id_type=MESH)
        pl.when(cond)(copy.start)
        self.some.append((cond, copy))

    def local(self, src, dst, sem):
        copy = pltpu.make_async_copy(src, dst, sem)
        copy.start()
        return copy

    def arrive(self, dst, send_sem, recv_sem, who):
        pltpu.make_async_remote_copy(dst, dst, send_sem, recv_sem, device_id=who, device_id_type=MESH).wait_recv()

    def gone(self, tag):
        for t, copy in self.sent:
            if t == tag:
                copy.wait_send()
        self.sent = [(t, copy) for t, copy in self.sent if t != tag]

    def finish(self):
        for _, copy in self.sent:
            copy.wait_send()
        for cond, copy in self.some:
            pl.when(cond)(copy.wait_send)


def swap_halves(v, low_half):
    return jnp.where(low_half, pltpu.roll(v, 96, 1), pltpu.roll(v, 32, 1))


def head_mask(rows, width):
    return lax.broadcasted_iota(jnp.int32, (rows, width), 1) % 128 < HEAD


def forward_kernel(
    x_ref, seg_ref, freq_ref, qkv_ref, outw_ref, par_ref, gate_ref, up_ref, dn_ref,
    y_ref, A_o, F_o, Q_o, ST_o, P_o, TG_o, TT_o, N_o, I_o, PV_o, cos_ref, sin_ref,
    A, F, Q, ST, Pb, TG, TT, N, I, PV, S, AT, MF, AC, H, bias, FD, RC, RY, W, GU,
    ls, s_gu, r_gu, s_az, r_az, s_ax, r_ax, s_ay, r_ay, s_ac, r_ac, s_fz, r_fz, s_fx, r_fx,
    s_m, r_m, s_rc, r_rc, s_ry, r_ry, os,
):
    pc = Place()
    y, z, x, c, g, slot = pc.y, pc.z, pc.x, pc.c, pc.g, pc.slot
    ml = Mail()
    LAY = (0, 1)
    mid = z % 3 != 0
    near, across = pc.zto(pc.near()), pc.zto(pc.across())
    THREE = (0, 1, 2)

    own_a, own_f = [], []
    for l in LAY:
        own_a.append([])
        for h in range(2):
            dst = A.at[l, h, g, c]
            own_a[l].append(ml.local(qkv_ref.at[l, :, pl.ds(QW * h, QW)], dst.at[:, pl.ds(0, QW)], ls.at[l, h]))
            own_a[l].append(ml.local(outw_ref.at[l, :, pl.ds(OW * h, OW)], dst.at[:, pl.ds(QW, OW)], ls.at[l, 2 + h]))
            own_a[l].append(ml.local(par_ref.at[l, h], dst.at[:, pl.ds(QW + OW, 128)], ls.at[l, 4 + h]))
    wide = [ml.local(gate_ref, W.at[0], ls.at[0, 6]), ml.local(up_ref, W.at[1], ls.at[1, 6])]
    for l in LAY:
        own_f.append(ml.local(dn_ref.at[l, pl.ds(pl.multiple_of(y * 96, 96), 96)], F.at[l, chip_rows(g), pl.ds(2 * FS, D)], ls.at[l, 7]))
    greet(pc.line())

    def gu_send(l):
        ml.send(GU.at[l, 1 - c, y], F.at[l, shard_rows(g, c), pl.ds(0, 2 * FS)], s_gu.at[l], r_gu.at[l], pc.core())

    def gu_arrive(l):
        ml.arrive(F.at[l, shard_rows(g, 1 - c), pl.ds(0, 2 * FS)], s_gu.at[l], r_gu.at[l], pc.core())

    def line_own(block, ss, rs):
        ml.send(block, block, ss.at[0], rs.at[0], near)
        ml.send_if(mid, block, block, ss.at[1], rs.at[1], across)

    def line_pass(i, block, ss, rs):
        ml.arrive(block, ss.at[0], rs.at[i], near)
        to, at = ((across, 2), (near, 1), (near, 2))[i]
        ml.send_if(mid, block, block, ss.at[2 + i], rs.at[at], to)

    def a_own(l):
        for copy in own_a[l]:
            copy.wait()
        block = A.at[l, y, g, c]
        ml.send(block, block, s_ax.at[l, 0], r_ax.at[l, 0], pc.xside())
        line_own(block, s_az.at[l], r_az.at[l])

    def a_z(l, i):
        block = A.at[l, y, pc.chip_from(i, x), c]
        line_pass(i, block, s_az.at[l], r_az.at[l])
        ml.send(block, block, s_ax.at[l, 1 + i], r_ax.at[l, 1 + i], pc.xside())

    def a_yo(l, i):
        block = A.at[l, y, pc.chip_from(i, x), c]
        ml.send(block, block, s_ay.at[l, i], r_ay.at[l, i], pc.yside())

    FOUR = (None, 0, 1, 2)

    def a_x(l, j):
        ml.arrive(A.at[l, y, pc.chip_from(FOUR[j], 1 - x), c], s_ax.at[l, j], r_ax.at[l, j], pc.xside())

    def a_yx(l, j):
        block = A.at[l, y, pc.chip_from(FOUR[j], 1 - x), c]
        ml.send(block, block, s_ay.at[l, 3 + j], r_ay.at[l, 3 + j], pc.yside())

    def a_c(l, h):
        block = A.at[l, h, :, c]
        ml.send(block, block, s_ac.at[l, h], r_ac.at[l, h], pc.core())

    def a_y(l, i, xx, n):
        ml.arrive(A.at[l, 1 - y, pc.chip_from(i, xx), c], s_ay.at[l, n], r_ay.at[l, n], pc.yside())

    def a_c_arrive(l, h):
        ml.arrive(A.at[l, h, :, 1 - c], s_ac.at[l, h], r_ac.at[l, h], pc.core())

    parts = (pl.ds(0, 2 * FS), pl.ds(2 * FS, D))

    def f_ready(l):
        for w in range(2):
            F[l, shard_rows(g, c), w * FS:w * FS + FS] = GU[l, c, y, :, w * FS:w * FS + FS]
        own_f[l].wait()
        gu_arrive(l)

    def f_own_z(l, p):
        line_own(F.at[l, chip_rows(g), parts[p]], s_fz.at[l, p], r_fz.at[l, p])

    def f_own_x(l, p):
        block = F.at[l, chip_rows(g), parts[p]]
        ml.send(block, block, s_fx.at[l, p, 0], r_fx.at[l, p, 0], pc.xside())

    def f_z(l, p, i):
        block = F.at[l, chip_rows(pc.chip_from(i, x)), parts[p]]
        line_pass(i, block, s_fz.at[l, p], r_fz.at[l, p])
        ml.send(block, block, s_fx.at[l, p, 1 + i], r_fx.at[l, p, 1 + i], pc.xside())

    def f_x(l, p):
        for j in range(4):
            ml.arrive(F.at[l, chip_rows(pc.chip_from(FOUR[j], 1 - x)), parts[p]], s_fx.at[l, p, j], r_fx.at[l, p, j], pc.xside())

    out_copies = []

    def save(src, dst):
        out_copies.append(ml.local(src, dst, os.at[len(out_copies)]))

    pair_mask = head_mask(T, 128)
    low_half = lax.broadcasted_iota(jnp.int32, (T, 128), 1) % HEAD < HEAD // 2
    onehot = (lax.broadcasted_iota(jnp.int32, (8, 128), 0) == lax.broadcasted_iota(jnp.int32, (8, 128), 1)).astype(F32).astype(BF)

    def tables():
        wide_row = jnp.broadcast_to(seg_ref[...].astype(F32), (T, T))
        same = wide_row.T == wide_row
        bias[...] = jnp.where(same, 0.0, masked_score)
        at = lax.broadcasted_iota(jnp.int32, (T, T), 1).astype(F32)
        first = jnp.min(jnp.where(same, at, float(T)), axis=1, keepdims=True)
        position = lax.broadcasted_iota(jnp.int32, (T, 128), 0).astype(F32) - first
        angle = position * freq_ref[0:1, :]
        sine = jnp.sin(angle)
        cos_ref[...] = jnp.cos(angle)
        sin_ref[...] = jnp.where(low_half, -sine, sine)

    def permute():
        for copy in wide:
            copy.wait()
        def of(i, carry):
            l, w = i // 2, i % 2
            v = W[w, l]
            for cc in range(2):
                for yy in range(2):
                    pieces = [v[:, 384 * j + 192 * cc + 96 * yy:384 * j + 192 * cc + 96 * yy + 96] for j in range(G)]
                    GU[l, cc, yy, :, tile(w, FS)] = jnp.concatenate(pieces, axis=1)
            return carry
        lax.fori_loop(0, 4, of, 0)

    def project(l):
        st = S[...]
        cos, sin = cos_ref[...], sin_ref[...]
        for j in range(6):
            h, off = j // 3, (j % 3) * 384
            w = A[l, h, :, :, :, off:off + 384].reshape(D, 384)
            r = dot(st, w)
            kind = j // 2
            for t in range(3):
                v = r[:, 128 * t:128 * t + 128]
                if kind < 2:
                    v = v * cos + swap_halves(v, low_half) * sin
                col = (j % 2) * 384 + 128 * t
                Q[l, kind, :, col:col + 128] = v.astype(BF)

    def attention(l):
        def pair(p, carry):
            cols = tile(p, 128)
            q, kk, v = Q[l, 0, :, cols], Q[l, 1, :, cols], Q[l, 2, :, cols]
            outs = []
            for h in range(2):
                qh = jnp.where(pair_mask == (h == 0), q, jnp.zeros_like(q))
                s = dot_t(qh, kk) * 0.125 + bias[...]
                e = jnp.exp(s - jnp.max(s, axis=1, keepdims=True))
                pr = (e * (1.0 / jnp.sum(e, axis=1, keepdims=True))).astype(BF)
                Pb[l, 2 * p + h] = pr
                outs.append(dot(pr, v))
            AT[:, cols] = jnp.where(pair_mask, outs[0], outs[1]).astype(BF)
            return carry
        lax.fori_loop(0, PAIRS, pair, 0)

    def params(l):
        for h in range(2):
            w = A[l, h, :, :, :, QW + OW:].reshape(D, 128)
            PV[l, h] = dot_t(onehot, w)

    def out_project(l):
        for h in range(2):
            w = A[l, h, :, :, :, QW:QW + OW].reshape(D, OW)
            H[:, h * OW:h * OW + OW] = H[:, h * OW:h * OW + OW] + dot(AT[...], w)

    def norm(l, i, dst, extra):
        gain, shift = PV[l, i, 0:1, :], PV[l, i, 1:2, :]
        def rows_of(j, carry):
            rows = tile(j, 32)
            v = H[rows, :]
            if extra is not None:
                v = v + extra(rows)
            cen = v - jnp.mean(v, axis=1, keepdims=True)
            inv = lax.rsqrt(jnp.mean(cen * cen, axis=1, keepdims=True) + eps_norm)
            n = cen * inv
            N[l, i, rows, :] = n
            I[l, i, rows, :] = jnp.broadcast_to(inv, (32, 128))
            m = n * gain + shift
            H[rows, :] = m
            dst[rows, :] = m.astype(BF)
            return carry
        lax.fori_loop(0, T // 32, rows_of, 0)

    def ffn_up(l, first, count):
        some = pl.ds(first, count)
        def cols_of(j, carry):
            cols = tile(j, 256)
            xx = MF[l, some].reshape(count * T, D)
            gate = dot(xx, F[l, :, cols])
            up = dot(xx, F[l, :, pl.ds(pl.multiple_of(FS + j * 256, 256), 256)])
            act = gate * jax.nn.sigmoid(gate) * up
            TG[l, 0, some, :, cols] = gate.astype(BF).reshape(count, T, 256)
            TG[l, 1, some, :, cols] = up.astype(BF).reshape(count, T, 256)
            AC[some, :, cols] = act.astype(BF).reshape(count, T, 256)
            return carry
        lax.fori_loop(0, FS // 256, cols_of, 0)

    def ffn_down(l, s_, plus=None):
        def cols_of(j, carry):
            cols = tile(j, 256)
            r = dot(AC[s_], F[l, :, pl.ds(pl.multiple_of(2 * FS + j * 256, 256), 256)])
            if plus is not None:
                r = r + plus[:, cols].astype(F32)
            FD[l, s_, :, cols] = r.astype(BF)
            return carry
        lax.fori_loop(0, D // 256, cols_of, 0)

    def turn(src, dst, col):
        def tile_of(j, carry):
            cols = tile(j, 128)
            dst[cols, pl.ds(pl.multiple_of(col, T), T)] = src[:, cols].T
            return carry
        lax.fori_loop(0, D // 128, tile_of, 0)

    def turn_slots(src, dst):
        def slot_of(i, carry):
            turn(src.at[i], dst, i * T)
            return carry
        lax.fori_loop(0, 4, slot_of, 0)

    def begin():
        H[...] = x_ref[...].astype(F32)
        S[...] = x_ref[...]
        permute()
        gu_send(0)
        gu_send(1)

    def projected(l):
        params(l)
        project(l)
        turn(S, ST.at[l, 0], 0)

    def scores(l):
        attention(l)
        save(Pb.at[l], P_o.at[l])
        save(Q.at[l], Q_o.at[l])

    def first_norm(l):
        out_project(l)
        norm(l, 0, MF.at[l, slot], None)
        mine = MF.at[l, slot]
        ml.send(mine, mine, s_m.at[l, 0], r_m.at[l, 0], pc.yside())
        ml.send(mine, mine, s_m.at[l, 1], r_m.at[l, 1], pc.core())

    def turn_attended(l):
        turn(AT, ST.at[l, 1], 0)
        save(ST.at[l], ST_o.at[l])

    def half_sums(l, i, yy):
        s_ = 2 * yy + 1 - c
        ffn_down(l, s_)
        ml.send(FD.at[l, s_], RC.at[l, yy], s_rc.at[l, i], r_rc.at[l, i], pc.core())

    def own_up(l):
        ml.arrive(MF.at[l, 2 * y + 1 - c], s_m.at[l, 1], r_m.at[l, 1], pc.core())
        f_x(l, 0)
        ffn_up(l, 2 * y, 2)

    def own_down(l):
        f_x(l, 1)
        half_sums(l, 1, y)
        ffn_down(l, slot)

    def pass_on(l):
        block = MF.at[l, 2 * (1 - y) + c]
        ml.arrive(block, s_m.at[l, 0], r_m.at[l, 0], pc.yside())
        ml.send(block, block, s_m.at[l, 2], r_m.at[l, 2], pc.core())

    def other_up(l):
        others = 2 * (1 - y)
        ffn_up(l, others + c, 1)
        ml.arrive(MF.at[l, others + 1 - c], s_m.at[l, 2], r_m.at[l, 2], pc.core())
        ffn_up(l, others + 1 - c, 1)

    def other_down(l):
        others = 2 * (1 - y)
        half_sums(l, 0, 1 - y)
        ml.arrive(RC.at[l, 1 - y], s_rc.at[l, 0], r_rc.at[l, 0], pc.core())
        ffn_down(l, others + c, RC.at[l, 1 - y])
        ml.send(FD.at[l, others + c], RY.at[l], s_ry.at[l], r_ry.at[l], pc.yside())

    def turn_middle(l):
        turn_slots(MF.at[l], TT.at[l, 0])

    def turn_activated(l):
        turn_slots(AC, TT.at[l, 1])
        save(F.at[l], F_o.at[l])
        save(TT.at[l], TT_o.at[l])
        save(TG.at[l], TG_o.at[l])

    def second_norm(l):
        ml.arrive(RC.at[l, y], s_rc.at[l, 1], r_rc.at[l, 1], pc.core())
        ml.arrive(RY.at[l], s_ry.at[l], r_ry.at[l], pc.yside())
        feed = lambda rows: FD[l, slot, rows, :].astype(F32) + RC[l, y, rows, :].astype(F32) + RY[l, rows, :].astype(F32)
        norm(l, 1, S if l == 0 else y_ref, feed)

    def ay_arrive(l, n):
        if n < 3:
            a_y(l, n, x, n)
        else:
            a_y(l, FOUR[n - 3], 1 - x, n)

    def ac_own(l):
        a_c(l, y)

    def ac_other(l):
        a_c(l, 1 - y)

    def attn_ready(l):
        a_c_arrive(l, y)
        a_c_arrive(l, 1 - y)
        save(A.at[l], A_o.at[l])

    a_own(0)
    begin()
    f_ready(0)
    a_own(1)
    a_z(0, 0)
    tables()
    a_yo(0, 0)
    f_own_x(0, 0)
    a_x(0, 0)
    f_own_z(0, 1)
    a_yx(0, 0)
    a_z(0, 1)
    a_z(1, 0)
    a_z(0, 2)
    a_x(1, 0)
    a_x(0, 1)
    f_z(0, 1, 0)
    ay_arrive(0, 0)
    a_yo(0, 1)
    f_own_z(0, 0)
    a_yo(0, 2)
    a_yo(1, 0)
    a_yx(0, 1)
    a_x(0, 2)
    ay_arrive(0, 1)
    ay_arrive(0, 2)
    a_z(1, 1)
    a_z(1, 2)
    a_yx(0, 2)
    a_x(0, 3)
    a_yx(0, 3)
    f_ready(1)
    a_x(1, 1)
    f_z(0, 0, 0)
    f_z(0, 0, 1)
    ay_arrive(0, 3)
    ac_own(0)
    ay_arrive(0, 4)
    ay_arrive(0, 5)
    a_yo(1, 1)
    a_yx(1, 0)
    f_own_x(0, 1)
    ay_arrive(0, 6)
    ac_other(0)
    a_x(1, 2)
    a_yo(1, 2)
    f_z(0, 0, 2)
    attn_ready(0)
    f_own_z(1, 0)
    ay_arrive(1, 0)
    a_yx(1, 1)
    a_x(1, 3)
    ay_arrive(1, 1)
    projected(0)
    scores(0)
    first_norm(0)
    ay_arrive(1, 2)
    f_z(0, 1, 1)
    ac_own(1)
    ay_arrive(1, 3)
    f_z(0, 1, 2)
    a_yx(1, 2)
    f_z(1, 0, 0)
    f_own_x(1, 1)
    f_z(1, 0, 1)
    ay_arrive(1, 4)
    own_up(0)
    pass_on(0)
    turn_attended(0)
    a_yx(1, 3)
    other_up(0)
    f_own_z(1, 1)
    f_own_x(1, 0)
    ay_arrive(1, 5)
    own_down(0)
    other_down(0)
    ay_arrive(1, 6)
    f_z(1, 0, 2)
    ac_other(1)
    turn_middle(0)
    f_z(1, 1, 0)
    f_z(1, 1, 1)
    attn_ready(1)
    second_norm(0)
    projected(1)
    scores(1)
    first_norm(1)
    f_z(1, 1, 2)
    turn_activated(0)
    own_up(1)
    own_down(1)
    pass_on(1)
    other_up(1)
    other_down(1)
    turn_middle(1)
    turn_attended(1)
    turn_activated(1)
    second_norm(1)
    for src, dst in ((N, N_o), (I, I_o), (PV, PV_o)):
        save(src, dst)
    for copy in out_copies:
        copy.wait()
    ml.finish()


FWD_SHAPES = [
    ((2, 2, G, 2, 48, AW), BF),
    ((2, D, 2 * FS + D), BF),
    ((2, 3, T, D), BF),
    ((2, 2, D, T), BF),
    ((2, HEADS, T, T), BF),
    ((2, 2, 4, T, FS), BF),
    ((2, 2, D, 4 * T), BF),
    ((2, 2, T, D), F32),
    ((2, 2, T, 128), F32),
    ((2, 2, 8, D), F32),
]


def sems(*shape):
    return pltpu.SemaphoreType.DMA(shape)


def forward_call(args):
    any_spec = pl.BlockSpec(memory_space=pl.ANY)
    vm = pl.BlockSpec(memory_space=pltpu.VMEM)
    return pl.pallas_call(
        forward_kernel,
        out_shape=[jax.ShapeDtypeStruct((T, D), BF)]
        + [jax.ShapeDtypeStruct(s, d) for s, d in FWD_SHAPES]
        + [jax.ShapeDtypeStruct((T, 128), F32)] * 2,
        in_specs=[vm] * 3 + [any_spec] * 6,
        out_specs=[vm] + [any_spec] * len(FWD_SHAPES) + [vm] * 2,
        scratch_shapes=[pltpu.VMEM(s, d) for s, d in FWD_SHAPES]
        + [
            pltpu.VMEM((T, D), BF),
            pltpu.VMEM((T, D), BF),
            pltpu.VMEM((2, 4, T, D), BF),
            pltpu.VMEM((4, T, FS), BF),
            pltpu.VMEM((T, D), F32),
            pltpu.VMEM((T, T), F32),
            pltpu.VMEM((2, 4, T, D), BF),
            pltpu.VMEM((2, 2, T, D), BF),
            pltpu.VMEM((2, T, D), BF),
            pltpu.VMEM((2, 2, 48, 4 * FS), BF),
            pltpu.VMEM((2, 2, 2, 48, 2 * FS), BF),
            sems(2, 8),
            sems(2), sems(2),
            sems(2, 5), sems(2, 3),
            sems(2, 4), sems(2, 4),
            sems(2, 7), sems(2, 7),
            sems(2, 2), sems(2, 2),
            sems(2, 2, 5), sems(2, 2, 3),
            sems(2, 2, 4), sems(2, 2, 4),
            sems(2, 3), sems(2, 3),
            sems(2, 2), sems(2, 2),
            sems(2), sems(2),
            sems(17),
        ],
        compiler_params=pltpu.CompilerParams(collective_id=0, has_side_effects=True, vmem_limit_bytes=60 * 2**20),
        cost_estimate=pl.CostEstimate(flops=10**10, bytes_accessed=10**8, transcendentals=0),
        name="forward",
    )(*args)


def backward_kernel(
    cot_ref, cos_ref, sin_ref, A_i, F_i, Q_i, ST_i, P_i, TG_i, TT_i, N_i, I_i, PV_i,
    gin_ref, GUG, DNG, AF,
    A, F, Q, ST, Pb, TG, TT, N, I, PV,
    U, GF, GB, GP, FD, RC, RY, FG, RFX, RFZ, FR, AG, RAC, RAY, RAX, RAZ, V,
    ls, s_m, r_m, s_rc, r_rc, s_ry, r_ry,
    s_fx, r_fx, s_fz, r_fz, s_fc, r_fc, s_fy, r_fy,
    s_ac, r_ac, s_ay, r_ay, s_ax, r_ax, s_az, r_az, s_af, r_af,
):
    pc = Place()
    y, z, x, c, slot = pc.y, pc.z, pc.x, pc.c, pc.slot
    ml = Mail()
    mid = z % 3 != 0
    zn = pc.near()
    near, across = pc.zto(zn), pc.zto(3 - z)
    planes = (3 - zn, 3 - z, zn, z)
    places = {
        "PV": (PV_i, PV, 0), "N": (N_i, N, 1), "I": (I_i, I, 2), "TT": (TT_i, TT, 3), "F": (F_i, F, 4), "TG": (TG_i, TG, 5),
        "ST": (ST_i, ST, 6), "A": (A_i, A, 7), "P": (P_i, Pb, 8), "Q": (Q_i, Q, 9),
    }
    loading = {}

    def load(l, *names):
        for name in names:
            src, dst, i = places[name]
            loading[name] = ml.local(src.at[l], dst, ls.at[i])

    def need(*names):
        for name in names:
            if name in loading:
                loading.pop(name).wait()

    load(1, "PV", "N", "I", "TT", "F", "TG", "ST", "A", "P", "Q")
    U[...] = cot_ref[...].astype(F32)
    greet(pc.line())

    fcols = (pl.ds(2 * FS, D), pl.ds(0, FS), pl.ds(FS, FS))

    def fx_send(l, j):
        for n in range(4):
            ml.send(FG.at[planes[n], 1 - x, :, fcols[j]], RFX.at[l, j, planes[n]], s_fx.at[l, j, n], r_fx.at[l, j, n], pc.xside(), ("fx", l, j))

    def line_start(n, part, R, ss, rs):
        slot_of = (1, 2, 0)[n]
        ml.send_if(z % 3 == 0, part(planes[n]), R.at[slot_of], ss.at[n], rs.at[slot_of], near)

    def plus(dst, src, rows, widths):
        for r in range(0, rows, 48):
            at = 0
            for w in widths:
                here = (pl.ds(r, 48), pl.ds(at, w))
                dst[here] = (dst[here].astype(F32) + src[here].astype(F32)).astype(BF)
                at += w

    def line_middle(part, R, ss, rs, rows, widths):
        far = [pltpu.make_async_remote_copy(R.at[n], R.at[n], ss.at[0], rs.at[n], device_id=near, device_id_type=MESH) for n in (1, 2)]
        on = [
            ml.later(part(plane), R.at[3 + n], ss.at[3 + n], rs.at[3 + n], across, mid)
            for n, plane in enumerate((3 - z, 3 - zn))
        ]
        dsts = [part(3 - z), part(3 - zn)]
        def go():
            for n in range(2):
                far[n].wait_recv()
                plus(dsts[n], R.at[1 + n], rows, widths)
                on[n].start()
        pl.when(mid)(go)

    def line_end(part, R, ss, rs, rows, widths):
        back = [pltpu.make_async_remote_copy(R.at[n], R.at[n], ss.at[0], rs.at[n], device_id=across, device_id_type=MESH) for n in (3, 4)]
        last = ml.later(part(zn), R.at[0], ss.at[5], rs.at[0], near, mid)
        dsts = [part(z), part(zn)]
        def go():
            back[1].wait_recv()
            plus(dsts[1], R.at[4], rows, widths)
            last.start()
            back[0].wait_recv()
            plus(dsts[0], R.at[3], rows, widths)
        pl.when(mid)(go)
        ml.arrive(R.at[0], ss.at[0], rs.at[0], near)

    FW, AWS = (D,), (768, 896)

    def fpart(l, j):
        return lambda zz: RFX.at[l, j, zz]

    def fx_task(l, j, n):
        if True:
            p = planes[n]
            ml.arrive(RFX.at[l, j, p], s_fx.at[l, j, n], r_fx.at[l, j, n], pc.xside())
            for half in range(2):
                rows = pl.ds(48 * half, 48)
                RFX[l, j, p, rows, :] = (RFX[l, j, p, rows, :].astype(F32) + FG[p, x, rows, fcols[j]].astype(F32)).astype(BF)
            if n < 3:
                line_start(n, fpart(l, j), RFZ.at[l, j], s_fz.at[l, j], r_fz.at[l, j])

    def fm_task(l, j):
        line_middle(fpart(l, j), RFZ.at[l, j], s_fz.at[l, j], r_fz.at[l, j], 96, FW)

    def fz_task(l, j):
        line_end(fpart(l, j), RFZ.at[l, j], s_fz.at[l, j], r_fz.at[l, j], 96, FW)
        def total(start):
            rows = pl.ds(start, 48)
            return (RFX[l, j, z, rows, :].astype(F32) + RFZ[l, j, 0, rows, :].astype(F32)).astype(BF)
        if j == 0:
            for half in range(2):
                DNG[l, y, pl.ds(48 * half, 48), :] = total(48 * half)
            ml.send(DNG.at[l, y], DNG.at[l, y], s_fy.at[l, 0], r_fy.at[l, 0], pc.yside())
        else:
            FR[l, j - 1] = total(pl.multiple_of((1 - c) * 48, 48))
            ml.send(FR.at[l, j - 1], GUG.at[l, j - 1, c, y], s_fc.at[l, j], r_fc.at[l, j], pc.core())
            GUG[l, j - 1, c, y] = total(pl.multiple_of(c * 48, 48))

    def fc_task(l, j):
        ml.arrive(GUG.at[l, j - 1, 1 - c, y], s_fc.at[l, j], r_fc.at[l, j], pc.core())
        block = GUG.at[l, j - 1, :, y]
        ml.send(block, block, s_fy.at[l, j], r_fy.at[l, j], pc.yside())

    def fy_task(l, j):
        block = DNG.at[l, 1 - y] if j == 0 else GUG.at[l, j - 1, :, 1 - y]
        ml.arrive(block, s_fy.at[l, j], r_fy.at[l, j], pc.yside())

    acols = (pl.ds(0, QW), pl.ds(QW, AW - QW))
    awide = ((768, 384), (512,))

    def ac_send(l, p, i):
        h = (1 - y, y)[i]
        ml.send(AG.at[h, :, :, 1 - c, :, acols[p]], RAC.at[l, i, :, :, :, acols[p]], s_ac.at[l, p, i], r_ac.at[l, p, i], pc.core(), ("ac", l))

    def ac_sum(l, p, i):
        h = (1 - y, y)[i]
        ml.arrive(RAC.at[l, i, :, :, :, acols[p]], s_ac.at[l, p, i], r_ac.at[l, p, i], pc.core())
        def add(n, carry):
            zz, xx = n // 2, n % 2
            plus(RAC.at[l, i, zz, xx, :, acols[p]], AG.at[h, zz, xx, c, :, acols[p]], 48, awide[p])
            return carry
        lax.fori_loop(0, 8, add, 0)

    def ay_send(l, p, n):
        q = planes[n]
        ml.send(RAC.at[l, 0, q, :, :, acols[p]], RAY.at[l, q, :, :, acols[p]], s_ay.at[l, p, n], r_ay.at[l, p, n], pc.yside())

    def ay_task(l, p, n):
        q = planes[n]
        ml.arrive(RAY.at[l, q, :, :, acols[p]], s_ay.at[l, p, n], r_ay.at[l, p, n], pc.yside())
        for xx in range(2):
            plus(RAC.at[l, 1, q, xx, :, acols[p]], RAY.at[l, q, xx, :, acols[p]], 48, awide[p])
        ml.send(RAC.at[l, 1, q, 1 - x, :, acols[p]], RAX.at[l, q, :, acols[p]], s_ax.at[l, p, n], r_ax.at[l, p, n], pc.xside())

    def apart(l, p):
        return lambda zz: RAX.at[l, zz, :, acols[p]]

    def ax_task(l, p, n):
        q = planes[n]
        ml.arrive(RAX.at[l, q, :, acols[p]], s_ax.at[l, p, n], r_ax.at[l, p, n], pc.xside())
        plus(RAX.at[l, q, :, acols[p]], RAC.at[l, 1, q, x, :, acols[p]], 48, awide[p])
        if n < 3:
            line_start(n, apart(l, p), RAZ.at[l, :, :, acols[p]], s_az.at[l, p], r_az.at[l, p])

    def am_task(l, p):
        line_middle(apart(l, p), RAZ.at[l, :, :, acols[p]], s_az.at[l, p], r_az.at[l, p], 48, awide[p])

    def az_task(l, p):
        line_end(apart(l, p), RAZ.at[l, :, :, acols[p]], s_az.at[l, p], r_az.at[l, p], 48, awide[p])
        mine = AF.at[l, y, :, acols[p]]
        mine[...] = (RAX[l, z, :, acols[p]].astype(F32) + RAZ[l, 0, :, acols[p]].astype(F32)).astype(BF)
        ml.send(mine, mine, s_af.at[l, p], r_af.at[l, p], pc.yside())

    def af_task(l, p):
        ml.arrive(AF.at[l, 1 - y, :, acols[p]], s_af.at[l, p], r_af.at[l, p], pc.yside())

    pair_mask = head_mask(T, 128)
    low_half = lax.broadcasted_iota(jnp.int32, (T, 128), 1) % HEAD < HEAD // 2
    onehot = (lax.broadcasted_iota(jnp.int32, (8, 128), 0) == lax.broadcasted_iota(jnp.int32, (8, 128), 1)).astype(F32).astype(BF)

    def norm_back(i, extra, dst):
        gain = PV[i, 0:1, :]
        def rows_of(j, carry):
            gs, bs = carry
            rows = tile(j, 32)
            u = U[rows, :]
            if extra is not None:
                u = u + extra(rows)
            n = N[i, rows, :]
            un = u * n
            gs = gs + un.reshape(4, 8, D).sum(0)
            bs = bs + u.reshape(4, 8, D).sum(0)
            m1 = jnp.mean(u * gain, axis=1, keepdims=True)
            m2 = jnp.mean(un * gain, axis=1, keepdims=True)
            r = I[i, rows, 0:1] * (u * gain - m1 - n * m2)
            U[rows, :] = r
            dst[rows, :] = r.astype(BF)
            return gs, bs
        zero = jnp.zeros((8, D), F32)
        gs, bs = lax.fori_loop(0, T // 32, rows_of, (zero, zero))
        row = lax.broadcasted_iota(jnp.int32, (8, D), 0)
        V[i] = jnp.where(row == 0, gs.sum(0, keepdims=True), jnp.where(row == 1, bs.sum(0, keepdims=True), 0.0))

    def act_back(l, first, count):
        some = pl.ds(first, count)
        def cols_of(j, carry):
            cols = tile(j, 256)
            ga = dot_t(GF[l, some].reshape(count * T, D), F[cols, 2 * FS:])
            gate = TG[0, some, :, cols].reshape(count * T, 256).astype(F32)
            up = TG[1, some, :, cols].reshape(count * T, 256).astype(F32)
            sg = jax.nn.sigmoid(gate)
            gg = ga * up * sg * (1.0 + gate * (1.0 - sg))
            gu = ga * gate * sg
            TG[0, some, :, cols] = gg.astype(BF).reshape(count, T, 256)
            TG[1, some, :, cols] = gu.astype(BF).reshape(count, T, 256)
            return carry
        lax.fori_loop(0, FS // 256, cols_of, 0)

    def mid_back(s_, plus=None):
        def cols_of(j, carry):
            cols = tile(j, 256)
            r = dot_t(TG[0, s_], F[cols, 0:FS]) + dot_t(TG[1, s_], F[cols, FS:2 * FS])
            if plus is not None:
                r = r + plus[:, cols].astype(F32)
            FD[s_, :, cols] = r.astype(BF)
            return carry
        lax.fori_loop(0, D // 256, cols_of, 0)

    def weight_grad(l, j):
        def cols_of(n, carry):
            cols = tile(n, 256)
            if j == 0:
                right = GF[l, :, :, cols].reshape(4 * T, 256)
            else:
                right = TG[j - 1, :, :, cols].reshape(4 * T, 256)
            r = dot(TT[0 if j else 1], right)
            off = (2 * FS, 0, FS)[j]
            FG[:, :, :, pl.ds(pl.multiple_of(off + n * 256, 256), 256)] = r.astype(BF).reshape(4, 2, 96, 256)
            return carry
        lax.fori_loop(0, 3, cols_of, 0)

    def out_back():
        acc = None
        for h in range(2):
            r = dot(ST[1], GB[:, h * OW:h * OW + OW])
            AG[h, :, :, :, :, QW:QW + OW] = r.astype(BF).reshape(4, 2, 2, 48, OW)
        for h in range(2):
            t = dot_t(GB[:, h * OW:h * OW + OW], A[h, :, :, :, QW:QW + OW].reshape(D, OW))
            acc = t if acc is None else acc + t
        GP[2] = acc.astype(BF)

    def attention_back():
        def pair(p, carry):
            cols = tile(p, 128)
            q, kk, v, ga = Q[0, :, cols], Q[1, :, cols], Q[2, :, cols], GP[2, :, cols]
            dq, dk, dv = [], [], []
            for h in range(2):
                pl_ = Pb[2 * p + h]
                pr = pl_.astype(F32)
                gh = jnp.where(pair_mask == (h == 0), ga, jnp.zeros_like(ga))
                dp = dot_t(gh, v)
                ds = (pr * (dp - jnp.sum(dp * pr, axis=1, keepdims=True))).astype(BF)
                dq.append(dot(ds, kk))
                dk.append(dot(ds.T, q))
                dv.append(dot(pl_.T, ga))
            cos, sin = cos_ref[...], sin_ref[...]
            def back(pair_of):
                m = jnp.where(pair_mask, pair_of[0], pair_of[1]) * 0.125
                return (m * cos - swap_halves(m, low_half) * sin).astype(BF)
            GP[0, :, cols] = back(dq)
            GP[1, :, cols] = back(dk)
            GP[2, :, cols] = jnp.where(pair_mask, dv[0], dv[1]).astype(BF)
            return carry
        lax.fori_loop(0, PAIRS, pair, 0)

    def gp_chunk(j):
        return GP[j // 2, :, (j % 2) * 384:(j % 2) * 384 + 384]

    def qkv_grad(h):
        for j in range(3 * h, 3 * h + 3):
            off = (j % 3) * 384
            r = dot(ST[0], gp_chunk(j))
            AG[h, :, :, :, :, off:off + 384] = r.astype(BF).reshape(4, 2, 2, 48, 384)

    def param_grad():
        for h in range(2):
            r = lax.dot_general(V[h].astype(BF), onehot, (((0,), (0,)), ((), ())), preferred_element_type=F32)
            AG[h, :, :, :, :, QW + OW:] = r.astype(BF).reshape(4, 2, 2, 48, 128)

    def input_back():
        acc = U[...]
        for j in range(6):
            off = (j % 3) * 384
            acc = acc + dot_t(gp_chunk(j), A[j // 3, :, :, :, off:off + 384].reshape(D, 384))
        U[...] = acc

    def run(steps):
        for step, *what in steps:
            step(*what)

    def upper(l):
        need("PV", "N", "I")
        norm_back(1, None, GF.at[l, slot])
        mine = GF.at[l, slot]
        ml.send(mine, mine, s_m.at[l, 0], r_m.at[l, 0], pc.yside())
        ml.send(mine, mine, s_m.at[l, 1], r_m.at[l, 1], pc.core())

    def half_sums(l, i, yy):
        s_ = 2 * yy + 1 - c
        mid_back(s_)
        ml.send(FD.at[s_], RC.at[yy], s_rc.at[l, i], r_rc.at[l, i], pc.core(), ("fd", l))

    def own_tokens(l):
        need("TT", "F", "TG")
        ml.gone(("fd", 1))
        ml.arrive(GF.at[l, 2 * y + 1 - c], s_m.at[l, 1], r_m.at[l, 1], pc.core())
        act_back(l, 2 * y, 2)
        half_sums(l, 1, y)
        mid_back(slot)

    def other_tokens(l):
        others = 2 * (1 - y)
        block = GF.at[l, others + c]
        ml.arrive(block, s_m.at[l, 0], r_m.at[l, 0], pc.yside())
        ml.send(block, block, s_m.at[l, 2], r_m.at[l, 2], pc.core())
        act_back(l, others + c, 1)
        ml.arrive(GF.at[l, others + 1 - c], s_m.at[l, 2], r_m.at[l, 2], pc.core())
        act_back(l, others + 1 - c, 1)

    def other_sums(l):
        others = 2 * (1 - y)
        half_sums(l, 0, 1 - y)
        ml.arrive(RC.at[1 - y], s_rc.at[l, 0], r_rc.at[l, 0], pc.core())
        mid_back(others + c, RC.at[1 - y])
        ml.send(FD.at[others + c], RY, s_ry.at[l], r_ry.at[l], pc.yside(), ("fd", l))
        if l == 1:
            load(0, "F")

    def weights(l, j):
        ml.gone(("fx", 1, j) if l == 0 else None)
        weight_grad(l, j)
        fx_send(l, j)
        if l == 1 and j == 2:
            load(0, "TT", "TG")

    def middle(l):
        ml.arrive(RC.at[y], s_rc.at[l, 1], r_rc.at[l, 1], pc.core())
        ml.arrive(RY, s_ry.at[l], r_ry.at[l], pc.yside())
        norm_back(0, lambda rows: FD[slot, rows, :].astype(F32) + RC[y, rows, :].astype(F32) + RY[rows, :].astype(F32), GB)
        if l == 1:
            load(0, "PV", "N", "I")

    QKV, OUT = 0, 1

    def out_sums(l):
        need("ST", "A")
        if l == 0:
            ml.gone(("ac", 1))
        param_grad()
        out_back()
        for i in range(2):
            ac_send(l, OUT, i)

    def scores(l):
        need("P", "Q")
        attention_back()
        if l == 1:
            load(0, "P", "Q")

    def below(l):
        input_back()
        if l == 0:
            gin_ref[...] = U[...]

    def qkv_sums(l):
        qkv_grad(0)
        qkv_grad(1)
        for i in range(2):
            ac_send(l, QKV, i)
        if l == 1:
            load(0, "ST", "A")

    upper(1)
    own_tokens(1)
    other_tokens(1)
    other_sums(1)
    weights(1, 0)
    weights(1, 1)
    weights(1, 2)
    fx_task(1, 0, 0)
    middle(1)
    out_sums(1)
    scores(1)
    ac_sum(1, 1, 0)
    ay_send(1, 1, 0)
    below(1)
    upper(0)
    fx_task(1, 1, 0)
    fx_task(1, 0, 1)
    qkv_sums(1)
    ay_send(1, 1, 1)
    own_tokens(0)
    ay_send(1, 1, 2)
    fx_task(1, 1, 1)
    ac_sum(1, 0, 0)
    fm_task(1, 0)
    fx_task(1, 0, 2)
    ay_send(1, 0, 0)
    ac_sum(1, 1, 1)
    ac_sum(1, 0, 1)
    ay_task(1, 1, 0)
    other_tokens(0)
    fx_task(1, 2, 0)
    ay_send(1, 1, 3)
    fx_task(1, 1, 2)
    fm_task(1, 1)
    fx_task(1, 0, 3)
    other_sums(0)
    weights(0, 0)
    fx_task(1, 1, 3)
    fz_task(1, 1)
    ay_send(1, 0, 1)
    fx_task(1, 2, 1)
    ax_task(1, 1, 0)
    weights(0, 1)
    ay_send(1, 0, 2)
    fx_task(0, 0, 0)
    fx_task(1, 2, 2)
    ay_task(1, 1, 1)
    middle(0)
    out_sums(0)
    scores(0)
    ay_send(1, 0, 3)
    qkv_sums(0)
    fx_task(1, 2, 3)
    ac_sum(0, 1, 1)
    fx_task(0, 1, 0)
    fx_task(0, 0, 1)
    ac_sum(0, 1, 0)
    ay_send(0, 1, 0)
    ay_task(1, 0, 0)
    ay_send(0, 1, 1)
    fm_task(1, 2)
    ac_sum(0, 0, 0)
    weights(0, 2)
    ac_sum(0, 0, 1)
    ay_send(0, 1, 2)
    fx_task(0, 1, 1)
    ay_task(0, 1, 0)
    ay_send(0, 0, 0)
    ay_send(0, 0, 1)
    fx_task(0, 0, 2)
    ay_send(0, 0, 2)
    fm_task(0, 0)
    fc_task(1, 1)
    ax_task(1, 1, 1)
    fx_task(0, 2, 0)
    ay_task(1, 1, 2)
    ay_send(0, 0, 3)
    ax_task(1, 0, 0)
    ay_task(0, 0, 0)
    fx_task(0, 0, 3)
    fx_task(0, 1, 2)
    fz_task(1, 0)
    ay_task(1, 0, 1)
    ay_task(1, 1, 3)
    below(0)
    fm_task(0, 1)
    fx_task(0, 2, 1)
    fz_task(1, 2)
    fm_task(0, 2)
    ax_task(0, 0, 0)
    ay_task(1, 0, 2)
    fx_task(0, 2, 2)
    ax_task(1, 0, 1)
    ay_task(0, 0, 1)
    ay_task(0, 1, 1)
    ay_task(0, 1, 2)
    fx_task(0, 1, 3)
    fc_task(1, 2)
    ay_task(0, 0, 2)
    fz_task(0, 1)
    ax_task(1, 0, 2)
    ax_task(1, 1, 2)
    fx_task(0, 2, 3)
    ay_send(0, 1, 3)
    am_task(1, 1)
    ay_task(0, 0, 3)
    fz_task(0, 0)
    ax_task(0, 0, 1)
    fc_task(0, 1)
    ax_task(1, 1, 3)
    ax_task(0, 1, 0)
    fz_task(0, 2)
    ax_task(0, 1, 1)
    am_task(1, 0)
    fc_task(0, 2)
    ay_task(1, 0, 3)
    ax_task(0, 1, 2)
    az_task(1, 1)
    am_task(0, 0)
    ax_task(1, 0, 3)
    ax_task(0, 0, 2)
    ay_task(0, 1, 3)
    am_task(0, 1)
    az_task(1, 0)
    ax_task(0, 1, 3)
    ax_task(0, 0, 3)
    az_task(0, 0)
    az_task(0, 1)
    for l in (1, 0):
        for j in range(3):
            fy_task(l, j)
        for p in range(2):
            af_task(l, p)
    ml.finish()


def backward_call(cot, cos, sin, kept):
    any_spec = pl.BlockSpec(memory_space=pl.ANY)
    vm = pl.BlockSpec(memory_space=pltpu.VMEM)
    return pl.pallas_call(
        backward_kernel,
        out_shape=[
            jax.ShapeDtypeStruct((T, D), F32),
            jax.ShapeDtypeStruct((2, 2, 2, 2, 48, FS), BF),
            jax.ShapeDtypeStruct((2, 2, 96, D), BF),
            jax.ShapeDtypeStruct((2, 2, 48, AW), BF),
        ],
        in_specs=[vm] * 3 + [any_spec] * len(kept),
        out_specs=[vm] * 4,
        scratch_shapes=[pltpu.VMEM(s[1:], d) for s, d in FWD_SHAPES]
        + [
            pltpu.VMEM((T, D), F32),
            pltpu.VMEM((2, 4, T, D), BF),
            pltpu.VMEM((T, D), BF),
            pltpu.VMEM((3, T, D), BF),
            pltpu.VMEM((4, T, D), BF),
            pltpu.VMEM((2, T, D), BF),
            pltpu.VMEM((T, D), BF),
            pltpu.VMEM((4, 2, 96, 2 * FS + D), BF),
            pltpu.VMEM((2, 3, 4, 96, D), BF),
            pltpu.VMEM((2, 3, 5, 96, D), BF),
            pltpu.VMEM((2, 2, 48, D), BF),
            pltpu.VMEM((2, 4, 2, 2, 48, AW), BF),
            pltpu.VMEM((2, 2, 4, 2, 48, AW), BF),
            pltpu.VMEM((2, 4, 2, 48, AW), BF),
            pltpu.VMEM((2, 4, 48, AW), BF),
            pltpu.VMEM((2, 5, 48, AW), BF),
            pltpu.VMEM((2, 8, D), F32),
            sems(10),
            sems(2, 3), sems(2, 3),
            sems(2, 2), sems(2, 2),
            sems(2), sems(2),
            sems(2, 3, 4), sems(2, 3, 4),
            sems(2, 3, 6), sems(2, 3, 5),
            sems(2, 3), sems(2, 3),
            sems(2, 3), sems(2, 3),
            sems(2, 2, 2), sems(2, 2, 2),
            sems(2, 2, 4), sems(2, 2, 4),
            sems(2, 2, 4), sems(2, 2, 4),
            sems(2, 2, 6), sems(2, 2, 5),
            sems(2, 2), sems(2, 2),
        ],
        compiler_params=pltpu.CompilerParams(collective_id=1, has_side_effects=True, vmem_limit_bytes=60 * 2**20),
        cost_estimate=pl.CostEstimate(flops=2 * 10**10, bytes_accessed=10**8, transcendentals=0),
        name="backward",
    )(cot, cos, sin, *kept)


def finish_kernel(gug, dng, af, qkv_o, out_o, gate_o, up_o, down_o, g1_o, b1_o, g2_o, b2_o):
    for l in range(2):
        for h in range(2):
            qkv_o[l, :, h * QW:h * QW + QW] = af[l, h, :, 0:QW].astype(F32)
            out_o[l, :, h * OW:h * OW + OW] = af[l, h, :, QW:QW + OW].astype(F32)
            turned = af[l, h, :, QW + OW:].astype(F32).T
            for i, ref in enumerate(((g1_o, b1_o), (g2_o, b2_o))[h]):
                ref[l:l + 1, :] = turned[i:i + 1, :]
            down_o[l, 96 * h:96 * h + 96, :] = dng[l, h].astype(F32)
    def of(n, carry):
        l, j = n // G, n % G
        for w, ref in enumerate((gate_o, up_o)):
            pairs = gug[l, w, :, :, :, tile(j // 4, 384)]
            for m in range(4):
                def put(m=m):
                    pieces = [pairs[cc, yy, :, 96 * m:96 * m + 96].astype(F32) for cc in range(2) for yy in range(2)]
                    ref[l, :, tile(j, 384)] = jnp.concatenate(pieces, axis=1)
                pl.when(j % 4 == m)(put)
        return carry
    lax.fori_loop(0, 2 * G, of, 0)


def epilogue(gug, dng, af):
    vm = pl.BlockSpec(memory_space=pltpu.VMEM)
    shapes = [(2, 48, 3 * D), (2, 48, D), (2, 48, 4 * FS), (2, 48, 4 * FS), (2, 192, D)] + [(2, 48)] * 4
    return tuple(pl.pallas_call(
        finish_kernel,
        out_shape=[jax.ShapeDtypeStruct(v, F32) for v in shapes],
        in_specs=[vm] * 3,
        out_specs=[vm] * len(shapes),
        compiler_params=pltpu.CompilerParams(vmem_limit_bytes=40 * 2**20),
        cost_estimate=pl.CostEstimate(flops=10**6, bytes_accessed=10**7, transcendentals=0),
        name="finish",
    )(gug, dng, af))


def positions_of(segment_row):
    token_index = jnp.arange(segment_row.shape[0], dtype=jnp.int32)
    before = jnp.concatenate([segment_row[:1] - 1, segment_row[:-1]])
    starts = jnp.where(segment_row != before, token_index, jnp.zeros_like(token_index))
    return token_index - lax.cummax(starts, axis=0)


def rotary_tables(position):
    half_width = HEAD // 2
    frequency = rope_base ** (-2.0 * jnp.arange(half_width, dtype=F32) / HEAD)
    angles = position.astype(F32)[:, None] * frequency[None, :]
    return jnp.cos(angles), jnp.sin(angles)


def prologue(inputs, segment_ids, qkv_weight, out_weight, gate_weight, up_weight, down_weight,
             first_gain, first_bias, second_gain, second_bias):
    frequency = rope_base ** (-2.0 * np.arange(HEAD // 2, dtype=np.float32) / HEAD)
    freq = jnp.asarray(np.tile(frequency.astype(np.float32)[None, :], (8, 4)))
    par = jnp.stack([jnp.stack([first_gain, first_bias], -1), jnp.stack([second_gain, second_bias], -1)], 1)
    par = jnp.pad(par, ((0, 0), (0, 0), (0, 0), (0, 126)))
    return inputs[0], segment_ids, freq, qkv_weight, out_weight, par, gate_weight, up_weight, down_weight


def rotate(values, cosine_table, sine_table):
    half_width = values.shape[-1] // 2
    lead_half = values[..., :half_width]
    tail_half = values[..., half_width:]
    cos_wide = cosine_table[:, None, :]
    sin_wide = sine_table[:, None, :]
    return jnp.concatenate(
        [lead_half * cos_wide - tail_half * sin_wide, tail_half * cos_wide + lead_half * sin_wide],
        axis=-1,
    )


def unrotate(values, cosine_table, sine_table):
    half_width = values.shape[-1] // 2
    lead_half = values[..., :half_width]
    tail_half = values[..., half_width:]
    cos_wide = cosine_table[:, None, :]
    sin_wide = sine_table[:, None, :]
    return jnp.concatenate(
        [lead_half * cos_wide + tail_half * sin_wide, tail_half * cos_wide - lead_half * sin_wide],
        axis=-1,
    )


def norm_forward(values, gain_row, bias_row):
    mean_row = jnp.mean(values, axis=-1, keepdims=True)
    centred = values - mean_row
    variance = jnp.mean(centred * centred, axis=-1, keepdims=True)
    inverse = lax.rsqrt(variance + eps_norm)
    normed = centred * inverse
    return (normed * gain_row + bias_row, normed, inverse)


def norm_backward(upstream, normed, inverse, gain_row):
    scaled = upstream * gain_row
    gain_sum = jnp.sum(upstream * normed, axis=0)
    bias_sum = jnp.sum(upstream, axis=0)
    grad_input = inverse * (
        scaled
        - jnp.mean(scaled, axis=-1, keepdims=True)
        - normed * jnp.mean(scaled * normed, axis=-1, keepdims=True)
    )
    return (grad_input, gain_sum, bias_sum)


def times_transposed(left_side, right_side):
    return lax.dot_general(
        left_side, right_side, (((1,), (1,)), ((), ())), preferred_element_type=jnp.float32
    )


def outer_sum(left_side, right_side):
    return lax.dot_general(
        left_side, right_side, (((0,), (0,)), ((), ())), preferred_element_type=jnp.float32
    )


def to_pairs(values):
    token_count = values.shape[0]
    return values.reshape(token_count, HEADS // 2, 2 * HEAD).transpose(1, 0, 2)


def from_pairs(values):
    return values.transpose(1, 0, 2).reshape(values.shape[1], HEADS * HEAD)


def pair_scores(query_pair, key_pair, allowed, score_scale):
    token_count = query_pair.shape[0]
    queries = query_pair.reshape(token_count, 2, HEAD)
    key_rows = key_pair.reshape(token_count, 2, HEAD)
    scores = (
        jnp.einsum("qhd,khd->hqk", queries, key_rows, preferred_element_type=jnp.float32)
        * score_scale
    )
    return (jnp.where(allowed[None], scores, masked_score), queries, key_rows)


def pair_forward(block_item, allowed, score_scale):
    query_pair, key_pair, value_pair = block_item
    token_count = query_pair.shape[0]
    scores, queries, key_rows = pair_scores(query_pair, key_pair, allowed, score_scale)
    row_top = jnp.max(scores, axis=-1, keepdims=True)
    exponent = jnp.exp(scores - row_top)
    row_total = jnp.sum(exponent, axis=-1, keepdims=True)
    probabilities = exponent / row_total
    logsum = row_top[..., 0] + jnp.log(row_total[..., 0])
    value_rows = value_pair.reshape(token_count, 2, HEAD)
    attended = jnp.einsum(
        "hqk,khd->qhd",
        probabilities.astype(jnp.bfloat16),
        value_rows,
        preferred_element_type=jnp.float32,
    )
    return (attended.reshape(token_count, 2 * HEAD), logsum)


def pair_backward(block_item, allowed, score_scale):
    query_pair, key_pair, value_pair, grad_pair, logsum = block_item
    token_count = query_pair.shape[0]
    scores, queries, key_rows = pair_scores(query_pair, key_pair, allowed, score_scale)
    probabilities = jnp.exp(scores - logsum[..., None])
    value_rows = value_pair.reshape(token_count, 2, HEAD)
    grad_rows = grad_pair.reshape(token_count, 2, HEAD)
    grad_probs = jnp.einsum(
        "qhd,khd->hqk", grad_rows, value_rows, preferred_element_type=jnp.float32
    )
    grad_values = jnp.einsum(
        "hqk,qhd->khd",
        probabilities.astype(jnp.bfloat16),
        grad_rows,
        preferred_element_type=jnp.float32,
    )
    grad_scores = probabilities * (
        grad_probs - jnp.sum(grad_probs * probabilities, axis=-1, keepdims=True)
    )
    grad_scores = grad_scores.astype(jnp.bfloat16)
    grad_queries = (
        jnp.einsum("hqk,khd->qhd", grad_scores, key_rows, preferred_element_type=jnp.float32)
        * score_scale
    )
    grad_keys = (
        jnp.einsum("hqk,qhd->khd", grad_scores, queries, preferred_element_type=jnp.float32)
        * score_scale
    )
    return (
        grad_queries.reshape(token_count, 2 * HEAD),
        grad_keys.reshape(token_count, 2 * HEAD),
        grad_values.reshape(token_count, 2 * HEAD),
    )


def layer_forward(hidden_state, weights, cosine_table, sine_table, allowed, score_scale):
    qkv_full, out_full, gate_full, up_full, down_full, gain_one, bias_one, gain_two, bias_two = (
        weights
    )
    token_count, model_width = hidden_state.shape
    state_low = hidden_state.astype(jnp.bfloat16)
    projected = jnp.dot(state_low, qkv_full, preferred_element_type=jnp.float32)
    queries = rotate(
        projected[:, :model_width].reshape(token_count, HEADS, HEAD), cosine_table, sine_table
    )
    queries = queries.astype(jnp.bfloat16).reshape(token_count, model_width)
    key_rows = rotate(
        projected[:, model_width : 2 * model_width].reshape(token_count, HEADS, HEAD),
        cosine_table,
        sine_table,
    )
    key_rows = key_rows.astype(jnp.bfloat16).reshape(token_count, model_width)
    value_rows = projected[:, 2 * model_width :].astype(jnp.bfloat16)

    def attend_pair(block_item):
        return pair_forward(block_item, allowed, score_scale)

    attended_pairs, logsum = lax.map(
        attend_pair, (to_pairs(queries), to_pairs(key_rows), to_pairs(value_rows))
    )
    attended = from_pairs(attended_pairs).astype(jnp.bfloat16)
    branch = jnp.dot(attended, out_full, preferred_element_type=jnp.float32)
    middle, normed_one, inverse_one = norm_forward(
        hidden_state + branch, gain_one.astype(jnp.float32), bias_one.astype(jnp.float32)
    )
    middle_low = middle.astype(jnp.bfloat16)
    gate_pre = jnp.dot(middle_low, gate_full, preferred_element_type=jnp.float32)
    up_pre = jnp.dot(middle_low, up_full, preferred_element_type=jnp.float32)
    activated = (jax.nn.silu(gate_pre) * up_pre).astype(jnp.bfloat16)
    feed = jnp.dot(activated, down_full, preferred_element_type=jnp.float32)
    result, normed_two, inverse_two = norm_forward(
        middle + feed, gain_two.astype(jnp.float32), bias_two.astype(jnp.float32)
    )
    stored = (
        state_low,
        queries,
        key_rows,
        value_rows,
        logsum,
        attended,
        normed_one,
        inverse_one,
        middle_low,
        gate_pre,
        up_pre,
        activated,
        normed_two,
        inverse_two,
    )
    return (result, stored)


def layer_backward(upstream, weights, stored, cosine_table, sine_table, allowed, score_scale):
    qkv_full, out_full, gate_full, up_full, down_full, gain_one, bias_one, gain_two, bias_two = (
        weights
    )
    (
        state_low,
        queries,
        key_rows,
        value_rows,
        logsum,
        attended,
        normed_one,
        inverse_one,
        middle_low,
        gate_pre,
        up_pre,
        activated,
        normed_two,
        inverse_two,
    ) = stored
    token_count, model_width = upstream.shape
    grad_mid, gain_two_sum, bias_two_sum = norm_backward(
        upstream, normed_two, inverse_two, gain_two.astype(jnp.float32)
    )
    grad_feed = grad_mid.astype(jnp.bfloat16)
    down_sum = outer_sum(activated, grad_feed)
    grad_act = times_transposed(grad_feed, down_full)
    sigmoid_gate = jax.nn.sigmoid(gate_pre)
    grad_gate = (grad_act * up_pre * sigmoid_gate * (1.0 + gate_pre * (1.0 - sigmoid_gate))).astype(
        jnp.bfloat16
    )
    grad_up = (grad_act * gate_pre * sigmoid_gate).astype(jnp.bfloat16)
    gate_sum = outer_sum(middle_low, grad_gate)
    up_sum = outer_sum(middle_low, grad_up)
    grad_middle = (
        grad_mid + times_transposed(grad_gate, gate_full) + times_transposed(grad_up, up_full)
    )
    grad_sum, gain_one_sum, bias_one_sum = norm_backward(
        grad_middle, normed_one, inverse_one, gain_one.astype(jnp.float32)
    )
    grad_branch = grad_sum.astype(jnp.bfloat16)
    out_sum = outer_sum(attended, grad_branch)
    grad_attended = times_transposed(grad_branch, out_full).astype(jnp.bfloat16)

    def attend_back(block_item):
        return pair_backward(block_item, allowed, score_scale)

    grad_query_pairs, grad_key_pairs, grad_value_pairs = lax.map(
        attend_back,
        (
            to_pairs(queries),
            to_pairs(key_rows),
            to_pairs(value_rows),
            to_pairs(grad_attended),
            logsum,
        ),
    )
    grad_queries = unrotate(
        from_pairs(grad_query_pairs).reshape(token_count, HEADS, HEAD), cosine_table, sine_table
    ).reshape(token_count, model_width)
    grad_keys = unrotate(
        from_pairs(grad_key_pairs).reshape(token_count, HEADS, HEAD), cosine_table, sine_table
    ).reshape(token_count, model_width)
    grad_projected = jnp.concatenate(
        [grad_queries, grad_keys, from_pairs(grad_value_pairs)], axis=1
    ).astype(jnp.bfloat16)
    qkv_sum = outer_sum(state_low, grad_projected)
    grad_input = grad_sum + times_transposed(grad_projected, qkv_full)
    return (
        grad_input,
        (
            qkv_sum,
            out_sum,
            gate_sum,
            up_sum,
            down_sum,
            gain_one_sum,
            bias_one_sum,
            gain_two_sum,
            bias_two_sum,
        ),
    )


def general(inputs, segment_ids, qkv_weight, out_weight, gate_weight, up_weight, down_weight,
            first_gain, first_bias, second_gain, second_bias, cotangent):
    params = (qkv_weight, out_weight, gate_weight, up_weight, down_weight, first_gain, first_bias, second_gain, second_bias)
    layers = qkv_weight.shape[0]
    segment_row = segment_ids[0]
    cosine_table, sine_table = rotary_tables(positions_of(segment_row))
    allowed = segment_row[:, None] == segment_row[None, :]
    score_scale = 1.0 / math.sqrt(HEAD)
    hidden_state = inputs[0].astype(F32)
    fetched, saved = [], []
    for layer_index in range(layers):
        weights = tuple(lax.all_gather(w[layer_index], "shard", axis=0, tiled=True) for w in params)
        fetched.append(weights)
        hidden_state, stored = layer_forward(hidden_state, weights, cosine_table, sine_table, allowed, score_scale)
        saved.append(stored)
    upstream = cotangent[0].astype(F32)
    shared = [None] * layers
    for layer_index in reversed(range(layers)):
        upstream, gradients = layer_backward(
            upstream, fetched[layer_index], saved[layer_index], cosine_table, sine_table, allowed, score_scale
        )
        owned = [lax.psum_scatter(v, "shard", scatter_dimension=0, tiled=True) for v in gradients]
        shared[layer_index] = [lax.psum(v.astype(BF), "rep").astype(F32) for v in owned]
    stacked = [jnp.stack([shared[layer_index][member] for layer_index in range(layers)]) for member in range(9)]
    return (hidden_state.astype(BF)[None], upstream[None], *stacked)


def special(inputs, segment_ids, qkv_weight, out_weight, gate_weight, up_weight, down_weight,
            first_gain, first_bias, second_gain, second_bias, cotangent):
    staged = prologue(inputs, segment_ids, qkv_weight, out_weight, gate_weight, up_weight, down_weight,
                      first_gain, first_bias, second_gain, second_bias)
    output, *kept, cos, sin = forward_call(staged)
    gin, gug, dng, af = backward_call(cotangent[0], cos, sin, kept)
    return (output[None], gin[None]) + epilogue(gug, dng, af)


IN_SPECS = (
    P(("rep", "shard"), None, None), P(("rep", "shard"), None),
) + (P(None, "shard", None),) * 5 + (P(None, "shard"),) * 4 + (P(("rep", "shard"), None, None),)
OUT_SPECS = (P(("rep", "shard"), None, None),) * 2 + (P(None, "shard", None),) * 5 + (P(None, "shard"),) * 4


def solution(mesh):
    fits = dict(mesh.shape) == {"rep": 2, "shard": 2 * G}
    return jax.shard_map(special if fits else general, mesh=mesh, in_specs=IN_SPECS, out_specs=OUT_SPECS, check_vma=False)
```

```python
import functools
import math

import jax
import jax.numpy as jnp
import numpy as np
from jax import lax
from jax.experimental import pallas as pl
from jax.experimental.pallas import tpu as pltpu
from jax.sharding import PartitionSpec as P

HEADS = 12
HEAD = 64
eps_norm = 1e-12
rope_base = 1000.0
masked_score = -1e30
MESH = pl.DeviceIdType.MESH
BF = jnp.bfloat16
F32 = jnp.float32
T = 256
D = 768
G = 8
QW = 1152
OW = 384
AW = QW + OW + 128
FS = 768
PAIRS = HEADS // 2


def dot(a, b):
    return jnp.dot(a, b, preferred_element_type=F32)


def dot_t(a, b):
    return lax.dot_general(a, b, (((1,), (1,)), ((), ())), preferred_element_type=F32)


def tile(j, width):
    return pl.ds(pl.multiple_of(j * width, width), width)


def chip_rows(g):
    return pl.ds(pl.multiple_of(g * 96, 96), 96)


def shard_rows(g, c):
    return pl.ds(pl.multiple_of(g * 96 + c * 48, 48), 48)


class Place:
    def __init__(self):
        self.y = lax.axis_index("rep")
        s = lax.axis_index("shard")
        self.c, self.x, self.z = s % 2, (s // 2) % 2, s // 4
        self.g = s // 2
        self.slot = 2 * self.y + self.c

    def at(self, y, z, x, c):
        return (y, z * 4 + x * 2 + c)

    def core(self):
        return self.at(self.y, self.z, self.x, 1 - self.c)

    def xside(self):
        return self.at(self.y, self.z, 1 - self.x, self.c)

    def yside(self):
        return self.at(1 - self.y, self.z, self.x, self.c)

    def zside(self, k):
        return self.at(self.y, (self.z + k) % 4, self.x, self.c)

    def zto(self, z):
        return self.at(self.y, z, self.x, self.c)

    def near(self):
        return self.z + 1 - 2 * (self.z % 2)

    def across(self):
        return 3 - self.z

    def source(self, i):
        return (self.near(), 2 - self.z // 2, 3 - 3 * (self.z // 2))[i]

    def chip_from(self, i, x):
        return 2 * (self.z if i is None else self.source(i)) + x

    def chip(self, k, x):
        return 2 * ((self.z + 4 - k) % 4) + x

    def line(self):
        return [self.core(), self.xside(), self.yside(), self.zto(self.near()), self.zto(self.across())]

    def everyone(self):
        return [self.core(), self.xside(), self.yside()] + [self.zside(k) for k in (1, 2, 3)]


def greet(partners):
    barrier = pltpu.get_barrier_semaphore()
    for who in partners:
        pl.semaphore_signal(barrier, inc=1, device_id=who, device_id_type=MESH)
    return lambda: pl.semaphore_wait(barrier, len(partners))


class Mail:
    def __init__(self):
        self.sent = []
        self.some = []

    def send(self, src, dst, send_sem, recv_sem, who, tag=None):
        copy = pltpu.make_async_remote_copy(src, dst, send_sem, recv_sem, device_id=who, device_id_type=MESH)
        copy.start()
        self.sent.append((tag, copy))

    def later(self, src, dst, send_sem, recv_sem, who, cond):
        copy = pltpu.make_async_remote_copy(src, dst, send_sem, recv_sem, device_id=who, device_id_type=MESH)
        self.some.append((cond, copy))
        return copy

    def send_if(self, cond, src, dst, send_sem, recv_sem, who):
        copy = pltpu.make_async_remote_copy(src, dst, send_sem, recv_sem, device_id=who, device_id_type=MESH)
        pl.when(cond)(copy.start)
        self.some.append((cond, copy))

    def local(self, src, dst, sem):
        copy = pltpu.make_async_copy(src, dst, sem)
        copy.start()
        return copy

    def arrive(self, dst, send_sem, recv_sem, who):
        pltpu.make_async_remote_copy(dst, dst, send_sem, recv_sem, device_id=who, device_id_type=MESH).wait_recv()

    def gone(self, tag):
        for t, copy in self.sent:
            if t == tag:
                copy.wait_send()
        self.sent = [(t, copy) for t, copy in self.sent if t != tag]

    def finish(self):
        for _, copy in self.sent:
            copy.wait_send()
        for cond, copy in self.some:
            pl.when(cond)(copy.wait_send)


def swap_halves(v, low_half):
    return jnp.where(low_half, pltpu.roll(v, 96, 1), pltpu.roll(v, 32, 1))


def head_mask(rows, width):
    return lax.broadcasted_iota(jnp.int32, (rows, width), 1) % 128 < HEAD


def forward_kernel(
    x_ref, seg_ref, freq_ref, g1_ref, b1_ref, g2_ref, b2_ref, qkv_ref, outw_ref, gate_ref, up_ref, dn_ref,
    y_ref, A_o, F_o, Q_o, ST_o, P_o, TG_o, TT_o, N_o, I_o, PV_o, cos_ref, sin_ref,
    A, F, Q, ST, Pb, TG, TT, N, I, PV, S, AT, MF, AC, H, bias, FD, RC, RY, W, GU,
    ls, s_gu, r_gu, s_az, r_az, s_ax, r_ax, s_ay, r_ay, s_ac, r_ac, s_fz, r_fz, s_fx, r_fx, s_fw, r_fw,
    s_m, r_m, s_rc, r_rc, s_ry, r_ry, os,
):
    pc = Place()
    y, z, x, c, g, slot = pc.y, pc.z, pc.x, pc.c, pc.g, pc.slot
    ml = Mail()
    LAY = (0, 1)
    mid = z % 3 != 0
    near, across = pc.zto(pc.near()), pc.zto(pc.across())
    THREE = (0, 1, 2)

    met = greet(pc.line())

    own_a, own_f = [], []
    for l in LAY:
        own_a.append([])
        for h in range(2):
            dst = A.at[l, h, g, c]
            own_a[l].append(ml.local(qkv_ref.at[l, :, pl.ds(QW * h, QW)], dst.at[:, pl.ds(0, QW)], ls.at[l, h]))
            own_a[l].append(ml.local(outw_ref.at[l, :, pl.ds(OW * h, OW)], dst.at[:, pl.ds(QW, OW)], ls.at[l, 2 + h]))
    wide = [ml.local(gate_ref, W.at[0], ls.at[0, 6]), ml.local(up_ref, W.at[1], ls.at[1, 6])]
    for l in LAY:
        own_f.append(ml.local(dn_ref.at[l, pl.ds(pl.multiple_of(y * 96, 96), 96)], F.at[l, chip_rows(g), pl.ds(2 * FS, D)], ls.at[l, 7]))

    def gu_send(l):
        ml.send(GU.at[l, 1 - c, y], F.at[l, shard_rows(g, c), pl.ds(0, 2 * FS)], s_gu.at[l], r_gu.at[l], pc.core())

    def gu_arrive(l):
        ml.arrive(F.at[l, shard_rows(g, 1 - c), pl.ds(0, 2 * FS)], s_gu.at[l], r_gu.at[l], pc.core())

    def line_own(block, ss, rs):
        ml.send(block, block, ss.at[0], rs.at[0], near)
        ml.send_if(mid, block, block, ss.at[1], rs.at[1], across)

    def line_pass(i, block, ss, rs):
        ml.arrive(block, ss.at[0], rs.at[i], near)
        to, at = ((across, 2), (near, 1), (near, 2))[i]
        ml.send_if(mid, block, block, ss.at[2 + i], rs.at[at], to)

    def own_params():
        for l in LAY:
            for h, refs in enumerate(((g1_ref, b1_ref), (g2_ref, b2_ref))):
                two = [ref[l:l + 1, :].astype(F32) for ref in refs]
                rows = jnp.concatenate(two + [jnp.zeros((6, 48), F32)], axis=0).astype(BF)
                wide_rows = lax.dot_general(rows, onehot, (((0,), (0,)), ((), ())), preferred_element_type=F32)
                A[l, h, g, c, :, QW + OW:] = wide_rows.astype(BF)

    def a_own(l):
        for copy in own_a[l]:
            copy.wait()
        block = A.at[l, y, g, c]
        ml.send(block, block, s_ax.at[l, 0], r_ax.at[l, 0], pc.xside())
        line_own(block, s_az.at[l], r_az.at[l])

    def a_z(l, i):
        block = A.at[l, y, pc.chip_from(i, x), c]
        line_pass(i, block, s_az.at[l], r_az.at[l])
        ml.send(block, block, s_ax.at[l, 1 + i], r_ax.at[l, 1 + i], pc.xside())

    def a_yo(l, i):
        block = A.at[l, y, pc.chip_from(i, x), c]
        ml.send(block, block, s_ay.at[l, i], r_ay.at[l, i], pc.yside())

    FOUR = (None, 0, 1, 2)

    def a_x(l, j):
        ml.arrive(A.at[l, y, pc.chip_from(FOUR[j], 1 - x), c], s_ax.at[l, j], r_ax.at[l, j], pc.xside())

    def a_yx(l, j):
        block = A.at[l, y, pc.chip_from(FOUR[j], 1 - x), c]
        ml.send(block, block, s_ay.at[l, 3 + j], r_ay.at[l, 3 + j], pc.yside())

    def a_c(l, h):
        block = A.at[l, h, :, c]
        ml.send(block, block, s_ac.at[l, h], r_ac.at[l, h], pc.core())

    def a_y(l, i, xx, n):
        ml.arrive(A.at[l, 1 - y, pc.chip_from(i, xx), c], s_ay.at[l, n], r_ay.at[l, n], pc.yside())

    def a_c_arrive(l, h):
        ml.arrive(A.at[l, h, :, 1 - c], s_ac.at[l, h], r_ac.at[l, h], pc.core())

    parts = (pl.ds(0, 2 * FS), pl.ds(2 * FS, D))
    ALONG = (1, 1)

    def f_ready(l):
        for w in range(2):
            F[l, shard_rows(g, c), w * FS:w * FS + FS] = GU[l, c, y, :, w * FS:w * FS + FS]
        own_f[l].wait()
        gu_arrive(l)

    def f_own_z(l, p):
        line_own(F.at[l, chip_rows(g), parts[p]], s_fz.at[l, p], r_fz.at[l, p])

    def f_own_x(l, p):
        block = F.at[l, chip_rows(g), parts[p]]
        ml.send(block, block, s_fx.at[l, p, 0], r_fx.at[l, p, 0], pc.xside())

    def f_z(l, p, i):
        block = F.at[l, chip_rows(pc.chip_from(i, x)), parts[p]]
        line_pass(i, block, s_fz.at[l, p], r_fz.at[l, p])
        if (l, p) != ALONG:
            ml.send(block, block, s_fx.at[l, p, 1 + i], r_fx.at[l, p, 1 + i], pc.xside())

    def f_cross():
        l, p = ALONG
        block = F.at[l, chip_rows(pc.chip_from(None, 1 - x)), parts[p]]
        ml.arrive(block, s_fx.at[l, p, 0], r_fx.at[l, p, 0], pc.xside())
        line_own(block, s_fw, r_fw)

    def f_w(i):
        l, p = ALONG
        line_pass(i, F.at[l, chip_rows(pc.chip_from(i, 1 - x)), parts[p]], s_fw, r_fw)

    def f_x(l, p):
        if (l, p) == ALONG:
            return
        for j in range(4):
            ml.arrive(F.at[l, chip_rows(pc.chip_from(FOUR[j], 1 - x)), parts[p]], s_fx.at[l, p, j], r_fx.at[l, p, j], pc.xside())

    out_copies = []

    def save(src, dst):
        out_copies.append(ml.local(src, dst, os.at[len(out_copies)]))

    pair_mask = head_mask(T, 128)
    low_half = lax.broadcasted_iota(jnp.int32, (T, 128), 1) % HEAD < HEAD // 2
    onehot = (lax.broadcasted_iota(jnp.int32, (8, 128), 0) == lax.broadcasted_iota(jnp.int32, (8, 128), 1)).astype(F32).astype(BF)

    def tables():
        wide_row = jnp.broadcast_to(seg_ref[...].astype(F32), (T, T))
        same = wide_row.T == wide_row
        bias[...] = jnp.where(same, 0.0, masked_score)
        at = lax.broadcasted_iota(jnp.int32, (T, T), 1).astype(F32)
        first = jnp.min(jnp.where(same, at, float(T)), axis=1, keepdims=True)
        position = lax.broadcasted_iota(jnp.int32, (T, 128), 0).astype(F32) - first
        angle = position * freq_ref[0:1, :]
        sine = jnp.sin(angle)
        cos_ref[...] = jnp.cos(angle)
        sin_ref[...] = jnp.where(low_half, -sine, sine)

    def permute():
        for copy in wide:
            copy.wait()
        def of(i, carry):
            l, w = i // 2, i % 2
            v = W[w, l]
            for cc in range(2):
                for yy in range(2):
                    pieces = [v[:, 384 * j + 192 * cc + 96 * yy:384 * j + 192 * cc + 96 * yy + 96] for j in range(G)]
                    GU[l, cc, yy, :, tile(w, FS)] = jnp.concatenate(pieces, axis=1)
            return carry
        lax.fori_loop(0, 4, of, 0)

    def project(l):
        st = S[...]
        cos, sin = cos_ref[...], sin_ref[...]
        for j in range(6):
            h, off = j // 3, (j % 3) * 384
            w = A[l, h, :, :, :, off:off + 384].reshape(D, 384)
            r = dot(st, w)
            kind = j // 2
            for t in range(3):
                v = r[:, 128 * t:128 * t + 128]
                if kind < 2:
                    v = v * cos + swap_halves(v, low_half) * sin
                col = (j % 2) * 384 + 128 * t
                Q[l, kind, :, col:col + 128] = v.astype(BF)

    def attention(l):
        def pair(p, carry):
            cols = tile(p, 128)
            q, kk, v = Q[l, 0, :, cols], Q[l, 1, :, cols], Q[l, 2, :, cols]
            outs = []
            for h in range(2):
                qh = jnp.where(pair_mask == (h == 0), q, jnp.zeros_like(q))
                s = dot_t(qh, kk) * 0.125 + bias[...]
                e = jnp.exp(s - jnp.max(s, axis=1, keepdims=True))
                pr = (e * (1.0 / jnp.sum(e, axis=1, keepdims=True))).astype(BF)
                Pb[l, 2 * p + h] = pr
                outs.append(dot(pr, v))
            AT[:, cols] = jnp.where(pair_mask, outs[0], outs[1]).astype(BF)
            return carry
        lax.fori_loop(0, PAIRS, pair, 0)

    def params(l):
        for h in range(2):
            w = A[l, h, :, :, :, QW + OW:].reshape(D, 128)
            PV[l, h] = dot_t(onehot, w)

    def out_project(l):
        for h in range(2):
            w = A[l, h, :, :, :, QW:QW + OW].reshape(D, OW)
            H[:, h * OW:h * OW + OW] = H[:, h * OW:h * OW + OW] + dot(AT[...], w)

    def norm(l, i, dst, extra):
        gain, shift = PV[l, i, 0:1, :], PV[l, i, 1:2, :]
        def rows_of(j, carry):
            rows = tile(j, 32)
            v = H[rows, :]
            if extra is not None:
                v = v + extra(rows)
            cen = v - jnp.mean(v, axis=1, keepdims=True)
            inv = lax.rsqrt(jnp.mean(cen * cen, axis=1, keepdims=True) + eps_norm)
            n = cen * inv
            N[l, i, rows, :] = n
            I[l, i, rows, :] = jnp.broadcast_to(inv, (32, 128))
            m = n * gain + shift
            H[rows, :] = m
            dst[rows, :] = m.astype(BF)
            return carry
        lax.fori_loop(0, T // 32, rows_of, 0)

    def ffn_up(l, first, count):
        some = pl.ds(first, count)
        def cols_of(j, carry):
            cols = tile(j, 256)
            xx = MF[l, some].reshape(count * T, D)
            gate = dot(xx, F[l, :, cols])
            up = dot(xx, F[l, :, pl.ds(pl.multiple_of(FS + j * 256, 256), 256)])
            act = gate * jax.nn.sigmoid(gate) * up
            TG[l, 0, some, :, cols] = gate.astype(BF).reshape(count, T, 256)
            TG[l, 1, some, :, cols] = up.astype(BF).reshape(count, T, 256)
            AC[some, :, cols] = act.astype(BF).reshape(count, T, 256)
            return carry
        lax.fori_loop(0, FS // 256, cols_of, 0)

    def ffn_down(l, s_, plus=None):
        def cols_of(j, carry):
            cols = tile(j, 256)
            r = dot(AC[s_], F[l, :, pl.ds(pl.multiple_of(2 * FS + j * 256, 256), 256)])
            if plus is not None:
                r = r + plus[:, cols].astype(F32)
            FD[l, s_, :, cols] = r.astype(BF)
            return carry
        lax.fori_loop(0, D // 256, cols_of, 0)

    def turn(src, dst, col):
        def tile_of(j, carry):
            cols = tile(j, 128)
            dst[cols, pl.ds(pl.multiple_of(col, T), T)] = src[:, cols].T
            return carry
        lax.fori_loop(0, D // 128, tile_of, 0)

    def turn_slots(src, dst):
        def slot_of(i, carry):
            turn(src.at[i], dst, i * T)
            return carry
        lax.fori_loop(0, 4, slot_of, 0)

    def begin():
        H[...] = x_ref[...].astype(F32)
        S[...] = x_ref[...]
        permute()
        gu_send(0)
        gu_send(1)

    def projected(l):
        params(l)
        project(l)

    def turn_state(l):
        turn(S, ST.at[l, 0], 0)

    def scores(l):
        attention(l)
        save(Pb.at[l], P_o.at[l])
        save(Q.at[l], Q_o.at[l])

    def first_norm(l):
        out_project(l)
        norm(l, 0, MF.at[l, slot], None)
        mine = MF.at[l, slot]
        ml.send(mine, mine, s_m.at[l, 0], r_m.at[l, 0], pc.yside())
        ml.send(mine, mine, s_m.at[l, 1], r_m.at[l, 1], pc.core())

    def turn_attended(l):
        turn(AT, ST.at[l, 1], 0)
        save(ST.at[l], ST_o.at[l])

    def half_sums(l, i, yy):
        s_ = 2 * yy + 1 - c
        ffn_down(l, s_)
        ml.send(FD.at[l, s_], RC.at[l, yy], s_rc.at[l, i], r_rc.at[l, i], pc.core())

    def own_up(l):
        ml.arrive(MF.at[l, 2 * y + 1 - c], s_m.at[l, 1], r_m.at[l, 1], pc.core())
        f_x(l, 0)
        ffn_up(l, 2 * y, 2)

    def own_down(l):
        f_x(l, 1)
        half_sums(l, 1, y)
        ffn_down(l, slot)

    def pass_on(l):
        block = MF.at[l, 2 * (1 - y) + c]
        ml.arrive(block, s_m.at[l, 0], r_m.at[l, 0], pc.yside())
        ml.send(block, block, s_m.at[l, 2], r_m.at[l, 2], pc.core())

    def other_up(l):
        others = 2 * (1 - y)
        ffn_up(l, others + c, 1)
        ml.arrive(MF.at[l, others + 1 - c], s_m.at[l, 2], r_m.at[l, 2], pc.core())
        ffn_up(l, others + 1 - c, 1)

    def other_down(l):
        others = 2 * (1 - y)
        half_sums(l, 0, 1 - y)
        ml.arrive(RC.at[l, 1 - y], s_rc.at[l, 0], r_rc.at[l, 0], pc.core())
        ffn_down(l, others + c, RC.at[l, 1 - y])
        ml.send(FD.at[l, others + c], RY.at[l], s_ry.at[l], r_ry.at[l], pc.yside())

    def turn_middle(l):
        turn_slots(MF.at[l], TT.at[l, 0])

    def turn_activated(l):
        turn_slots(AC, TT.at[l, 1])
        save(F.at[l], F_o.at[l])
        save(TT.at[l], TT_o.at[l])
        save(TG.at[l], TG_o.at[l])

    def second_norm(l):
        ml.arrive(RC.at[l, y], s_rc.at[l, 1], r_rc.at[l, 1], pc.core())
        ml.arrive(RY.at[l], s_ry.at[l], r_ry.at[l], pc.yside())
        feed = lambda rows: FD[l, slot, rows, :].astype(F32) + RC[l, y, rows, :].astype(F32) + RY[l, rows, :].astype(F32)
        norm(l, 1, S if l == 0 else y_ref, feed)

    def ay_arrive(l, n):
        if n < 3:
            a_y(l, n, x, n)
        else:
            a_y(l, FOUR[n - 3], 1 - x, n)

    def ac_own(l):
        a_c(l, y)

    def ac_other(l):
        a_c(l, 1 - y)

    def attn_ready(l):
        a_c_arrive(l, y)
        a_c_arrive(l, 1 - y)
        save(A.at[l], A_o.at[l])

    own_params()
    met()
    a_own(0)
    begin()
    a_own(1)
    a_z(0, 0)
    f_ready(0)
    a_yo(0, 0)
    f_ready(1)
    a_z(0, 1)
    tables()
    a_z(1, 0)
    a_yo(0, 1)
    a_z(1, 1)
    a_x(0, 0)
    a_z(0, 2)
    a_yo(0, 2)
    a_x(0, 1)
    f_own_x(0, 0)
    a_x(0, 2)
    ay_arrive(0, 0)
    f_own_z(0, 0)
    a_yx(0, 0)
    a_yo(1, 0)
    a_x(1, 0)
    ay_arrive(0, 1)
    a_yx(0, 1)
    f_own_z(1, 1)
    a_x(0, 3)
    a_x(1, 1)
    ay_arrive(1, 0)
    ay_arrive(0, 2)
    a_z(1, 2)
    a_yx(0, 2)
    f_own_z(0, 1)
    a_yx(0, 3)
    ac_own(0)
    turn_state(0)
    ay_arrive(0, 3)
    f_z(0, 0, 0)
    ay_arrive(0, 4)
    a_yo(1, 1)
    f_z(0, 0, 1)
    ay_arrive(0, 5)
    a_yo(1, 2)
    ay_arrive(0, 6)
    ac_other(0)
    a_x(1, 2)
    attn_ready(0)
    projected(0)
    f_z(0, 0, 2)
    a_yx(1, 0)
    f_own_z(1, 0)
    a_yx(1, 1)
    f_z(0, 1, 0)
    scores(0)
    f_own_x(0, 1)
    f_z(1, 1, 0)
    first_norm(0)
    ay_arrive(1, 1)
    f_z(0, 1, 1)
    f_z(0, 1, 2)
    ay_arrive(1, 2)
    a_yx(1, 2)
    own_up(0)
    turn_attended(0)
    f_own_x(1, 1)
    f_z(1, 1, 1)
    ay_arrive(1, 3)
    f_z(1, 0, 0)
    pass_on(0)
    f_own_x(1, 0)
    a_x(1, 3)
    ay_arrive(1, 4)
    other_up(0)
    a_yx(1, 3)
    f_z(1, 0, 1)
    own_down(0)
    other_down(0)
    ay_arrive(1, 5)
    ay_arrive(1, 6)
    ac_other(1)
    ac_own(1)
    f_z(1, 1, 2)
    turn_middle(0)
    f_z(1, 0, 2)
    f_cross()
    attn_ready(1)
    second_norm(0)
    projected(1)
    scores(1)
    first_norm(1)
    turn_state(1)
    f_w(0)
    f_w(1)
    turn_activated(0)
    turn_attended(1)
    own_up(1)
    f_w(2)
    own_down(1)
    pass_on(1)
    other_up(1)
    other_down(1)
    turn_middle(1)
    turn_activated(1)
    second_norm(1)
    for src, dst in ((N, N_o), (I, I_o), (PV, PV_o)):
        save(src, dst)
    for copy in out_copies:
        copy.wait()
    ml.finish()


FWD_SHAPES = [
    ((2, 2, G, 2, 48, AW), BF),
    ((2, D, 2 * FS + D), BF),
    ((2, 3, T, D), BF),
    ((2, 2, D, T), BF),
    ((2, HEADS, T, T), BF),
    ((2, 2, 4, T, FS), BF),
    ((2, 2, D, 4 * T), BF),
    ((2, 2, T, D), F32),
    ((2, 2, T, 128), F32),
    ((2, 2, 8, D), F32),
]


def sems(*shape):
    return pltpu.SemaphoreType.DMA(shape)


def forward_call(args):
    any_spec = pl.BlockSpec(memory_space=pl.ANY)
    vm = pl.BlockSpec(memory_space=pltpu.VMEM)
    return pl.pallas_call(
        forward_kernel,
        out_shape=[jax.ShapeDtypeStruct((T, D), BF)]
        + [jax.ShapeDtypeStruct(s, d) for s, d in FWD_SHAPES]
        + [jax.ShapeDtypeStruct((T, 128), F32)] * 2,
        in_specs=[vm] * 7 + [any_spec] * 5,
        out_specs=[vm] + [any_spec] * len(FWD_SHAPES) + [vm] * 2,
        scratch_shapes=[pltpu.VMEM(s, d) for s, d in FWD_SHAPES]
        + [
            pltpu.VMEM((T, D), BF),
            pltpu.VMEM((T, D), BF),
            pltpu.VMEM((2, 4, T, D), BF),
            pltpu.VMEM((4, T, FS), BF),
            pltpu.VMEM((T, D), F32),
            pltpu.VMEM((T, T), F32),
            pltpu.VMEM((2, 4, T, D), BF),
            pltpu.VMEM((2, 2, T, D), BF),
            pltpu.VMEM((2, T, D), BF),
            pltpu.VMEM((2, 2, 48, 4 * FS), BF),
            pltpu.VMEM((2, 2, 2, 48, 2 * FS), BF),
            sems(2, 8),
            sems(2), sems(2),
            sems(2, 5), sems(2, 3),
            sems(2, 4), sems(2, 4),
            sems(2, 7), sems(2, 7),
            sems(2, 2), sems(2, 2),
            sems(2, 2, 5), sems(2, 2, 3),
            sems(2, 2, 4), sems(2, 2, 4),
            sems(5), sems(3),
            sems(2, 3), sems(2, 3),
            sems(2, 2), sems(2, 2),
            sems(2), sems(2),
            sems(17),
        ],
        compiler_params=pltpu.CompilerParams(collective_id=0, has_side_effects=True, vmem_limit_bytes=60 * 2**20),
        cost_estimate=pl.CostEstimate(flops=10**10, bytes_accessed=10**8, transcendentals=0),
        name="forward",
    )(*args)


def backward_kernel(
    cot_ref, cos_ref, sin_ref, A_i, F_i, Q_i, ST_i, P_i, TG_i, TT_i, N_i, I_i, PV_i,
    gin_ref, GUG, DNG, AF,
    A, F, Q, ST, Pb, TG, TT, N, I, PV,
    U, GF, GB, GP, FD, RC, RY, FG, RFX, RFZ, FR, AG, RAC, RAY, RAX, RAZ, V,
    ls, s_m, r_m, s_rc, r_rc, s_ry, r_ry,
    s_fx, r_fx, s_fz, r_fz, s_fc, r_fc, s_fy, r_fy,
    s_ac, r_ac, s_ay, r_ay, s_ax, r_ax, s_az, r_az, s_af, r_af,
):
    pc = Place()
    y, z, x, c, slot = pc.y, pc.z, pc.x, pc.c, pc.slot
    ml = Mail()
    mid = z % 3 != 0
    zn = pc.near()
    near, across = pc.zto(zn), pc.zto(3 - z)
    planes = (3 - zn, 3 - z, zn, z)
    places = {
        "PV": (PV_i, PV, 0), "N": (N_i, N, 1), "I": (I_i, I, 2), "TT": (TT_i, TT, 3), "F": (F_i, F, 4), "TG": (TG_i, TG, 5),
        "ST": (ST_i, ST, 6), "A": (A_i, A, 7), "P": (P_i, Pb, 8), "Q": (Q_i, Q, 9),
    }
    loading = {}

    def load(l, *names):
        for name in names:
            src, dst, i = places[name]
            loading[name] = ml.local(src.at[l], dst, ls.at[i])

    def need(*names):
        for name in names:
            if name in loading:
                loading.pop(name).wait()

    met = greet(pc.line())
    load(1, "PV", "N", "I", "F", "TG", "TT", "ST", "A", "P", "Q")
    U[...] = cot_ref[...].astype(F32)

    fcols = (pl.ds(2 * FS, D), pl.ds(0, FS), pl.ds(FS, FS))

    def fx_send(l, j):
        for n in range(4):
            ml.send(FG.at[planes[n], 1 - x, :, fcols[j]], RFX.at[l, j, planes[n]], s_fx.at[l, j, n], r_fx.at[l, j, n], pc.xside(), ("fx", l, j))

    def line_start(n, part, R, ss, rs):
        slot_of = (1, 2, 0)[n]
        ml.send_if(z % 3 == 0, part(planes[n]), R.at[slot_of], ss.at[n], rs.at[slot_of], near)

    def plus(dst, src, rows, widths):
        for r in range(0, rows, 48):
            at = 0
            for w in widths:
                here = (pl.ds(r, 48), pl.ds(at, w))
                dst[here] = (dst[here].astype(F32) + src[here].astype(F32)).astype(BF)
                at += w

    def line_middle(part, R, ss, rs, rows, widths):
        far = [pltpu.make_async_remote_copy(R.at[n], R.at[n], ss.at[0], rs.at[n], device_id=near, device_id_type=MESH) for n in (1, 2)]
        on = [
            ml.later(part(plane), R.at[3 + n], ss.at[3 + n], rs.at[3 + n], across, mid)
            for n, plane in enumerate((3 - z, 3 - zn))
        ]
        dsts = [part(3 - z), part(3 - zn)]
        def go():
            for n in range(2):
                far[n].wait_recv()
                plus(dsts[n], R.at[1 + n], rows, widths)
                on[n].start()
        pl.when(mid)(go)

    def line_end(part, R, ss, rs, rows, widths):
        back = [pltpu.make_async_remote_copy(R.at[n], R.at[n], ss.at[0], rs.at[n], device_id=across, device_id_type=MESH) for n in (3, 4)]
        last = ml.later(part(zn), R.at[0], ss.at[5], rs.at[0], near, mid)
        dsts = [part(z), part(zn)]
        def go():
            back[1].wait_recv()
            plus(dsts[1], R.at[4], rows, widths)
            last.start()
            back[0].wait_recv()
            plus(dsts[0], R.at[3], rows, widths)
        pl.when(mid)(go)
        ml.arrive(R.at[0], ss.at[0], rs.at[0], near)

    FW, AWS = (D,), (768, 896)

    def fpart(l, j):
        return lambda zz: RFX.at[l, j, zz]

    def fx_task(l, j, n):
        if True:
            p = planes[n]
            ml.arrive(RFX.at[l, j, p], s_fx.at[l, j, n], r_fx.at[l, j, n], pc.xside())
            for half in range(2):
                rows = pl.ds(48 * half, 48)
                RFX[l, j, p, rows, :] = (RFX[l, j, p, rows, :].astype(F32) + FG[p, x, rows, fcols[j]].astype(F32)).astype(BF)
            if n < 3:
                line_start(n, fpart(l, j), RFZ.at[l, j], s_fz.at[l, j], r_fz.at[l, j])

    def fm_task(l, j):
        line_middle(fpart(l, j), RFZ.at[l, j], s_fz.at[l, j], r_fz.at[l, j], 96, FW)

    def fz_task(l, j):
        line_end(fpart(l, j), RFZ.at[l, j], s_fz.at[l, j], r_fz.at[l, j], 96, FW)
        def total(start):
            rows = pl.ds(start, 48)
            return (RFX[l, j, z, rows, :].astype(F32) + RFZ[l, j, 0, rows, :].astype(F32)).astype(BF)
        if j == 0:
            for half in range(2):
                DNG[l, y, pl.ds(48 * half, 48), :] = total(48 * half)
            ml.send(DNG.at[l, y], DNG.at[l, y], s_fy.at[l, 0], r_fy.at[l, 0], pc.yside())
        else:
            FR[l, j - 1] = total(pl.multiple_of((1 - c) * 48, 48))
            ml.send(FR.at[l, j - 1], GUG.at[l, j - 1, c, y], s_fc.at[l, j], r_fc.at[l, j], pc.core())
            GUG[l, j - 1, c, y] = total(pl.multiple_of(c * 48, 48))

    def fc_task(l, j):
        ml.arrive(GUG.at[l, j - 1, 1 - c, y], s_fc.at[l, j], r_fc.at[l, j], pc.core())
        block = GUG.at[l, j - 1, :, y]
        ml.send(block, block, s_fy.at[l, j], r_fy.at[l, j], pc.yside())

    def fy_task(l, j):
        block = DNG.at[l, 1 - y] if j == 0 else GUG.at[l, j - 1, :, 1 - y]
        ml.arrive(block, s_fy.at[l, j], r_fy.at[l, j], pc.yside())

    acols = (pl.ds(0, QW), pl.ds(QW, AW - QW))
    awide = ((768, 384), (512,))

    def ac_send(l, p, i):
        h = (1 - y, y)[i]
        ml.send(AG.at[h, :, :, 1 - c, :, acols[p]], RAC.at[l, i, :, :, :, acols[p]], s_ac.at[l, p, i], r_ac.at[l, p, i], pc.core(), ("ac", l))

    def ac_sum(l, p, i):
        h = (1 - y, y)[i]
        ml.arrive(RAC.at[l, i, :, :, :, acols[p]], s_ac.at[l, p, i], r_ac.at[l, p, i], pc.core())
        def add(n, carry):
            zz, xx = n // 2, n % 2
            plus(RAC.at[l, i, zz, xx, :, acols[p]], AG.at[h, zz, xx, c, :, acols[p]], 48, awide[p])
            return carry
        lax.fori_loop(0, 8, add, 0)

    def ay_send(l, p, n):
        q = planes[n]
        ml.send(RAC.at[l, 0, q, :, :, acols[p]], RAY.at[l, q, :, :, acols[p]], s_ay.at[l, p, n], r_ay.at[l, p, n], pc.yside())

    def ay_task(l, p, n):
        q = planes[n]
        ml.arrive(RAY.at[l, q, :, :, acols[p]], s_ay.at[l, p, n], r_ay.at[l, p, n], pc.yside())
        for xx in range(2):
            plus(RAC.at[l, 1, q, xx, :, acols[p]], RAY.at[l, q, xx, :, acols[p]], 48, awide[p])
        ml.send(RAC.at[l, 1, q, 1 - x, :, acols[p]], RAX.at[l, q, :, acols[p]], s_ax.at[l, p, n], r_ax.at[l, p, n], pc.xside())

    def apart(l, p):
        return lambda zz: RAX.at[l, zz, :, acols[p]]

    def ax_task(l, p, n):
        q = planes[n]
        ml.arrive(RAX.at[l, q, :, acols[p]], s_ax.at[l, p, n], r_ax.at[l, p, n], pc.xside())
        plus(RAX.at[l, q, :, acols[p]], RAC.at[l, 1, q, x, :, acols[p]], 48, awide[p])
        if n < 3:
            line_start(n, apart(l, p), RAZ.at[l, :, :, acols[p]], s_az.at[l, p], r_az.at[l, p])

    def am_task(l, p):
        line_middle(apart(l, p), RAZ.at[l, :, :, acols[p]], s_az.at[l, p], r_az.at[l, p], 48, awide[p])

    def az_task(l, p):
        line_end(apart(l, p), RAZ.at[l, :, :, acols[p]], s_az.at[l, p], r_az.at[l, p], 48, awide[p])
        mine = AF.at[l, y, :, acols[p]]
        mine[...] = (RAX[l, z, :, acols[p]].astype(F32) + RAZ[l, 0, :, acols[p]].astype(F32)).astype(BF)
        ml.send(mine, mine, s_af.at[l, p], r_af.at[l, p], pc.yside())

    def af_task(l, p):
        ml.arrive(AF.at[l, 1 - y, :, acols[p]], s_af.at[l, p], r_af.at[l, p], pc.yside())

    pair_mask = head_mask(T, 128)
    low_half = lax.broadcasted_iota(jnp.int32, (T, 128), 1) % HEAD < HEAD // 2
    onehot = (lax.broadcasted_iota(jnp.int32, (8, 128), 0) == lax.broadcasted_iota(jnp.int32, (8, 128), 1)).astype(F32).astype(BF)

    def norm_back(i, extra, dst):
        gain = PV[i, 0:1, :]
        def rows_of(j, carry):
            gs, bs = carry
            rows = tile(j, 32)
            u = U[rows, :]
            if extra is not None:
                u = u + extra(rows)
            n = N[i, rows, :]
            un = u * n
            gs = gs + un.reshape(4, 8, D).sum(0)
            bs = bs + u.reshape(4, 8, D).sum(0)
            m1 = jnp.mean(u * gain, axis=1, keepdims=True)
            m2 = jnp.mean(un * gain, axis=1, keepdims=True)
            r = I[i, rows, 0:1] * (u * gain - m1 - n * m2)
            U[rows, :] = r
            dst[rows, :] = r.astype(BF)
            return gs, bs
        zero = jnp.zeros((8, D), F32)
        gs, bs = lax.fori_loop(0, T // 32, rows_of, (zero, zero))
        row = lax.broadcasted_iota(jnp.int32, (8, D), 0)
        V[i] = jnp.where(row == 0, gs.sum(0, keepdims=True), jnp.where(row == 1, bs.sum(0, keepdims=True), 0.0))

    def act_back(l, first, count):
        some = pl.ds(first, count)
        def cols_of(j, carry):
            cols = tile(j, 256)
            ga = dot_t(GF[l, some].reshape(count * T, D), F[cols, 2 * FS:])
            gate = TG[0, some, :, cols].reshape(count * T, 256).astype(F32)
            up = TG[1, some, :, cols].reshape(count * T, 256).astype(F32)
            sg = jax.nn.sigmoid(gate)
            gg = ga * up * sg * (1.0 + gate * (1.0 - sg))
            gu = ga * gate * sg
            TG[0, some, :, cols] = gg.astype(BF).reshape(count, T, 256)
            TG[1, some, :, cols] = gu.astype(BF).reshape(count, T, 256)
            return carry
        lax.fori_loop(0, FS // 256, cols_of, 0)

    def mid_back(s_, plus=None):
        def cols_of(j, carry):
            cols = tile(j, 256)
            r = dot_t(TG[0, s_], F[cols, 0:FS]) + dot_t(TG[1, s_], F[cols, FS:2 * FS])
            if plus is not None:
                r = r + plus[:, cols].astype(F32)
            FD[s_, :, cols] = r.astype(BF)
            return carry
        lax.fori_loop(0, D // 256, cols_of, 0)

    def weight_grad(l, j):
        def cols_of(n, carry):
            cols = tile(n, 256)
            if j == 0:
                right = GF[l, :, :, cols].reshape(4 * T, 256)
            else:
                right = TG[j - 1, :, :, cols].reshape(4 * T, 256)
            r = dot(TT[0 if j else 1], right)
            off = (2 * FS, 0, FS)[j]
            FG[:, :, :, pl.ds(pl.multiple_of(off + n * 256, 256), 256)] = r.astype(BF).reshape(4, 2, 96, 256)
            return carry
        lax.fori_loop(0, 3, cols_of, 0)

    def out_back():
        acc = None
        for h in range(2):
            r = dot(ST[1], GB[:, h * OW:h * OW + OW])
            AG[h, :, :, :, :, QW:QW + OW] = r.astype(BF).reshape(4, 2, 2, 48, OW)
        for h in range(2):
            t = dot_t(GB[:, h * OW:h * OW + OW], A[h, :, :, :, QW:QW + OW].reshape(D, OW))
            acc = t if acc is None else acc + t
        GP[2] = acc.astype(BF)

    def attention_back():
        def pair(p, carry):
            cols = tile(p, 128)
            q, kk, v, ga = Q[0, :, cols], Q[1, :, cols], Q[2, :, cols], GP[2, :, cols]
            dq, dk, dv = [], [], []
            for h in range(2):
                pl_ = Pb[2 * p + h]
                pr = pl_.astype(F32)
                gh = jnp.where(pair_mask == (h == 0), ga, jnp.zeros_like(ga))
                dp = dot_t(gh, v)
                ds = (pr * (dp - jnp.sum(dp * pr, axis=1, keepdims=True))).astype(BF)
                dq.append(dot(ds, kk))
                dk.append(dot(ds.T, q))
                dv.append(dot(pl_.T, ga))
            cos, sin = cos_ref[...], sin_ref[...]
            def back(pair_of):
                m = jnp.where(pair_mask, pair_of[0], pair_of[1]) * 0.125
                return (m * cos - swap_halves(m, low_half) * sin).astype(BF)
            GP[0, :, cols] = back(dq)
            GP[1, :, cols] = back(dk)
            GP[2, :, cols] = jnp.where(pair_mask, dv[0], dv[1]).astype(BF)
            return carry
        lax.fori_loop(0, PAIRS, pair, 0)

    def gp_chunk(j):
        return GP[j // 2, :, (j % 2) * 384:(j % 2) * 384 + 384]

    def qkv_grad(h):
        for j in range(3 * h, 3 * h + 3):
            off = (j % 3) * 384
            r = dot(ST[0], gp_chunk(j))
            AG[h, :, :, :, :, off:off + 384] = r.astype(BF).reshape(4, 2, 2, 48, 384)

    def param_grad():
        for h in range(2):
            r = lax.dot_general(V[h].astype(BF), onehot, (((0,), (0,)), ((), ())), preferred_element_type=F32)
            AG[h, :, :, :, :, QW + OW:] = r.astype(BF).reshape(4, 2, 2, 48, 128)

    def input_back():
        acc = U[...]
        for j in range(6):
            off = (j % 3) * 384
            acc = acc + dot_t(gp_chunk(j), A[j // 3, :, :, :, off:off + 384].reshape(D, 384))
        U[...] = acc

    def run(steps):
        for step, *what in steps:
            step(*what)

    def upper(l):
        need("PV", "N", "I")
        norm_back(1, None, GF.at[l, slot])
        if l == 1:
            met()
        mine = GF.at[l, slot]
        ml.send(mine, mine, s_m.at[l, 0], r_m.at[l, 0], pc.yside())
        ml.send(mine, mine, s_m.at[l, 1], r_m.at[l, 1], pc.core())

    def half_sums(l, i, yy):
        s_ = 2 * yy + 1 - c
        mid_back(s_)
        ml.send(FD.at[s_], RC.at[yy], s_rc.at[l, i], r_rc.at[l, i], pc.core(), ("fd", l))

    def own_tokens(l):
        need("F", "TG")
        ml.gone(("fd", 1))
        ml.arrive(GF.at[l, 2 * y + 1 - c], s_m.at[l, 1], r_m.at[l, 1], pc.core())
        act_back(l, 2 * y, 2)
        half_sums(l, 1, y)
        mid_back(slot)

    def other_tokens(l):
        others = 2 * (1 - y)
        block = GF.at[l, others + c]
        ml.arrive(block, s_m.at[l, 0], r_m.at[l, 0], pc.yside())
        ml.send(block, block, s_m.at[l, 2], r_m.at[l, 2], pc.core())
        act_back(l, others + c, 1)
        ml.arrive(GF.at[l, others + 1 - c], s_m.at[l, 2], r_m.at[l, 2], pc.core())
        act_back(l, others + 1 - c, 1)

    def other_sums(l):
        others = 2 * (1 - y)
        half_sums(l, 0, 1 - y)
        ml.arrive(RC.at[1 - y], s_rc.at[l, 0], r_rc.at[l, 0], pc.core())
        mid_back(others + c, RC.at[1 - y])
        ml.send(FD.at[others + c], RY, s_ry.at[l], r_ry.at[l], pc.yside(), ("fd", l))
        if l == 1:
            load(0, "F")

    def weights(l, j):
        need("TT")
        ml.gone(("fx", 1, j) if l == 0 else None)
        weight_grad(l, j)
        fx_send(l, j)
        if l == 1 and j == 2:
            load(0, "TT", "TG")

    def middle(l):
        ml.arrive(RC.at[y], s_rc.at[l, 1], r_rc.at[l, 1], pc.core())
        ml.arrive(RY, s_ry.at[l], r_ry.at[l], pc.yside())
        norm_back(0, lambda rows: FD[slot, rows, :].astype(F32) + RC[y, rows, :].astype(F32) + RY[rows, :].astype(F32), GB)
        if l == 1:
            load(0, "PV", "N", "I")

    QKV, OUT = 0, 1

    def out_sums(l):
        need("ST", "A")
        if l == 0:
            ml.gone(("ac", 1))
        param_grad()
        out_back()
        for i in range(2):
            ac_send(l, OUT, i)

    def scores(l):
        need("P", "Q")
        attention_back()
        if l == 1:
            load(0, "P", "Q")

    def below(l):
        input_back()
        if l == 0:
            gin_ref[...] = U[...]

    def qkv_sums(l):
        qkv_grad(0)
        qkv_grad(1)
        for i in range(2):
            ac_send(l, QKV, i)
        if l == 1:
            load(0, "ST", "A")

    upper(1)
    own_tokens(1)
    other_tokens(1)
    other_sums(1)
    weights(1, 0)
    weights(1, 1)
    weights(1, 2)
    fx_task(1, 0, 0)
    middle(1)
    out_sums(1)
    scores(1)
    ac_sum(1, 1, 0)
    ay_send(1, 1, 0)
    below(1)
    upper(0)
    fx_task(1, 1, 0)
    fx_task(1, 0, 1)
    qkv_sums(1)
    ay_send(1, 1, 1)
    own_tokens(0)
    ay_send(1, 1, 2)
    fx_task(1, 1, 1)
    ac_sum(1, 0, 0)
    fm_task(1, 0)
    fx_task(1, 0, 2)
    ay_send(1, 0, 0)
    ac_sum(1, 1, 1)
    ac_sum(1, 0, 1)
    ay_task(1, 1, 0)
    other_tokens(0)
    fx_task(1, 2, 0)
    ay_send(1, 1, 3)
    fx_task(1, 1, 2)
    fm_task(1, 1)
    fx_task(1, 0, 3)
    other_sums(0)
    weights(0, 0)
    fx_task(1, 1, 3)
    fz_task(1, 1)
    ay_send(1, 0, 1)
    fx_task(1, 2, 1)
    ax_task(1, 1, 0)
    weights(0, 1)
    ay_send(1, 0, 2)
    fx_task(0, 0, 0)
    fx_task(1, 2, 2)
    ay_task(1, 1, 1)
    middle(0)
    out_sums(0)
    scores(0)
    ay_send(1, 0, 3)
    qkv_sums(0)
    fx_task(1, 2, 3)
    ac_sum(0, 1, 1)
    fx_task(0, 1, 0)
    fx_task(0, 0, 1)
    ac_sum(0, 1, 0)
    ay_send(0, 1, 0)
    ay_task(1, 0, 0)
    ay_send(0, 1, 1)
    fm_task(1, 2)
    ac_sum(0, 0, 0)
    weights(0, 2)
    ac_sum(0, 0, 1)
    ay_send(0, 1, 2)
    fx_task(0, 1, 1)
    ay_task(0, 1, 0)
    ay_send(0, 0, 0)
    ay_send(0, 0, 1)
    fx_task(0, 0, 2)
    ay_send(0, 0, 2)
    fm_task(0, 0)
    fc_task(1, 1)
    ax_task(1, 1, 1)
    fx_task(0, 2, 0)
    ay_task(1, 1, 2)
    ay_send(0, 0, 3)
    ax_task(1, 0, 0)
    ay_task(0, 0, 0)
    fx_task(0, 0, 3)
    fx_task(0, 1, 2)
    fz_task(1, 0)
    ay_task(1, 0, 1)
    ay_task(1, 1, 3)
    below(0)
    fm_task(0, 1)
    fx_task(0, 2, 1)
    fz_task(1, 2)
    fm_task(0, 2)
    ax_task(0, 0, 0)
    ay_task(1, 0, 2)
    fx_task(0, 2, 2)
    ax_task(1, 0, 1)
    ay_task(0, 0, 1)
    ay_task(0, 1, 1)
    ay_task(0, 1, 2)
    fx_task(0, 1, 3)
    fc_task(1, 2)
    ay_task(0, 0, 2)
    fz_task(0, 1)
    ax_task(1, 0, 2)
    ax_task(1, 1, 2)
    fx_task(0, 2, 3)
    ay_send(0, 1, 3)
    am_task(1, 1)
    ay_task(0, 0, 3)
    fz_task(0, 0)
    ax_task(0, 0, 1)
    fc_task(0, 1)
    ax_task(1, 1, 3)
    ax_task(0, 1, 0)
    fz_task(0, 2)
    ax_task(0, 1, 1)
    am_task(1, 0)
    fc_task(0, 2)
    ay_task(1, 0, 3)
    ax_task(0, 1, 2)
    az_task(1, 1)
    am_task(0, 0)
    ax_task(1, 0, 3)
    ax_task(0, 0, 2)
    ay_task(0, 1, 3)
    am_task(0, 1)
    az_task(1, 0)
    ax_task(0, 1, 3)
    ax_task(0, 0, 3)
    az_task(0, 0)
    az_task(0, 1)
    for l in (1, 0):
        for j in range(3):
            fy_task(l, j)
        for p in range(2):
            af_task(l, p)
    ml.finish()


def backward_call(cot, cos, sin, kept):
    any_spec = pl.BlockSpec(memory_space=pl.ANY)
    vm = pl.BlockSpec(memory_space=pltpu.VMEM)
    return pl.pallas_call(
        backward_kernel,
        out_shape=[
            jax.ShapeDtypeStruct((T, D), F32),
            jax.ShapeDtypeStruct((2, 2, 2, 2, 48, FS), BF),
            jax.ShapeDtypeStruct((2, 2, 96, D), BF),
            jax.ShapeDtypeStruct((2, 2, 48, AW), BF),
        ],
        in_specs=[vm] * 3 + [any_spec] * len(kept),
        out_specs=[vm] * 4,
        scratch_shapes=[pltpu.VMEM(s[1:], d) for s, d in FWD_SHAPES]
        + [
            pltpu.VMEM((T, D), F32),
            pltpu.VMEM((2, 4, T, D), BF),
            pltpu.VMEM((T, D), BF),
            pltpu.VMEM((3, T, D), BF),
            pltpu.VMEM((4, T, D), BF),
            pltpu.VMEM((2, T, D), BF),
            pltpu.VMEM((T, D), BF),
            pltpu.VMEM((4, 2, 96, 2 * FS + D), BF),
            pltpu.VMEM((2, 3, 4, 96, D), BF),
            pltpu.VMEM((2, 3, 5, 96, D), BF),
            pltpu.VMEM((2, 2, 48, D), BF),
            pltpu.VMEM((2, 4, 2, 2, 48, AW), BF),
            pltpu.VMEM((2, 2, 4, 2, 48, AW), BF),
            pltpu.VMEM((2, 4, 2, 48, AW), BF),
            pltpu.VMEM((2, 4, 48, AW), BF),
            pltpu.VMEM((2, 5, 48, AW), BF),
            pltpu.VMEM((2, 8, D), F32),
            sems(10),
            sems(2, 3), sems(2, 3),
            sems(2, 2), sems(2, 2),
            sems(2), sems(2),
            sems(2, 3, 4), sems(2, 3, 4),
            sems(2, 3, 6), sems(2, 3, 5),
            sems(2, 3), sems(2, 3),
            sems(2, 3), sems(2, 3),
            sems(2, 2, 2), sems(2, 2, 2),
            sems(2, 2, 4), sems(2, 2, 4),
            sems(2, 2, 4), sems(2, 2, 4),
            sems(2, 2, 6), sems(2, 2, 5),
            sems(2, 2), sems(2, 2),
        ],
        compiler_params=pltpu.CompilerParams(collective_id=1, has_side_effects=True, vmem_limit_bytes=60 * 2**20),
        cost_estimate=pl.CostEstimate(flops=2 * 10**10, bytes_accessed=10**8, transcendentals=0),
        name="backward",
    )(cot, cos, sin, *kept)


def finish_kernel(
    y_i, gin_i, gug_i, dng_i, af_i, y_o, gin_o, qkv_o, out_o, gate_o, up_o, down_o, g1_o, b1_o, g2_o, b2_o,
    y_v, gin_v, gug, dng, af, qkv, out, gate, up, down, in_sem, out_sem,
):
    def copy(src, dst, sem):
        c = pltpu.make_async_copy(src, dst, sem)
        c.start()
        return c
    arriving = [[copy(src.at[l], dst.at[l], in_sem.at[l, i]) for i, (src, dst) in enumerate(((af_i, af), (gug_i, gug), (dng_i, dng)))] for l in range(2)]
    passing = [copy(y_i, y_v, in_sem.at[0, 3]), copy(gin_i, gin_v, in_sem.at[1, 3])]
    leaving = []
    for l in range(2):
        arriving[l][0].wait()
        for h in range(2):
            qkv[l, :, h * QW:h * QW + QW] = af[l, h, :, 0:QW].astype(F32)
            out[l, :, h * OW:h * OW + OW] = af[l, h, :, QW:QW + OW].astype(F32)
            turned = af[l, h, :, QW + OW:].astype(F32).T
            for i, ref in enumerate(((g1_o, b1_o), (g2_o, b2_o))[h]):
                ref[l:l + 1, :] = turned[i:i + 1, :]
        leaving.append(copy(qkv.at[l], qkv_o.at[l], out_sem.at[l, 0]))
        leaving.append(copy(out.at[l], out_o.at[l], out_sem.at[l, 1]))
        arriving[l][1].wait()
        for w, ref in enumerate((gate, up)):
            for j in range(G):
                pieces = [gug[l, w, cc, yy, :, 96 * j:96 * j + 96] for cc in range(2) for yy in range(2)]
                ref[l, :, 384 * j:384 * j + 384] = jnp.concatenate(pieces, axis=1).astype(F32)
            leaving.append(copy(ref.at[l], (gate_o, up_o)[w].at[l], out_sem.at[l, 2 + w]))
        passing[l].wait()
        leaving.append(copy((y_v, gin_v)[l], (y_o, gin_o)[l], out_sem.at[l, 5]))
        arriving[l][2].wait()
        for h in range(2):
            down[l, 96 * h:96 * h + 96, :] = dng[l, h].astype(F32)
        leaving.append(copy(down.at[l], down_o.at[l], out_sem.at[l, 4]))
    for c in leaving:
        c.wait()


def epilogue(y, gin, gug, dng, af):
    vm = pl.BlockSpec(memory_space=pltpu.VMEM)
    any_spec = pl.BlockSpec(memory_space=pl.ANY)
    large = [(2, 48, 3 * D), (2, 48, D), (2, 48, 4 * FS), (2, 48, 4 * FS), (2, 192, D)]
    return tuple(pl.pallas_call(
        finish_kernel,
        out_shape=[jax.ShapeDtypeStruct(v.shape, v.dtype) for v in (y, gin)]
        + [jax.ShapeDtypeStruct(v, F32) for v in large + [(2, 48)] * 4],
        in_specs=[any_spec] * 5,
        out_specs=[any_spec] * 7 + [vm] * 4,
        scratch_shapes=[pltpu.VMEM(v.shape, v.dtype) for v in (y, gin, gug, dng, af)]
        + [pltpu.VMEM(v, F32) for v in large]
        + [sems(2, 4), sems(2, 6)],
        compiler_params=pltpu.CompilerParams(vmem_limit_bytes=60 * 2**20),
        cost_estimate=pl.CostEstimate(flops=10**6, bytes_accessed=10**7, transcendentals=0),
        name="finish",
    )(y, gin, gug, dng, af))


def positions_of(segment_row):
    token_index = jnp.arange(segment_row.shape[0], dtype=jnp.int32)
    before = jnp.concatenate([segment_row[:1] - 1, segment_row[:-1]])
    starts = jnp.where(segment_row != before, token_index, jnp.zeros_like(token_index))
    return token_index - lax.cummax(starts, axis=0)


def rotary_tables(position):
    half_width = HEAD // 2
    frequency = rope_base ** (-2.0 * jnp.arange(half_width, dtype=F32) / HEAD)
    angles = position.astype(F32)[:, None] * frequency[None, :]
    return jnp.cos(angles), jnp.sin(angles)


def prologue(inputs, segment_ids, qkv_weight, out_weight, gate_weight, up_weight, down_weight,
             first_gain, first_bias, second_gain, second_bias):
    frequency = rope_base ** (-2.0 * np.arange(HEAD // 2, dtype=np.float32) / HEAD)
    freq = jnp.asarray(np.tile(frequency.astype(np.float32)[None, :], (8, 4)))
    return (inputs[0], segment_ids, freq, first_gain, first_bias, second_gain, second_bias, qkv_weight, out_weight,
            gate_weight, up_weight, down_weight)


def rotate(values, cosine_table, sine_table):
    half_width = values.shape[-1] // 2
    lead_half = values[..., :half_width]
    tail_half = values[..., half_width:]
    cos_wide = cosine_table[:, None, :]
    sin_wide = sine_table[:, None, :]
    return jnp.concatenate(
        [lead_half * cos_wide - tail_half * sin_wide, tail_half * cos_wide + lead_half * sin_wide],
        axis=-1,
    )


def unrotate(values, cosine_table, sine_table):
    half_width = values.shape[-1] // 2
    lead_half = values[..., :half_width]
    tail_half = values[..., half_width:]
    cos_wide = cosine_table[:, None, :]
    sin_wide = sine_table[:, None, :]
    return jnp.concatenate(
        [lead_half * cos_wide + tail_half * sin_wide, tail_half * cos_wide - lead_half * sin_wide],
        axis=-1,
    )


def norm_forward(values, gain_row, bias_row):
    mean_row = jnp.mean(values, axis=-1, keepdims=True)
    centred = values - mean_row
    variance = jnp.mean(centred * centred, axis=-1, keepdims=True)
    inverse = lax.rsqrt(variance + eps_norm)
    normed = centred * inverse
    return (normed * gain_row + bias_row, normed, inverse)


def norm_backward(upstream, normed, inverse, gain_row):
    scaled = upstream * gain_row
    gain_sum = jnp.sum(upstream * normed, axis=0)
    bias_sum = jnp.sum(upstream, axis=0)
    grad_input = inverse * (
        scaled
        - jnp.mean(scaled, axis=-1, keepdims=True)
        - normed * jnp.mean(scaled * normed, axis=-1, keepdims=True)
    )
    return (grad_input, gain_sum, bias_sum)


def times_transposed(left_side, right_side):
    return lax.dot_general(
        left_side, right_side, (((1,), (1,)), ((), ())), preferred_element_type=jnp.float32
    )


def outer_sum(left_side, right_side):
    return lax.dot_general(
        left_side, right_side, (((0,), (0,)), ((), ())), preferred_element_type=jnp.float32
    )


def to_pairs(values):
    token_count = values.shape[0]
    return values.reshape(token_count, HEADS // 2, 2 * HEAD).transpose(1, 0, 2)


def from_pairs(values):
    return values.transpose(1, 0, 2).reshape(values.shape[1], HEADS * HEAD)


def pair_scores(query_pair, key_pair, allowed, score_scale):
    token_count = query_pair.shape[0]
    queries = query_pair.reshape(token_count, 2, HEAD)
    key_rows = key_pair.reshape(token_count, 2, HEAD)
    scores = (
        jnp.einsum("qhd,khd->hqk", queries, key_rows, preferred_element_type=jnp.float32)
        * score_scale
    )
    return (jnp.where(allowed[None], scores, masked_score), queries, key_rows)


def pair_forward(block_item, allowed, score_scale):
    query_pair, key_pair, value_pair = block_item
    token_count = query_pair.shape[0]
    scores, queries, key_rows = pair_scores(query_pair, key_pair, allowed, score_scale)
    row_top = jnp.max(scores, axis=-1, keepdims=True)
    exponent = jnp.exp(scores - row_top)
    row_total = jnp.sum(exponent, axis=-1, keepdims=True)
    probabilities = exponent / row_total
    logsum = row_top[..., 0] + jnp.log(row_total[..., 0])
    value_rows = value_pair.reshape(token_count, 2, HEAD)
    attended = jnp.einsum(
        "hqk,khd->qhd",
        probabilities.astype(jnp.bfloat16),
        value_rows,
        preferred_element_type=jnp.float32,
    )
    return (attended.reshape(token_count, 2 * HEAD), logsum)


def pair_backward(block_item, allowed, score_scale):
    query_pair, key_pair, value_pair, grad_pair, logsum = block_item
    token_count = query_pair.shape[0]
    scores, queries, key_rows = pair_scores(query_pair, key_pair, allowed, score_scale)
    probabilities = jnp.exp(scores - logsum[..., None])
    value_rows = value_pair.reshape(token_count, 2, HEAD)
    grad_rows = grad_pair.reshape(token_count, 2, HEAD)
    grad_probs = jnp.einsum(
        "qhd,khd->hqk", grad_rows, value_rows, preferred_element_type=jnp.float32
    )
    grad_values = jnp.einsum(
        "hqk,qhd->khd",
        probabilities.astype(jnp.bfloat16),
        grad_rows,
        preferred_element_type=jnp.float32,
    )
    grad_scores = probabilities * (
        grad_probs - jnp.sum(grad_probs * probabilities, axis=-1, keepdims=True)
    )
    grad_scores = grad_scores.astype(jnp.bfloat16)
    grad_queries = (
        jnp.einsum("hqk,khd->qhd", grad_scores, key_rows, preferred_element_type=jnp.float32)
        * score_scale
    )
    grad_keys = (
        jnp.einsum("hqk,qhd->khd", grad_scores, queries, preferred_element_type=jnp.float32)
        * score_scale
    )
    return (
        grad_queries.reshape(token_count, 2 * HEAD),
        grad_keys.reshape(token_count, 2 * HEAD),
        grad_values.reshape(token_count, 2 * HEAD),
    )


def layer_forward(hidden_state, weights, cosine_table, sine_table, allowed, score_scale):
    qkv_full, out_full, gate_full, up_full, down_full, gain_one, bias_one, gain_two, bias_two = (
        weights
    )
    token_count, model_width = hidden_state.shape
    state_low = hidden_state.astype(jnp.bfloat16)
    projected = jnp.dot(state_low, qkv_full, preferred_element_type=jnp.float32)
    queries = rotate(
        projected[:, :model_width].reshape(token_count, HEADS, HEAD), cosine_table, sine_table
    )
    queries = queries.astype(jnp.bfloat16).reshape(token_count, model_width)
    key_rows = rotate(
        projected[:, model_width : 2 * model_width].reshape(token_count, HEADS, HEAD),
        cosine_table,
        sine_table,
    )
    key_rows = key_rows.astype(jnp.bfloat16).reshape(token_count, model_width)
    value_rows = projected[:, 2 * model_width :].astype(jnp.bfloat16)

    def attend_pair(block_item):
        return pair_forward(block_item, allowed, score_scale)

    attended_pairs, logsum = lax.map(
        attend_pair, (to_pairs(queries), to_pairs(key_rows), to_pairs(value_rows))
    )
    attended = from_pairs(attended_pairs).astype(jnp.bfloat16)
    branch = jnp.dot(attended, out_full, preferred_element_type=jnp.float32)
    middle, normed_one, inverse_one = norm_forward(
        hidden_state + branch, gain_one.astype(jnp.float32), bias_one.astype(jnp.float32)
    )
    middle_low = middle.astype(jnp.bfloat16)
    gate_pre = jnp.dot(middle_low, gate_full, preferred_element_type=jnp.float32)
    up_pre = jnp.dot(middle_low, up_full, preferred_element_type=jnp.float32)
    activated = (jax.nn.silu(gate_pre) * up_pre).astype(jnp.bfloat16)
    feed = jnp.dot(activated, down_full, preferred_element_type=jnp.float32)
    result, normed_two, inverse_two = norm_forward(
        middle + feed, gain_two.astype(jnp.float32), bias_two.astype(jnp.float32)
    )
    stored = (
        state_low,
        queries,
        key_rows,
        value_rows,
        logsum,
        attended,
        normed_one,
        inverse_one,
        middle_low,
        gate_pre,
        up_pre,
        activated,
        normed_two,
        inverse_two,
    )
    return (result, stored)


def layer_backward(upstream, weights, stored, cosine_table, sine_table, allowed, score_scale):
    qkv_full, out_full, gate_full, up_full, down_full, gain_one, bias_one, gain_two, bias_two = (
        weights
    )
    (
        state_low,
        queries,
        key_rows,
        value_rows,
        logsum,
        attended,
        normed_one,
        inverse_one,
        middle_low,
        gate_pre,
        up_pre,
        activated,
        normed_two,
        inverse_two,
    ) = stored
    token_count, model_width = upstream.shape
    grad_mid, gain_two_sum, bias_two_sum = norm_backward(
        upstream, normed_two, inverse_two, gain_two.astype(jnp.float32)
    )
    grad_feed = grad_mid.astype(jnp.bfloat16)
    down_sum = outer_sum(activated, grad_feed)
    grad_act = times_transposed(grad_feed, down_full)
    sigmoid_gate = jax.nn.sigmoid(gate_pre)
    grad_gate = (grad_act * up_pre * sigmoid_gate * (1.0 + gate_pre * (1.0 - sigmoid_gate))).astype(
        jnp.bfloat16
    )
    grad_up = (grad_act * gate_pre * sigmoid_gate).astype(jnp.bfloat16)
    gate_sum = outer_sum(middle_low, grad_gate)
    up_sum = outer_sum(middle_low, grad_up)
    grad_middle = (
        grad_mid + times_transposed(grad_gate, gate_full) + times_transposed(grad_up, up_full)
    )
    grad_sum, gain_one_sum, bias_one_sum = norm_backward(
        grad_middle, normed_one, inverse_one, gain_one.astype(jnp.float32)
    )
    grad_branch = grad_sum.astype(jnp.bfloat16)
    out_sum = outer_sum(attended, grad_branch)
    grad_attended = times_transposed(grad_branch, out_full).astype(jnp.bfloat16)

    def attend_back(block_item):
        return pair_backward(block_item, allowed, score_scale)

    grad_query_pairs, grad_key_pairs, grad_value_pairs = lax.map(
        attend_back,
        (
            to_pairs(queries),
            to_pairs(key_rows),
            to_pairs(value_rows),
            to_pairs(grad_attended),
            logsum,
        ),
    )
    grad_queries = unrotate(
        from_pairs(grad_query_pairs).reshape(token_count, HEADS, HEAD), cosine_table, sine_table
    ).reshape(token_count, model_width)
    grad_keys = unrotate(
        from_pairs(grad_key_pairs).reshape(token_count, HEADS, HEAD), cosine_table, sine_table
    ).reshape(token_count, model_width)
    grad_projected = jnp.concatenate(
        [grad_queries, grad_keys, from_pairs(grad_value_pairs)], axis=1
    ).astype(jnp.bfloat16)
    qkv_sum = outer_sum(state_low, grad_projected)
    grad_input = grad_sum + times_transposed(grad_projected, qkv_full)
    return (
        grad_input,
        (
            qkv_sum,
            out_sum,
            gate_sum,
            up_sum,
            down_sum,
            gain_one_sum,
            bias_one_sum,
            gain_two_sum,
            bias_two_sum,
        ),
    )


def general(inputs, segment_ids, qkv_weight, out_weight, gate_weight, up_weight, down_weight,
            first_gain, first_bias, second_gain, second_bias, cotangent):
    params = (qkv_weight, out_weight, gate_weight, up_weight, down_weight, first_gain, first_bias, second_gain, second_bias)
    layers = qkv_weight.shape[0]
    segment_row = segment_ids[0]
    cosine_table, sine_table = rotary_tables(positions_of(segment_row))
    allowed = segment_row[:, None] == segment_row[None, :]
    score_scale = 1.0 / math.sqrt(HEAD)
    hidden_state = inputs[0].astype(F32)
    fetched, saved = [], []
    for layer_index in range(layers):
        weights = tuple(lax.all_gather(w[layer_index], "shard", axis=0, tiled=True) for w in params)
        fetched.append(weights)
        hidden_state, stored = layer_forward(hidden_state, weights, cosine_table, sine_table, allowed, score_scale)
        saved.append(stored)
    upstream = cotangent[0].astype(F32)
    shared = [None] * layers
    for layer_index in reversed(range(layers)):
        upstream, gradients = layer_backward(
            upstream, fetched[layer_index], saved[layer_index], cosine_table, sine_table, allowed, score_scale
        )
        owned = [lax.psum_scatter(v, "shard", scatter_dimension=0, tiled=True) for v in gradients]
        shared[layer_index] = [lax.psum(v.astype(BF), "rep").astype(F32) for v in owned]
    stacked = [jnp.stack([shared[layer_index][member] for layer_index in range(layers)]) for member in range(9)]
    return (hidden_state.astype(BF)[None], upstream[None], *stacked)


def special(inputs, segment_ids, qkv_weight, out_weight, gate_weight, up_weight, down_weight,
            first_gain, first_bias, second_gain, second_bias, cotangent):
    staged = prologue(inputs, segment_ids, qkv_weight, out_weight, gate_weight, up_weight, down_weight,
                      first_gain, first_bias, second_gain, second_bias)
    output, *kept, cos, sin = forward_call(staged)
    gin, gug, dng, af = backward_call(cotangent[0], cos, sin, kept)
    output, gin, *gradients = epilogue(output, gin, gug, dng, af)
    return (output[None], gin[None], *gradients)


IN_SPECS = (
    P(("rep", "shard"), None, None), P(("rep", "shard"), None),
) + (P(None, "shard", None),) * 5 + (P(None, "shard"),) * 4 + (P(("rep", "shard"), None, None),)
OUT_SPECS = (P(("rep", "shard"), None, None),) * 2 + (P(None, "shard", None),) * 5 + (P(None, "shard"),) * 4


def solution(mesh):
    fits = dict(mesh.shape) == {"rep": 2, "shard": 2 * G}
    return jax.shard_map(special if fits else general, mesh=mesh, in_specs=IN_SPECS, out_specs=OUT_SPECS, check_vma=False)
```

```python
import functools
import math

import jax
import jax.numpy as jnp
import numpy as np
from jax import lax
from jax.experimental import pallas as pl
from jax.experimental.pallas import tpu as pltpu
from jax.sharding import PartitionSpec as P

HEADS = 12
HEAD = 64
eps_norm = 1e-12
rope_base = 1000.0
masked_score = -1e30
MESH = pl.DeviceIdType.MESH
BF = jnp.bfloat16
F32 = jnp.float32
T = 256
D = 768
G = 8
QW = 1152
OW = 384
AW = QW + OW + 128
FS = 768
PAIRS = HEADS // 2
HT = T // 2


def part_of(half):
    return pl.ds(half * HT, HT)


def dot(a, b):
    return jnp.dot(a, b, preferred_element_type=F32)


def dot_t(a, b):
    return lax.dot_general(a, b, (((1,), (1,)), ((), ())), preferred_element_type=F32)


def tile(j, width):
    return pl.ds(pl.multiple_of(j * width, width), width)


def chip_rows(g):
    return pl.ds(pl.multiple_of(g * 96, 96), 96)


def shard_rows(g, c):
    return pl.ds(pl.multiple_of(g * 96 + c * 48, 48), 48)


class Place:
    def __init__(self):
        self.y = lax.axis_index("rep")
        s = lax.axis_index("shard")
        self.c, self.x, self.z = s % 2, (s // 2) % 2, s // 4
        self.g = s // 2
        self.slot = 2 * self.y + self.c

    def at(self, y, z, x, c):
        return (y, z * 4 + x * 2 + c)

    def core(self):
        return self.at(self.y, self.z, self.x, 1 - self.c)

    def xside(self):
        return self.at(self.y, self.z, 1 - self.x, self.c)

    def yside(self):
        return self.at(1 - self.y, self.z, self.x, self.c)

    def zside(self, k):
        return self.at(self.y, (self.z + k) % 4, self.x, self.c)

    def zto(self, z):
        return self.at(self.y, z, self.x, self.c)

    def near(self):
        return self.z + 1 - 2 * (self.z % 2)

    def across(self):
        return 3 - self.z

    def source(self, i):
        return (self.near(), 2 - self.z // 2, 3 - 3 * (self.z // 2))[i]

    def chip_from(self, i, x):
        return 2 * (self.z if i is None else self.source(i)) + x

    def chip(self, k, x):
        return 2 * ((self.z + 4 - k) % 4) + x

    def line(self):
        return [self.core(), self.xside(), self.yside(), self.zto(self.near()), self.zto(self.across())]

    def everyone(self):
        return [self.core(), self.xside(), self.yside()] + [self.zside(k) for k in (1, 2, 3)]


def greet(partners):
    barrier = pltpu.get_barrier_semaphore()
    for who in partners:
        pl.semaphore_signal(barrier, inc=1, device_id=who, device_id_type=MESH)
    return lambda: pl.semaphore_wait(barrier, len(partners))


class Mail:
    def __init__(self):
        self.sent = []
        self.some = []

    def send(self, src, dst, send_sem, recv_sem, who, tag=None):
        copy = pltpu.make_async_remote_copy(src, dst, send_sem, recv_sem, device_id=who, device_id_type=MESH)
        copy.start()
        self.sent.append((tag, copy))

    def later(self, src, dst, send_sem, recv_sem, who, cond):
        copy = pltpu.make_async_remote_copy(src, dst, send_sem, recv_sem, device_id=who, device_id_type=MESH)
        self.some.append((cond, copy))
        return copy

    def send_if(self, cond, src, dst, send_sem, recv_sem, who):
        copy = pltpu.make_async_remote_copy(src, dst, send_sem, recv_sem, device_id=who, device_id_type=MESH)
        pl.when(cond)(copy.start)
        self.some.append((cond, copy))

    def local(self, src, dst, sem):
        copy = pltpu.make_async_copy(src, dst, sem)
        copy.start()
        return copy

    def arrive(self, dst, send_sem, recv_sem, who):
        pltpu.make_async_remote_copy(dst, dst, send_sem, recv_sem, device_id=who, device_id_type=MESH).wait_recv()

    def gone(self, tag):
        for t, copy in self.sent:
            if t == tag:
                copy.wait_send()
        self.sent = [(t, copy) for t, copy in self.sent if t != tag]

    def finish(self):
        for _, copy in self.sent:
            copy.wait_send()
        for cond, copy in self.some:
            pl.when(cond)(copy.wait_send)


def swap_halves(v, low_half):
    return jnp.where(low_half, pltpu.roll(v, 96, 1), pltpu.roll(v, 32, 1))


def head_mask(rows, width):
    return lax.broadcasted_iota(jnp.int32, (rows, width), 1) % 128 < HEAD


def forward_kernel(
    x_ref, seg_ref, freq_ref, g1_ref, b1_ref, g2_ref, b2_ref, qkv_ref, outw_ref, gate_ref, up_ref, dn_ref,
    y_ref, A_o, F_o, Q_o, ST_o, P_o, TG_o, TT_o, N_o, I_o, PV_o, cos_ref, sin_ref,
    A, F, Q, ST, Pb, TG, TT, N, I, PV, S, AT, MF, AC, H, bias, FD, RC, RY, W, GU,
    ls, s_gu, r_gu, s_az, r_az, s_ax, r_ax, s_ay, r_ay, s_ac, r_ac, s_fz, r_fz, s_fx, r_fx, s_fw, r_fw,
    s_m, r_m, s_rc, r_rc, s_ry, r_ry, os,
):
    pc = Place()
    y, z, x, c, g, slot = pc.y, pc.z, pc.x, pc.c, pc.g, pc.slot
    ml = Mail()
    LAY = (0, 1)
    mid = z % 3 != 0
    near, across = pc.zto(pc.near()), pc.zto(pc.across())
    THREE = (0, 1, 2)

    met = greet(pc.line())

    own_a, own_f = [], []
    for l in LAY:
        own_a.append([])
        for h in range(2):
            dst = A.at[l, h, g, c]
            own_a[l].append(ml.local(qkv_ref.at[l, :, pl.ds(QW * h, QW)], dst.at[:, pl.ds(0, QW)], ls.at[l, h]))
            own_a[l].append(ml.local(outw_ref.at[l, :, pl.ds(OW * h, OW)], dst.at[:, pl.ds(QW, OW)], ls.at[l, 2 + h]))
    wide = [ml.local(gate_ref, W.at[0], ls.at[0, 6]), ml.local(up_ref, W.at[1], ls.at[1, 6])]
    for l in LAY:
        own_f.append(ml.local(dn_ref.at[l, pl.ds(pl.multiple_of(y * 96, 96), 96)], F.at[l, chip_rows(g), pl.ds(2 * FS, D)], ls.at[l, 7]))

    def gu_send(l):
        ml.send(GU.at[l, 1 - c, y], F.at[l, shard_rows(g, c), pl.ds(0, 2 * FS)], s_gu.at[l], r_gu.at[l], pc.core())

    def gu_arrive(l):
        ml.arrive(F.at[l, shard_rows(g, 1 - c), pl.ds(0, 2 * FS)], s_gu.at[l], r_gu.at[l], pc.core())

    def line_own(block, ss, rs):
        ml.send(block, block, ss.at[0], rs.at[0], near)
        ml.send_if(mid, block, block, ss.at[1], rs.at[1], across)

    def line_pass(i, block, ss, rs):
        ml.arrive(block, ss.at[0], rs.at[i], near)
        to, at = ((across, 2), (near, 1), (near, 2))[i]
        ml.send_if(mid, block, block, ss.at[2 + i], rs.at[at], to)

    def own_params():
        for l in LAY:
            for h, refs in enumerate(((g1_ref, b1_ref), (g2_ref, b2_ref))):
                two = [ref[l:l + 1, :].astype(F32) for ref in refs]
                rows = jnp.concatenate(two + [jnp.zeros((6, 48), F32)], axis=0).astype(BF)
                wide_rows = lax.dot_general(rows, onehot, (((0,), (0,)), ((), ())), preferred_element_type=F32)
                A[l, h, g, c, :, QW + OW:] = wide_rows.astype(BF)

    def a_own(l):
        for copy in own_a[l]:
            copy.wait()
        block = A.at[l, y, g, c]
        ml.send(block, block, s_ax.at[l, 0], r_ax.at[l, 0], pc.xside())
        line_own(block, s_az.at[l], r_az.at[l])

    def a_z(l, i):
        block = A.at[l, y, pc.chip_from(i, x), c]
        line_pass(i, block, s_az.at[l], r_az.at[l])
        ml.send(block, block, s_ax.at[l, 1 + i], r_ax.at[l, 1 + i], pc.xside())

    def a_yo(l, i):
        block = A.at[l, y, pc.chip_from(i, x), c]
        ml.send(block, block, s_ay.at[l, i], r_ay.at[l, i], pc.yside())

    FOUR = (None, 0, 1, 2)

    def a_x(l, j):
        ml.arrive(A.at[l, y, pc.chip_from(FOUR[j], 1 - x), c], s_ax.at[l, j], r_ax.at[l, j], pc.xside())

    def a_yx(l, j):
        block = A.at[l, y, pc.chip_from(FOUR[j], 1 - x), c]
        ml.send(block, block, s_ay.at[l, 3 + j], r_ay.at[l, 3 + j], pc.yside())

    def a_c(l, h):
        block = A.at[l, h, :, c]
        ml.send(block, block, s_ac.at[l, h], r_ac.at[l, h], pc.core())

    def a_y(l, i, xx, n):
        ml.arrive(A.at[l, 1 - y, pc.chip_from(i, xx), c], s_ay.at[l, n], r_ay.at[l, n], pc.yside())

    def a_c_arrive(l, h):
        ml.arrive(A.at[l, h, :, 1 - c], s_ac.at[l, h], r_ac.at[l, h], pc.core())

    parts = (pl.ds(0, 2 * FS), pl.ds(2 * FS, D))
    ALONG = (1, 1)

    def f_ready(l):
        for w in range(2):
            F[l, shard_rows(g, c), w * FS:w * FS + FS] = GU[l, c, y, :, w * FS:w * FS + FS]
        own_f[l].wait()
        gu_arrive(l)

    def f_own_z(l, p):
        line_own(F.at[l, chip_rows(g), parts[p]], s_fz.at[l, p], r_fz.at[l, p])

    def f_own_x(l, p):
        block = F.at[l, chip_rows(g), parts[p]]
        ml.send(block, block, s_fx.at[l, p, 0], r_fx.at[l, p, 0], pc.xside())

    def f_z(l, p, i):
        block = F.at[l, chip_rows(pc.chip_from(i, x)), parts[p]]
        line_pass(i, block, s_fz.at[l, p], r_fz.at[l, p])
        if (l, p) != ALONG:
            ml.send(block, block, s_fx.at[l, p, 1 + i], r_fx.at[l, p, 1 + i], pc.xside())

    def f_cross():
        l, p = ALONG
        block = F.at[l, chip_rows(pc.chip_from(None, 1 - x)), parts[p]]
        ml.arrive(block, s_fx.at[l, p, 0], r_fx.at[l, p, 0], pc.xside())
        line_own(block, s_fw, r_fw)

    def f_w(i):
        l, p = ALONG
        line_pass(i, F.at[l, chip_rows(pc.chip_from(i, 1 - x)), parts[p]], s_fw, r_fw)

    def f_x(l, p):
        if (l, p) == ALONG:
            return
        for j in range(4):
            ml.arrive(F.at[l, chip_rows(pc.chip_from(FOUR[j], 1 - x)), parts[p]], s_fx.at[l, p, j], r_fx.at[l, p, j], pc.xside())

    out_copies = []

    def save(src, dst):
        out_copies.append(ml.local(src, dst, os.at[len(out_copies)]))

    pair_mask = head_mask(T, 128)
    low_half = lax.broadcasted_iota(jnp.int32, (T, 128), 1) % HEAD < HEAD // 2
    onehot = (lax.broadcasted_iota(jnp.int32, (8, 128), 0) == lax.broadcasted_iota(jnp.int32, (8, 128), 1)).astype(F32).astype(BF)

    def tables():
        wide_row = jnp.broadcast_to(seg_ref[...].astype(F32), (T, T))
        same = wide_row.T == wide_row
        bias[...] = jnp.where(same, 0.0, masked_score)
        at = lax.broadcasted_iota(jnp.int32, (T, T), 1).astype(F32)
        first = jnp.min(jnp.where(same, at, float(T)), axis=1, keepdims=True)
        position = lax.broadcasted_iota(jnp.int32, (T, 128), 0).astype(F32) - first
        angle = position * freq_ref[0:1, :]
        sine = jnp.sin(angle)
        cos_ref[...] = jnp.cos(angle)
        sin_ref[...] = jnp.where(low_half, -sine, sine)

    def permute():
        for copy in wide:
            copy.wait()
        def of(i, carry):
            l, w = i // 2, i % 2
            v = W[w, l]
            for cc in range(2):
                for yy in range(2):
                    pieces = [v[:, 384 * j + 192 * cc + 96 * yy:384 * j + 192 * cc + 96 * yy + 96] for j in range(G)]
                    GU[l, cc, yy, :, tile(w, FS)] = jnp.concatenate(pieces, axis=1)
            return carry
        lax.fori_loop(0, 4, of, 0)

    def project(l):
        st = S[...]
        cos, sin = cos_ref[...], sin_ref[...]
        for j in range(6):
            h, off = j // 3, (j % 3) * 384
            w = A[l, h, :, :, :, off:off + 384].reshape(D, 384)
            r = dot(st, w)
            kind = j // 2
            for t in range(3):
                v = r[:, 128 * t:128 * t + 128]
                if kind < 2:
                    v = v * cos + swap_halves(v, low_half) * sin
                col = (j % 2) * 384 + 128 * t
                Q[l, kind, :, col:col + 128] = v.astype(BF)

    def attention(l):
        def pair(p, carry):
            cols = tile(p, 128)
            q, kk, v = Q[l, 0, :, cols] * jnp.asarray(0.125, BF), Q[l, 1, :, cols], Q[l, 2, :, cols]
            outs = []
            for h in range(2):
                qh = jnp.where(pair_mask == (h == 0), q, jnp.zeros_like(q))
                s = dot_t(qh, kk) + bias[...]
                e = jnp.exp(s - jnp.max(s, axis=1, keepdims=True))
                pr = (e * (1.0 / jnp.sum(e, axis=1, keepdims=True))).astype(BF)
                Pb[l, 2 * p + h] = pr
                outs.append(dot(pr, v))
            AT[:, cols] = jnp.where(pair_mask, outs[0], outs[1]).astype(BF)
            return carry
        lax.fori_loop(0, PAIRS, pair, 0)

    def params(l):
        for h in range(2):
            w = A[l, h, :, :, :, QW + OW:].reshape(D, 128)
            PV[l, h] = dot_t(onehot, w)

    def out_project(l):
        for h in range(2):
            w = A[l, h, :, :, :, QW:QW + OW].reshape(D, OW)
            H[:, h * OW:h * OW + OW] = H[:, h * OW:h * OW + OW] + dot(AT[...], w)

    def norm(l, i, dst, extra, half):
        gain, shift = PV[l, i, 0:1, :], PV[l, i, 1:2, :]
        def rows_of(j, carry):
            rows = tile(j, 32)
            v = H[rows, :]
            if extra is not None:
                v = v + extra(rows)
            cen = v - jnp.mean(v, axis=1, keepdims=True)
            inv = lax.rsqrt(jnp.mean(cen * cen, axis=1, keepdims=True) + eps_norm)
            n = cen * inv
            N[l, i, rows, :] = n
            I[l, i, rows, :] = jnp.broadcast_to(inv, (32, 128))
            m = n * gain + shift
            H[rows, :] = m
            dst[rows, :] = m.astype(BF)
            return carry
        lax.fori_loop(half * (HT // 32), (half + 1) * (HT // 32), rows_of, 0)

    def ffn_up(l, first, toks):
        two, n = pl.ds(first, 2), toks.size
        def cols_of(j, carry):
            cols = tile(j, 256)
            xx = MF[l, two, toks].reshape(2 * n, D)
            gate = dot(xx, F[l, :, cols])
            up = dot(xx, F[l, :, pl.ds(pl.multiple_of(FS + j * 256, 256), 256)])
            act = gate * jax.nn.sigmoid(gate) * up
            TG[l, 0, two, toks, cols] = gate.astype(BF).reshape(2, n, 256)
            TG[l, 1, two, toks, cols] = up.astype(BF).reshape(2, n, 256)
            AC[two, toks, cols] = act.astype(BF).reshape(2, n, 256)
            return carry
        lax.fori_loop(0, FS // 256, cols_of, 0)

    def ffn_down(l, s_, toks, plus=None):
        def cols_of(j, carry):
            cols = tile(j, 256)
            r = dot(AC[s_, toks], F[l, :, pl.ds(pl.multiple_of(2 * FS + j * 256, 256), 256)])
            if plus is not None:
                r = r + plus[toks, cols].astype(F32)
            FD[l, s_, toks, cols] = r.astype(BF)
            return carry
        lax.fori_loop(0, D // 256, cols_of, 0)

    def turn(src, dst, col):
        def tile_of(j, carry):
            cols = tile(j, 128)
            dst[cols, pl.ds(pl.multiple_of(col, T), T)] = src[:, cols].T
            return carry
        lax.fori_loop(0, D // 128, tile_of, 0)

    def turn_slots(src, dst):
        def slot_of(i, carry):
            turn(src.at[i], dst, i * T)
            return carry
        lax.fori_loop(0, 4, slot_of, 0)

    def begin():
        H[...] = x_ref[...].astype(F32)
        S[...] = x_ref[...]
        permute()
        gu_send(0)
        gu_send(1)

    def projected(l):
        params(l)
        project(l)

    def turn_state(l):
        turn(S, ST.at[l, 0], 0)

    def scores(l):
        attention(l)
        save(Pb.at[l], P_o.at[l])
        save(Q.at[l], Q_o.at[l])

    WHOLE = pl.ds(0, T)

    def branch(l):
        out_project(l)

    def first_norm(l, h):
        norm(l, 0, MF.at[l, slot], None, h)
        mine = MF.at[l, slot, part_of(h)]
        ml.send(mine, mine, s_m.at[l, 0, h], r_m.at[l, 0, h], pc.yside())
        ml.send(mine, mine, s_m.at[l, 1, h], r_m.at[l, 1, h], pc.core())

    def turn_attended(l):
        turn(AT, ST.at[l, 1], 0)
        save(ST.at[l], ST_o.at[l])

    def own_up(l):
        for h in range(2):
            ml.arrive(MF.at[l, 2 * y + 1 - c, part_of(h)], s_m.at[l, 1, h], r_m.at[l, 1, h], pc.core())
        f_x(l, 0)
        ffn_up(l, 2 * y, WHOLE)

    def own_down(l):
        f_x(l, 1)
        s_ = 2 * y + 1 - c
        ffn_down(l, s_, WHOLE)
        ml.send(FD.at[l, s_], RC.at[l, y], s_rc.at[l, 2], r_rc.at[l, 2], pc.core())
        ffn_down(l, slot, WHOLE)

    def pass_on(l, h):
        block = MF.at[l, 2 * (1 - y) + c, part_of(h)]
        ml.arrive(block, s_m.at[l, 0, h], r_m.at[l, 0, h], pc.yside())
        ml.send(block, block, s_m.at[l, 2, h], r_m.at[l, 2, h], pc.core())

    def other_up(l, h):
        others = 2 * (1 - y)
        ml.arrive(MF.at[l, others + 1 - c, part_of(h)], s_m.at[l, 2, h], r_m.at[l, 2, h], pc.core())
        ffn_up(l, others, part_of(h))

    def other_down(l, h):
        s_ = 2 * (1 - y) + 1 - c
        ffn_down(l, s_, part_of(h))
        ml.send(FD.at[l, s_, part_of(h)], RC.at[l, 1 - y, part_of(h)], s_rc.at[l, h], r_rc.at[l, h], pc.core())

    def other_sum(l, h):
        s_ = 2 * (1 - y) + c
        ml.arrive(RC.at[l, 1 - y, part_of(h)], s_rc.at[l, h], r_rc.at[l, h], pc.core())
        ffn_down(l, s_, part_of(h), RC.at[l, 1 - y])
        ml.send(FD.at[l, s_, part_of(h)], RY.at[l, part_of(h)], s_ry.at[l, h], r_ry.at[l, h], pc.yside())

    def turn_middle(l):
        turn_slots(MF.at[l], TT.at[l, 0])

    def turn_activated(l):
        turn_slots(AC, TT.at[l, 1])
        save(F.at[l], F_o.at[l])
        save(TT.at[l], TT_o.at[l])
        save(TG.at[l], TG_o.at[l])

    def second_norm(l, h):
        if h == 0:
            ml.arrive(RC.at[l, y], s_rc.at[l, 2], r_rc.at[l, 2], pc.core())
        ml.arrive(RY.at[l, part_of(h)], s_ry.at[l, h], r_ry.at[l, h], pc.yside())
        feed = lambda rows: FD[l, slot, rows, :].astype(F32) + RC[l, y, rows, :].astype(F32) + RY[l, rows, :].astype(F32)
        norm(l, 1, S if l == 0 else y_ref, feed, h)

    def ay_arrive(l, n):
        if n < 3:
            a_y(l, n, x, n)
        else:
            a_y(l, FOUR[n - 3], 1 - x, n)

    def ac_own(l):
        a_c(l, y)

    def ac_other(l):
        a_c(l, 1 - y)

    def attn_ready(l):
        a_c_arrive(l, y)
        a_c_arrive(l, 1 - y)
        save(A.at[l], A_o.at[l])

    own_params()
    met()
    a_own(0)
    a_own(1)
    a_z(0, 0)
    a_z(0, 1)
    begin()
    a_x(1, 0)
    a_x(0, 0)
    a_z(1, 0)
    f_ready(0)
    a_z(1, 1)
    a_yo(0, 0)
    a_z(0, 2)
    a_yx(0, 0)
    a_yo(0, 1)
    ay_arrive(0, 0)
    f_own_x(0, 1)
    a_x(0, 1)
    f_own_z(0, 0)
    a_yo(0, 2)
    a_z(1, 2)
    f_ready(1)
    a_x(1, 1)
    a_x(0, 2)
    tables()
    a_yx(0, 1)
    ay_arrive(0, 1)
    ay_arrive(0, 2)
    a_x(1, 2)
    ay_arrive(0, 3)
    a_yo(1, 0)
    f_own_x(0, 0)
    f_own_z(0, 1)
    ay_arrive(0, 4)
    a_x(0, 3)
    a_yx(0, 2)
    f_own_z(1, 1)
    a_yx(0, 3)
    ac_own(0)
    a_yx(1, 0)
    turn_state(0)
    f_z(0, 0, 0)
    f_z(0, 0, 1)
    ay_arrive(0, 5)
    ay_arrive(0, 6)
    f_z(0, 0, 2)
    ay_arrive(1, 0)
    ac_other(0)
    a_yo(1, 1)
    f_z(1, 1, 0)
    a_yo(1, 2)
    f_z(0, 1, 0)
    a_yx(1, 1)
    attn_ready(0)
    projected(0)
    f_own_z(1, 0)
    a_x(1, 3)
    scores(0)
    f_z(0, 1, 1)
    branch(0)
    ay_arrive(1, 1)
    first_norm(0, 0)
    first_norm(0, 1)
    turn_attended(0)
    ay_arrive(1, 2)
    ay_arrive(1, 3)
    f_z(0, 1, 2)
    own_up(0)
    ay_arrive(1, 4)
    f_own_x(1, 0)
    a_yx(1, 2)
    a_yx(1, 3)
    f_z(1, 1, 1)
    pass_on(0, 0)
    ac_own(1)
    other_up(0, 0)
    f_own_x(1, 1)
    pass_on(0, 1)
    f_z(1, 0, 0)
    f_z(1, 0, 1)
    own_down(0)
    other_down(0, 0)
    other_up(0, 1)
    ay_arrive(1, 5)
    other_sum(0, 0)
    f_z(1, 1, 2)
    ay_arrive(1, 6)
    other_down(0, 1)
    other_sum(0, 1)
    ac_other(1)
    f_z(1, 0, 2)
    f_cross()
    attn_ready(1)
    turn_middle(0)
    second_norm(0, 0)
    second_norm(0, 1)
    projected(1)
    scores(1)
    f_w(0)
    branch(1)
    first_norm(1, 0)
    f_w(1)
    first_norm(1, 1)
    turn_activated(0)
    f_w(2)
    own_up(1)
    pass_on(1, 0)
    own_down(1)
    other_up(1, 0)
    other_down(1, 0)
    pass_on(1, 1)
    turn_state(1)
    other_sum(1, 0)
    other_up(1, 1)
    other_down(1, 1)
    turn_middle(1)
    other_sum(1, 1)
    turn_activated(1)
    second_norm(1, 0)
    turn_attended(1)
    second_norm(1, 1)
    for src, dst in ((N, N_o), (I, I_o), (PV, PV_o)):
        save(src, dst)
    for copy in out_copies:
        copy.wait()
    ml.finish()


FWD_SHAPES = [
    ((2, 2, G, 2, 48, AW), BF),
    ((2, D, 2 * FS + D), BF),
    ((2, 3, T, D), BF),
    ((2, 2, D, T), BF),
    ((2, HEADS, T, T), BF),
    ((2, 2, 4, T, FS), BF),
    ((2, 2, D, 4 * T), BF),
    ((2, 2, T, D), F32),
    ((2, 2, T, 128), F32),
    ((2, 2, 8, D), F32),
]


def sems(*shape):
    return pltpu.SemaphoreType.DMA(shape)


def forward_call(args):
    any_spec = pl.BlockSpec(memory_space=pl.ANY)
    vm = pl.BlockSpec(memory_space=pltpu.VMEM)
    return pl.pallas_call(
        forward_kernel,
        out_shape=[jax.ShapeDtypeStruct((T, D), BF)]
        + [jax.ShapeDtypeStruct(s, d) for s, d in FWD_SHAPES]
        + [jax.ShapeDtypeStruct((T, 128), F32)] * 2,
        in_specs=[vm] * 7 + [any_spec] * 5,
        out_specs=[vm] + [any_spec] * len(FWD_SHAPES) + [vm] * 2,
        scratch_shapes=[pltpu.VMEM(s, d) for s, d in FWD_SHAPES]
        + [
            pltpu.VMEM((T, D), BF),
            pltpu.VMEM((T, D), BF),
            pltpu.VMEM((2, 4, T, D), BF),
            pltpu.VMEM((4, T, FS), BF),
            pltpu.VMEM((T, D), F32),
            pltpu.VMEM((T, T), F32),
            pltpu.VMEM((2, 4, T, D), BF),
            pltpu.VMEM((2, 2, T, D), BF),
            pltpu.VMEM((2, T, D), BF),
            pltpu.VMEM((2, 2, 48, 4 * FS), BF),
            pltpu.VMEM((2, 2, 2, 48, 2 * FS), BF),
            sems(2, 8),
            sems(2), sems(2),
            sems(2, 5), sems(2, 3),
            sems(2, 4), sems(2, 4),
            sems(2, 7), sems(2, 7),
            sems(2, 2), sems(2, 2),
            sems(2, 2, 5), sems(2, 2, 3),
            sems(2, 2, 4), sems(2, 2, 4),
            sems(5), sems(3),
            sems(2, 3, 2), sems(2, 3, 2),
            sems(2, 3), sems(2, 3),
            sems(2, 2), sems(2, 2),
            sems(17),
        ],
        compiler_params=pltpu.CompilerParams(collective_id=0, has_side_effects=True, vmem_limit_bytes=60 * 2**20),
        cost_estimate=pl.CostEstimate(flops=10**10, bytes_accessed=10**8, transcendentals=0),
        name="forward",
    )(*args)


def backward_kernel(
    cot_ref, cos_ref, sin_ref, A_i, F_i, Q_i, ST_i, P_i, TG_i, TT_i, N_i, I_i, PV_i,
    gin_ref, GUG, DNG, AF,
    A, F, Q, ST, Pb, TG, TT, N, I, PV,
    U, GF, GB, GP, FD, RC, RY, FG, RFX, RFZ, FR, AG, RAC, RAY, RAX, RAZ, RO, OX, OR, OT, OY, V,
    ls, s_m, r_m, s_rc, r_rc, s_ry, r_ry,
    s_fx, r_fx, s_fz, r_fz, s_fc, r_fc, s_fy, r_fy,
    s_ac, r_ac, s_ay, r_ay, s_ax, r_ax, s_az, r_az, s_af, r_af, s_oz, r_oz, s_ox, r_ox, s_oy, r_oy,
):
    pc = Place()
    y, z, x, c, slot = pc.y, pc.z, pc.x, pc.c, pc.slot
    ml = Mail()
    mid = z % 3 != 0
    zn = pc.near()
    near, across = pc.zto(zn), pc.zto(3 - z)
    planes = (3 - zn, 3 - z, zn, z)
    places = {
        "PV": (PV_i, PV, 0), "N": (N_i, N, 1), "I": (I_i, I, 2), "TT": (TT_i, TT, 3), "F": (F_i, F, 4), "TG": (TG_i, TG, 5),
        "ST": (ST_i, ST, 6), "A": (A_i, A, 7), "P": (P_i, Pb, 8), "Q": (Q_i, Q, 9),
    }
    loading = {}

    def load(l, *names):
        for name in names:
            src, dst, i = places[name]
            loading[name] = ml.local(src.at[l], dst, ls.at[i])

    def need(*names):
        for name in names:
            if name in loading:
                loading.pop(name).wait()

    met = greet(pc.line())
    load(1, "PV", "N", "I", "F", "TG", "TT", "ST", "A", "P", "Q")
    U[...] = cot_ref[...].astype(F32)

    fcols = (pl.ds(2 * FS, D), pl.ds(0, FS), pl.ds(FS, FS))

    def fx_send(l, j):
        for n in range(4):
            ml.send(FG.at[planes[n], 1 - x, :, fcols[j]], RFX.at[l, j, planes[n]], s_fx.at[l, j, n], r_fx.at[l, j, n], pc.xside(), ("fx", l, j))

    def line_start(n, part, R, ss, rs):
        slot_of = (1, 2, 0)[n]
        ml.send_if(z % 3 == 0, part(planes[n]), R.at[slot_of], ss.at[n], rs.at[slot_of], near)

    def plus(dst, src, rows, widths):
        for r in range(0, rows, 48):
            at = 0
            for w in widths:
                here = (pl.ds(r, 48), pl.ds(at, w))
                dst[here] = (dst[here].astype(F32) + src[here].astype(F32)).astype(BF)
                at += w

    def line_middle(part, R, ss, rs, add):
        far = [pltpu.make_async_remote_copy(R.at[n], R.at[n], ss.at[0], rs.at[n], device_id=near, device_id_type=MESH) for n in (1, 2)]
        on = [
            ml.later(part(plane), R.at[3 + n], ss.at[3 + n], rs.at[3 + n], across, mid)
            for n, plane in enumerate((3 - z, 3 - zn))
        ]
        dsts = [part(3 - z), part(3 - zn)]
        def go():
            for n in range(2):
                far[n].wait_recv()
                add(dsts[n], R.at[1 + n])
                on[n].start()
        pl.when(mid)(go)

    def line_end(part, R, ss, rs, add):
        back = [pltpu.make_async_remote_copy(R.at[n], R.at[n], ss.at[0], rs.at[n], device_id=across, device_id_type=MESH) for n in (3, 4)]
        last = ml.later(part(zn), R.at[0], ss.at[5], rs.at[0], near, mid)
        dsts = [part(z), part(zn)]
        def go():
            back[1].wait_recv()
            add(dsts[1], R.at[4])
            last.start()
            back[0].wait_recv()
            add(dsts[0], R.at[3])
        pl.when(mid)(go)
        ml.arrive(R.at[0], ss.at[0], rs.at[0], near)

    def add_f(dst, src):
        plus(dst, src, 96, (D,))

    def add_a(dst, src):
        plus(dst, src, 48, awide[0])

    def add_o(dst, src):
        for i in range(2):
            for xx in range(2):
                plus(dst.at[i, xx], src.at[i, xx], 48, awide[1])

    def fpart(l, j):
        return lambda zz: RFX.at[l, j, zz]

    def fx_task(l, j, n):
        if True:
            p = planes[n]
            ml.arrive(RFX.at[l, j, p], s_fx.at[l, j, n], r_fx.at[l, j, n], pc.xside())
            for half in range(2):
                rows = pl.ds(48 * half, 48)
                RFX[l, j, p, rows, :] = (RFX[l, j, p, rows, :].astype(F32) + FG[p, x, rows, fcols[j]].astype(F32)).astype(BF)
            if n < 3:
                line_start(n, fpart(l, j), RFZ.at[l, j], s_fz.at[l, j], r_fz.at[l, j])

    def fm_task(l, j):
        line_middle(fpart(l, j), RFZ.at[l, j], s_fz.at[l, j], r_fz.at[l, j], add_f)

    def fz_task(l, j):
        line_end(fpart(l, j), RFZ.at[l, j], s_fz.at[l, j], r_fz.at[l, j], add_f)
        def total(start):
            rows = pl.ds(start, 48)
            return (RFX[l, j, z, rows, :].astype(F32) + RFZ[l, j, 0, rows, :].astype(F32)).astype(BF)
        if j == 0:
            for half in range(2):
                DNG[l, y, pl.ds(48 * half, 48), :] = total(48 * half)
            ml.send(DNG.at[l, y], DNG.at[l, y], s_fy.at[l, 0], r_fy.at[l, 0], pc.yside())
        else:
            FR[l, j - 1] = total(pl.multiple_of((1 - c) * 48, 48))
            ml.send(FR.at[l, j - 1], GUG.at[l, j - 1, c, y], s_fc.at[l, j], r_fc.at[l, j], pc.core())
            GUG[l, j - 1, c, y] = total(pl.multiple_of(c * 48, 48))

    def fc_task(l, j):
        ml.arrive(GUG.at[l, j - 1, 1 - c, y], s_fc.at[l, j], r_fc.at[l, j], pc.core())
        block = GUG.at[l, j - 1, :, y]
        ml.send(block, block, s_fy.at[l, j], r_fy.at[l, j], pc.yside())

    def fy_task(l, j):
        block = DNG.at[l, 1 - y] if j == 0 else GUG.at[l, j - 1, :, 1 - y]
        ml.arrive(block, s_fy.at[l, j], r_fy.at[l, j], pc.yside())

    acols = (pl.ds(0, QW), pl.ds(QW, AW - QW))
    awide = ((768, 384), (512,))

    def ac_send(l, p, i):
        h = (1 - y, y)[i]
        ml.send(AG.at[h, :, :, 1 - c, :, acols[p]], RAC.at[l, i, :, :, :, acols[p]], s_ac.at[l, p, i], r_ac.at[l, p, i], pc.core(), ("ac", l))

    def ac_sum(l, p, i):
        h = (1 - y, y)[i]
        ml.arrive(RAC.at[l, i, :, :, :, acols[p]], s_ac.at[l, p, i], r_ac.at[l, p, i], pc.core())
        def add(n, carry):
            zz, xx = n // 2, n % 2
            plus(RAC.at[l, i, zz, xx, :, acols[p]], AG.at[h, zz, xx, c, :, acols[p]], 48, awide[p])
            return carry
        lax.fori_loop(0, 8, add, 0)

    def ay_send(l, p, n):
        q = planes[n]
        ml.send(RAC.at[l, 0, q, :, :, acols[p]], RAY.at[l, q], s_ay.at[l, p, n], r_ay.at[l, p, n], pc.yside())

    def ay_task(l, p, n):
        q = planes[n]
        ml.arrive(RAY.at[l, q], s_ay.at[l, p, n], r_ay.at[l, p, n], pc.yside())
        for xx in range(2):
            plus(RAC.at[l, 1, q, xx, :, acols[p]], RAY.at[l, q, xx], 48, awide[p])
        ml.send(RAC.at[l, 1, q, 1 - x, :, acols[p]], RAX.at[l, q], s_ax.at[l, p, n], r_ax.at[l, p, n], pc.xside())

    def apart(l, p):
        return lambda zz: RAX.at[l, zz]

    def ax_task(l, p, n):
        q = planes[n]
        ml.arrive(RAX.at[l, q], s_ax.at[l, p, n], r_ax.at[l, p, n], pc.xside())
        plus(RAX.at[l, q], RAC.at[l, 1, q, x, :, acols[p]], 48, awide[p])
        if n < 3:
            line_start(n, apart(l, p), RAZ.at[l], s_az.at[l, p], r_az.at[l, p])

    def am_task(l, p):
        line_middle(apart(l, p), RAZ.at[l], s_az.at[l, p], r_az.at[l, p], add_a)

    def az_task(l, p):
        line_end(apart(l, p), RAZ.at[l], s_az.at[l, p], r_az.at[l, p], add_a)
        mine = AF.at[l, y, :, acols[p]]
        mine[...] = (RAX[l, z].astype(F32) + RAZ[l, 0].astype(F32)).astype(BF)
        ml.send(mine, mine, s_af.at[l, p], r_af.at[l, p], pc.yside())

    def af_task(l, p):
        ml.arrive(AF.at[l, 1 - y, :, acols[p]], s_af.at[l, p], r_af.at[l, p], pc.yside())

    def opart(l):
        return lambda zz: RAC.at[l, :, zz, :, :, acols[1]]

    def o_start(l):
        for n in range(3):
            line_start(n, opart(l), RO.at[l], s_oz.at[l], r_oz.at[l])

    def om_task(l):
        line_middle(opart(l), RO.at[l], s_oz.at[l], r_oz.at[l], add_o)

    def oz_task(l):
        line_end(opart(l), RO.at[l], s_oz.at[l], r_oz.at[l], add_o)
        for i, h in ((0, 1 - y), (1, y)):
            both = lambda xx: (RAC[l, i, z, xx, :, acols[1]].astype(F32) + RO[l, 0, i, xx].astype(F32)).astype(BF)
            OX[l, h] = both(1 - x)
            OT[l, h] = both(x)
        ml.send(OX.at[l], OR.at[l], s_ox.at[l], r_ox.at[l], pc.xside())

    def ox_task(l):
        ml.arrive(OR.at[l], s_ox.at[l], r_ox.at[l], pc.xside())
        for h in range(2):
            plus(OT.at[l, h], OR.at[l, h], 48, awide[1])
        ml.send(OT.at[l], OY.at[l], s_oy.at[l], r_oy.at[l], pc.yside())

    def oy_task(l):
        ml.arrive(OY.at[l], s_oy.at[l], r_oy.at[l], pc.yside())
        for h in range(2):
            AF[l, h, :, acols[1]] = (OT[l, h].astype(F32) + OY[l, h].astype(F32)).astype(BF)

    pair_mask = head_mask(T, 128)
    low_half = lax.broadcasted_iota(jnp.int32, (T, 128), 1) % HEAD < HEAD // 2
    onehot = (lax.broadcasted_iota(jnp.int32, (8, 128), 0) == lax.broadcasted_iota(jnp.int32, (8, 128), 1)).astype(F32).astype(BF)

    def norm_back(i, extra, dst, half):
        gain = PV[i, 0:1, :]
        def rows_of(j, carry):
            gs, bs = carry
            rows = tile(j, 32)
            u = U[rows, :]
            if extra is not None:
                u = u + extra(rows)
            n = N[i, rows, :]
            un = u * n
            gs = gs + un.reshape(4, 8, D).sum(0)
            bs = bs + u.reshape(4, 8, D).sum(0)
            m1 = jnp.mean(u * gain, axis=1, keepdims=True)
            m2 = jnp.mean(un * gain, axis=1, keepdims=True)
            r = I[i, rows, 0:1] * (u * gain - m1 - n * m2)
            U[rows, :] = r
            dst[rows, :] = r.astype(BF)
            return gs, bs
        zero = jnp.zeros((8, D), F32)
        gs, bs = lax.fori_loop(half * (HT // 32), (half + 1) * (HT // 32), rows_of, (zero, zero))
        row = lax.broadcasted_iota(jnp.int32, (8, D), 0)
        sums = jnp.where(row == 0, gs.sum(0, keepdims=True), jnp.where(row == 1, bs.sum(0, keepdims=True), 0.0))
        V[i] = sums if half == 0 else V[i] + sums

    def act_back(l, first, toks):
        two, n = pl.ds(first, 2), toks.size
        def cols_of(j, carry):
            cols = tile(j, 256)
            ga = dot_t(GF[l, two, toks].reshape(2 * n, D), F[cols, 2 * FS:])
            gate = TG[0, two, toks, cols].reshape(2 * n, 256).astype(F32)
            up = TG[1, two, toks, cols].reshape(2 * n, 256).astype(F32)
            sg = jax.nn.sigmoid(gate)
            gg = ga * up * sg * (1.0 + gate * (1.0 - sg))
            gu = ga * gate * sg
            TG[0, two, toks, cols] = gg.astype(BF).reshape(2, n, 256)
            TG[1, two, toks, cols] = gu.astype(BF).reshape(2, n, 256)
            return carry
        lax.fori_loop(0, FS // 256, cols_of, 0)

    def mid_back(s_, toks, plus=None):
        def cols_of(j, carry):
            cols = tile(j, 256)
            r = dot_t(TG[0, s_, toks], F[cols, 0:FS]) + dot_t(TG[1, s_, toks], F[cols, FS:2 * FS])
            if plus is not None:
                r = r + plus[toks, cols].astype(F32)
            FD[s_, toks, cols] = r.astype(BF)
            return carry
        lax.fori_loop(0, D // 256, cols_of, 0)

    def weight_grad(l, j):
        def cols_of(n, carry):
            cols = tile(n, 256)
            if j == 0:
                right = GF[l, :, :, cols].reshape(4 * T, 256)
            else:
                right = TG[j - 1, :, :, cols].reshape(4 * T, 256)
            r = dot(TT[0 if j else 1], right)
            off = (2 * FS, 0, FS)[j]
            FG[:, :, :, pl.ds(pl.multiple_of(off + n * 256, 256), 256)] = r.astype(BF).reshape(4, 2, 96, 256)
            return carry
        lax.fori_loop(0, 3, cols_of, 0)

    def out_back():
        acc = None
        for h in range(2):
            r = dot(ST[1], GB[:, h * OW:h * OW + OW])
            AG[h, :, :, :, :, QW:QW + OW] = r.astype(BF).reshape(4, 2, 2, 48, OW)
        for h in range(2):
            t = dot_t(GB[:, h * OW:h * OW + OW], A[h, :, :, :, QW:QW + OW].reshape(D, OW))
            acc = t if acc is None else acc + t
        GP[2] = acc.astype(BF)

    def attention_back():
        def pair(p, carry):
            cols = tile(p, 128)
            q, kk, v, ga = Q[0, :, cols], Q[1, :, cols], Q[2, :, cols], GP[2, :, cols]
            dq, dk, dv = [], [], []
            for h in range(2):
                pl_ = Pb[2 * p + h]
                pr = pl_.astype(F32)
                gh = jnp.where(pair_mask == (h == 0), ga, jnp.zeros_like(ga))
                dp = dot_t(gh, v)
                ds = (pr * (dp - jnp.sum(dp * pr, axis=1, keepdims=True))).astype(BF)
                dq.append(dot(ds, kk))
                dk.append(dot(ds.T, q))
                dv.append(dot(pl_.T, ga))
            cos, sin = cos_ref[...], sin_ref[...]
            def back(pair_of):
                m = jnp.where(pair_mask, pair_of[0], pair_of[1]) * 0.125
                return (m * cos - swap_halves(m, low_half) * sin).astype(BF)
            GP[0, :, cols] = back(dq)
            GP[1, :, cols] = back(dk)
            GP[2, :, cols] = jnp.where(pair_mask, dv[0], dv[1]).astype(BF)
            return carry
        lax.fori_loop(0, PAIRS, pair, 0)

    def gp_chunk(j):
        return GP[j // 2, :, (j % 2) * 384:(j % 2) * 384 + 384]

    def qkv_grad(h):
        for j in range(3 * h, 3 * h + 3):
            off = (j % 3) * 384
            r = dot(ST[0], gp_chunk(j))
            AG[h, :, :, :, :, off:off + 384] = r.astype(BF).reshape(4, 2, 2, 48, 384)

    def param_grad():
        for h in range(2):
            r = lax.dot_general(V[h].astype(BF), onehot, (((0,), (0,)), ((), ())), preferred_element_type=F32)
            AG[h, :, :, :, :, QW + OW:] = r.astype(BF).reshape(4, 2, 2, 48, 128)

    def input_back():
        acc = U[...]
        for j in range(6):
            off = (j % 3) * 384
            acc = acc + dot_t(gp_chunk(j), A[j // 3, :, :, :, off:off + 384].reshape(D, 384))
        U[...] = acc

    def run(steps):
        for step, *what in steps:
            step(*what)

    WHOLE = pl.ds(0, T)

    def upper(l, h):
        need("PV", "N", "I")
        norm_back(1, None, GF.at[l, slot], h)
        if l == 1 and h == 0:
            met()
        mine = GF.at[l, slot, part_of(h)]
        ml.send(mine, mine, s_m.at[l, 0, h], r_m.at[l, 0, h], pc.yside())
        ml.send(mine, mine, s_m.at[l, 1, h], r_m.at[l, 1, h], pc.core())

    def own_tokens(l):
        need("F", "TG")
        ml.gone(("fd", 1))
        for h in range(2):
            ml.arrive(GF.at[l, 2 * y + 1 - c, part_of(h)], s_m.at[l, 1, h], r_m.at[l, 1, h], pc.core())
        act_back(l, 2 * y, WHOLE)
        s_ = 2 * y + 1 - c
        mid_back(s_, WHOLE)
        ml.send(FD.at[s_], RC.at[y], s_rc.at[l, 2], r_rc.at[l, 2], pc.core(), ("fd", l))
        mid_back(slot, WHOLE)

    def pass_on(l, h):
        block = GF.at[l, 2 * (1 - y) + c, part_of(h)]
        ml.arrive(block, s_m.at[l, 0, h], r_m.at[l, 0, h], pc.yside())
        ml.send(block, block, s_m.at[l, 2, h], r_m.at[l, 2, h], pc.core())

    def other_tokens(l, h):
        others = 2 * (1 - y)
        ml.arrive(GF.at[l, others + 1 - c, part_of(h)], s_m.at[l, 2, h], r_m.at[l, 2, h], pc.core())
        act_back(l, others, part_of(h))

    def other_mids(l, h):
        s_ = 2 * (1 - y) + 1 - c
        mid_back(s_, part_of(h))
        ml.send(FD.at[s_, part_of(h)], RC.at[1 - y, part_of(h)], s_rc.at[l, h], r_rc.at[l, h], pc.core(), ("fd", l))

    def other_sums(l, h):
        s_ = 2 * (1 - y) + c
        ml.arrive(RC.at[1 - y, part_of(h)], s_rc.at[l, h], r_rc.at[l, h], pc.core())
        mid_back(s_, part_of(h), RC.at[1 - y])
        ml.send(FD.at[s_, part_of(h)], RY.at[part_of(h)], s_ry.at[l, h], r_ry.at[l, h], pc.yside(), ("fd", l))
        if l == 1 and h == 1:
            load(0, "F")

    def weights(l, j):
        need("TT")
        ml.gone(("fx", 1, j) if l == 0 else None)
        weight_grad(l, j)
        fx_send(l, j)
        if l == 1 and j == 2:
            load(0, "TT", "TG")

    def middle(l, h):
        if h == 0:
            ml.arrive(RC.at[y], s_rc.at[l, 2], r_rc.at[l, 2], pc.core())
        ml.arrive(RY.at[part_of(h)], s_ry.at[l, h], r_ry.at[l, h], pc.yside())
        norm_back(0, lambda rows: FD[slot, rows, :].astype(F32) + RC[y, rows, :].astype(F32) + RY[rows, :].astype(F32), GB, h)
        if l == 1 and h == 1:
            load(0, "PV", "N", "I")

    QKV, OUT = 0, 1

    def out_sums(l):
        need("ST", "A")
        if l == 0:
            ml.gone(("ac", 1))
        param_grad()
        out_back()
        for i in range(2):
            ac_send(l, OUT, i)

    def scores(l):
        need("P", "Q")
        attention_back()
        if l == 1:
            load(0, "P", "Q")

    def below(l):
        input_back()
        if l == 0:
            gin_ref[...] = U[...]

    def qkv_sums(l):
        qkv_grad(0)
        qkv_grad(1)
        for i in range(2):
            ac_send(l, QKV, i)
        if l == 1:
            load(0, "ST", "A")

    upper(1, 0)
    upper(1, 1)
    own_tokens(1)
    pass_on(1, 0)
    other_tokens(1, 0)
    other_mids(1, 0)
    pass_on(1, 1)
    other_sums(1, 0)
    other_tokens(1, 1)
    other_mids(1, 1)
    weights(1, 0)
    other_sums(1, 1)
    fx_task(1, 0, 0)
    middle(1, 0)
    weights(1, 1)
    middle(1, 1)
    fx_task(1, 0, 1)
    out_sums(1)
    weights(1, 2)
    fx_task(1, 0, 2)
    ac_sum(1, 1, 0)
    ac_sum(1, 1, 1)
    o_start(1)
    scores(1)
    below(1)
    upper(0, 0)
    fx_task(1, 1, 0)
    upper(0, 1)
    qkv_sums(1)
    own_tokens(0)
    ac_sum(1, 0, 1)
    fx_task(1, 1, 1)
    fx_task(1, 0, 3)
    pass_on(0, 0)
    ac_sum(1, 0, 0)
    ay_send(1, 0, 0)
    other_tokens(0, 0)
    fx_task(1, 1, 2)
    pass_on(0, 1)
    other_mids(0, 0)
    om_task(1)
    fx_task(1, 1, 3)
    fx_task(1, 2, 0)
    other_tokens(0, 1)
    other_sums(0, 0)
    other_mids(0, 1)
    weights(0, 0)
    fm_task(1, 0)
    ay_task(1, 0, 0)
    fx_task(1, 2, 1)
    other_sums(0, 1)
    weights(0, 1)
    fx_task(1, 2, 2)
    middle(0, 0)
    fx_task(0, 0, 0)
    ay_send(1, 0, 1)
    middle(0, 1)
    fm_task(1, 1)
    out_sums(0)
    ay_send(1, 0, 2)
    fx_task(1, 2, 3)
    ac_sum(0, 1, 0)
    fx_task(0, 0, 1)
    ac_sum(0, 1, 1)
    fm_task(1, 2)
    o_start(0)
    ay_send(1, 0, 3)
    scores(0)
    qkv_sums(0)
    fx_task(0, 0, 2)
    ay_task(1, 0, 1)
    ac_sum(0, 0, 0)
    fx_task(0, 0, 3)
    ay_send(0, 0, 0)
    fz_task(1, 0)
    weights(0, 2)
    fx_task(0, 1, 0)
    ay_send(0, 0, 1)
    ac_sum(0, 0, 1)
    om_task(0)
    ay_send(0, 0, 2)
    ax_task(1, 0, 0)
    fz_task(1, 1)
    below(0)
    ay_task(0, 0, 0)
    fx_task(0, 1, 1)
    fc_task(1, 1)
    oz_task(1)
    fm_task(0, 0)
    fx_task(0, 2, 0)
    ay_send(0, 0, 3)
    ax_task(1, 0, 1)
    fz_task(1, 2)
    fx_task(0, 2, 1)
    oz_task(0)
    ay_task(0, 0, 1)
    fx_task(0, 1, 2)
    fm_task(0, 1)
    fx_task(0, 2, 2)
    fz_task(0, 0)
    ay_task(1, 0, 2)
    ay_task(0, 0, 2)
    fx_task(0, 1, 3)
    fm_task(0, 2)
    fc_task(1, 2)
    ax_task(0, 0, 0)
    am_task(1, 0)
    ay_task(1, 0, 3)
    ox_task(0)
    fx_task(0, 2, 3)
    ay_task(0, 0, 3)
    ax_task(0, 0, 1)
    ox_task(1)
    fz_task(0, 1)
    ax_task(1, 0, 2)
    fc_task(0, 1)
    fz_task(0, 2)
    fc_task(0, 2)
    am_task(0, 0)
    ax_task(1, 0, 3)
    ax_task(0, 0, 2)
    az_task(1, 0)
    ax_task(0, 0, 3)
    az_task(0, 0)
    for l in (1, 0):
        for j in range(3):
            fy_task(l, j)
        af_task(l, 0)
        oy_task(l)
    ml.finish()


def backward_call(cot, cos, sin, kept):
    any_spec = pl.BlockSpec(memory_space=pl.ANY)
    vm = pl.BlockSpec(memory_space=pltpu.VMEM)
    return pl.pallas_call(
        backward_kernel,
        out_shape=[
            jax.ShapeDtypeStruct((T, D), F32),
            jax.ShapeDtypeStruct((2, 2, 2, 2, 48, FS), BF),
            jax.ShapeDtypeStruct((2, 2, 96, D), BF),
            jax.ShapeDtypeStruct((2, 2, 48, AW), BF),
        ],
        in_specs=[vm] * 3 + [any_spec] * len(kept),
        out_specs=[vm] * 4,
        scratch_shapes=[pltpu.VMEM(s[1:], d) for s, d in FWD_SHAPES]
        + [
            pltpu.VMEM((T, D), F32),
            pltpu.VMEM((2, 4, T, D), BF),
            pltpu.VMEM((T, D), BF),
            pltpu.VMEM((3, T, D), BF),
            pltpu.VMEM((4, T, D), BF),
            pltpu.VMEM((2, T, D), BF),
            pltpu.VMEM((T, D), BF),
            pltpu.VMEM((4, 2, 96, 2 * FS + D), BF),
            pltpu.VMEM((2, 3, 4, 96, D), BF),
            pltpu.VMEM((2, 3, 5, 96, D), BF),
            pltpu.VMEM((2, 2, 48, D), BF),
            pltpu.VMEM((2, 4, 2, 2, 48, AW), BF),
            pltpu.VMEM((2, 2, 4, 2, 48, AW), BF),
            pltpu.VMEM((2, 4, 2, 48, QW), BF),
            pltpu.VMEM((2, 4, 48, QW), BF),
            pltpu.VMEM((2, 5, 48, QW), BF),
            pltpu.VMEM((2, 5, 2, 2, 48, AW - QW), BF),
            pltpu.VMEM((2, 2, 48, AW - QW), BF),
            pltpu.VMEM((2, 2, 48, AW - QW), BF),
            pltpu.VMEM((2, 2, 48, AW - QW), BF),
            pltpu.VMEM((2, 2, 48, AW - QW), BF),
            pltpu.VMEM((2, 8, D), F32),
            sems(10),
            sems(2, 3, 2), sems(2, 3, 2),
            sems(2, 3), sems(2, 3),
            sems(2, 2), sems(2, 2),
            sems(2, 3, 4), sems(2, 3, 4),
            sems(2, 3, 6), sems(2, 3, 5),
            sems(2, 3), sems(2, 3),
            sems(2, 3), sems(2, 3),
            sems(2, 2, 2), sems(2, 2, 2),
            sems(2, 2, 4), sems(2, 2, 4),
            sems(2, 2, 4), sems(2, 2, 4),
            sems(2, 2, 6), sems(2, 2, 5),
            sems(2, 2), sems(2, 2),
            sems(2, 6), sems(2, 5),
            sems(2), sems(2),
            sems(2), sems(2),
        ],
        compiler_params=pltpu.CompilerParams(collective_id=1, has_side_effects=True, vmem_limit_bytes=62 * 2**20),
        cost_estimate=pl.CostEstimate(flops=2 * 10**10, bytes_accessed=10**8, transcendentals=0),
        name="backward",
    )(cot, cos, sin, *kept)


def finish_kernel(
    y_i, gin_i, gug_i, dng_i, af_i, y_o, gin_o, qkv_o, out_o, gate_o, up_o, down_o, g1_o, b1_o, g2_o, b2_o,
    y_v, gin_v, gug, dng, af, qkv, out, gate, up, down, in_sem, out_sem,
):
    def copy(src, dst, sem):
        c = pltpu.make_async_copy(src, dst, sem)
        c.start()
        return c
    arriving = [[copy(src.at[l], dst.at[l], in_sem.at[l, i]) for i, (src, dst) in enumerate(((af_i, af), (gug_i, gug), (dng_i, dng)))] for l in range(2)]
    passing = [copy(y_i, y_v, in_sem.at[0, 3]), copy(gin_i, gin_v, in_sem.at[1, 3])]
    leaving = []
    for l in range(2):
        arriving[l][0].wait()
        for h in range(2):
            qkv[l, :, h * QW:h * QW + QW] = af[l, h, :, 0:QW].astype(F32)
            out[l, :, h * OW:h * OW + OW] = af[l, h, :, QW:QW + OW].astype(F32)
            turned = af[l, h, :, QW + OW:].astype(F32).T
            for i, ref in enumerate(((g1_o, b1_o), (g2_o, b2_o))[h]):
                ref[l:l + 1, :] = turned[i:i + 1, :]
        leaving.append(copy(qkv.at[l], qkv_o.at[l], out_sem.at[l, 0]))
        leaving.append(copy(out.at[l], out_o.at[l], out_sem.at[l, 1]))
        arriving[l][1].wait()
        for w, ref in enumerate((gate, up)):
            for j in range(G):
                pieces = [gug[l, w, cc, yy, :, 96 * j:96 * j + 96] for cc in range(2) for yy in range(2)]
                ref[l, :, 384 * j:384 * j + 384] = jnp.concatenate(pieces, axis=1).astype(F32)
            leaving.append(copy(ref.at[l], (gate_o, up_o)[w].at[l], out_sem.at[l, 2 + w]))
        passing[l].wait()
        leaving.append(copy((y_v, gin_v)[l], (y_o, gin_o)[l], out_sem.at[l, 5]))
        arriving[l][2].wait()
        for h in range(2):
            down[l, 96 * h:96 * h + 96, :] = dng[l, h].astype(F32)
        leaving.append(copy(down.at[l], down_o.at[l], out_sem.at[l, 4]))
    for c in leaving:
        c.wait()


def epilogue(y, gin, gug, dng, af):
    vm = pl.BlockSpec(memory_space=pltpu.VMEM)
    any_spec = pl.BlockSpec(memory_space=pl.ANY)
    large = [(2, 48, 3 * D), (2, 48, D), (2, 48, 4 * FS), (2, 48, 4 * FS), (2, 192, D)]
    return tuple(pl.pallas_call(
        finish_kernel,
        out_shape=[jax.ShapeDtypeStruct(v.shape, v.dtype) for v in (y, gin)]
        + [jax.ShapeDtypeStruct(v, F32) for v in large + [(2, 48)] * 4],
        in_specs=[any_spec] * 5,
        out_specs=[any_spec] * 7 + [vm] * 4,
        scratch_shapes=[pltpu.VMEM(v.shape, v.dtype) for v in (y, gin, gug, dng, af)]
        + [pltpu.VMEM(v, F32) for v in large]
        + [sems(2, 4), sems(2, 6)],
        compiler_params=pltpu.CompilerParams(vmem_limit_bytes=60 * 2**20),
        cost_estimate=pl.CostEstimate(flops=10**6, bytes_accessed=10**7, transcendentals=0),
        name="finish",
    )(y, gin, gug, dng, af))


def positions_of(segment_row):
    token_index = jnp.arange(segment_row.shape[0], dtype=jnp.int32)
    before = jnp.concatenate([segment_row[:1] - 1, segment_row[:-1]])
    starts = jnp.where(segment_row != before, token_index, jnp.zeros_like(token_index))
    return token_index - lax.cummax(starts, axis=0)


def rotary_tables(position):
    half_width = HEAD // 2
    frequency = rope_base ** (-2.0 * jnp.arange(half_width, dtype=F32) / HEAD)
    angles = position.astype(F32)[:, None] * frequency[None, :]
    return jnp.cos(angles), jnp.sin(angles)


def prologue(inputs, segment_ids, qkv_weight, out_weight, gate_weight, up_weight, down_weight,
             first_gain, first_bias, second_gain, second_bias):
    frequency = rope_base ** (-2.0 * np.arange(HEAD // 2, dtype=np.float32) / HEAD)
    freq = jnp.asarray(np.tile(frequency.astype(np.float32)[None, :], (8, 4)))
    return (inputs[0], segment_ids, freq, first_gain, first_bias, second_gain, second_bias, qkv_weight, out_weight,
            gate_weight, up_weight, down_weight)


def rotate(values, cosine_table, sine_table):
    half_width = values.shape[-1] // 2
    lead_half = values[..., :half_width]
    tail_half = values[..., half_width:]
    cos_wide = cosine_table[:, None, :]
    sin_wide = sine_table[:, None, :]
    return jnp.concatenate(
        [lead_half * cos_wide - tail_half * sin_wide, tail_half * cos_wide + lead_half * sin_wide],
        axis=-1,
    )


def unrotate(values, cosine_table, sine_table):
    half_width = values.shape[-1] // 2
    lead_half = values[..., :half_width]
    tail_half = values[..., half_width:]
    cos_wide = cosine_table[:, None, :]
    sin_wide = sine_table[:, None, :]
    return jnp.concatenate(
        [lead_half * cos_wide + tail_half * sin_wide, tail_half * cos_wide - lead_half * sin_wide],
        axis=-1,
    )


def norm_forward(values, gain_row, bias_row):
    mean_row = jnp.mean(values, axis=-1, keepdims=True)
    centred = values - mean_row
    variance = jnp.mean(centred * centred, axis=-1, keepdims=True)
    inverse = lax.rsqrt(variance + eps_norm)
    normed = centred * inverse
    return (normed * gain_row + bias_row, normed, inverse)


def norm_backward(upstream, normed, inverse, gain_row):
    scaled = upstream * gain_row
    gain_sum = jnp.sum(upstream * normed, axis=0)
    bias_sum = jnp.sum(upstream, axis=0)
    grad_input = inverse * (
        scaled
        - jnp.mean(scaled, axis=-1, keepdims=True)
        - normed * jnp.mean(scaled * normed, axis=-1, keepdims=True)
    )
    return (grad_input, gain_sum, bias_sum)


def times_transposed(left_side, right_side):
    return lax.dot_general(
        left_side, right_side, (((1,), (1,)), ((), ())), preferred_element_type=jnp.float32
    )


def outer_sum(left_side, right_side):
    return lax.dot_general(
        left_side, right_side, (((0,), (0,)), ((), ())), preferred_element_type=jnp.float32
    )


def to_pairs(values):
    token_count = values.shape[0]
    return values.reshape(token_count, HEADS // 2, 2 * HEAD).transpose(1, 0, 2)


def from_pairs(values):
    return values.transpose(1, 0, 2).reshape(values.shape[1], HEADS * HEAD)


def pair_scores(query_pair, key_pair, allowed, score_scale):
    token_count = query_pair.shape[0]
    queries = query_pair.reshape(token_count, 2, HEAD)
    key_rows = key_pair.reshape(token_count, 2, HEAD)
    scores = (
        jnp.einsum("qhd,khd->hqk", queries, key_rows, preferred_element_type=jnp.float32)
        * score_scale
    )
    return (jnp.where(allowed[None], scores, masked_score), queries, key_rows)


def pair_forward(block_item, allowed, score_scale):
    query_pair, key_pair, value_pair = block_item
    token_count = query_pair.shape[0]
    scores, queries, key_rows = pair_scores(query_pair, key_pair, allowed, score_scale)
    row_top = jnp.max(scores, axis=-1, keepdims=True)
    exponent = jnp.exp(scores - row_top)
    row_total = jnp.sum(exponent, axis=-1, keepdims=True)
    probabilities = exponent / row_total
    logsum = row_top[..., 0] + jnp.log(row_total[..., 0])
    value_rows = value_pair.reshape(token_count, 2, HEAD)
    attended = jnp.einsum(
        "hqk,khd->qhd",
        probabilities.astype(jnp.bfloat16),
        value_rows,
        preferred_element_type=jnp.float32,
    )
    return (attended.reshape(token_count, 2 * HEAD), logsum)


def pair_backward(block_item, allowed, score_scale):
    query_pair, key_pair, value_pair, grad_pair, logsum = block_item
    token_count = query_pair.shape[0]
    scores, queries, key_rows = pair_scores(query_pair, key_pair, allowed, score_scale)
    probabilities = jnp.exp(scores - logsum[..., None])
    value_rows = value_pair.reshape(token_count, 2, HEAD)
    grad_rows = grad_pair.reshape(token_count, 2, HEAD)
    grad_probs = jnp.einsum(
        "qhd,khd->hqk", grad_rows, value_rows, preferred_element_type=jnp.float32
    )
    grad_values = jnp.einsum(
        "hqk,qhd->khd",
        probabilities.astype(jnp.bfloat16),
        grad_rows,
        preferred_element_type=jnp.float32,
    )
    grad_scores = probabilities * (
        grad_probs - jnp.sum(grad_probs * probabilities, axis=-1, keepdims=True)
    )
    grad_scores = grad_scores.astype(jnp.bfloat16)
    grad_queries = (
        jnp.einsum("hqk,khd->qhd", grad_scores, key_rows, preferred_element_type=jnp.float32)
        * score_scale
    )
    grad_keys = (
        jnp.einsum("hqk,qhd->khd", grad_scores, queries, preferred_element_type=jnp.float32)
        * score_scale
    )
    return (
        grad_queries.reshape(token_count, 2 * HEAD),
        grad_keys.reshape(token_count, 2 * HEAD),
        grad_values.reshape(token_count, 2 * HEAD),
    )


def layer_forward(hidden_state, weights, cosine_table, sine_table, allowed, score_scale):
    qkv_full, out_full, gate_full, up_full, down_full, gain_one, bias_one, gain_two, bias_two = (
        weights
    )
    token_count, model_width = hidden_state.shape
    state_low = hidden_state.astype(jnp.bfloat16)
    projected = jnp.dot(state_low, qkv_full, preferred_element_type=jnp.float32)
    queries = rotate(
        projected[:, :model_width].reshape(token_count, HEADS, HEAD), cosine_table, sine_table
    )
    queries = queries.astype(jnp.bfloat16).reshape(token_count, model_width)
    key_rows = rotate(
        projected[:, model_width : 2 * model_width].reshape(token_count, HEADS, HEAD),
        cosine_table,
        sine_table,
    )
    key_rows = key_rows.astype(jnp.bfloat16).reshape(token_count, model_width)
    value_rows = projected[:, 2 * model_width :].astype(jnp.bfloat16)

    def attend_pair(block_item):
        return pair_forward(block_item, allowed, score_scale)

    attended_pairs, logsum = lax.map(
        attend_pair, (to_pairs(queries), to_pairs(key_rows), to_pairs(value_rows))
    )
    attended = from_pairs(attended_pairs).astype(jnp.bfloat16)
    branch = jnp.dot(attended, out_full, preferred_element_type=jnp.float32)
    middle, normed_one, inverse_one = norm_forward(
        hidden_state + branch, gain_one.astype(jnp.float32), bias_one.astype(jnp.float32)
    )
    middle_low = middle.astype(jnp.bfloat16)
    gate_pre = jnp.dot(middle_low, gate_full, preferred_element_type=jnp.float32)
    up_pre = jnp.dot(middle_low, up_full, preferred_element_type=jnp.float32)
    activated = (jax.nn.silu(gate_pre) * up_pre).astype(jnp.bfloat16)
    feed = jnp.dot(activated, down_full, preferred_element_type=jnp.float32)
    result, normed_two, inverse_two = norm_forward(
        middle + feed, gain_two.astype(jnp.float32), bias_two.astype(jnp.float32)
    )
    stored = (
        state_low,
        queries,
        key_rows,
        value_rows,
        logsum,
        attended,
        normed_one,
        inverse_one,
        middle_low,
        gate_pre,
        up_pre,
        activated,
        normed_two,
        inverse_two,
    )
    return (result, stored)


def layer_backward(upstream, weights, stored, cosine_table, sine_table, allowed, score_scale):
    qkv_full, out_full, gate_full, up_full, down_full, gain_one, bias_one, gain_two, bias_two = (
        weights
    )
    (
        state_low,
        queries,
        key_rows,
        value_rows,
        logsum,
        attended,
        normed_one,
        inverse_one,
        middle_low,
        gate_pre,
        up_pre,
        activated,
        normed_two,
        inverse_two,
    ) = stored
    token_count, model_width = upstream.shape
    grad_mid, gain_two_sum, bias_two_sum = norm_backward(
        upstream, normed_two, inverse_two, gain_two.astype(jnp.float32)
    )
    grad_feed = grad_mid.astype(jnp.bfloat16)
    down_sum = outer_sum(activated, grad_feed)
    grad_act = times_transposed(grad_feed, down_full)
    sigmoid_gate = jax.nn.sigmoid(gate_pre)
    grad_gate = (grad_act * up_pre * sigmoid_gate * (1.0 + gate_pre * (1.0 - sigmoid_gate))).astype(
        jnp.bfloat16
    )
    grad_up = (grad_act * gate_pre * sigmoid_gate).astype(jnp.bfloat16)
    gate_sum = outer_sum(middle_low, grad_gate)
    up_sum = outer_sum(middle_low, grad_up)
    grad_middle = (
        grad_mid + times_transposed(grad_gate, gate_full) + times_transposed(grad_up, up_full)
    )
    grad_sum, gain_one_sum, bias_one_sum = norm_backward(
        grad_middle, normed_one, inverse_one, gain_one.astype(jnp.float32)
    )
    grad_branch = grad_sum.astype(jnp.bfloat16)
    out_sum = outer_sum(attended, grad_branch)
    grad_attended = times_transposed(grad_branch, out_full).astype(jnp.bfloat16)

    def attend_back(block_item):
        return pair_backward(block_item, allowed, score_scale)

    grad_query_pairs, grad_key_pairs, grad_value_pairs = lax.map(
        attend_back,
        (
            to_pairs(queries),
            to_pairs(key_rows),
            to_pairs(value_rows),
            to_pairs(grad_attended),
            logsum,
        ),
    )
    grad_queries = unrotate(
        from_pairs(grad_query_pairs).reshape(token_count, HEADS, HEAD), cosine_table, sine_table
    ).reshape(token_count, model_width)
    grad_keys = unrotate(
        from_pairs(grad_key_pairs).reshape(token_count, HEADS, HEAD), cosine_table, sine_table
    ).reshape(token_count, model_width)
    grad_projected = jnp.concatenate(
        [grad_queries, grad_keys, from_pairs(grad_value_pairs)], axis=1
    ).astype(jnp.bfloat16)
    qkv_sum = outer_sum(state_low, grad_projected)
    grad_input = grad_sum + times_transposed(grad_projected, qkv_full)
    return (
        grad_input,
        (
            qkv_sum,
            out_sum,
            gate_sum,
            up_sum,
            down_sum,
            gain_one_sum,
            bias_one_sum,
            gain_two_sum,
            bias_two_sum,
        ),
    )


def general(inputs, segment_ids, qkv_weight, out_weight, gate_weight, up_weight, down_weight,
            first_gain, first_bias, second_gain, second_bias, cotangent):
    params = (qkv_weight, out_weight, gate_weight, up_weight, down_weight, first_gain, first_bias, second_gain, second_bias)
    layers = qkv_weight.shape[0]
    segment_row = segment_ids[0]
    cosine_table, sine_table = rotary_tables(positions_of(segment_row))
    allowed = segment_row[:, None] == segment_row[None, :]
    score_scale = 1.0 / math.sqrt(HEAD)
    hidden_state = inputs[0].astype(F32)
    fetched, saved = [], []
    for layer_index in range(layers):
        weights = tuple(lax.all_gather(w[layer_index], "shard", axis=0, tiled=True) for w in params)
        fetched.append(weights)
        hidden_state, stored = layer_forward(hidden_state, weights, cosine_table, sine_table, allowed, score_scale)
        saved.append(stored)
    upstream = cotangent[0].astype(F32)
    shared = [None] * layers
    for layer_index in reversed(range(layers)):
        upstream, gradients = layer_backward(
            upstream, fetched[layer_index], saved[layer_index], cosine_table, sine_table, allowed, score_scale
        )
        owned = [lax.psum_scatter(v, "shard", scatter_dimension=0, tiled=True) for v in gradients]
        shared[layer_index] = [lax.psum(v.astype(BF), "rep").astype(F32) for v in owned]
    stacked = [jnp.stack([shared[layer_index][member] for layer_index in range(layers)]) for member in range(9)]
    return (hidden_state.astype(BF)[None], upstream[None], *stacked)


def special(inputs, segment_ids, qkv_weight, out_weight, gate_weight, up_weight, down_weight,
            first_gain, first_bias, second_gain, second_bias, cotangent):
    staged = prologue(inputs, segment_ids, qkv_weight, out_weight, gate_weight, up_weight, down_weight,
                      first_gain, first_bias, second_gain, second_bias)
    output, *kept, cos, sin = forward_call(staged)
    gin, gug, dng, af = backward_call(cotangent[0], cos, sin, kept)
    output, gin, *gradients = epilogue(output, gin, gug, dng, af)
    return (output[None], gin[None], *gradients)


IN_SPECS = (
    P(("rep", "shard"), None, None), P(("rep", "shard"), None),
) + (P(None, "shard", None),) * 5 + (P(None, "shard"),) * 4 + (P(("rep", "shard"), None, None),)
OUT_SPECS = (P(("rep", "shard"), None, None),) * 2 + (P(None, "shard", None),) * 5 + (P(None, "shard"),) * 4


def solution(mesh):
    fits = dict(mesh.shape) == {"rep": 2, "shard": 2 * G}
    return jax.shard_map(special if fits else general, mesh=mesh, in_specs=IN_SPECS, out_specs=OUT_SPECS, check_vma=False)
```

```python
import functools
import math

import jax
import jax.numpy as jnp
import numpy as np
from jax import lax
from jax.experimental import pallas as pl
from jax.experimental.pallas import tpu as pltpu
from jax.sharding import PartitionSpec as P

HEADS = 12
HEAD = 64
eps_norm = 1e-12
rope_base = 1000.0
masked_score = -1e30
MESH = pl.DeviceIdType.MESH
BF = jnp.bfloat16
F32 = jnp.float32
T = 256
D = 768
G = 8
QW = 1152
OW = 384
AW = QW + OW + 128
FS = 768
PAIRS = HEADS // 2
HT = T // 2


def part_of(half):
    return pl.ds(half * HT, HT)


def dot(a, b):
    return jnp.dot(a, b, preferred_element_type=F32)


def dot_t(a, b):
    return lax.dot_general(a, b, (((1,), (1,)), ((), ())), preferred_element_type=F32)


def tile(j, width):
    return pl.ds(pl.multiple_of(j * width, width), width)


def chip_rows(g):
    return pl.ds(pl.multiple_of(g * 96, 96), 96)


def shard_rows(g, c):
    return pl.ds(pl.multiple_of(g * 96 + c * 48, 48), 48)


class Place:
    def __init__(self):
        self.y = lax.axis_index("rep")
        s = lax.axis_index("shard")
        self.c, self.x, self.z = s % 2, (s // 2) % 2, s // 4
        self.g = s // 2
        self.slot = 2 * self.y + self.c

    def at(self, y, z, x, c):
        return (y, z * 4 + x * 2 + c)

    def core(self):
        return self.at(self.y, self.z, self.x, 1 - self.c)

    def xside(self):
        return self.at(self.y, self.z, 1 - self.x, self.c)

    def yside(self):
        return self.at(1 - self.y, self.z, self.x, self.c)

    def zside(self, k):
        return self.at(self.y, (self.z + k) % 4, self.x, self.c)

    def zto(self, z):
        return self.at(self.y, z, self.x, self.c)

    def near(self):
        return self.z + 1 - 2 * (self.z % 2)

    def across(self):
        return 3 - self.z

    def source(self, i):
        return (self.near(), 2 - self.z // 2, 3 - 3 * (self.z // 2))[i]

    def chip_from(self, i, x):
        return 2 * (self.z if i is None else self.source(i)) + x

    def chip(self, k, x):
        return 2 * ((self.z + 4 - k) % 4) + x

    def line(self):
        return [self.core(), self.xside(), self.yside(), self.zto(self.near()), self.zto(self.across())]

    def everyone(self):
        return [self.core(), self.xside(), self.yside()] + [self.zside(k) for k in (1, 2, 3)]


def greet(partners):
    barrier = pltpu.get_barrier_semaphore()
    for who in partners:
        pl.semaphore_signal(barrier, inc=1, device_id=who, device_id_type=MESH)
    return lambda: pl.semaphore_wait(barrier, len(partners))


class Mail:
    def __init__(self):
        self.sent = []
        self.some = []

    def send(self, src, dst, send_sem, recv_sem, who, tag=None):
        copy = pltpu.make_async_remote_copy(src, dst, send_sem, recv_sem, device_id=who, device_id_type=MESH)
        copy.start()
        self.sent.append((tag, copy))

    def later(self, src, dst, send_sem, recv_sem, who, cond):
        copy = pltpu.make_async_remote_copy(src, dst, send_sem, recv_sem, device_id=who, device_id_type=MESH)
        self.some.append((cond, copy))
        return copy

    def send_if(self, cond, src, dst, send_sem, recv_sem, who):
        copy = pltpu.make_async_remote_copy(src, dst, send_sem, recv_sem, device_id=who, device_id_type=MESH)
        pl.when(cond)(copy.start)
        self.some.append((cond, copy))

    def local(self, src, dst, sem):
        copy = pltpu.make_async_copy(src, dst, sem)
        copy.start()
        return copy

    def arrive(self, dst, send_sem, recv_sem, who):
        pltpu.make_async_remote_copy(dst, dst, send_sem, recv_sem, device_id=who, device_id_type=MESH).wait_recv()

    def gone(self, tag):
        for t, copy in self.sent:
            if t == tag:
                copy.wait_send()
        self.sent = [(t, copy) for t, copy in self.sent if t != tag]

    def finish(self):
        for _, copy in self.sent:
            copy.wait_send()
        for cond, copy in self.some:
            pl.when(cond)(copy.wait_send)


def swap_halves(v, low_half):
    return jnp.where(low_half, pltpu.roll(v, 96, 1), pltpu.roll(v, 32, 1))


def head_mask(rows, width):
    return lax.broadcasted_iota(jnp.int32, (rows, width), 1) % 128 < HEAD


def forward_kernel(
    x_ref, seg_ref, freq_ref, g1_ref, b1_ref, g2_ref, b2_ref, qkv_ref, outw_ref, gate_ref, up_ref, dn_ref,
    y_ref, A_o, F_o, Q_o, ST_o, P_o, TG_o, TT_o, N_o, I_o, PV_o, cos_ref, sin_ref,
    A, F, Q, ST, Pb, TG, TT, N, I, PV, S, AT, MF, AC, H, bias, FD, RC, RY, W, GU,
    ls, s_gu, r_gu, s_az, r_az, s_ax, r_ax, s_ay, r_ay, s_ac, r_ac, s_ad, r_ad, s_fz, r_fz, s_fx, r_fx, s_fw, r_fw,
    s_m, r_m, s_rc, r_rc, s_ry, r_ry, os,
):
    pc = Place()
    y, z, x, c, g, slot = pc.y, pc.z, pc.x, pc.c, pc.g, pc.slot
    ml = Mail()
    LAY = (0, 1)
    mid = z % 3 != 0
    near, across = pc.zto(pc.near()), pc.zto(pc.across())
    THREE = (0, 1, 2)

    met = greet(pc.line())

    own_a, own_f = [], []
    for l in LAY:
        own_a.append([])
        for h in range(2):
            dst = A.at[l, h, g, c]
            own_a[l].append(ml.local(qkv_ref.at[l, :, pl.ds(QW * h, QW)], dst.at[:, pl.ds(0, QW)], ls.at[l, h]))
            own_a[l].append(ml.local(outw_ref.at[l, :, pl.ds(OW * h, OW)], dst.at[:, pl.ds(QW, OW)], ls.at[l, 2 + h]))
    wide = [ml.local(gate_ref, W.at[0], ls.at[0, 6]), ml.local(up_ref, W.at[1], ls.at[1, 6])]
    for l in LAY:
        own_f.append(ml.local(dn_ref.at[l, pl.ds(pl.multiple_of(y * 96, 96), 96)], F.at[l, chip_rows(g), pl.ds(2 * FS, D)], ls.at[l, 7]))

    def gu_send(l):
        ml.send(GU.at[l, 1 - c, y], F.at[l, shard_rows(g, c), pl.ds(0, 2 * FS)], s_gu.at[l], r_gu.at[l], pc.core())

    def gu_arrive(l):
        ml.arrive(F.at[l, shard_rows(g, 1 - c), pl.ds(0, 2 * FS)], s_gu.at[l], r_gu.at[l], pc.core())

    def line_own(block, ss, rs):
        ml.send(block, block, ss.at[0], rs.at[0], near)
        ml.send_if(mid, block, block, ss.at[1], rs.at[1], across)

    def line_pass(i, block, ss, rs):
        ml.arrive(block, ss.at[0], rs.at[i], near)
        to, at = ((across, 2), (near, 1), (near, 2))[i]
        ml.send_if(mid, block, block, ss.at[2 + i], rs.at[at], to)

    def own_params():
        for l in LAY:
            for h, refs in enumerate(((g1_ref, b1_ref), (g2_ref, b2_ref))):
                two = [ref[l:l + 1, :].astype(F32) for ref in refs]
                rows = jnp.concatenate(two + [jnp.zeros((6, 48), F32)], axis=0).astype(BF)
                wide_rows = lax.dot_general(rows, onehot, (((0,), (0,)), ((), ())), preferred_element_type=F32)
                A[l, h, g, c, :, QW + OW:] = wide_rows.astype(BF)

    def a_own(l):
        for copy in own_a[l]:
            copy.wait()
        block = A.at[l, y, g, c]
        ml.send(block, block, s_ax.at[l, 0], r_ax.at[l, 0], pc.xside())
        line_own(block, s_az.at[l], r_az.at[l])

    def a_z(l, i):
        block = A.at[l, y, pc.chip_from(i, x), c]
        line_pass(i, block, s_az.at[l], r_az.at[l])
        ml.send(block, block, s_ax.at[l, 1 + i], r_ax.at[l, 1 + i], pc.xside())

    def a_yo(l, i):
        block = A.at[l, y, pc.chip_from(i, x), c]
        ml.send(block, block, s_ay.at[l, i], r_ay.at[l, i], pc.yside())

    FOUR = (None, 0, 1, 2)

    def a_x(l, j):
        ml.arrive(A.at[l, y, pc.chip_from(FOUR[j], 1 - x), c], s_ax.at[l, j], r_ax.at[l, j], pc.xside())

    def a_yx(l, j):
        block = A.at[l, y, pc.chip_from(FOUR[j], 1 - x), c]
        ml.send(block, block, s_ay.at[l, 3 + j], r_ay.at[l, 3 + j], pc.yside())

    def a_c(l, h):
        block = A.at[l, h, :, c]
        ml.send(block, block, s_ac.at[l, h], r_ac.at[l, h], pc.core())

    def a_y(l, i, xx, n):
        ml.arrive(A.at[l, 1 - y, pc.chip_from(i, xx), c], s_ay.at[l, n], r_ay.at[l, n], pc.yside())

    def a_c_arrive(l, h):
        ml.arrive(A.at[l, h, :, 1 - c], s_ac.at[l, h], r_ac.at[l, h], pc.core())

    parts = (pl.ds(0, 2 * FS), pl.ds(2 * FS, D))
    ALONG = (1, 1)

    def f_ready(l):
        for w in range(2):
            F[l, shard_rows(g, c), w * FS:w * FS + FS] = GU[l, c, y, :, w * FS:w * FS + FS]
        own_f[l].wait()
        gu_arrive(l)

    def f_own_z(l, p):
        line_own(F.at[l, chip_rows(g), parts[p]], s_fz.at[l, p], r_fz.at[l, p])

    def f_own_x(l, p):
        block = F.at[l, chip_rows(g), parts[p]]
        ml.send(block, block, s_fx.at[l, p, 0], r_fx.at[l, p, 0], pc.xside())

    def f_z(l, p, i):
        block = F.at[l, chip_rows(pc.chip_from(i, x)), parts[p]]
        line_pass(i, block, s_fz.at[l, p], r_fz.at[l, p])
        if (l, p) != ALONG:
            ml.send(block, block, s_fx.at[l, p, 1 + i], r_fx.at[l, p, 1 + i], pc.xside())

    def f_cross():
        l, p = ALONG
        block = F.at[l, chip_rows(pc.chip_from(None, 1 - x)), parts[p]]
        ml.arrive(block, s_fx.at[l, p, 0], r_fx.at[l, p, 0], pc.xside())
        line_own(block, s_fw, r_fw)

    def f_w(i):
        l, p = ALONG
        line_pass(i, F.at[l, chip_rows(pc.chip_from(i, 1 - x)), parts[p]], s_fw, r_fw)

    def f_x(l, p):
        if (l, p) == ALONG:
            return
        for j in range(4):
            ml.arrive(F.at[l, chip_rows(pc.chip_from(FOUR[j], 1 - x)), parts[p]], s_fx.at[l, p, j], r_fx.at[l, p, j], pc.xside())

    out_copies = []

    def save(src, dst):
        out_copies.append(ml.local(src, dst, os.at[len(out_copies)]))

    pair_mask = head_mask(T, 128)
    low_half = lax.broadcasted_iota(jnp.int32, (T, 128), 1) % HEAD < HEAD // 2
    onehot = (lax.broadcasted_iota(jnp.int32, (8, 128), 0) == lax.broadcasted_iota(jnp.int32, (8, 128), 1)).astype(F32).astype(BF)

    def tables():
        wide_row = jnp.broadcast_to(seg_ref[...].astype(F32), (T, T))
        same = wide_row.T == wide_row
        bias[...] = jnp.where(same, 0.0, masked_score)
        at = lax.broadcasted_iota(jnp.int32, (T, T), 1).astype(F32)
        first = jnp.min(jnp.where(same, at, float(T)), axis=1, keepdims=True)
        position = lax.broadcasted_iota(jnp.int32, (T, 128), 0).astype(F32) - first
        angle = position * freq_ref[0:1, :]
        sine = jnp.sin(angle)
        cos_ref[...] = jnp.cos(angle)
        sin_ref[...] = jnp.where(low_half, -sine, sine)

    def permute():
        for copy in wide:
            copy.wait()
        def of(i, carry):
            l, w = i // 2, i % 2
            v = W[w, l]
            for cc in range(2):
                for yy in range(2):
                    pieces = [v[:, 384 * j + 192 * cc + 96 * yy:384 * j + 192 * cc + 96 * yy + 96] for j in range(G)]
                    GU[l, cc, yy, :, tile(w, FS)] = jnp.concatenate(pieces, axis=1)
            return carry
        lax.fori_loop(0, 4, of, 0)

    def project(l):
        st = S[...]
        cos, sin = cos_ref[...], sin_ref[...]
        for j in range(6):
            h, off = j // 3, (j % 3) * 384
            w = A[l, h, :, :, :, off:off + 384].reshape(D, 384)
            r = dot(st, w)
            kind = j // 2
            for t in range(3):
                v = r[:, 128 * t:128 * t + 128]
                if kind < 2:
                    v = v * cos + swap_halves(v, low_half) * sin
                col = (j % 2) * 384 + 128 * t
                Q[l, kind, :, col:col + 128] = v.astype(BF)

    def attention(l):
        def pair(p, carry):
            cols = tile(p, 128)
            q, kk, v = Q[l, 0, :, cols] * jnp.asarray(0.125, BF), Q[l, 1, :, cols], Q[l, 2, :, cols]
            outs = []
            for h in range(2):
                qh = jnp.where(pair_mask == (h == 0), q, jnp.zeros_like(q))
                s = dot_t(qh, kk) + bias[...]
                e = jnp.exp(s - jnp.max(s, axis=1, keepdims=True))
                pr = (e * (1.0 / jnp.sum(e, axis=1, keepdims=True))).astype(BF)
                Pb[l, 2 * p + h] = pr
                outs.append(dot(pr, v))
            AT[:, cols] = jnp.where(pair_mask, outs[0], outs[1]).astype(BF)
            return carry
        def some(p, carry):
            for n in range(3):
                pair(p * 3 + n, carry)
            return carry
        lax.fori_loop(0, PAIRS // 3, some, 0)

    def params(l):
        for h in range(2):
            w = A[l, h, :, :, :, QW + OW:].reshape(D, 128)
            PV[l, h] = dot_t(onehot, w)

    def out_project(l):
        for h in range(2):
            w = A[l, h, :, :, :, QW:QW + OW].reshape(D, OW)
            H[:, h * OW:h * OW + OW] = H[:, h * OW:h * OW + OW] + dot(AT[...], w)

    def norm(l, i, dst, extra, half):
        gain, shift = PV[l, i, 0:1, :], PV[l, i, 1:2, :]
        def rows_of(j, carry):
            rows = tile(j, 32)
            v = H[rows, :]
            if extra is not None:
                v = v + extra(rows)
            cen = v - jnp.mean(v, axis=1, keepdims=True)
            inv = lax.rsqrt(jnp.mean(cen * cen, axis=1, keepdims=True) + eps_norm)
            n = cen * inv
            N[l, i, rows, :] = n
            I[l, i, rows, :] = jnp.broadcast_to(inv, (32, 128))
            m = n * gain + shift
            H[rows, :] = m
            dst[rows, :] = m.astype(BF)
            return carry
        lax.fori_loop(half * (HT // 32), (half + 1) * (HT // 32), rows_of, 0)

    def ffn_up(l, first, toks):
        two, n = pl.ds(first, 2), toks.size
        def cols_of(j, carry):
            cols = tile(j, 256)
            xx = MF[l, two, toks].reshape(2 * n, D)
            gate = dot(xx, F[l, :, cols])
            up = dot(xx, F[l, :, pl.ds(pl.multiple_of(FS + j * 256, 256), 256)])
            act = gate * jax.nn.sigmoid(gate) * up
            TG[l, 0, two, toks, cols] = gate.astype(BF).reshape(2, n, 256)
            TG[l, 1, two, toks, cols] = up.astype(BF).reshape(2, n, 256)
            AC[two, toks, cols] = act.astype(BF).reshape(2, n, 256)
            return carry
        lax.fori_loop(0, FS // 256, cols_of, 0)

    def ffn_down(l, s_, toks, plus=None):
        def cols_of(j, carry):
            cols = tile(j, 256)
            r = dot(AC[s_, toks], F[l, :, pl.ds(pl.multiple_of(2 * FS + j * 256, 256), 256)])
            if plus is not None:
                r = r + plus[toks, cols].astype(F32)
            FD[l, s_, toks, cols] = r.astype(BF)
            return carry
        lax.fori_loop(0, D // 256, cols_of, 0)

    def turn(src, dst, col):
        def tile_of(j, carry):
            cols = tile(j, 128)
            dst[cols, pl.ds(pl.multiple_of(col, T), T)] = src[:, cols].T
            return carry
        lax.fori_loop(0, D // 128, tile_of, 0)

    def turn_slots(src, dst):
        def slot_of(i, carry):
            turn(src.at[i], dst, i * T)
            return carry
        lax.fori_loop(0, 4, slot_of, 0)

    def begin():
        H[...] = x_ref[...].astype(F32)
        S[...] = x_ref[...]
        permute()
        gu_send(0)
        gu_send(1)

    def projected(l):
        params(l)
        project(l)

    def turn_state(l):
        turn(S, ST.at[l, 0], 0)

    def scores(l):
        attention(l)
        save(Pb.at[l], P_o.at[l])
        save(Q.at[l], Q_o.at[l])

    WHOLE = pl.ds(0, T)

    def branch(l):
        out_project(l)

    def first_norm(l, h):
        norm(l, 0, MF.at[l, slot], None, h)
        mine = MF.at[l, slot, part_of(h)]
        ml.send(mine, mine, s_m.at[l, 0, h], r_m.at[l, 0, h], pc.yside())
        ml.send(mine, mine, s_m.at[l, 1, h], r_m.at[l, 1, h], pc.core())

    def turn_attended(l):
        turn(AT, ST.at[l, 1], 0)
        save(ST.at[l], ST_o.at[l])

    def own_up(l):
        for h in range(2):
            ml.arrive(MF.at[l, 2 * y + 1 - c, part_of(h)], s_m.at[l, 1, h], r_m.at[l, 1, h], pc.core())
        f_x(l, 0)
        ffn_up(l, 2 * y, WHOLE)

    def own_down(l):
        f_x(l, 1)
        s_ = 2 * y + 1 - c
        ffn_down(l, s_, WHOLE)
        ml.send(FD.at[l, s_], RC.at[l, y], s_rc.at[l, 2], r_rc.at[l, 2], pc.core())
        ffn_down(l, slot, WHOLE)
        save(F.at[l], F_o.at[l])

    def pass_on(l, h):
        block = MF.at[l, 2 * (1 - y) + c, part_of(h)]
        ml.arrive(block, s_m.at[l, 0, h], r_m.at[l, 0, h], pc.yside())
        ml.send(block, block, s_m.at[l, 2, h], r_m.at[l, 2, h], pc.core())

    def other_up(l, h):
        others = 2 * (1 - y)
        ml.arrive(MF.at[l, others + 1 - c, part_of(h)], s_m.at[l, 2, h], r_m.at[l, 2, h], pc.core())
        ffn_up(l, others, part_of(h))

    def other_down(l, h):
        s_ = 2 * (1 - y) + 1 - c
        ffn_down(l, s_, part_of(h))
        ml.send(FD.at[l, s_, part_of(h)], RC.at[l, 1 - y, part_of(h)], s_rc.at[l, h], r_rc.at[l, h], pc.core())

    def other_sum(l, h):
        s_ = 2 * (1 - y) + c
        ml.arrive(RC.at[l, 1 - y, part_of(h)], s_rc.at[l, h], r_rc.at[l, h], pc.core())
        ffn_down(l, s_, part_of(h), RC.at[l, 1 - y])
        ml.send(FD.at[l, s_, part_of(h)], RY.at[l, part_of(h)], s_ry.at[l, h], r_ry.at[l, h], pc.yside())

    def turn_middle(l):
        turn_slots(MF.at[l], TT.at[l, 0])
        save(TG.at[l], TG_o.at[l])
        save(TT.at[l, 0], TT_o.at[l, 0])

    def turn_activated(l):
        turn_slots(AC, TT.at[l, 1])
        save(TT.at[l, 1], TT_o.at[l, 1])

    def second_norm(l, h):
        if h == 0:
            ml.arrive(RC.at[l, y], s_rc.at[l, 2], r_rc.at[l, 2], pc.core())
        ml.arrive(RY.at[l, part_of(h)], s_ry.at[l, h], r_ry.at[l, h], pc.yside())
        feed = lambda rows: FD[l, slot, rows, :].astype(F32) + RC[l, y, rows, :].astype(F32) + RY[l, rows, :].astype(F32)
        norm(l, 1, S if l == 0 else y_ref, feed, h)

    def other_block(l, n, cc):
        at = g if n == 7 else pc.chip_from(n, x) if n < 3 else pc.chip_from(FOUR[n - 3], 1 - x)
        return A.at[l, 1 - y, at, cc]

    def to_other_core(l, n):
        block = other_block(l, n, c)
        ml.send(block, block, s_ad.at[l, n], r_ad.at[l, n], pc.core())

    def ay_arrive(l, n):
        ml.arrive(other_block(l, n, c), s_ay.at[l, n], r_ay.at[l, n], pc.yside())
        to_other_core(l, n)

    def ac_own(l):
        a_c(l, y)

    def ac_other(l):
        to_other_core(l, 7)

    def attn_ready(l):
        a_c_arrive(l, y)
        for n in (7, 0, 1, 2, 3, 4, 5, 6):
            ml.arrive(other_block(l, n, 1 - c), s_ad.at[l, n], r_ad.at[l, n], pc.core())
        save(A.at[l], A_o.at[l])

    own_params()
    met()
    a_own(0)
    a_own(1)
    begin()
    a_x(0, 0)
    a_z(0, 0)
    a_yx(0, 0)
    ac_other(1)
    a_yo(0, 0)
    a_z(0, 1)
    a_z(1, 0)
    a_z(1, 1)
    a_z(0, 2)
    a_yo(0, 1)
    a_x(0, 1)
    a_yo(1, 0)
    a_x(1, 0)
    f_ready(1)
    f_ready(0)
    a_yo(1, 1)
    f_own_z(0, 0)
    a_x(0, 2)
    ay_arrive(0, 0)
    a_yx(0, 1)
    f_own_x(0, 1)
    a_z(1, 2)
    f_own_x(0, 0)
    f_own_z(1, 1)
    a_yo(0, 2)
    turn_state(0)
    a_yx(0, 2)
    f_own_z(0, 1)
    a_x(0, 3)
    a_x(1, 1)
    ac_own(0)
    f_z(0, 0, 0)
    a_yx(0, 3)
    f_z(0, 0, 1)
    a_yo(1, 2)
    ay_arrive(0, 1)
    ay_arrive(0, 2)
    ay_arrive(0, 3)
    tables()
    ay_arrive(0, 4)
    a_x(1, 2)
    ac_other(0)
    a_yx(1, 0)
    ay_arrive(0, 5)
    f_z(1, 1, 0)
    ay_arrive(0, 6)
    ay_arrive(1, 0)
    attn_ready(0)
    f_z(1, 1, 1)
    a_yx(1, 1)
    projected(0)
    a_yx(1, 2)
    f_z(0, 0, 2)
    f_own_z(1, 0)
    ay_arrive(1, 1)
    ay_arrive(1, 2)
    f_z(0, 1, 0)
    scores(0)
    branch(0)
    a_x(1, 3)
    first_norm(0, 0)
    f_z(0, 1, 1)
    ac_own(1)
    first_norm(0, 1)
    turn_attended(0)
    pass_on(0, 0)
    ay_arrive(1, 3)
    f_z(0, 1, 2)
    ay_arrive(1, 4)
    a_yx(1, 3)
    f_own_x(1, 1)
    own_up(0)
    other_up(0, 0)
    f_z(1, 0, 0)
    ay_arrive(1, 5)
    pass_on(0, 1)
    f_z(1, 0, 1)
    other_up(0, 1)
    own_down(0)
    other_down(0, 0)
    f_z(1, 1, 2)
    ay_arrive(1, 6)
    other_down(0, 1)
    other_sum(0, 0)
    f_own_x(1, 0)
    f_cross()
    other_sum(0, 1)
    turn_middle(0)
    attn_ready(1)
    f_z(1, 0, 2)
    second_norm(0, 0)
    f_w(0)
    second_norm(0, 1)
    projected(1)
    scores(1)
    branch(1)
    first_norm(1, 0)
    f_w(1)
    first_norm(1, 1)
    turn_activated(0)
    f_w(2)
    own_up(1)
    pass_on(1, 0)
    own_down(1)
    other_up(1, 0)
    other_down(1, 0)
    pass_on(1, 1)
    turn_state(1)
    other_sum(1, 0)
    other_up(1, 1)
    other_down(1, 1)
    turn_attended(1)
    other_sum(1, 1)
    turn_middle(1)
    second_norm(1, 0)
    turn_activated(1)
    second_norm(1, 1)
    for src, dst in ((N, N_o), (I, I_o), (PV, PV_o)):
        save(src, dst)
    for copy in out_copies:
        copy.wait()
    ml.finish()


FWD_SHAPES = [
    ((2, 2, G, 2, 48, AW), BF),
    ((2, D, 2 * FS + D), BF),
    ((2, 3, T, D), BF),
    ((2, 2, D, T), BF),
    ((2, HEADS, T, T), BF),
    ((2, 2, 4, T, FS), BF),
    ((2, 2, D, 4 * T), BF),
    ((2, 2, T, D), F32),
    ((2, 2, T, 128), F32),
    ((2, 2, 8, D), F32),
]


def sems(*shape):
    return pltpu.SemaphoreType.DMA(shape)


def forward_call(args):
    any_spec = pl.BlockSpec(memory_space=pl.ANY)
    vm = pl.BlockSpec(memory_space=pltpu.VMEM)
    return pl.pallas_call(
        forward_kernel,
        out_shape=[jax.ShapeDtypeStruct((T, D), BF)]
        + [jax.ShapeDtypeStruct(s, d) for s, d in FWD_SHAPES]
        + [jax.ShapeDtypeStruct((T, 128), F32)] * 2,
        in_specs=[vm] * 7 + [any_spec] * 5,
        out_specs=[vm] + [any_spec] * len(FWD_SHAPES) + [vm] * 2,
        scratch_shapes=[pltpu.VMEM(s, d) for s, d in FWD_SHAPES]
        + [
            pltpu.VMEM((T, D), BF),
            pltpu.VMEM((T, D), BF),
            pltpu.VMEM((2, 4, T, D), BF),
            pltpu.VMEM((4, T, FS), BF),
            pltpu.VMEM((T, D), F32),
            pltpu.VMEM((T, T), F32),
            pltpu.VMEM((2, 4, T, D), BF),
            pltpu.VMEM((2, 2, T, D), BF),
            pltpu.VMEM((2, T, D), BF),
            pltpu.VMEM((2, 2, 48, 4 * FS), BF),
            pltpu.VMEM((2, 2, 2, 48, 2 * FS), BF),
            sems(2, 8),
            sems(2), sems(2),
            sems(2, 5), sems(2, 3),
            sems(2, 4), sems(2, 4),
            sems(2, 7), sems(2, 7),
            sems(2, 2), sems(2, 2),
            sems(2, 8), sems(2, 8),
            sems(2, 2, 5), sems(2, 2, 3),
            sems(2, 2, 4), sems(2, 2, 4),
            sems(5), sems(3),
            sems(2, 3, 2), sems(2, 3, 2),
            sems(2, 3), sems(2, 3),
            sems(2, 2), sems(2, 2),
            sems(19),
        ],
        compiler_params=pltpu.CompilerParams(collective_id=0, has_side_effects=True, vmem_limit_bytes=60 * 2**20),
        cost_estimate=pl.CostEstimate(flops=10**10, bytes_accessed=10**8, transcendentals=0),
        name="forward",
    )(*args)


def backward_kernel(
    cot_ref, cos_ref, sin_ref, A_i, F_i, Q_i, ST_i, P_i, TG_i, TT_i, N_i, I_i, PV_i,
    gin_ref, GUG, DNG, AF,
    A, F, Q, ST, Pb, TG, TT, N, I, PV,
    U, GF, GB, GP, FD, RC, RY, FG, RFX, RFZ, FR, AG, RAC, RAY, RAX, RAZ, RO, OX, OR, OT, OY, V,
    ls, s_m, r_m, s_rc, r_rc, s_ry, r_ry,
    s_fx, r_fx, s_fz, r_fz, s_fc, r_fc, s_fy, r_fy,
    s_ac, r_ac, s_ay, r_ay, s_ax, r_ax, s_az, r_az, s_af, r_af, s_oz, r_oz, s_ox, r_ox, s_oy, r_oy,
):
    pc = Place()
    y, z, x, c, slot = pc.y, pc.z, pc.x, pc.c, pc.slot
    ml = Mail()
    mid = z % 3 != 0
    zn = pc.near()
    near, across = pc.zto(zn), pc.zto(3 - z)
    planes = (3 - zn, 3 - z, zn, z)
    places = {
        "PV": (PV_i, PV, 0), "N": (N_i, N, 1), "I": (I_i, I, 2), "TT": (TT_i, TT, 3), "F": (F_i, F, 4), "TG": (TG_i, TG, 5),
        "ST": (ST_i, ST, 6), "A": (A_i, A, 7), "P": (P_i, Pb, 8), "Q": (Q_i, Q, 9),
    }
    loading = {}

    def load(l, *names):
        for name in names:
            src, dst, i = places[name]
            loading[name] = ml.local(src.at[l], dst, ls.at[i])

    def need(*names):
        for name in names:
            if name in loading:
                loading.pop(name).wait()

    met = greet(pc.line())
    load(1, "PV", "N", "I", "F", "TG", "TT", "ST", "A", "P", "Q")
    U[...] = cot_ref[...].astype(F32)

    fcols = (pl.ds(2 * FS, D), pl.ds(0, FS), pl.ds(FS, FS))

    def fx_send(l, j):
        for n in range(4):
            ml.send(FG.at[planes[n], 1 - x, :, fcols[j]], RFX.at[l, j, planes[n]], s_fx.at[l, j, n], r_fx.at[l, j, n], pc.xside(), ("fx", l, j))

    def line_start(n, part, R, ss, rs):
        slot_of = (1, 2, 0)[n]
        ml.send_if(z % 3 == 0, part(planes[n]), R.at[slot_of], ss.at[n], rs.at[slot_of], near)

    def plus(dst, src, rows, widths):
        for r in range(0, rows, 48):
            at = 0
            for w in widths:
                here = (pl.ds(r, 48), pl.ds(at, w))
                dst[here] = (dst[here].astype(F32) + src[here].astype(F32)).astype(BF)
                at += w

    def line_middle(part, R, ss, rs, add):
        far = [pltpu.make_async_remote_copy(R.at[n], R.at[n], ss.at[0], rs.at[n], device_id=near, device_id_type=MESH) for n in (1, 2)]
        on = [
            ml.later(part(plane), R.at[3 + n], ss.at[3 + n], rs.at[3 + n], across, mid)
            for n, plane in enumerate((3 - z, 3 - zn))
        ]
        dsts = [part(3 - z), part(3 - zn)]
        def go():
            for n in range(2):
                far[n].wait_recv()
                add(dsts[n], R.at[1 + n])
                on[n].start()
        pl.when(mid)(go)

    def line_end(part, R, ss, rs, add):
        back = [pltpu.make_async_remote_copy(R.at[n], R.at[n], ss.at[0], rs.at[n], device_id=across, device_id_type=MESH) for n in (3, 4)]
        last = ml.later(part(zn), R.at[0], ss.at[5], rs.at[0], near, mid)
        dsts = [part(z), part(zn)]
        def go():
            back[1].wait_recv()
            add(dsts[1], R.at[4])
            last.start()
            back[0].wait_recv()
            add(dsts[0], R.at[3])
        pl.when(mid)(go)
        ml.arrive(R.at[0], ss.at[0], rs.at[0], near)

    def add_f(dst, src):
        plus(dst, src, 96, (D,))

    def add_a(dst, src):
        plus(dst, src, 48, awide[0])

    def add_o(dst, src):
        for i in range(2):
            for xx in range(2):
                plus(dst.at[i, xx], src.at[i, xx], 48, awide[1])

    def fpart(l, j):
        return lambda zz: RFX.at[l, j, zz]

    def fx_task(l, j, n):
        if True:
            p = planes[n]
            ml.arrive(RFX.at[l, j, p], s_fx.at[l, j, n], r_fx.at[l, j, n], pc.xside())
            for half in range(2):
                rows = pl.ds(48 * half, 48)
                RFX[l, j, p, rows, :] = (RFX[l, j, p, rows, :].astype(F32) + FG[p, x, rows, fcols[j]].astype(F32)).astype(BF)
            if n < 3:
                line_start(n, fpart(l, j), RFZ.at[l, j], s_fz.at[l, j], r_fz.at[l, j])

    def fm_task(l, j):
        line_middle(fpart(l, j), RFZ.at[l, j], s_fz.at[l, j], r_fz.at[l, j], add_f)

    def fz_task(l, j):
        line_end(fpart(l, j), RFZ.at[l, j], s_fz.at[l, j], r_fz.at[l, j], add_f)
        def total(start):
            rows = pl.ds(start, 48)
            return (RFX[l, j, z, rows, :].astype(F32) + RFZ[l, j, 0, rows, :].astype(F32)).astype(BF)
        if j == 0:
            for half in range(2):
                DNG[l, y, pl.ds(48 * half, 48), :] = total(48 * half)
            ml.send(DNG.at[l, y], DNG.at[l, y], s_fy.at[l, 0], r_fy.at[l, 0], pc.yside())
        else:
            FR[l, j - 1] = total(pl.multiple_of((1 - c) * 48, 48))
            ml.send(FR.at[l, j - 1], GUG.at[l, j - 1, c, y], s_fc.at[l, j], r_fc.at[l, j], pc.core())
            GUG[l, j - 1, c, y] = total(pl.multiple_of(c * 48, 48))

    def fc_task(l, j):
        ml.arrive(GUG.at[l, j - 1, 1 - c, y], s_fc.at[l, j], r_fc.at[l, j], pc.core())
        block = GUG.at[l, j - 1, :, y]
        ml.send(block, block, s_fy.at[l, j], r_fy.at[l, j], pc.yside())

    def fy_task(l, j):
        block = DNG.at[l, 1 - y] if j == 0 else GUG.at[l, j - 1, :, 1 - y]
        ml.arrive(block, s_fy.at[l, j], r_fy.at[l, j], pc.yside())

    acols = (pl.ds(0, QW), pl.ds(QW, AW - QW))
    awide = ((768, 384), (512,))

    def ac_send(l, p, i):
        h = (1 - y, y)[i]
        ml.send(AG.at[h, :, :, 1 - c, :, acols[p]], RAC.at[l, i, :, :, :, acols[p]], s_ac.at[l, p, i], r_ac.at[l, p, i], pc.core(), ("ac", l))

    def ac_sum(l, p, i):
        h = (1 - y, y)[i]
        ml.arrive(RAC.at[l, i, :, :, :, acols[p]], s_ac.at[l, p, i], r_ac.at[l, p, i], pc.core())
        def add(n, carry):
            zz, xx = n // 2, n % 2
            plus(RAC.at[l, i, zz, xx, :, acols[p]], AG.at[h, zz, xx, c, :, acols[p]], 48, awide[p])
            return carry
        lax.fori_loop(0, 8, add, 0)

    def ay_send(l, p, n):
        q = planes[n]
        ml.send(RAC.at[l, 0, q, :, :, acols[p]], RAY.at[l, q], s_ay.at[l, p, n], r_ay.at[l, p, n], pc.yside())

    def ay_task(l, p, n):
        q = planes[n]
        ml.arrive(RAY.at[l, q], s_ay.at[l, p, n], r_ay.at[l, p, n], pc.yside())
        for xx in range(2):
            plus(RAC.at[l, 1, q, xx, :, acols[p]], RAY.at[l, q, xx], 48, awide[p])
        ml.send(RAC.at[l, 1, q, 1 - x, :, acols[p]], RAX.at[l, q], s_ax.at[l, p, n], r_ax.at[l, p, n], pc.xside())

    def apart(l, p):
        return lambda zz: RAX.at[l, zz]

    def ax_task(l, p, n):
        q = planes[n]
        ml.arrive(RAX.at[l, q], s_ax.at[l, p, n], r_ax.at[l, p, n], pc.xside())
        plus(RAX.at[l, q], RAC.at[l, 1, q, x, :, acols[p]], 48, awide[p])
        if n < 3:
            line_start(n, apart(l, p), RAZ.at[l], s_az.at[l, p], r_az.at[l, p])

    def am_task(l, p):
        line_middle(apart(l, p), RAZ.at[l], s_az.at[l, p], r_az.at[l, p], add_a)

    def az_task(l, p):
        line_end(apart(l, p), RAZ.at[l], s_az.at[l, p], r_az.at[l, p], add_a)
        mine = AF.at[l, y, :, acols[p]]
        mine[...] = (RAX[l, z].astype(F32) + RAZ[l, 0].astype(F32)).astype(BF)
        ml.send(mine, mine, s_af.at[l, p], r_af.at[l, p], pc.yside())

    def af_task(l, p):
        ml.arrive(AF.at[l, 1 - y, :, acols[p]], s_af.at[l, p], r_af.at[l, p], pc.yside())

    def opart(l):
        return lambda zz: RAC.at[l, :, zz, :, :, acols[1]]

    def o_start(l):
        for n in range(3):
            line_start(n, opart(l), RO.at[l], s_oz.at[l], r_oz.at[l])

    def om_task(l):
        line_middle(opart(l), RO.at[l], s_oz.at[l], r_oz.at[l], add_o)

    def oz_task(l):
        line_end(opart(l), RO.at[l], s_oz.at[l], r_oz.at[l], add_o)
        for i, h in ((0, 1 - y), (1, y)):
            both = lambda xx: (RAC[l, i, z, xx, :, acols[1]].astype(F32) + RO[l, 0, i, xx].astype(F32)).astype(BF)
            OX[l, h] = both(1 - x)
            OT[l, h] = both(x)
        ml.send(OX.at[l], OR.at[l], s_ox.at[l], r_ox.at[l], pc.xside())

    def ox_task(l):
        ml.arrive(OR.at[l], s_ox.at[l], r_ox.at[l], pc.xside())
        for h in range(2):
            plus(OT.at[l, h], OR.at[l, h], 48, awide[1])
        ml.send(OT.at[l], OY.at[l], s_oy.at[l], r_oy.at[l], pc.yside())

    def oy_task(l):
        ml.arrive(OY.at[l], s_oy.at[l], r_oy.at[l], pc.yside())
        for h in range(2):
            AF[l, h, :, acols[1]] = (OT[l, h].astype(F32) + OY[l, h].astype(F32)).astype(BF)

    pair_mask = head_mask(T, 128)
    low_half = lax.broadcasted_iota(jnp.int32, (T, 128), 1) % HEAD < HEAD // 2
    onehot = (lax.broadcasted_iota(jnp.int32, (8, 128), 0) == lax.broadcasted_iota(jnp.int32, (8, 128), 1)).astype(F32).astype(BF)

    def norm_back(i, extra, dst, half):
        gain = PV[i, 0:1, :]
        def rows_of(j, carry):
            gs, bs = carry
            rows = tile(j, 32)
            u = U[rows, :]
            if extra is not None:
                u = u + extra(rows)
            n = N[i, rows, :]
            un = u * n
            gs = gs + un.reshape(4, 8, D).sum(0)
            bs = bs + u.reshape(4, 8, D).sum(0)
            m1 = jnp.mean(u * gain, axis=1, keepdims=True)
            m2 = jnp.mean(un * gain, axis=1, keepdims=True)
            r = I[i, rows, 0:1] * (u * gain - m1 - n * m2)
            U[rows, :] = r
            dst[rows, :] = r.astype(BF)
            return gs, bs
        zero = jnp.zeros((8, D), F32)
        gs, bs = lax.fori_loop(half * (HT // 32), (half + 1) * (HT // 32), rows_of, (zero, zero))
        row = lax.broadcasted_iota(jnp.int32, (8, D), 0)
        sums = jnp.where(row == 0, gs.sum(0, keepdims=True), jnp.where(row == 1, bs.sum(0, keepdims=True), 0.0))
        V[i] = sums if half == 0 else V[i] + sums

    def act_back(l, first, toks):
        two, n = pl.ds(first, 2), toks.size
        def cols_of(j, carry):
            cols = tile(j, 256)
            ga = dot_t(GF[l, two, toks].reshape(2 * n, D), F[cols, 2 * FS:])
            gate = TG[0, two, toks, cols].reshape(2 * n, 256).astype(F32)
            up = TG[1, two, toks, cols].reshape(2 * n, 256).astype(F32)
            sg = jax.nn.sigmoid(gate)
            gg = ga * up * sg * (1.0 + gate * (1.0 - sg))
            gu = ga * gate * sg
            TG[0, two, toks, cols] = gg.astype(BF).reshape(2, n, 256)
            TG[1, two, toks, cols] = gu.astype(BF).reshape(2, n, 256)
            return carry
        lax.fori_loop(0, FS // 256, cols_of, 0)

    def mid_back(s_, toks, plus=None):
        def cols_of(j, carry):
            cols = tile(j, 256)
            r = dot_t(TG[0, s_, toks], F[cols, 0:FS]) + dot_t(TG[1, s_, toks], F[cols, FS:2 * FS])
            if plus is not None:
                r = r + plus[toks, cols].astype(F32)
            FD[s_, toks, cols] = r.astype(BF)
            return carry
        lax.fori_loop(0, D // 256, cols_of, 0)

    def weight_grad(l, j):
        def cols_of(n, carry):
            cols = tile(n, 256)
            if j == 0:
                right = GF[l, :, :, cols].reshape(4 * T, 256)
            else:
                right = TG[j - 1, :, :, cols].reshape(4 * T, 256)
            r = dot(TT[0 if j else 1], right)
            off = (2 * FS, 0, FS)[j]
            FG[:, :, :, pl.ds(pl.multiple_of(off + n * 256, 256), 256)] = r.astype(BF).reshape(4, 2, 96, 256)
            return carry
        lax.fori_loop(0, 3, cols_of, 0)

    def out_back():
        acc = None
        for h in range(2):
            r = dot(ST[1], GB[:, h * OW:h * OW + OW])
            AG[h, :, :, :, :, QW:QW + OW] = r.astype(BF).reshape(4, 2, 2, 48, OW)
        for h in range(2):
            t = dot_t(GB[:, h * OW:h * OW + OW], A[h, :, :, :, QW:QW + OW].reshape(D, OW))
            acc = t if acc is None else acc + t
        GP[2] = acc.astype(BF)

    def attention_back():
        def pair(p, carry):
            cols = tile(p, 128)
            q, kk, v, ga = Q[0, :, cols], Q[1, :, cols], Q[2, :, cols], GP[2, :, cols]
            dq, dk, dv = [], [], []
            for h in range(2):
                pl_ = Pb[2 * p + h]
                pr = pl_.astype(F32)
                gh = jnp.where(pair_mask == (h == 0), ga, jnp.zeros_like(ga))
                dp = dot_t(gh, v)
                ds = (pr * (dp - jnp.sum(dp * pr, axis=1, keepdims=True))).astype(BF)
                dq.append(dot(ds, kk))
                dk.append(dot(ds.T, q))
                dv.append(dot(pl_.T, ga))
            cos, sin = cos_ref[...], sin_ref[...]
            def back(pair_of):
                m = jnp.where(pair_mask, pair_of[0], pair_of[1]) * 0.125
                return (m * cos - swap_halves(m, low_half) * sin).astype(BF)
            GP[0, :, cols] = back(dq)
            GP[1, :, cols] = back(dk)
            GP[2, :, cols] = jnp.where(pair_mask, dv[0], dv[1]).astype(BF)
            return carry
        def some(p, carry):
            for n in range(3):
                pair(p * 3 + n, carry)
            return carry
        lax.fori_loop(0, PAIRS // 3, some, 0)

    def gp_chunk(j):
        return GP[j // 2, :, (j % 2) * 384:(j % 2) * 384 + 384]

    def qkv_grad(h):
        for j in range(3 * h, 3 * h + 3):
            off = (j % 3) * 384
            r = dot(ST[0], gp_chunk(j))
            AG[h, :, :, :, :, off:off + 384] = r.astype(BF).reshape(4, 2, 2, 48, 384)

    def param_grad():
        for h in range(2):
            r = lax.dot_general(V[h].astype(BF), onehot, (((0,), (0,)), ((), ())), preferred_element_type=F32)
            AG[h, :, :, :, :, QW + OW:] = r.astype(BF).reshape(4, 2, 2, 48, 128)

    def input_back():
        acc = U[...]
        for j in range(6):
            off = (j % 3) * 384
            acc = acc + dot_t(gp_chunk(j), A[j // 3, :, :, :, off:off + 384].reshape(D, 384))
        U[...] = acc

    def run(steps):
        for step, *what in steps:
            step(*what)

    WHOLE = pl.ds(0, T)

    def upper(l, h):
        need("PV", "N", "I")
        norm_back(1, None, GF.at[l, slot], h)
        if l == 1 and h == 0:
            met()
        mine = GF.at[l, slot, part_of(h)]
        ml.send(mine, mine, s_m.at[l, 0, h], r_m.at[l, 0, h], pc.yside())
        ml.send(mine, mine, s_m.at[l, 1, h], r_m.at[l, 1, h], pc.core())

    def own_tokens(l):
        need("F", "TG")
        ml.gone(("fd", 1))
        for h in range(2):
            ml.arrive(GF.at[l, 2 * y + 1 - c, part_of(h)], s_m.at[l, 1, h], r_m.at[l, 1, h], pc.core())
        act_back(l, 2 * y, WHOLE)
        s_ = 2 * y + 1 - c
        mid_back(s_, WHOLE)
        ml.send(FD.at[s_], RC.at[y], s_rc.at[l, 2], r_rc.at[l, 2], pc.core(), ("fd", l))
        mid_back(slot, WHOLE)

    def pass_on(l, h):
        block = GF.at[l, 2 * (1 - y) + c, part_of(h)]
        ml.arrive(block, s_m.at[l, 0, h], r_m.at[l, 0, h], pc.yside())
        ml.send(block, block, s_m.at[l, 2, h], r_m.at[l, 2, h], pc.core())

    def other_tokens(l, h):
        others = 2 * (1 - y)
        ml.arrive(GF.at[l, others + 1 - c, part_of(h)], s_m.at[l, 2, h], r_m.at[l, 2, h], pc.core())
        act_back(l, others, part_of(h))

    def other_mids(l, h):
        s_ = 2 * (1 - y) + 1 - c
        mid_back(s_, part_of(h))
        ml.send(FD.at[s_, part_of(h)], RC.at[1 - y, part_of(h)], s_rc.at[l, h], r_rc.at[l, h], pc.core(), ("fd", l))

    def other_sums(l, h):
        s_ = 2 * (1 - y) + c
        ml.arrive(RC.at[1 - y, part_of(h)], s_rc.at[l, h], r_rc.at[l, h], pc.core())
        mid_back(s_, part_of(h), RC.at[1 - y])
        ml.send(FD.at[s_, part_of(h)], RY.at[part_of(h)], s_ry.at[l, h], r_ry.at[l, h], pc.yside(), ("fd", l))
        if l == 1 and h == 1:
            load(0, "F")

    def weights(l, j):
        need("TT")
        ml.gone(("fx", 1, j) if l == 0 else None)
        weight_grad(l, j)
        fx_send(l, j)
        if l == 1 and j == 2:
            load(0, "TT", "TG")

    def middle(l, h):
        if h == 0:
            ml.arrive(RC.at[y], s_rc.at[l, 2], r_rc.at[l, 2], pc.core())
        ml.arrive(RY.at[part_of(h)], s_ry.at[l, h], r_ry.at[l, h], pc.yside())
        norm_back(0, lambda rows: FD[slot, rows, :].astype(F32) + RC[y, rows, :].astype(F32) + RY[rows, :].astype(F32), GB, h)
        if l == 1 and h == 1:
            load(0, "PV", "N", "I")

    QKV, OUT = 0, 1

    def out_sums(l):
        need("ST", "A")
        if l == 0:
            ml.gone(("ac", 1))
        param_grad()
        out_back()
        for i in range(2):
            ac_send(l, OUT, i)

    def scores(l):
        need("P", "Q")
        attention_back()
        if l == 1:
            load(0, "P", "Q")

    def below(l):
        input_back()
        if l == 0:
            gin_ref[...] = U[...]

    def qkv_sums(l):
        qkv_grad(0)
        qkv_grad(1)
        for i in range(2):
            ac_send(l, QKV, i)
        if l == 1:
            load(0, "ST", "A")

    upper(1, 0)
    upper(1, 1)
    own_tokens(1)
    pass_on(1, 0)
    other_tokens(1, 0)
    other_mids(1, 0)
    pass_on(1, 1)
    other_sums(1, 0)
    other_tokens(1, 1)
    weights(1, 0)
    other_mids(1, 1)
    weights(1, 1)
    other_sums(1, 1)
    fx_task(1, 0, 0)
    middle(1, 0)
    weights(1, 2)
    fx_task(1, 0, 1)
    middle(1, 1)
    out_sums(1)
    fx_task(1, 0, 2)
    ac_sum(1, 1, 0)
    ac_sum(1, 1, 1)
    o_start(1)
    scores(1)
    below(1)
    upper(0, 0)
    fx_task(1, 1, 0)
    upper(0, 1)
    fx_task(1, 1, 1)
    qkv_sums(1)
    om_task(1)
    fm_task(1, 0)
    own_tokens(0)
    pass_on(0, 0)
    fx_task(1, 0, 3)
    ac_sum(1, 0, 1)
    ac_sum(1, 0, 0)
    fx_task(1, 1, 2)
    other_tokens(0, 0)
    ay_send(1, 0, 0)
    pass_on(0, 1)
    other_mids(0, 0)
    fx_task(1, 2, 0)
    other_tokens(0, 1)
    other_sums(0, 0)
    weights(0, 0)
    fx_task(1, 2, 1)
    fx_task(1, 2, 2)
    other_mids(0, 1)
    fx_task(1, 1, 3)
    other_sums(0, 1)
    fx_task(0, 0, 0)
    weights(0, 1)
    fm_task(1, 1)
    ay_send(1, 0, 1)
    middle(0, 0)
    ay_send(1, 0, 2)
    ay_task(1, 0, 0)
    middle(0, 1)
    ay_send(1, 0, 3)
    fm_task(1, 2)
    fx_task(0, 0, 1)
    out_sums(0)
    fx_task(0, 0, 2)
    scores(0)
    fx_task(0, 1, 0)
    qkv_sums(0)
    fx_task(0, 1, 1)
    fm_task(0, 0)
    ac_sum(0, 1, 0)
    ac_sum(0, 0, 0)
    ay_send(0, 0, 0)
    ay_task(1, 0, 1)
    fx_task(1, 2, 3)
    ac_sum(0, 1, 1)
    o_start(0)
    weights(0, 2)
    ay_send(0, 0, 1)
    fx_task(0, 1, 2)
    fm_task(0, 1)
    fz_task(1, 1)
    ay_send(0, 0, 2)
    oz_task(1)
    fc_task(1, 1)
    fx_task(0, 1, 3)
    ac_sum(0, 0, 1)
    fz_task(1, 2)
    fx_task(0, 0, 3)
    om_task(0)
    ax_task(1, 0, 0)
    ay_task(0, 0, 0)
    fx_task(0, 2, 0)
    fz_task(1, 0)
    fx_task(0, 2, 1)
    fz_task(0, 0)
    below(0)
    ay_task(0, 0, 1)
    fx_task(0, 2, 2)
    ax_task(1, 0, 1)
    ay_send(0, 0, 3)
    ay_task(1, 0, 2)
    fc_task(1, 2)
    oz_task(0)
    ox_task(1)
    ay_task(0, 0, 2)
    ay_task(1, 0, 3)
    fm_task(0, 2)
    ax_task(0, 0, 0)
    fx_task(0, 2, 3)
    fz_task(0, 1)
    ax_task(0, 0, 1)
    am_task(1, 0)
    fc_task(0, 1)
    ox_task(0)
    ax_task(1, 0, 2)
    fz_task(0, 2)
    ay_task(0, 0, 3)
    am_task(0, 0)
    ax_task(1, 0, 3)
    fc_task(0, 2)
    ax_task(0, 0, 2)
    az_task(1, 0)
    ax_task(0, 0, 3)
    az_task(0, 0)
    for l in (1, 0):
        for j in range(3):
            fy_task(l, j)
        af_task(l, 0)
        oy_task(l)
    ml.finish()


def backward_call(cot, cos, sin, kept):
    any_spec = pl.BlockSpec(memory_space=pl.ANY)
    vm = pl.BlockSpec(memory_space=pltpu.VMEM)
    return pl.pallas_call(
        backward_kernel,
        out_shape=[
            jax.ShapeDtypeStruct((T, D), F32),
            jax.ShapeDtypeStruct((2, 2, 2, 2, 48, FS), BF),
            jax.ShapeDtypeStruct((2, 2, 96, D), BF),
            jax.ShapeDtypeStruct((2, 2, 48, AW), BF),
        ],
        in_specs=[vm] * 3 + [any_spec] * len(kept),
        out_specs=[vm] * 4,
        scratch_shapes=[pltpu.VMEM(s[1:], d) for s, d in FWD_SHAPES]
        + [
            pltpu.VMEM((T, D), F32),
            pltpu.VMEM((2, 4, T, D), BF),
            pltpu.VMEM((T, D), BF),
            pltpu.VMEM((3, T, D), BF),
            pltpu.VMEM((4, T, D), BF),
            pltpu.VMEM((2, T, D), BF),
            pltpu.VMEM((T, D), BF),
            pltpu.VMEM((4, 2, 96, 2 * FS + D), BF),
            pltpu.VMEM((2, 3, 4, 96, D), BF),
            pltpu.VMEM((2, 3, 5, 96, D), BF),
            pltpu.VMEM((2, 2, 48, D), BF),
            pltpu.VMEM((2, 4, 2, 2, 48, AW), BF),
            pltpu.VMEM((2, 2, 4, 2, 48, AW), BF),
            pltpu.VMEM((2, 4, 2, 48, QW), BF),
            pltpu.VMEM((2, 4, 48, QW), BF),
            pltpu.VMEM((2, 5, 48, QW), BF),
            pltpu.VMEM((2, 5, 2, 2, 48, AW - QW), BF),
            pltpu.VMEM((2, 2, 48, AW - QW), BF),
            pltpu.VMEM((2, 2, 48, AW - QW), BF),
            pltpu.VMEM((2, 2, 48, AW - QW), BF),
            pltpu.VMEM((2, 2, 48, AW - QW), BF),
            pltpu.VMEM((2, 8, D), F32),
            sems(10),
            sems(2, 3, 2), sems(2, 3, 2),
            sems(2, 3), sems(2, 3),
            sems(2, 2), sems(2, 2),
            sems(2, 3, 4), sems(2, 3, 4),
            sems(2, 3, 6), sems(2, 3, 5),
            sems(2, 3), sems(2, 3),
            sems(2, 3), sems(2, 3),
            sems(2, 2, 2), sems(2, 2, 2),
            sems(2, 2, 4), sems(2, 2, 4),
            sems(2, 2, 4), sems(2, 2, 4),
            sems(2, 2, 6), sems(2, 2, 5),
            sems(2, 2), sems(2, 2),
            sems(2, 6), sems(2, 5),
            sems(2), sems(2),
            sems(2), sems(2),
        ],
        compiler_params=pltpu.CompilerParams(collective_id=1, has_side_effects=True, vmem_limit_bytes=62 * 2**20),
        cost_estimate=pl.CostEstimate(flops=2 * 10**10, bytes_accessed=10**8, transcendentals=0),
        name="backward",
    )(cot, cos, sin, *kept)


def finish_kernel(
    y_i, gin_i, gug_i, dng_i, af_i, y_o, gin_o, qkv_o, out_o, gate_o, up_o, down_o, g1_o, b1_o, g2_o, b2_o,
    y_v, gin_v, gug, dng, af, qkv, out, gate, up, down, in_sem, out_sem,
):
    def copy(src, dst, sem):
        c = pltpu.make_async_copy(src, dst, sem)
        c.start()
        return c
    arriving = [[copy(src.at[l], dst.at[l], in_sem.at[l, i]) for i, (src, dst) in enumerate(((af_i, af), (gug_i, gug), (dng_i, dng)))] for l in range(2)]
    passing = [copy(y_i, y_v, in_sem.at[0, 3]), copy(gin_i, gin_v, in_sem.at[1, 3])]
    leaving = []
    for l in range(2):
        arriving[l][0].wait()
        for h in range(2):
            qkv[l, :, h * QW:h * QW + QW] = af[l, h, :, 0:QW].astype(F32)
            out[l, :, h * OW:h * OW + OW] = af[l, h, :, QW:QW + OW].astype(F32)
            turned = af[l, h, :, QW + OW:].astype(F32).T
            for i, ref in enumerate(((g1_o, b1_o), (g2_o, b2_o))[h]):
                ref[l:l + 1, :] = turned[i:i + 1, :]
        leaving.append(copy(qkv.at[l], qkv_o.at[l], out_sem.at[l, 0]))
        leaving.append(copy(out.at[l], out_o.at[l], out_sem.at[l, 1]))
        arriving[l][1].wait()
        for w, ref in enumerate((gate, up)):
            for j in range(G):
                pieces = [gug[l, w, cc, yy, :, 96 * j:96 * j + 96] for cc in range(2) for yy in range(2)]
                ref[l, :, 384 * j:384 * j + 384] = jnp.concatenate(pieces, axis=1).astype(F32)
            leaving.append(copy(ref.at[l], (gate_o, up_o)[w].at[l], out_sem.at[l, 2 + w]))
        passing[l].wait()
        leaving.append(copy((y_v, gin_v)[l], (y_o, gin_o)[l], out_sem.at[l, 5]))
        arriving[l][2].wait()
        for h in range(2):
            down[l, 96 * h:96 * h + 96, :] = dng[l, h].astype(F32)
        leaving.append(copy(down.at[l], down_o.at[l], out_sem.at[l, 4]))
    for c in leaving:
        c.wait()


def epilogue(y, gin, gug, dng, af):
    vm = pl.BlockSpec(memory_space=pltpu.VMEM)
    any_spec = pl.BlockSpec(memory_space=pl.ANY)
    large = [(2, 48, 3 * D), (2, 48, D), (2, 48, 4 * FS), (2, 48, 4 * FS), (2, 192, D)]
    return tuple(pl.pallas_call(
        finish_kernel,
        out_shape=[jax.ShapeDtypeStruct(v.shape, v.dtype) for v in (y, gin)]
        + [jax.ShapeDtypeStruct(v, F32) for v in large + [(2, 48)] * 4],
        in_specs=[any_spec] * 5,
        out_specs=[any_spec] * 7 + [vm] * 4,
        scratch_shapes=[pltpu.VMEM(v.shape, v.dtype) for v in (y, gin, gug, dng, af)]
        + [pltpu.VMEM(v, F32) for v in large]
        + [sems(2, 4), sems(2, 6)],
        compiler_params=pltpu.CompilerParams(vmem_limit_bytes=60 * 2**20),
        cost_estimate=pl.CostEstimate(flops=10**6, bytes_accessed=10**7, transcendentals=0),
        name="finish",
    )(y, gin, gug, dng, af))


def positions_of(segment_row):
    token_index = jnp.arange(segment_row.shape[0], dtype=jnp.int32)
    before = jnp.concatenate([segment_row[:1] - 1, segment_row[:-1]])
    starts = jnp.where(segment_row != before, token_index, jnp.zeros_like(token_index))
    return token_index - lax.cummax(starts, axis=0)


def rotary_tables(position):
    half_width = HEAD // 2
    frequency = rope_base ** (-2.0 * jnp.arange(half_width, dtype=F32) / HEAD)
    angles = position.astype(F32)[:, None] * frequency[None, :]
    return jnp.cos(angles), jnp.sin(angles)


def prologue(inputs, segment_ids, qkv_weight, out_weight, gate_weight, up_weight, down_weight,
             first_gain, first_bias, second_gain, second_bias):
    frequency = rope_base ** (-2.0 * np.arange(HEAD // 2, dtype=np.float32) / HEAD)
    freq = jnp.asarray(np.tile(frequency.astype(np.float32)[None, :], (8, 4)))
    return (inputs[0], segment_ids, freq, first_gain, first_bias, second_gain, second_bias, qkv_weight, out_weight,
            gate_weight, up_weight, down_weight)


def rotate(values, cosine_table, sine_table):
    half_width = values.shape[-1] // 2
    lead_half = values[..., :half_width]
    tail_half = values[..., half_width:]
    cos_wide = cosine_table[:, None, :]
    sin_wide = sine_table[:, None, :]
    return jnp.concatenate(
        [lead_half * cos_wide - tail_half * sin_wide, tail_half * cos_wide + lead_half * sin_wide],
        axis=-1,
    )


def unrotate(values, cosine_table, sine_table):
    half_width = values.shape[-1] // 2
    lead_half = values[..., :half_width]
    tail_half = values[..., half_width:]
    cos_wide = cosine_table[:, None, :]
    sin_wide = sine_table[:, None, :]
    return jnp.concatenate(
        [lead_half * cos_wide + tail_half * sin_wide, tail_half * cos_wide - lead_half * sin_wide],
        axis=-1,
    )


def norm_forward(values, gain_row, bias_row):
    mean_row = jnp.mean(values, axis=-1, keepdims=True)
    centred = values - mean_row
    variance = jnp.mean(centred * centred, axis=-1, keepdims=True)
    inverse = lax.rsqrt(variance + eps_norm)
    normed = centred * inverse
    return (normed * gain_row + bias_row, normed, inverse)


def norm_backward(upstream, normed, inverse, gain_row):
    scaled = upstream * gain_row
    gain_sum = jnp.sum(upstream * normed, axis=0)
    bias_sum = jnp.sum(upstream, axis=0)
    grad_input = inverse * (
        scaled
        - jnp.mean(scaled, axis=-1, keepdims=True)
        - normed * jnp.mean(scaled * normed, axis=-1, keepdims=True)
    )
    return (grad_input, gain_sum, bias_sum)


def times_transposed(left_side, right_side):
    return lax.dot_general(
        left_side, right_side, (((1,), (1,)), ((), ())), preferred_element_type=jnp.float32
    )


def outer_sum(left_side, right_side):
    return lax.dot_general(
        left_side, right_side, (((0,), (0,)), ((), ())), preferred_element_type=jnp.float32
    )


def to_pairs(values):
    token_count = values.shape[0]
    return values.reshape(token_count, HEADS // 2, 2 * HEAD).transpose(1, 0, 2)


def from_pairs(values):
    return values.transpose(1, 0, 2).reshape(values.shape[1], HEADS * HEAD)


def pair_scores(query_pair, key_pair, allowed, score_scale):
    token_count = query_pair.shape[0]
    queries = query_pair.reshape(token_count, 2, HEAD)
    key_rows = key_pair.reshape(token_count, 2, HEAD)
    scores = (
        jnp.einsum("qhd,khd->hqk", queries, key_rows, preferred_element_type=jnp.float32)
        * score_scale
    )
    return (jnp.where(allowed[None], scores, masked_score), queries, key_rows)


def pair_forward(block_item, allowed, score_scale):
    query_pair, key_pair, value_pair = block_item
    token_count = query_pair.shape[0]
    scores, queries, key_rows = pair_scores(query_pair, key_pair, allowed, score_scale)
    row_top = jnp.max(scores, axis=-1, keepdims=True)
    exponent = jnp.exp(scores - row_top)
    row_total = jnp.sum(exponent, axis=-1, keepdims=True)
    probabilities = exponent / row_total
    logsum = row_top[..., 0] + jnp.log(row_total[..., 0])
    value_rows = value_pair.reshape(token_count, 2, HEAD)
    attended = jnp.einsum(
        "hqk,khd->qhd",
        probabilities.astype(jnp.bfloat16),
        value_rows,
        preferred_element_type=jnp.float32,
    )
    return (attended.reshape(token_count, 2 * HEAD), logsum)


def pair_backward(block_item, allowed, score_scale):
    query_pair, key_pair, value_pair, grad_pair, logsum = block_item
    token_count = query_pair.shape[0]
    scores, queries, key_rows = pair_scores(query_pair, key_pair, allowed, score_scale)
    probabilities = jnp.exp(scores - logsum[..., None])
    value_rows = value_pair.reshape(token_count, 2, HEAD)
    grad_rows = grad_pair.reshape(token_count, 2, HEAD)
    grad_probs = jnp.einsum(
        "qhd,khd->hqk", grad_rows, value_rows, preferred_element_type=jnp.float32
    )
    grad_values = jnp.einsum(
        "hqk,qhd->khd",
        probabilities.astype(jnp.bfloat16),
        grad_rows,
        preferred_element_type=jnp.float32,
    )
    grad_scores = probabilities * (
        grad_probs - jnp.sum(grad_probs * probabilities, axis=-1, keepdims=True)
    )
    grad_scores = grad_scores.astype(jnp.bfloat16)
    grad_queries = (
        jnp.einsum("hqk,khd->qhd", grad_scores, key_rows, preferred_element_type=jnp.float32)
        * score_scale
    )
    grad_keys = (
        jnp.einsum("hqk,qhd->khd", grad_scores, queries, preferred_element_type=jnp.float32)
        * score_scale
    )
    return (
        grad_queries.reshape(token_count, 2 * HEAD),
        grad_keys.reshape(token_count, 2 * HEAD),
        grad_values.reshape(token_count, 2 * HEAD),
    )


def layer_forward(hidden_state, weights, cosine_table, sine_table, allowed, score_scale):
    qkv_full, out_full, gate_full, up_full, down_full, gain_one, bias_one, gain_two, bias_two = (
        weights
    )
    token_count, model_width = hidden_state.shape
    state_low = hidden_state.astype(jnp.bfloat16)
    projected = jnp.dot(state_low, qkv_full, preferred_element_type=jnp.float32)
    queries = rotate(
        projected[:, :model_width].reshape(token_count, HEADS, HEAD), cosine_table, sine_table
    )
    queries = queries.astype(jnp.bfloat16).reshape(token_count, model_width)
    key_rows = rotate(
        projected[:, model_width : 2 * model_width].reshape(token_count, HEADS, HEAD),
        cosine_table,
        sine_table,
    )
    key_rows = key_rows.astype(jnp.bfloat16).reshape(token_count, model_width)
    value_rows = projected[:, 2 * model_width :].astype(jnp.bfloat16)

    def attend_pair(block_item):
        return pair_forward(block_item, allowed, score_scale)

    attended_pairs, logsum = lax.map(
        attend_pair, (to_pairs(queries), to_pairs(key_rows), to_pairs(value_rows))
    )
    attended = from_pairs(attended_pairs).astype(jnp.bfloat16)
    branch = jnp.dot(attended, out_full, preferred_element_type=jnp.float32)
    middle, normed_one, inverse_one = norm_forward(
        hidden_state + branch, gain_one.astype(jnp.float32), bias_one.astype(jnp.float32)
    )
    middle_low = middle.astype(jnp.bfloat16)
    gate_pre = jnp.dot(middle_low, gate_full, preferred_element_type=jnp.float32)
    up_pre = jnp.dot(middle_low, up_full, preferred_element_type=jnp.float32)
    activated = (jax.nn.silu(gate_pre) * up_pre).astype(jnp.bfloat16)
    feed = jnp.dot(activated, down_full, preferred_element_type=jnp.float32)
    result, normed_two, inverse_two = norm_forward(
        middle + feed, gain_two.astype(jnp.float32), bias_two.astype(jnp.float32)
    )
    stored = (
        state_low,
        queries,
        key_rows,
        value_rows,
        logsum,
        attended,
        normed_one,
        inverse_one,
        middle_low,
        gate_pre,
        up_pre,
        activated,
        normed_two,
        inverse_two,
    )
    return (result, stored)


def layer_backward(upstream, weights, stored, cosine_table, sine_table, allowed, score_scale):
    qkv_full, out_full, gate_full, up_full, down_full, gain_one, bias_one, gain_two, bias_two = (
        weights
    )
    (
        state_low,
        queries,
        key_rows,
        value_rows,
        logsum,
        attended,
        normed_one,
        inverse_one,
        middle_low,
        gate_pre,
        up_pre,
        activated,
        normed_two,
        inverse_two,
    ) = stored
    token_count, model_width = upstream.shape
    grad_mid, gain_two_sum, bias_two_sum = norm_backward(
        upstream, normed_two, inverse_two, gain_two.astype(jnp.float32)
    )
    grad_feed = grad_mid.astype(jnp.bfloat16)
    down_sum = outer_sum(activated, grad_feed)
    grad_act = times_transposed(grad_feed, down_full)
    sigmoid_gate = jax.nn.sigmoid(gate_pre)
    grad_gate = (grad_act * up_pre * sigmoid_gate * (1.0 + gate_pre * (1.0 - sigmoid_gate))).astype(
        jnp.bfloat16
    )
    grad_up = (grad_act * gate_pre * sigmoid_gate).astype(jnp.bfloat16)
    gate_sum = outer_sum(middle_low, grad_gate)
    up_sum = outer_sum(middle_low, grad_up)
    grad_middle = (
        grad_mid + times_transposed(grad_gate, gate_full) + times_transposed(grad_up, up_full)
    )
    grad_sum, gain_one_sum, bias_one_sum = norm_backward(
        grad_middle, normed_one, inverse_one, gain_one.astype(jnp.float32)
    )
    grad_branch = grad_sum.astype(jnp.bfloat16)
    out_sum = outer_sum(attended, grad_branch)
    grad_attended = times_transposed(grad_branch, out_full).astype(jnp.bfloat16)

    def attend_back(block_item):
        return pair_backward(block_item, allowed, score_scale)

    grad_query_pairs, grad_key_pairs, grad_value_pairs = lax.map(
        attend_back,
        (
            to_pairs(queries),
            to_pairs(key_rows),
            to_pairs(value_rows),
            to_pairs(grad_attended),
            logsum,
        ),
    )
    grad_queries = unrotate(
        from_pairs(grad_query_pairs).reshape(token_count, HEADS, HEAD), cosine_table, sine_table
    ).reshape(token_count, model_width)
    grad_keys = unrotate(
        from_pairs(grad_key_pairs).reshape(token_count, HEADS, HEAD), cosine_table, sine_table
    ).reshape(token_count, model_width)
    grad_projected = jnp.concatenate(
        [grad_queries, grad_keys, from_pairs(grad_value_pairs)], axis=1
    ).astype(jnp.bfloat16)
    qkv_sum = outer_sum(state_low, grad_projected)
    grad_input = grad_sum + times_transposed(grad_projected, qkv_full)
    return (
        grad_input,
        (
            qkv_sum,
            out_sum,
            gate_sum,
            up_sum,
            down_sum,
            gain_one_sum,
            bias_one_sum,
            gain_two_sum,
            bias_two_sum,
        ),
    )


def general(inputs, segment_ids, qkv_weight, out_weight, gate_weight, up_weight, down_weight,
            first_gain, first_bias, second_gain, second_bias, cotangent):
    params = (qkv_weight, out_weight, gate_weight, up_weight, down_weight, first_gain, first_bias, second_gain, second_bias)
    layers = qkv_weight.shape[0]
    segment_row = segment_ids[0]
    cosine_table, sine_table = rotary_tables(positions_of(segment_row))
    allowed = segment_row[:, None] == segment_row[None, :]
    score_scale = 1.0 / math.sqrt(HEAD)
    hidden_state = inputs[0].astype(F32)
    fetched, saved = [], []
    for layer_index in range(layers):
        weights = tuple(lax.all_gather(w[layer_index], "shard", axis=0, tiled=True) for w in params)
        fetched.append(weights)
        hidden_state, stored = layer_forward(hidden_state, weights, cosine_table, sine_table, allowed, score_scale)
        saved.append(stored)
    upstream = cotangent[0].astype(F32)
    shared = [None] * layers
    for layer_index in reversed(range(layers)):
        upstream, gradients = layer_backward(
            upstream, fetched[layer_index], saved[layer_index], cosine_table, sine_table, allowed, score_scale
        )
        owned = [lax.psum_scatter(v, "shard", scatter_dimension=0, tiled=True) for v in gradients]
        shared[layer_index] = [lax.psum(v.astype(BF), "rep").astype(F32) for v in owned]
    stacked = [jnp.stack([shared[layer_index][member] for layer_index in range(layers)]) for member in range(9)]
    return (hidden_state.astype(BF)[None], upstream[None], *stacked)


def special(inputs, segment_ids, qkv_weight, out_weight, gate_weight, up_weight, down_weight,
            first_gain, first_bias, second_gain, second_bias, cotangent):
    staged = prologue(inputs, segment_ids, qkv_weight, out_weight, gate_weight, up_weight, down_weight,
                      first_gain, first_bias, second_gain, second_bias)
    output, *kept, cos, sin = forward_call(staged)
    gin, gug, dng, af = backward_call(cotangent[0], cos, sin, kept)
    output, gin, *gradients = epilogue(output, gin, gug, dng, af)
    return (output[None], gin[None], *gradients)


IN_SPECS = (
    P(("rep", "shard"), None, None), P(("rep", "shard"), None),
) + (P(None, "shard", None),) * 5 + (P(None, "shard"),) * 4 + (P(("rep", "shard"), None, None),)
OUT_SPECS = (P(("rep", "shard"), None, None),) * 2 + (P(None, "shard", None),) * 5 + (P(None, "shard"),) * 4


def solution(mesh):
    fits = dict(mesh.shape) == {"rep": 2, "shard": 2 * G}
    return jax.shard_map(special if fits else general, mesh=mesh, in_specs=IN_SPECS, out_specs=OUT_SPECS, check_vma=False)
```

```python
import functools
import math

import jax
import jax.numpy as jnp
import numpy as np
from jax import lax
from jax.experimental import pallas as pl
from jax.experimental.pallas import tpu as pltpu
from jax.sharding import PartitionSpec as P

HEADS = 12
HEAD = 64
eps_norm = 1e-12
rope_base = 1000.0
masked_score = -1e30
MESH = pl.DeviceIdType.MESH
BF = jnp.bfloat16
F32 = jnp.float32
T = 256
D = 768
G = 8
QW = 1152
OW = 384
AW = QW + OW + 128
FS = 768
PAIRS = HEADS // 2
HT = T // 2


def part_of(half):
    return pl.ds(half * HT, HT)


def dot(a, b):
    return jnp.dot(a, b, preferred_element_type=F32)


def dot_t(a, b):
    return lax.dot_general(a, b, (((1,), (1,)), ((), ())), preferred_element_type=F32)


def tile(j, width):
    return pl.ds(pl.multiple_of(j * width, width), width)


def chip_rows(g):
    return pl.ds(pl.multiple_of(g * 96, 96), 96)


def shard_rows(g, c):
    return pl.ds(pl.multiple_of(g * 96 + c * 48, 48), 48)


class Place:
    def __init__(self):
        self.y = lax.axis_index("rep")
        s = lax.axis_index("shard")
        self.c, self.x, self.z = s % 2, (s // 2) % 2, s // 4
        self.g = s // 2
        self.slot = 2 * self.y + self.c

    def at(self, y, z, x, c):
        return (y, z * 4 + x * 2 + c)

    def core(self):
        return self.at(self.y, self.z, self.x, 1 - self.c)

    def xside(self):
        return self.at(self.y, self.z, 1 - self.x, self.c)

    def yside(self):
        return self.at(1 - self.y, self.z, self.x, self.c)

    def zside(self, k):
        return self.at(self.y, (self.z + k) % 4, self.x, self.c)

    def zto(self, z):
        return self.at(self.y, z, self.x, self.c)

    def near(self):
        return self.z + 1 - 2 * (self.z % 2)

    def across(self):
        return 3 - self.z

    def source(self, i):
        return (self.near(), 2 - self.z // 2, 3 - 3 * (self.z // 2))[i]

    def chip_from(self, i, x):
        return 2 * (self.z if i is None else self.source(i)) + x

    def chip(self, k, x):
        return 2 * ((self.z + 4 - k) % 4) + x

    def line(self):
        return [self.core(), self.xside(), self.yside(), self.zto(self.near()), self.zto(self.across())]

    def everyone(self):
        return [self.core(), self.xside(), self.yside()] + [self.zside(k) for k in (1, 2, 3)]


def greet(partners):
    barrier = pltpu.get_barrier_semaphore()
    for who in partners:
        pl.semaphore_signal(barrier, inc=1, device_id=who, device_id_type=MESH)
    return lambda: pl.semaphore_wait(barrier, len(partners))


class Mail:
    def __init__(self):
        self.sent = []
        self.some = []

    def send(self, src, dst, send_sem, recv_sem, who, tag=None):
        copy = pltpu.make_async_remote_copy(src, dst, send_sem, recv_sem, device_id=who, device_id_type=MESH)
        copy.start()
        self.sent.append((tag, copy))

    def later(self, src, dst, send_sem, recv_sem, who, cond):
        copy = pltpu.make_async_remote_copy(src, dst, send_sem, recv_sem, device_id=who, device_id_type=MESH)
        self.some.append((cond, copy))
        return copy

    def send_if(self, cond, src, dst, send_sem, recv_sem, who):
        copy = pltpu.make_async_remote_copy(src, dst, send_sem, recv_sem, device_id=who, device_id_type=MESH)
        pl.when(cond)(copy.start)
        self.some.append((cond, copy))

    def local(self, src, dst, sem):
        copy = pltpu.make_async_copy(src, dst, sem)
        copy.start()
        return copy

    def arrive(self, dst, send_sem, recv_sem, who):
        pltpu.make_async_remote_copy(dst, dst, send_sem, recv_sem, device_id=who, device_id_type=MESH).wait_recv()

    def gone(self, tag):
        for t, copy in self.sent:
            if t == tag:
                copy.wait_send()
        self.sent = [(t, copy) for t, copy in self.sent if t != tag]

    def finish(self):
        for _, copy in self.sent:
            copy.wait_send()
        for cond, copy in self.some:
            pl.when(cond)(copy.wait_send)


def swap_halves(v, low_half):
    return jnp.where(low_half, pltpu.roll(v, 96, 1), pltpu.roll(v, 32, 1))


def head_mask(rows, width):
    return lax.broadcasted_iota(jnp.int32, (rows, width), 1) % 128 < HEAD


def forward_kernel(
    x_ref, seg_ref, freq_ref, g1_ref, b1_ref, g2_ref, b2_ref, qkv_ref, outw_ref, gate_ref, up_ref, dn_ref,
    y_ref, A_o, F_o, Q_o, ST_o, P_o, TG_o, TT_o, N_o, I_o, PV_o, cos_ref, sin_ref,
    A, F, Q, ST, Pb, TG, TT, N, I, PV, S, AT, MF, AC, H, bias, FD, RC, RY, W, GU,
    ls, s_gu, r_gu, s_az, r_az, s_ax, r_ax, s_ay, r_ay, s_ac, r_ac, s_ad, r_ad, s_fz, r_fz, s_fx, r_fx, s_fw, r_fw,
    s_m, r_m, s_rc, r_rc, s_ry, r_ry, os,
):
    pc = Place()
    y, z, x, c, g, slot = pc.y, pc.z, pc.x, pc.c, pc.g, pc.slot
    ml = Mail()
    LAY = (0, 1)
    mid = z % 3 != 0
    near, across = pc.zto(pc.near()), pc.zto(pc.across())
    THREE = (0, 1, 2)

    met = greet(pc.line())

    own_a, own_f = [], []
    for l in LAY:
        own_a.append([])
        for h in range(2):
            dst = A.at[l, h, g, c]
            own_a[l].append(ml.local(qkv_ref.at[l, :, pl.ds(QW * h, QW)], dst.at[:, pl.ds(0, QW)], ls.at[l, h]))
            own_a[l].append(ml.local(outw_ref.at[l, :, pl.ds(OW * h, OW)], dst.at[:, pl.ds(QW, OW)], ls.at[l, 2 + h]))
    wide = [ml.local(gate_ref, W.at[0], ls.at[0, 6]), ml.local(up_ref, W.at[1], ls.at[1, 6])]
    for l in LAY:
        own_f.append(ml.local(dn_ref.at[l, pl.ds(pl.multiple_of(y * 96, 96), 96)], F.at[l, chip_rows(g), pl.ds(2 * FS, D)], ls.at[l, 7]))

    def gu_send(l):
        ml.send(GU.at[l, 1 - c, y], F.at[l, shard_rows(g, c), pl.ds(0, 2 * FS)], s_gu.at[l], r_gu.at[l], pc.core())

    def gu_arrive(l):
        ml.arrive(F.at[l, shard_rows(g, 1 - c), pl.ds(0, 2 * FS)], s_gu.at[l], r_gu.at[l], pc.core())

    def line_own(block, ss, rs):
        ml.send(block, block, ss.at[0], rs.at[0], near)
        ml.send_if(mid, block, block, ss.at[1], rs.at[1], across)

    def line_pass(i, block, ss, rs):
        ml.arrive(block, ss.at[0], rs.at[i], near)
        to, at = ((across, 2), (near, 1), (near, 2))[i]
        ml.send_if(mid, block, block, ss.at[2 + i], rs.at[at], to)

    def own_params():
        for l in LAY:
            for h, refs in enumerate(((g1_ref, b1_ref), (g2_ref, b2_ref))):
                two = [ref[l:l + 1, :].astype(F32) for ref in refs]
                rows = jnp.concatenate(two + [jnp.zeros((6, 48), F32)], axis=0).astype(BF)
                wide_rows = lax.dot_general(rows, onehot, (((0,), (0,)), ((), ())), preferred_element_type=F32)
                A[l, h, g, c, :, QW + OW:] = wide_rows.astype(BF)

    def a_own(l):
        for copy in own_a[l]:
            copy.wait()
        block = A.at[l, y, g, c]
        ml.send(block, block, s_ax.at[l, 0], r_ax.at[l, 0], pc.xside())
        line_own(block, s_az.at[l], r_az.at[l])

    def a_z(l, i):
        block = A.at[l, y, pc.chip_from(i, x), c]
        line_pass(i, block, s_az.at[l], r_az.at[l])
        ml.send(block, block, s_ax.at[l, 1 + i], r_ax.at[l, 1 + i], pc.xside())

    def a_yo(l, i):
        block = A.at[l, y, pc.chip_from(i, x), c]
        ml.send(block, block, s_ay.at[l, i], r_ay.at[l, i], pc.yside())

    FOUR = (None, 0, 1, 2)

    def a_x(l, j):
        ml.arrive(A.at[l, y, pc.chip_from(FOUR[j], 1 - x), c], s_ax.at[l, j], r_ax.at[l, j], pc.xside())

    def a_yx(l, j):
        block = A.at[l, y, pc.chip_from(FOUR[j], 1 - x), c]
        ml.send(block, block, s_ay.at[l, 3 + j], r_ay.at[l, 3 + j], pc.yside())

    def a_c(l, h):
        block = A.at[l, h, :, c]
        ml.send(block, block, s_ac.at[l, h], r_ac.at[l, h], pc.core())

    def a_y(l, i, xx, n):
        ml.arrive(A.at[l, 1 - y, pc.chip_from(i, xx), c], s_ay.at[l, n], r_ay.at[l, n], pc.yside())

    def a_c_arrive(l, h):
        ml.arrive(A.at[l, h, :, 1 - c], s_ac.at[l, h], r_ac.at[l, h], pc.core())

    parts = (pl.ds(0, 2 * FS), pl.ds(2 * FS, D))
    ALONG = (1, 1)

    def f_ready(l):
        for w in range(2):
            F[l, shard_rows(g, c), w * FS:w * FS + FS] = GU[l, c, y, :, w * FS:w * FS + FS]
        own_f[l].wait()
        gu_arrive(l)

    def f_own_z(l, p):
        line_own(F.at[l, chip_rows(g), parts[p]], s_fz.at[l, p], r_fz.at[l, p])

    def f_own_x(l, p):
        block = F.at[l, chip_rows(g), parts[p]]
        ml.send(block, block, s_fx.at[l, p, 0], r_fx.at[l, p, 0], pc.xside())

    def f_z(l, p, i):
        block = F.at[l, chip_rows(pc.chip_from(i, x)), parts[p]]
        line_pass(i, block, s_fz.at[l, p], r_fz.at[l, p])
        if (l, p) != ALONG:
            ml.send(block, block, s_fx.at[l, p, 1 + i], r_fx.at[l, p, 1 + i], pc.xside())

    def f_cross():
        l, p = ALONG
        block = F.at[l, chip_rows(pc.chip_from(None, 1 - x)), parts[p]]
        ml.arrive(block, s_fx.at[l, p, 0], r_fx.at[l, p, 0], pc.xside())
        line_own(block, s_fw, r_fw)

    def f_w(i):
        l, p = ALONG
        line_pass(i, F.at[l, chip_rows(pc.chip_from(i, 1 - x)), parts[p]], s_fw, r_fw)

    def f_x(l, p):
        if (l, p) == ALONG:
            return
        for j in range(4):
            ml.arrive(F.at[l, chip_rows(pc.chip_from(FOUR[j], 1 - x)), parts[p]], s_fx.at[l, p, j], r_fx.at[l, p, j], pc.xside())

    out_copies = []

    def save(src, dst):
        out_copies.append(ml.local(src, dst, os.at[len(out_copies)]))

    pair_mask = head_mask(T, 128)
    low_half = lax.broadcasted_iota(jnp.int32, (T, 128), 1) % HEAD < HEAD // 2
    onehot = (lax.broadcasted_iota(jnp.int32, (8, 128), 0) == lax.broadcasted_iota(jnp.int32, (8, 128), 1)).astype(F32).astype(BF)

    def tables():
        wide_row = jnp.broadcast_to(seg_ref[...].astype(F32), (T, T))
        same = wide_row.T == wide_row
        bias[...] = jnp.where(same, 0.0, masked_score)
        at = lax.broadcasted_iota(jnp.int32, (T, T), 1).astype(F32)
        first = jnp.min(jnp.where(same, at, float(T)), axis=1, keepdims=True)
        position = lax.broadcasted_iota(jnp.int32, (T, 128), 0).astype(F32) - first
        angle = position * freq_ref[0:1, :]
        sine = jnp.sin(angle)
        cos_ref[...] = jnp.cos(angle)
        sin_ref[...] = jnp.where(low_half, -sine, sine)

    def permute():
        for copy in wide:
            copy.wait()
        def of(i, carry):
            l, w = i // 2, i % 2
            v = W[w, l]
            for cc in range(2):
                for yy in range(2):
                    pieces = [v[:, 384 * j + 192 * cc + 96 * yy:384 * j + 192 * cc + 96 * yy + 96] for j in range(G)]
                    GU[l, cc, yy, :, tile(w, FS)] = jnp.concatenate(pieces, axis=1)
            return carry
        lax.fori_loop(0, 4, of, 0)

    def project(l):
        st = S[...]
        cos, sin = cos_ref[...], sin_ref[...]
        for j in range(6):
            h, off = j // 3, (j % 3) * 384
            w = A[l, h, :, :, :, off:off + 384].reshape(D, 384)
            r = dot(st, w)
            kind = j // 2
            for t in range(3):
                v = r[:, 128 * t:128 * t + 128]
                if kind < 2:
                    v = v * cos + swap_halves(v, low_half) * sin
                col = (j % 2) * 384 + 128 * t
                Q[l, kind, :, col:col + 128] = v.astype(BF)

    def attention(l):
        def pair(p, carry):
            cols = tile(p, 128)
            q, kk, v = Q[l, 0, :, cols] * jnp.asarray(0.125, BF), Q[l, 1, :, cols], Q[l, 2, :, cols]
            outs = []
            for h in range(2):
                qh = jnp.where(pair_mask == (h == 0), q, jnp.zeros_like(q))
                s = dot_t(qh, kk) + bias[...]
                e = jnp.exp(s - jnp.max(s, axis=1, keepdims=True))
                pr = (e * (1.0 / jnp.sum(e, axis=1, keepdims=True))).astype(BF)
                Pb[l, 2 * p + h] = pr
                outs.append(dot(pr, v))
            AT[:, cols] = jnp.where(pair_mask, outs[0], outs[1]).astype(BF)
            return carry
        def some(p, carry):
            for n in range(3):
                pair(p * 3 + n, carry)
            return carry
        lax.fori_loop(0, PAIRS // 3, some, 0)

    def params(l):
        for h in range(2):
            w = A[l, h, :, :, :, QW + OW:].reshape(D, 128)
            PV[l, h] = dot_t(onehot, w)

    def out_project(l):
        for h in range(2):
            w = A[l, h, :, :, :, QW:QW + OW].reshape(D, OW)
            H[:, h * OW:h * OW + OW] = H[:, h * OW:h * OW + OW] + dot(AT[...], w)

    def norm(l, i, dst, extra, half):
        gain, shift = PV[l, i, 0:1, :], PV[l, i, 1:2, :]
        def rows_of(j, carry):
            rows = tile(j, 32)
            v = H[rows, :]
            if extra is not None:
                v = v + extra(rows)
            cen = v - jnp.mean(v, axis=1, keepdims=True)
            inv = lax.rsqrt(jnp.mean(cen * cen, axis=1, keepdims=True) + eps_norm)
            n = cen * inv
            N[l, i, rows, :] = n
            I[l, i, rows, :] = jnp.broadcast_to(inv, (32, 128))
            m = n * gain + shift
            H[rows, :] = m
            dst[rows, :] = m.astype(BF)
            return carry
        lax.fori_loop(half * (HT // 32), (half + 1) * (HT // 32), rows_of, 0)

    def ffn_up(l, first, toks):
        two, n = pl.ds(first, 2), toks.size
        def cols_of(j, carry):
            cols = tile(j, 256)
            xx = MF[l, two, toks].reshape(2 * n, D)
            gate = dot(xx, F[l, :, cols])
            up = dot(xx, F[l, :, pl.ds(pl.multiple_of(FS + j * 256, 256), 256)])
            act = gate * jax.nn.sigmoid(gate) * up
            TG[l, 0, two, toks, cols] = gate.astype(BF).reshape(2, n, 256)
            TG[l, 1, two, toks, cols] = up.astype(BF).reshape(2, n, 256)
            AC[two, toks, cols] = act.astype(BF).reshape(2, n, 256)
            return carry
        lax.fori_loop(0, FS // 256, cols_of, 0)

    def ffn_down(l, s_, toks, plus=None):
        def cols_of(j, carry):
            cols = tile(j, 256)
            r = dot(AC[s_, toks], F[l, :, pl.ds(pl.multiple_of(2 * FS + j * 256, 256), 256)])
            if plus is not None:
                r = r + plus[toks, cols].astype(F32)
            FD[l, s_, toks, cols] = r.astype(BF)
            return carry
        lax.fori_loop(0, D // 256, cols_of, 0)

    def turn(src, dst, col):
        def tile_of(j, carry):
            cols = tile(j, 128)
            dst[cols, pl.ds(pl.multiple_of(col, T), T)] = src[:, cols].T
            return carry
        lax.fori_loop(0, D // 128, tile_of, 0)

    def turn_slots(src, dst):
        def slot_of(i, carry):
            turn(src.at[i], dst, i * T)
            return carry
        lax.fori_loop(0, 4, slot_of, 0)

    def begin():
        H[...] = x_ref[...].astype(F32)
        S[...] = x_ref[...]
        permute()
        gu_send(0)
        gu_send(1)

    def projected(l):
        params(l)
        project(l)

    def turn_state(l):
        turn(S, ST.at[l, 0], 0)

    def scores(l):
        attention(l)
        save(Pb.at[l], P_o.at[l])
        save(Q.at[l], Q_o.at[l])

    WHOLE = pl.ds(0, T)

    def branch(l):
        out_project(l)

    def first_norm(l, h):
        norm(l, 0, MF.at[l, slot], None, h)
        mine = MF.at[l, slot, part_of(h)]
        ml.send(mine, mine, s_m.at[l, 0, h], r_m.at[l, 0, h], pc.yside())
        ml.send(mine, mine, s_m.at[l, 1, h], r_m.at[l, 1, h], pc.core())

    def turn_attended(l):
        turn(AT, ST.at[l, 1], 0)
        save(ST.at[l], ST_o.at[l])

    def own_up(l):
        for h in range(2):
            ml.arrive(MF.at[l, 2 * y + 1 - c, part_of(h)], s_m.at[l, 1, h], r_m.at[l, 1, h], pc.core())
        f_x(l, 0)
        ffn_up(l, 2 * y, WHOLE)

    def own_down(l):
        f_x(l, 1)
        s_ = 2 * y + 1 - c
        ffn_down(l, s_, WHOLE)
        ml.send(FD.at[l, s_], RC.at[l, y], s_rc.at[l, 2], r_rc.at[l, 2], pc.core())
        ffn_down(l, slot, WHOLE)
        save(F.at[l], F_o.at[l])

    def pass_on(l, h):
        block = MF.at[l, 2 * (1 - y) + c, part_of(h)]
        ml.arrive(block, s_m.at[l, 0, h], r_m.at[l, 0, h], pc.yside())
        ml.send(block, block, s_m.at[l, 2, h], r_m.at[l, 2, h], pc.core())

    def other_up(l, h):
        others = 2 * (1 - y)
        ml.arrive(MF.at[l, others + 1 - c, part_of(h)], s_m.at[l, 2, h], r_m.at[l, 2, h], pc.core())
        ffn_up(l, others, part_of(h))

    def other_down(l, h):
        s_ = 2 * (1 - y) + 1 - c
        ffn_down(l, s_, part_of(h))
        ml.send(FD.at[l, s_, part_of(h)], RC.at[l, 1 - y, part_of(h)], s_rc.at[l, h], r_rc.at[l, h], pc.core())

    def other_sum(l, h):
        s_ = 2 * (1 - y) + c
        ml.arrive(RC.at[l, 1 - y, part_of(h)], s_rc.at[l, h], r_rc.at[l, h], pc.core())
        ffn_down(l, s_, part_of(h), RC.at[l, 1 - y])
        ml.send(FD.at[l, s_, part_of(h)], RY.at[l, part_of(h)], s_ry.at[l, h], r_ry.at[l, h], pc.yside())

    def turn_middle(l):
        turn_slots(MF.at[l], TT.at[l, 0])
        save(TG.at[l], TG_o.at[l])
        save(TT.at[l, 0], TT_o.at[l, 0])

    def turn_activated(l):
        turn_slots(AC, TT.at[l, 1])
        save(TT.at[l, 1], TT_o.at[l, 1])

    def second_norm(l, h):
        if h == 0:
            ml.arrive(RC.at[l, y], s_rc.at[l, 2], r_rc.at[l, 2], pc.core())
        ml.arrive(RY.at[l, part_of(h)], s_ry.at[l, h], r_ry.at[l, h], pc.yside())
        feed = lambda rows: FD[l, slot, rows, :].astype(F32) + RC[l, y, rows, :].astype(F32) + RY[l, rows, :].astype(F32)
        norm(l, 1, S if l == 0 else y_ref, feed, h)

    def other_block(l, n, cc):
        at = g if n == 7 else pc.chip_from(n, x) if n < 3 else pc.chip_from(FOUR[n - 3], 1 - x)
        return A.at[l, 1 - y, at, cc]

    def to_other_core(l, n):
        block = other_block(l, n, c)
        ml.send(block, block, s_ad.at[l, n], r_ad.at[l, n], pc.core())

    def ay_arrive(l, n):
        ml.arrive(other_block(l, n, c), s_ay.at[l, n], r_ay.at[l, n], pc.yside())
        to_other_core(l, n)

    def ac_own(l):
        a_c(l, y)

    def ac_other(l):
        to_other_core(l, 7)

    def attn_ready(l):
        a_c_arrive(l, y)
        for n in (7, 0, 1, 2, 3, 4, 5, 6):
            ml.arrive(other_block(l, n, 1 - c), s_ad.at[l, n], r_ad.at[l, n], pc.core())
        save(A.at[l], A_o.at[l])

    own_params()
    met()
    a_own(0)
    a_own(1)
    begin()
    a_x(0, 0)
    a_z(0, 0)
    a_yx(0, 0)
    ac_other(1)
    a_yo(0, 0)
    a_z(0, 1)
    a_z(1, 0)
    a_z(1, 1)
    a_z(0, 2)
    a_yo(0, 1)
    a_x(0, 1)
    a_yo(1, 0)
    a_x(1, 0)
    f_ready(1)
    f_ready(0)
    a_yo(1, 1)
    f_own_z(0, 0)
    a_x(0, 2)
    ay_arrive(0, 0)
    a_yx(0, 1)
    f_own_x(0, 1)
    a_z(1, 2)
    f_own_x(0, 0)
    f_own_z(1, 1)
    a_yo(0, 2)
    turn_state(0)
    a_yx(0, 2)
    f_own_z(0, 1)
    a_x(0, 3)
    a_x(1, 1)
    ac_own(0)
    f_z(0, 0, 0)
    a_yx(0, 3)
    f_z(0, 0, 1)
    a_yo(1, 2)
    ay_arrive(0, 1)
    ay_arrive(0, 2)
    ay_arrive(0, 3)
    tables()
    ay_arrive(0, 4)
    a_x(1, 2)
    ac_other(0)
    a_yx(1, 0)
    ay_arrive(0, 5)
    f_z(1, 1, 0)
    ay_arrive(0, 6)
    ay_arrive(1, 0)
    attn_ready(0)
    f_z(1, 1, 1)
    a_yx(1, 1)
    projected(0)
    a_yx(1, 2)
    f_z(0, 0, 2)
    f_own_z(1, 0)
    ay_arrive(1, 1)
    ay_arrive(1, 2)
    f_z(0, 1, 0)
    scores(0)
    branch(0)
    a_x(1, 3)
    first_norm(0, 0)
    f_z(0, 1, 1)
    ac_own(1)
    first_norm(0, 1)
    turn_attended(0)
    pass_on(0, 0)
    ay_arrive(1, 3)
    f_z(0, 1, 2)
    ay_arrive(1, 4)
    a_yx(1, 3)
    f_own_x(1, 1)
    own_up(0)
    other_up(0, 0)
    f_z(1, 0, 0)
    ay_arrive(1, 5)
    pass_on(0, 1)
    f_z(1, 0, 1)
    other_up(0, 1)
    own_down(0)
    other_down(0, 0)
    f_z(1, 1, 2)
    ay_arrive(1, 6)
    other_down(0, 1)
    other_sum(0, 0)
    f_own_x(1, 0)
    f_cross()
    other_sum(0, 1)
    turn_middle(0)
    attn_ready(1)
    f_z(1, 0, 2)
    second_norm(0, 0)
    f_w(0)
    second_norm(0, 1)
    projected(1)
    scores(1)
    branch(1)
    first_norm(1, 0)
    f_w(1)
    first_norm(1, 1)
    turn_activated(0)
    f_w(2)
    own_up(1)
    pass_on(1, 0)
    own_down(1)
    other_up(1, 0)
    other_down(1, 0)
    pass_on(1, 1)
    turn_state(1)
    other_sum(1, 0)
    other_up(1, 1)
    other_down(1, 1)
    turn_attended(1)
    other_sum(1, 1)
    turn_middle(1)
    second_norm(1, 0)
    turn_activated(1)
    second_norm(1, 1)
    for src, dst in ((N, N_o), (I, I_o), (PV, PV_o)):
        save(src, dst)
    for copy in out_copies:
        copy.wait()
    ml.finish()


FWD_SHAPES = [
    ((2, 2, G, 2, 48, AW), BF),
    ((2, D, 2 * FS + D), BF),
    ((2, 3, T, D), BF),
    ((2, 2, D, T), BF),
    ((2, HEADS, T, T), BF),
    ((2, 2, 4, T, FS), BF),
    ((2, 2, D, 4 * T), BF),
    ((2, 2, T, D), F32),
    ((2, 2, T, 128), F32),
    ((2, 2, 8, D), F32),
]


def sems(*shape):
    return pltpu.SemaphoreType.DMA(shape)


def forward_call(args):
    any_spec = pl.BlockSpec(memory_space=pl.ANY)
    vm = pl.BlockSpec(memory_space=pltpu.VMEM)
    return pl.pallas_call(
        forward_kernel,
        out_shape=[jax.ShapeDtypeStruct((T, D), BF)]
        + [jax.ShapeDtypeStruct(s, d) for s, d in FWD_SHAPES]
        + [jax.ShapeDtypeStruct((T, 128), F32)] * 2,
        in_specs=[vm] * 7 + [any_spec] * 5,
        out_specs=[vm] + [any_spec] * len(FWD_SHAPES) + [vm] * 2,
        scratch_shapes=[pltpu.VMEM(s, d) for s, d in FWD_SHAPES]
        + [
            pltpu.VMEM((T, D), BF),
            pltpu.VMEM((T, D), BF),
            pltpu.VMEM((2, 4, T, D), BF),
            pltpu.VMEM((4, T, FS), BF),
            pltpu.VMEM((T, D), F32),
            pltpu.VMEM((T, T), F32),
            pltpu.VMEM((2, 4, T, D), BF),
            pltpu.VMEM((2, 2, T, D), BF),
            pltpu.VMEM((2, T, D), BF),
            pltpu.VMEM((2, 2, 48, 4 * FS), BF),
            pltpu.VMEM((2, 2, 2, 48, 2 * FS), BF),
            sems(2, 8),
            sems(2), sems(2),
            sems(2, 5), sems(2, 3),
            sems(2, 4), sems(2, 4),
            sems(2, 7), sems(2, 7),
            sems(2, 2), sems(2, 2),
            sems(2, 8), sems(2, 8),
            sems(2, 2, 5), sems(2, 2, 3),
            sems(2, 2, 4), sems(2, 2, 4),
            sems(5), sems(3),
            sems(2, 3, 2), sems(2, 3, 2),
            sems(2, 3), sems(2, 3),
            sems(2, 2), sems(2, 2),
            sems(19),
        ],
        compiler_params=pltpu.CompilerParams(collective_id=0, has_side_effects=True, vmem_limit_bytes=60 * 2**20),
        cost_estimate=pl.CostEstimate(flops=10**10, bytes_accessed=10**8, transcendentals=0),
        name="forward",
    )(*args)


def backward_kernel(
    cot_ref, cos_ref, sin_ref, A_i, F_i, Q_i, ST_i, P_i, TG_i, TT_i, N_i, I_i, PV_i,
    gin_ref, GUG, DNG, AF,
    A, F, Q, ST, Pb, TG, TT, N, I, PV,
    U, GF, GB, GP, FD, RC, RY, FG, RFX, RFZ, FR, AG, RAC, RAY, RAX, RAZ, RO, OX, OR, OT, OY, V,
    ls, s_m, r_m, s_rc, r_rc, s_ry, r_ry,
    s_fx, r_fx, s_fz, r_fz, s_fc, r_fc, s_fy, r_fy,
    s_ac, r_ac, s_ay, r_ay, s_ax, r_ax, s_az, r_az, s_af, r_af, s_oz, r_oz, s_ox, r_ox, s_oy, r_oy,
):
    pc = Place()
    y, z, x, c, slot = pc.y, pc.z, pc.x, pc.c, pc.slot
    ml = Mail()
    mid = z % 3 != 0
    zn = pc.near()
    near, across = pc.zto(zn), pc.zto(3 - z)
    planes = (3 - zn, 3 - z, zn, z)
    places = {
        "PV": (PV_i, PV, 0), "N": (N_i, N, 1), "I": (I_i, I, 2), "TT": (TT_i, TT, 3), "F": (F_i, F, 4), "TG": (TG_i, TG, 5),
        "ST": (ST_i, ST, 6), "A": (A_i, A, 7), "P": (P_i, Pb, 8), "Q": (Q_i, Q, 9),
    }
    loading = {}

    def load(l, *names):
        for name in names:
            src, dst, i = places[name]
            loading[name] = ml.local(src.at[l], dst, ls.at[i])

    def need(*names):
        for name in names:
            if name in loading:
                loading.pop(name).wait()

    met = greet(pc.line())
    load(1, "PV", "N", "I", "F", "TG", "TT", "ST", "A", "P", "Q")
    U[...] = cot_ref[...].astype(F32)

    fcols = (pl.ds(2 * FS, D), pl.ds(0, FS), pl.ds(FS, FS))

    def fx_send(l, j):
        for n in range(4):
            ml.send(FG.at[planes[n], 1 - x, :, fcols[j]], RFX.at[l, j, planes[n]], s_fx.at[l, j, n], r_fx.at[l, j, n], pc.xside(), ("fx", l, j))

    def line_start(n, part, R, ss, rs):
        slot_of = (1, 2, 0)[n]
        ml.send_if(z % 3 == 0, part(planes[n]), R.at[slot_of], ss.at[n], rs.at[slot_of], near)

    def plus(dst, src, rows, widths):
        for r in range(0, rows, 48):
            at = 0
            for w in widths:
                here = (pl.ds(r, 48), pl.ds(at, w))
                dst[here] = (dst[here].astype(F32) + src[here].astype(F32)).astype(BF)
                at += w

    def line_middle(part, R, ss, rs, add):
        far = [pltpu.make_async_remote_copy(R.at[n], R.at[n], ss.at[0], rs.at[n], device_id=near, device_id_type=MESH) for n in (1, 2)]
        on = [
            ml.later(part(plane), R.at[3 + n], ss.at[3 + n], rs.at[3 + n], across, mid)
            for n, plane in enumerate((3 - z, 3 - zn))
        ]
        dsts = [part(3 - z), part(3 - zn)]
        def go():
            for n in range(2):
                far[n].wait_recv()
                add(dsts[n], R.at[1 + n])
                on[n].start()
        pl.when(mid)(go)

    def line_end(part, R, ss, rs, add):
        back = [pltpu.make_async_remote_copy(R.at[n], R.at[n], ss.at[0], rs.at[n], device_id=across, device_id_type=MESH) for n in (3, 4)]
        last = ml.later(part(zn), R.at[0], ss.at[5], rs.at[0], near, mid)
        dsts = [part(z), part(zn)]
        def go():
            back[1].wait_recv()
            add(dsts[1], R.at[4])
            last.start()
            back[0].wait_recv()
            add(dsts[0], R.at[3])
        pl.when(mid)(go)
        ml.arrive(R.at[0], ss.at[0], rs.at[0], near)

    def add_f(dst, src):
        plus(dst, src, 96, (D,))

    def add_a(dst, src):
        plus(dst, src, 48, awide[0])

    def add_o(dst, src):
        for i in range(2):
            for xx in range(2):
                plus(dst.at[i, xx], src.at[i, xx], 48, awide[1])

    def fpart(l, j):
        return lambda zz: RFX.at[l, j, zz]

    def fx_task(l, j, n):
        if True:
            p = planes[n]
            ml.arrive(RFX.at[l, j, p], s_fx.at[l, j, n], r_fx.at[l, j, n], pc.xside())
            for half in range(2):
                rows = pl.ds(48 * half, 48)
                RFX[l, j, p, rows, :] = (RFX[l, j, p, rows, :].astype(F32) + FG[p, x, rows, fcols[j]].astype(F32)).astype(BF)
            if n < 3:
                line_start(n, fpart(l, j), RFZ.at[l, j], s_fz.at[l, j], r_fz.at[l, j])

    def fm_task(l, j):
        line_middle(fpart(l, j), RFZ.at[l, j], s_fz.at[l, j], r_fz.at[l, j], add_f)

    def fz_task(l, j):
        line_end(fpart(l, j), RFZ.at[l, j], s_fz.at[l, j], r_fz.at[l, j], add_f)
        def total(start):
            rows = pl.ds(start, 48)
            return (RFX[l, j, z, rows, :].astype(F32) + RFZ[l, j, 0, rows, :].astype(F32)).astype(BF)
        if j == 0:
            for half in range(2):
                DNG[l, y, pl.ds(48 * half, 48), :] = total(48 * half)
            ml.send(DNG.at[l, y], DNG.at[l, y], s_fy.at[l, 0], r_fy.at[l, 0], pc.yside())
        else:
            FR[l, j - 1] = total(pl.multiple_of((1 - c) * 48, 48))
            ml.send(FR.at[l, j - 1], GUG.at[l, j - 1, c, y], s_fc.at[l, j], r_fc.at[l, j], pc.core())
            GUG[l, j - 1, c, y] = total(pl.multiple_of(c * 48, 48))

    def fc_task(l, j):
        ml.arrive(GUG.at[l, j - 1, 1 - c, y], s_fc.at[l, j], r_fc.at[l, j], pc.core())
        block = GUG.at[l, j - 1, :, y]
        ml.send(block, block, s_fy.at[l, j], r_fy.at[l, j], pc.yside())

    def fy_task(l, j):
        block = DNG.at[l, 1 - y] if j == 0 else GUG.at[l, j - 1, :, 1 - y]
        ml.arrive(block, s_fy.at[l, j], r_fy.at[l, j], pc.yside())

    acols = (pl.ds(0, QW), pl.ds(QW, AW - QW))
    awide = ((768, 384), (512,))

    def ac_send(l, p, i):
        h = (1 - y, y)[i]
        ml.send(AG.at[h, :, :, 1 - c, :, acols[p]], RAC.at[l, i, :, :, :, acols[p]], s_ac.at[l, p, i], r_ac.at[l, p, i], pc.core(), ("ac", l))

    def ac_sum(l, p, i):
        h = (1 - y, y)[i]
        ml.arrive(RAC.at[l, i, :, :, :, acols[p]], s_ac.at[l, p, i], r_ac.at[l, p, i], pc.core())
        def add(n, carry):
            zz, xx = n // 2, n % 2
            plus(RAC.at[l, i, zz, xx, :, acols[p]], AG.at[h, zz, xx, c, :, acols[p]], 48, awide[p])
            return carry
        lax.fori_loop(0, 8, add, 0)

    def ay_send(l, p, n):
        q = planes[n]
        ml.send(RAC.at[l, 0, q, :, :, acols[p]], RAY.at[l, q], s_ay.at[l, p, n], r_ay.at[l, p, n], pc.yside())

    def ay_task(l, p, n):
        q = planes[n]
        ml.arrive(RAY.at[l, q], s_ay.at[l, p, n], r_ay.at[l, p, n], pc.yside())
        for xx in range(2):
            plus(RAC.at[l, 1, q, xx, :, acols[p]], RAY.at[l, q, xx], 48, awide[p])
        ml.send(RAC.at[l, 1, q, 1 - x, :, acols[p]], RAX.at[l, q], s_ax.at[l, p, n], r_ax.at[l, p, n], pc.xside())

    def apart(l, p):
        return lambda zz: RAX.at[l, zz]

    def ax_task(l, p, n):
        q = planes[n]
        ml.arrive(RAX.at[l, q], s_ax.at[l, p, n], r_ax.at[l, p, n], pc.xside())
        plus(RAX.at[l, q], RAC.at[l, 1, q, x, :, acols[p]], 48, awide[p])
        if n < 3:
            line_start(n, apart(l, p), RAZ.at[l], s_az.at[l, p], r_az.at[l, p])

    def am_task(l, p):
        line_middle(apart(l, p), RAZ.at[l], s_az.at[l, p], r_az.at[l, p], add_a)

    def az_task(l, p):
        line_end(apart(l, p), RAZ.at[l], s_az.at[l, p], r_az.at[l, p], add_a)
        mine = AF.at[l, y, :, acols[p]]
        mine[...] = (RAX[l, z].astype(F32) + RAZ[l, 0].astype(F32)).astype(BF)
        ml.send(mine, mine, s_af.at[l, p], r_af.at[l, p], pc.yside())

    def af_task(l, p):
        ml.arrive(AF.at[l, 1 - y, :, acols[p]], s_af.at[l, p], r_af.at[l, p], pc.yside())

    def opart(l):
        return lambda zz: RAC.at[l, :, zz, :, :, acols[1]]

    def o_start(l):
        for n in range(3):
            line_start(n, opart(l), RO.at[l], s_oz.at[l], r_oz.at[l])

    def om_task(l):
        line_middle(opart(l), RO.at[l], s_oz.at[l], r_oz.at[l], add_o)

    def oz_task(l):
        line_end(opart(l), RO.at[l], s_oz.at[l], r_oz.at[l], add_o)
        for i, h in ((0, 1 - y), (1, y)):
            both = lambda xx: (RAC[l, i, z, xx, :, acols[1]].astype(F32) + RO[l, 0, i, xx].astype(F32)).astype(BF)
            OX[l, h] = both(1 - x)
            OT[l, h] = both(x)
        ml.send(OX.at[l], OR.at[l], s_ox.at[l], r_ox.at[l], pc.xside())

    def ox_task(l):
        ml.arrive(OR.at[l], s_ox.at[l], r_ox.at[l], pc.xside())
        for h in range(2):
            plus(OT.at[l, h], OR.at[l, h], 48, awide[1])
        ml.send(OT.at[l], OY.at[l], s_oy.at[l], r_oy.at[l], pc.yside())

    def oy_task(l):
        ml.arrive(OY.at[l], s_oy.at[l], r_oy.at[l], pc.yside())
        for h in range(2):
            AF[l, h, :, acols[1]] = (OT[l, h].astype(F32) + OY[l, h].astype(F32)).astype(BF)

    pair_mask = head_mask(T, 128)
    low_half = lax.broadcasted_iota(jnp.int32, (T, 128), 1) % HEAD < HEAD // 2
    onehot = (lax.broadcasted_iota(jnp.int32, (8, 128), 0) == lax.broadcasted_iota(jnp.int32, (8, 128), 1)).astype(F32).astype(BF)

    def norm_back(i, extra, dst, half):
        gain = PV[i, 0:1, :]
        def rows_of(j, carry):
            gs, bs = carry
            rows = tile(j, 32)
            u = U[rows, :]
            if extra is not None:
                u = u + extra(rows)
            n = N[i, rows, :]
            un = u * n
            gs = gs + un.reshape(4, 8, D).sum(0)
            bs = bs + u.reshape(4, 8, D).sum(0)
            m1 = jnp.mean(u * gain, axis=1, keepdims=True)
            m2 = jnp.mean(un * gain, axis=1, keepdims=True)
            r = I[i, rows, 0:1] * (u * gain - m1 - n * m2)
            U[rows, :] = r
            dst[rows, :] = r.astype(BF)
            return gs, bs
        zero = jnp.zeros((8, D), F32)
        gs, bs = lax.fori_loop(half * (HT // 32), (half + 1) * (HT // 32), rows_of, (zero, zero))
        row = lax.broadcasted_iota(jnp.int32, (8, D), 0)
        sums = jnp.where(row == 0, gs.sum(0, keepdims=True), jnp.where(row == 1, bs.sum(0, keepdims=True), 0.0))
        V[i] = sums if half == 0 else V[i] + sums

    def act_back(l, first, toks):
        two, n = pl.ds(first, 2), toks.size
        def cols_of(j, carry):
            cols = tile(j, 256)
            ga = dot_t(GF[l, two, toks].reshape(2 * n, D), F[cols, 2 * FS:])
            gate = TG[0, two, toks, cols].reshape(2 * n, 256).astype(F32)
            up = TG[1, two, toks, cols].reshape(2 * n, 256).astype(F32)
            sg = jax.nn.sigmoid(gate)
            gg = ga * up * sg * (1.0 + gate * (1.0 - sg))
            gu = ga * gate * sg
            TG[0, two, toks, cols] = gg.astype(BF).reshape(2, n, 256)
            TG[1, two, toks, cols] = gu.astype(BF).reshape(2, n, 256)
            return carry
        lax.fori_loop(0, FS // 256, cols_of, 0)

    def mid_back(s_, toks, plus=None):
        def cols_of(j, carry):
            cols = tile(j, 256)
            r = dot_t(TG[0, s_, toks], F[cols, 0:FS]) + dot_t(TG[1, s_, toks], F[cols, FS:2 * FS])
            if plus is not None:
                r = r + plus[toks, cols].astype(F32)
            FD[s_, toks, cols] = r.astype(BF)
            return carry
        lax.fori_loop(0, D // 256, cols_of, 0)

    def weight_grad(l, j):
        def cols_of(n, carry):
            cols = tile(n, 256)
            if j == 0:
                right = GF[l, :, :, cols].reshape(4 * T, 256)
            else:
                right = TG[j - 1, :, :, cols].reshape(4 * T, 256)
            r = dot(TT[0 if j else 1], right)
            off = (2 * FS, 0, FS)[j]
            FG[:, :, :, pl.ds(pl.multiple_of(off + n * 256, 256), 256)] = r.astype(BF).reshape(4, 2, 96, 256)
            return carry
        lax.fori_loop(0, 3, cols_of, 0)

    def out_back():
        acc = None
        for h in range(2):
            r = dot(ST[1], GB[:, h * OW:h * OW + OW])
            AG[h, :, :, :, :, QW:QW + OW] = r.astype(BF).reshape(4, 2, 2, 48, OW)
        for h in range(2):
            t = dot_t(GB[:, h * OW:h * OW + OW], A[h, :, :, :, QW:QW + OW].reshape(D, OW))
            acc = t if acc is None else acc + t
        GP[2] = acc.astype(BF)

    def attention_back():
        def pair(p, carry):
            cols = tile(p, 128)
            q, kk, v, ga = Q[0, :, cols], Q[1, :, cols], Q[2, :, cols], GP[2, :, cols]
            dq, dk, dv = [], [], []
            for h in range(2):
                pl_ = Pb[2 * p + h]
                pr = pl_.astype(F32)
                gh = jnp.where(pair_mask == (h == 0), ga, jnp.zeros_like(ga))
                dp = dot_t(gh, v)
                ds = (pr * (dp - jnp.sum(dp * pr, axis=1, keepdims=True))).astype(BF)
                dq.append(dot(ds, kk))
                dk.append(dot(ds.T, q))
                dv.append(dot(pl_.T, ga))
            cos, sin = cos_ref[...], sin_ref[...]
            def back(pair_of):
                m = jnp.where(pair_mask, pair_of[0], pair_of[1]) * 0.125
                return (m * cos - swap_halves(m, low_half) * sin).astype(BF)
            GP[0, :, cols] = back(dq)
            GP[1, :, cols] = back(dk)
            GP[2, :, cols] = jnp.where(pair_mask, dv[0], dv[1]).astype(BF)
            return carry
        def some(p, carry):
            for n in range(1):
                pair(p * 1 + n, carry)
            return carry
        lax.fori_loop(0, PAIRS // 1, some, 0)

    def gp_chunk(j):
        return GP[j // 2, :, (j % 2) * 384:(j % 2) * 384 + 384]

    def qkv_grad(h):
        for j in range(3 * h, 3 * h + 3):
            off = (j % 3) * 384
            r = dot(ST[0], gp_chunk(j))
            AG[h, :, :, :, :, off:off + 384] = r.astype(BF).reshape(4, 2, 2, 48, 384)

    def param_grad():
        for h in range(2):
            r = lax.dot_general(V[h].astype(BF), onehot, (((0,), (0,)), ((), ())), preferred_element_type=F32)
            AG[h, :, :, :, :, QW + OW:] = r.astype(BF).reshape(4, 2, 2, 48, 128)

    def input_back():
        acc = U[...]
        for j in range(6):
            off = (j % 3) * 384
            acc = acc + dot_t(gp_chunk(j), A[j // 3, :, :, :, off:off + 384].reshape(D, 384))
        U[...] = acc

    def run(steps):
        for step, *what in steps:
            step(*what)

    WHOLE = pl.ds(0, T)

    def upper(l, h):
        need("PV", "N", "I")
        norm_back(1, None, GF.at[l, slot], h)
        if l == 1 and h == 0:
            met()
        mine = GF.at[l, slot, part_of(h)]
        ml.send(mine, mine, s_m.at[l, 0, h], r_m.at[l, 0, h], pc.yside())
        ml.send(mine, mine, s_m.at[l, 1, h], r_m.at[l, 1, h], pc.core())

    def own_tokens(l):
        need("F", "TG")
        ml.gone(("fd", 1))
        for h in range(2):
            ml.arrive(GF.at[l, 2 * y + 1 - c, part_of(h)], s_m.at[l, 1, h], r_m.at[l, 1, h], pc.core())
        act_back(l, 2 * y, WHOLE)
        s_ = 2 * y + 1 - c
        mid_back(s_, WHOLE)
        ml.send(FD.at[s_], RC.at[y], s_rc.at[l, 2], r_rc.at[l, 2], pc.core(), ("fd", l))
        mid_back(slot, WHOLE)

    def pass_on(l, h):
        block = GF.at[l, 2 * (1 - y) + c, part_of(h)]
        ml.arrive(block, s_m.at[l, 0, h], r_m.at[l, 0, h], pc.yside())
        ml.send(block, block, s_m.at[l, 2, h], r_m.at[l, 2, h], pc.core())

    def other_tokens(l, h):
        others = 2 * (1 - y)
        ml.arrive(GF.at[l, others + 1 - c, part_of(h)], s_m.at[l, 2, h], r_m.at[l, 2, h], pc.core())
        act_back(l, others, part_of(h))

    def other_mids(l, h):
        s_ = 2 * (1 - y) + 1 - c
        mid_back(s_, part_of(h))
        ml.send(FD.at[s_, part_of(h)], RC.at[1 - y, part_of(h)], s_rc.at[l, h], r_rc.at[l, h], pc.core(), ("fd", l))

    def other_sums(l, h):
        s_ = 2 * (1 - y) + c
        ml.arrive(RC.at[1 - y, part_of(h)], s_rc.at[l, h], r_rc.at[l, h], pc.core())
        mid_back(s_, part_of(h), RC.at[1 - y])
        ml.send(FD.at[s_, part_of(h)], RY.at[part_of(h)], s_ry.at[l, h], r_ry.at[l, h], pc.yside(), ("fd", l))
        if l == 1 and h == 1:
            load(0, "F")

    def weights(l, j):
        need("TT")
        ml.gone(("fx", 1, j) if l == 0 else None)
        weight_grad(l, j)
        fx_send(l, j)
        if l == 1 and j == 2:
            load(0, "TT", "TG")

    def middle(l, h):
        if h == 0:
            ml.arrive(RC.at[y], s_rc.at[l, 2], r_rc.at[l, 2], pc.core())
        ml.arrive(RY.at[part_of(h)], s_ry.at[l, h], r_ry.at[l, h], pc.yside())
        norm_back(0, lambda rows: FD[slot, rows, :].astype(F32) + RC[y, rows, :].astype(F32) + RY[rows, :].astype(F32), GB, h)
        if l == 1 and h == 1:
            load(0, "PV", "N", "I")

    QKV, OUT = 0, 1

    def out_sums(l):
        need("ST", "A")
        if l == 0:
            ml.gone(("ac", 1))
        param_grad()
        out_back()
        for i in range(2):
            ac_send(l, OUT, i)

    def scores(l):
        need("P", "Q")
        attention_back()
        if l == 1:
            load(0, "P", "Q")

    def below(l):
        input_back()
        if l == 0:
            gin_ref[...] = U[...]

    def qkv_sums(l):
        qkv_grad(0)
        qkv_grad(1)
        for i in range(2):
            ac_send(l, QKV, i)
        if l == 1:
            load(0, "ST", "A")

    upper(1, 0)
    upper(1, 1)
    own_tokens(1)
    pass_on(1, 0)
    other_tokens(1, 0)
    other_mids(1, 0)
    pass_on(1, 1)
    other_sums(1, 0)
    other_tokens(1, 1)
    weights(1, 0)
    other_mids(1, 1)
    weights(1, 1)
    other_sums(1, 1)
    fx_task(1, 0, 0)
    middle(1, 0)
    weights(1, 2)
    fx_task(1, 0, 1)
    middle(1, 1)
    out_sums(1)
    fx_task(1, 0, 2)
    ac_sum(1, 1, 0)
    ac_sum(1, 1, 1)
    o_start(1)
    scores(1)
    below(1)
    upper(0, 0)
    fx_task(1, 1, 0)
    upper(0, 1)
    fx_task(1, 1, 1)
    qkv_sums(1)
    om_task(1)
    fm_task(1, 0)
    own_tokens(0)
    pass_on(0, 0)
    fx_task(1, 0, 3)
    ac_sum(1, 0, 1)
    ac_sum(1, 0, 0)
    fx_task(1, 1, 2)
    other_tokens(0, 0)
    ay_send(1, 0, 0)
    pass_on(0, 1)
    other_mids(0, 0)
    fx_task(1, 2, 0)
    other_tokens(0, 1)
    other_sums(0, 0)
    weights(0, 0)
    fx_task(1, 2, 1)
    fx_task(1, 2, 2)
    other_mids(0, 1)
    fx_task(1, 1, 3)
    other_sums(0, 1)
    fx_task(0, 0, 0)
    weights(0, 1)
    fm_task(1, 1)
    ay_send(1, 0, 1)
    middle(0, 0)
    ay_send(1, 0, 2)
    ay_task(1, 0, 0)
    middle(0, 1)
    ay_send(1, 0, 3)
    fm_task(1, 2)
    fx_task(0, 0, 1)
    out_sums(0)
    fx_task(0, 0, 2)
    scores(0)
    fx_task(0, 1, 0)
    qkv_sums(0)
    fx_task(0, 1, 1)
    fm_task(0, 0)
    ac_sum(0, 1, 0)
    ac_sum(0, 0, 0)
    ay_send(0, 0, 0)
    ay_task(1, 0, 1)
    fx_task(1, 2, 3)
    ac_sum(0, 1, 1)
    o_start(0)
    weights(0, 2)
    ay_send(0, 0, 1)
    fx_task(0, 1, 2)
    fm_task(0, 1)
    fz_task(1, 1)
    ay_send(0, 0, 2)
    oz_task(1)
    fc_task(1, 1)
    fx_task(0, 1, 3)
    ac_sum(0, 0, 1)
    fz_task(1, 2)
    fx_task(0, 0, 3)
    om_task(0)
    ax_task(1, 0, 0)
    ay_task(0, 0, 0)
    fx_task(0, 2, 0)
    fz_task(1, 0)
    fx_task(0, 2, 1)
    fz_task(0, 0)
    below(0)
    ay_task(0, 0, 1)
    fx_task(0, 2, 2)
    ax_task(1, 0, 1)
    ay_send(0, 0, 3)
    ay_task(1, 0, 2)
    fc_task(1, 2)
    oz_task(0)
    ox_task(1)
    ay_task(0, 0, 2)
    ay_task(1, 0, 3)
    fm_task(0, 2)
    ax_task(0, 0, 0)
    fx_task(0, 2, 3)
    fz_task(0, 1)
    ax_task(0, 0, 1)
    am_task(1, 0)
    fc_task(0, 1)
    ox_task(0)
    ax_task(1, 0, 2)
    fz_task(0, 2)
    ay_task(0, 0, 3)
    am_task(0, 0)
    ax_task(1, 0, 3)
    fc_task(0, 2)
    ax_task(0, 0, 2)
    az_task(1, 0)
    ax_task(0, 0, 3)
    az_task(0, 0)
    for l in (1, 0):
        for j in range(3):
            fy_task(l, j)
        af_task(l, 0)
        oy_task(l)
    ml.finish()


def backward_call(cot, cos, sin, kept):
    any_spec = pl.BlockSpec(memory_space=pl.ANY)
    vm = pl.BlockSpec(memory_space=pltpu.VMEM)
    return pl.pallas_call(
        backward_kernel,
        out_shape=[
            jax.ShapeDtypeStruct((T, D), F32),
            jax.ShapeDtypeStruct((2, 2, 2, 2, 48, FS), BF),
            jax.ShapeDtypeStruct((2, 2, 96, D), BF),
            jax.ShapeDtypeStruct((2, 2, 48, AW), BF),
        ],
        in_specs=[vm] * 3 + [any_spec] * len(kept),
        out_specs=[vm] * 4,
        scratch_shapes=[pltpu.VMEM(s[1:], d) for s, d in FWD_SHAPES]
        + [
            pltpu.VMEM((T, D), F32),
            pltpu.VMEM((2, 4, T, D), BF),
            pltpu.VMEM((T, D), BF),
            pltpu.VMEM((3, T, D), BF),
            pltpu.VMEM((4, T, D), BF),
            pltpu.VMEM((2, T, D), BF),
            pltpu.VMEM((T, D), BF),
            pltpu.VMEM((4, 2, 96, 2 * FS + D), BF),
            pltpu.VMEM((2, 3, 4, 96, D), BF),
            pltpu.VMEM((2, 3, 5, 96, D), BF),
            pltpu.VMEM((2, 2, 48, D), BF),
            pltpu.VMEM((2, 4, 2, 2, 48, AW), BF),
            pltpu.VMEM((2, 2, 4, 2, 48, AW), BF),
            pltpu.VMEM((2, 4, 2, 48, QW), BF),
            pltpu.VMEM((2, 4, 48, QW), BF),
            pltpu.VMEM((2, 5, 48, QW), BF),
            pltpu.VMEM((2, 5, 2, 2, 48, AW - QW), BF),
            pltpu.VMEM((2, 2, 48, AW - QW), BF),
            pltpu.VMEM((2, 2, 48, AW - QW), BF),
            pltpu.VMEM((2, 2, 48, AW - QW), BF),
            pltpu.VMEM((2, 2, 48, AW - QW), BF),
            pltpu.VMEM((2, 8, D), F32),
            sems(10),
            sems(2, 3, 2), sems(2, 3, 2),
            sems(2, 3), sems(2, 3),
            sems(2, 2), sems(2, 2),
            sems(2, 3, 4), sems(2, 3, 4),
            sems(2, 3, 6), sems(2, 3, 5),
            sems(2, 3), sems(2, 3),
            sems(2, 3), sems(2, 3),
            sems(2, 2, 2), sems(2, 2, 2),
            sems(2, 2, 4), sems(2, 2, 4),
            sems(2, 2, 4), sems(2, 2, 4),
            sems(2, 2, 6), sems(2, 2, 5),
            sems(2, 2), sems(2, 2),
            sems(2, 6), sems(2, 5),
            sems(2), sems(2),
            sems(2), sems(2),
        ],
        compiler_params=pltpu.CompilerParams(collective_id=1, has_side_effects=True, vmem_limit_bytes=62 * 2**20),
        cost_estimate=pl.CostEstimate(flops=2 * 10**10, bytes_accessed=10**8, transcendentals=0),
        name="backward",
    )(cot, cos, sin, *kept)


def finish_kernel(
    y_i, gin_i, gug_i, dng_i, af_i, y_o, gin_o, qkv_o, out_o, gate_o, up_o, down_o, g1_o, b1_o, g2_o, b2_o,
    y_v, gin_v, gug, dng, af, qkv, out, gate, up, down, in_sem, out_sem,
):
    def copy(src, dst, sem):
        c = pltpu.make_async_copy(src, dst, sem)
        c.start()
        return c
    arriving = [[copy(src.at[l], dst.at[l], in_sem.at[l, i]) for i, (src, dst) in enumerate(((af_i, af), (gug_i, gug), (dng_i, dng)))] for l in range(2)]
    passing = [copy(y_i, y_v, in_sem.at[0, 3]), copy(gin_i, gin_v, in_sem.at[1, 3])]
    leaving = []
    for l in range(2):
        arriving[l][0].wait()
        for h in range(2):
            qkv[l, :, h * QW:h * QW + QW] = af[l, h, :, 0:QW].astype(F32)
            out[l, :, h * OW:h * OW + OW] = af[l, h, :, QW:QW + OW].astype(F32)
            turned = af[l, h, :, QW + OW:].astype(F32).T
            for i, ref in enumerate(((g1_o, b1_o), (g2_o, b2_o))[h]):
                ref[l:l + 1, :] = turned[i:i + 1, :]
        leaving.append(copy(qkv.at[l], qkv_o.at[l], out_sem.at[l, 0]))
        leaving.append(copy(out.at[l], out_o.at[l], out_sem.at[l, 1]))
        arriving[l][1].wait()
        for w, ref in enumerate((gate, up)):
            for j in range(G):
                pieces = [gug[l, w, cc, yy, :, 96 * j:96 * j + 96] for cc in range(2) for yy in range(2)]
                ref[l, :, 384 * j:384 * j + 384] = jnp.concatenate(pieces, axis=1).astype(F32)
            leaving.append(copy(ref.at[l], (gate_o, up_o)[w].at[l], out_sem.at[l, 2 + w]))
        passing[l].wait()
        leaving.append(copy((y_v, gin_v)[l], (y_o, gin_o)[l], out_sem.at[l, 5]))
        arriving[l][2].wait()
        for h in range(2):
            down[l, 96 * h:96 * h + 96, :] = dng[l, h].astype(F32)
        leaving.append(copy(down.at[l], down_o.at[l], out_sem.at[l, 4]))
    for c in leaving:
        c.wait()


def epilogue(y, gin, gug, dng, af):
    vm = pl.BlockSpec(memory_space=pltpu.VMEM)
    any_spec = pl.BlockSpec(memory_space=pl.ANY)
    large = [(2, 48, 3 * D), (2, 48, D), (2, 48, 4 * FS), (2, 48, 4 * FS), (2, 192, D)]
    return tuple(pl.pallas_call(
        finish_kernel,
        out_shape=[jax.ShapeDtypeStruct(v.shape, v.dtype) for v in (y, gin)]
        + [jax.ShapeDtypeStruct(v, F32) for v in large + [(2, 48)] * 4],
        in_specs=[any_spec] * 5,
        out_specs=[any_spec] * 7 + [vm] * 4,
        scratch_shapes=[pltpu.VMEM(v.shape, v.dtype) for v in (y, gin, gug, dng, af)]
        + [pltpu.VMEM(v, F32) for v in large]
        + [sems(2, 4), sems(2, 6)],
        compiler_params=pltpu.CompilerParams(vmem_limit_bytes=60 * 2**20),
        cost_estimate=pl.CostEstimate(flops=10**6, bytes_accessed=10**7, transcendentals=0),
        name="finish",
    )(y, gin, gug, dng, af))


def positions_of(segment_row):
    token_index = jnp.arange(segment_row.shape[0], dtype=jnp.int32)
    before = jnp.concatenate([segment_row[:1] - 1, segment_row[:-1]])
    starts = jnp.where(segment_row != before, token_index, jnp.zeros_like(token_index))
    return token_index - lax.cummax(starts, axis=0)


def rotary_tables(position):
    half_width = HEAD // 2
    frequency = rope_base ** (-2.0 * jnp.arange(half_width, dtype=F32) / HEAD)
    angles = position.astype(F32)[:, None] * frequency[None, :]
    return jnp.cos(angles), jnp.sin(angles)


def prologue(inputs, segment_ids, qkv_weight, out_weight, gate_weight, up_weight, down_weight,
             first_gain, first_bias, second_gain, second_bias):
    frequency = rope_base ** (-2.0 * np.arange(HEAD // 2, dtype=np.float32) / HEAD)
    freq = jnp.asarray(np.tile(frequency.astype(np.float32)[None, :], (8, 4)))
    return (inputs[0], segment_ids, freq, first_gain, first_bias, second_gain, second_bias, qkv_weight, out_weight,
            gate_weight, up_weight, down_weight)


def rotate(values, cosine_table, sine_table):
    half_width = values.shape[-1] // 2
    lead_half = values[..., :half_width]
    tail_half = values[..., half_width:]
    cos_wide = cosine_table[:, None, :]
    sin_wide = sine_table[:, None, :]
    return jnp.concatenate(
        [lead_half * cos_wide - tail_half * sin_wide, tail_half * cos_wide + lead_half * sin_wide],
        axis=-1,
    )


def unrotate(values, cosine_table, sine_table):
    half_width = values.shape[-1] // 2
    lead_half = values[..., :half_width]
    tail_half = values[..., half_width:]
    cos_wide = cosine_table[:, None, :]
    sin_wide = sine_table[:, None, :]
    return jnp.concatenate(
        [lead_half * cos_wide + tail_half * sin_wide, tail_half * cos_wide - lead_half * sin_wide],
        axis=-1,
    )


def norm_forward(values, gain_row, bias_row):
    mean_row = jnp.mean(values, axis=-1, keepdims=True)
    centred = values - mean_row
    variance = jnp.mean(centred * centred, axis=-1, keepdims=True)
    inverse = lax.rsqrt(variance + eps_norm)
    normed = centred * inverse
    return (normed * gain_row + bias_row, normed, inverse)


def norm_backward(upstream, normed, inverse, gain_row):
    scaled = upstream * gain_row
    gain_sum = jnp.sum(upstream * normed, axis=0)
    bias_sum = jnp.sum(upstream, axis=0)
    grad_input = inverse * (
        scaled
        - jnp.mean(scaled, axis=-1, keepdims=True)
        - normed * jnp.mean(scaled * normed, axis=-1, keepdims=True)
    )
    return (grad_input, gain_sum, bias_sum)


def times_transposed(left_side, right_side):
    return lax.dot_general(
        left_side, right_side, (((1,), (1,)), ((), ())), preferred_element_type=jnp.float32
    )


def outer_sum(left_side, right_side):
    return lax.dot_general(
        left_side, right_side, (((0,), (0,)), ((), ())), preferred_element_type=jnp.float32
    )


def to_pairs(values):
    token_count = values.shape[0]
    return values.reshape(token_count, HEADS // 2, 2 * HEAD).transpose(1, 0, 2)


def from_pairs(values):
    return values.transpose(1, 0, 2).reshape(values.shape[1], HEADS * HEAD)


def pair_scores(query_pair, key_pair, allowed, score_scale):
    token_count = query_pair.shape[0]
    queries = query_pair.reshape(token_count, 2, HEAD)
    key_rows = key_pair.reshape(token_count, 2, HEAD)
    scores = (
        jnp.einsum("qhd,khd->hqk", queries, key_rows, preferred_element_type=jnp.float32)
        * score_scale
    )
    return (jnp.where(allowed[None], scores, masked_score), queries, key_rows)


def pair_forward(block_item, allowed, score_scale):
    query_pair, key_pair, value_pair = block_item
    token_count = query_pair.shape[0]
    scores, queries, key_rows = pair_scores(query_pair, key_pair, allowed, score_scale)
    row_top = jnp.max(scores, axis=-1, keepdims=True)
    exponent = jnp.exp(scores - row_top)
    row_total = jnp.sum(exponent, axis=-1, keepdims=True)
    probabilities = exponent / row_total
    logsum = row_top[..., 0] + jnp.log(row_total[..., 0])
    value_rows = value_pair.reshape(token_count, 2, HEAD)
    attended = jnp.einsum(
        "hqk,khd->qhd",
        probabilities.astype(jnp.bfloat16),
        value_rows,
        preferred_element_type=jnp.float32,
    )
    return (attended.reshape(token_count, 2 * HEAD), logsum)


def pair_backward(block_item, allowed, score_scale):
    query_pair, key_pair, value_pair, grad_pair, logsum = block_item
    token_count = query_pair.shape[0]
    scores, queries, key_rows = pair_scores(query_pair, key_pair, allowed, score_scale)
    probabilities = jnp.exp(scores - logsum[..., None])
    value_rows = value_pair.reshape(token_count, 2, HEAD)
    grad_rows = grad_pair.reshape(token_count, 2, HEAD)
    grad_probs = jnp.einsum(
        "qhd,khd->hqk", grad_rows, value_rows, preferred_element_type=jnp.float32
    )
    grad_values = jnp.einsum(
        "hqk,qhd->khd",
        probabilities.astype(jnp.bfloat16),
        grad_rows,
        preferred_element_type=jnp.float32,
    )
    grad_scores = probabilities * (
        grad_probs - jnp.sum(grad_probs * probabilities, axis=-1, keepdims=True)
    )
    grad_scores = grad_scores.astype(jnp.bfloat16)
    grad_queries = (
        jnp.einsum("hqk,khd->qhd", grad_scores, key_rows, preferred_element_type=jnp.float32)
        * score_scale
    )
    grad_keys = (
        jnp.einsum("hqk,qhd->khd", grad_scores, queries, preferred_element_type=jnp.float32)
        * score_scale
    )
    return (
        grad_queries.reshape(token_count, 2 * HEAD),
        grad_keys.reshape(token_count, 2 * HEAD),
        grad_values.reshape(token_count, 2 * HEAD),
    )


def layer_forward(hidden_state, weights, cosine_table, sine_table, allowed, score_scale):
    qkv_full, out_full, gate_full, up_full, down_full, gain_one, bias_one, gain_two, bias_two = (
        weights
    )
    token_count, model_width = hidden_state.shape
    state_low = hidden_state.astype(jnp.bfloat16)
    projected = jnp.dot(state_low, qkv_full, preferred_element_type=jnp.float32)
    queries = rotate(
        projected[:, :model_width].reshape(token_count, HEADS, HEAD), cosine_table, sine_table
    )
    queries = queries.astype(jnp.bfloat16).reshape(token_count, model_width)
    key_rows = rotate(
        projected[:, model_width : 2 * model_width].reshape(token_count, HEADS, HEAD),
        cosine_table,
        sine_table,
    )
    key_rows = key_rows.astype(jnp.bfloat16).reshape(token_count, model_width)
    value_rows = projected[:, 2 * model_width :].astype(jnp.bfloat16)

    def attend_pair(block_item):
        return pair_forward(block_item, allowed, score_scale)

    attended_pairs, logsum = lax.map(
        attend_pair, (to_pairs(queries), to_pairs(key_rows), to_pairs(value_rows))
    )
    attended = from_pairs(attended_pairs).astype(jnp.bfloat16)
    branch = jnp.dot(attended, out_full, preferred_element_type=jnp.float32)
    middle, normed_one, inverse_one = norm_forward(
        hidden_state + branch, gain_one.astype(jnp.float32), bias_one.astype(jnp.float32)
    )
    middle_low = middle.astype(jnp.bfloat16)
    gate_pre = jnp.dot(middle_low, gate_full, preferred_element_type=jnp.float32)
    up_pre = jnp.dot(middle_low, up_full, preferred_element_type=jnp.float32)
    activated = (jax.nn.silu(gate_pre) * up_pre).astype(jnp.bfloat16)
    feed = jnp.dot(activated, down_full, preferred_element_type=jnp.float32)
    result, normed_two, inverse_two = norm_forward(
        middle + feed, gain_two.astype(jnp.float32), bias_two.astype(jnp.float32)
    )
    stored = (
        state_low,
        queries,
        key_rows,
        value_rows,
        logsum,
        attended,
        normed_one,
        inverse_one,
        middle_low,
        gate_pre,
        up_pre,
        activated,
        normed_two,
        inverse_two,
    )
    return (result, stored)


def layer_backward(upstream, weights, stored, cosine_table, sine_table, allowed, score_scale):
    qkv_full, out_full, gate_full, up_full, down_full, gain_one, bias_one, gain_two, bias_two = (
        weights
    )
    (
        state_low,
        queries,
        key_rows,
        value_rows,
        logsum,
        attended,
        normed_one,
        inverse_one,
        middle_low,
        gate_pre,
        up_pre,
        activated,
        normed_two,
        inverse_two,
    ) = stored
    token_count, model_width = upstream.shape
    grad_mid, gain_two_sum, bias_two_sum = norm_backward(
        upstream, normed_two, inverse_two, gain_two.astype(jnp.float32)
    )
    grad_feed = grad_mid.astype(jnp.bfloat16)
    down_sum = outer_sum(activated, grad_feed)
    grad_act = times_transposed(grad_feed, down_full)
    sigmoid_gate = jax.nn.sigmoid(gate_pre)
    grad_gate = (grad_act * up_pre * sigmoid_gate * (1.0 + gate_pre * (1.0 - sigmoid_gate))).astype(
        jnp.bfloat16
    )
    grad_up = (grad_act * gate_pre * sigmoid_gate).astype(jnp.bfloat16)
    gate_sum = outer_sum(middle_low, grad_gate)
    up_sum = outer_sum(middle_low, grad_up)
    grad_middle = (
        grad_mid + times_transposed(grad_gate, gate_full) + times_transposed(grad_up, up_full)
    )
    grad_sum, gain_one_sum, bias_one_sum = norm_backward(
        grad_middle, normed_one, inverse_one, gain_one.astype(jnp.float32)
    )
    grad_branch = grad_sum.astype(jnp.bfloat16)
    out_sum = outer_sum(attended, grad_branch)
    grad_attended = times_transposed(grad_branch, out_full).astype(jnp.bfloat16)

    def attend_back(block_item):
        return pair_backward(block_item, allowed, score_scale)

    grad_query_pairs, grad_key_pairs, grad_value_pairs = lax.map(
        attend_back,
        (
            to_pairs(queries),
            to_pairs(key_rows),
            to_pairs(value_rows),
            to_pairs(grad_attended),
            logsum,
        ),
    )
    grad_queries = unrotate(
        from_pairs(grad_query_pairs).reshape(token_count, HEADS, HEAD), cosine_table, sine_table
    ).reshape(token_count, model_width)
    grad_keys = unrotate(
        from_pairs(grad_key_pairs).reshape(token_count, HEADS, HEAD), cosine_table, sine_table
    ).reshape(token_count, model_width)
    grad_projected = jnp.concatenate(
        [grad_queries, grad_keys, from_pairs(grad_value_pairs)], axis=1
    ).astype(jnp.bfloat16)
    qkv_sum = outer_sum(state_low, grad_projected)
    grad_input = grad_sum + times_transposed(grad_projected, qkv_full)
    return (
        grad_input,
        (
            qkv_sum,
            out_sum,
            gate_sum,
            up_sum,
            down_sum,
            gain_one_sum,
            bias_one_sum,
            gain_two_sum,
            bias_two_sum,
        ),
    )


def general(inputs, segment_ids, qkv_weight, out_weight, gate_weight, up_weight, down_weight,
            first_gain, first_bias, second_gain, second_bias, cotangent):
    params = (qkv_weight, out_weight, gate_weight, up_weight, down_weight, first_gain, first_bias, second_gain, second_bias)
    layers = qkv_weight.shape[0]
    segment_row = segment_ids[0]
    cosine_table, sine_table = rotary_tables(positions_of(segment_row))
    allowed = segment_row[:, None] == segment_row[None, :]
    score_scale = 1.0 / math.sqrt(HEAD)
    hidden_state = inputs[0].astype(F32)
    fetched, saved = [], []
    for layer_index in range(layers):
        weights = tuple(lax.all_gather(w[layer_index], "shard", axis=0, tiled=True) for w in params)
        fetched.append(weights)
        hidden_state, stored = layer_forward(hidden_state, weights, cosine_table, sine_table, allowed, score_scale)
        saved.append(stored)
    upstream = cotangent[0].astype(F32)
    shared = [None] * layers
    for layer_index in reversed(range(layers)):
        upstream, gradients = layer_backward(
            upstream, fetched[layer_index], saved[layer_index], cosine_table, sine_table, allowed, score_scale
        )
        owned = [lax.psum_scatter(v, "shard", scatter_dimension=0, tiled=True) for v in gradients]
        shared[layer_index] = [lax.psum(v.astype(BF), "rep").astype(F32) for v in owned]
    stacked = [jnp.stack([shared[layer_index][member] for layer_index in range(layers)]) for member in range(9)]
    return (hidden_state.astype(BF)[None], upstream[None], *stacked)


def special(inputs, segment_ids, qkv_weight, out_weight, gate_weight, up_weight, down_weight,
            first_gain, first_bias, second_gain, second_bias, cotangent):
    staged = prologue(inputs, segment_ids, qkv_weight, out_weight, gate_weight, up_weight, down_weight,
                      first_gain, first_bias, second_gain, second_bias)
    output, *kept, cos, sin = forward_call(staged)
    gin, gug, dng, af = backward_call(cotangent[0], cos, sin, kept)
    output, gin, *gradients = epilogue(output, gin, gug, dng, af)
    return (output[None], gin[None], *gradients)


IN_SPECS = (
    P(("rep", "shard"), None, None), P(("rep", "shard"), None),
) + (P(None, "shard", None),) * 5 + (P(None, "shard"),) * 4 + (P(("rep", "shard"), None, None),)
OUT_SPECS = (P(("rep", "shard"), None, None),) * 2 + (P(None, "shard", None),) * 5 + (P(None, "shard"),) * 4


def solution(mesh):
    fits = dict(mesh.shape) == {"rep": 2, "shard": 2 * G}
    return jax.shard_map(special if fits else general, mesh=mesh, in_specs=IN_SPECS, out_specs=OUT_SPECS, check_vma=False)
```
